32 devices in a mesh: shard: 4 (over z), ctx: 4 (over x, core), tp: 2 (over y).
Axes of the slice: x: 2, y: 2, z: 4, core: 2. Of those that a mesh axis runs over, the one named last changes fastest.
Arguments:
- x_in: bfloat16 [1024, 4, 512], P(('ctx', 'tp'), 'shard'), may hold values from -6 to 6
- w_qkv: bfloat16 [2, 3, 512, 512], P(None, None, 'shard', 'tp'), may hold values from -0.25 to 0.25
- b_qv: bfloat16 [2, 2, 8, 64], P(None, None, 'tp', 'shard'), may hold values from -3 to 3
- w_proj: bfloat16 [2, 512, 512], P(None, 'tp', 'shard'), may hold values from -1.5 to 1.5
- w_fc1: bfloat16 [2, 512, 2048], P(None, 'shard', 'tp'), may hold values from -0.25 to 0.25
- b_fc1: bfloat16 [2, 32, 64], P(None, 'tp', 'shard'), may hold values from -3 to 3
- w_fc2: bfloat16 [2, 2048, 512], P(None, 'tp', 'shard'), may hold values from -0.125 to 0.125
- gains: bfloat16 [2, 2, 512], P(None, None, 'shard'), may hold values from 0.099609375 to 1.8984375
- biases: bfloat16 [2, 4, 512], P(None, None, 'shard'), may hold values from -3 to 3
- cotangent: bfloat16 [1024, 4, 512], P(('ctx', 'tp'), 'shard'), may hold values from -6 to 6
Outputs:
- activations: bfloat16 [1024, 4, 512], P(('ctx', 'tp'), 'shard')
- grad_x: float32 [1024, 4, 512], P(('ctx', 'tp'), 'shard')
- grad_w_qkv: float32 [2, 3, 512, 512], P(None, None, 'shard', 'tp')
- grad_b_qv: float32 [2, 2, 8, 64], P(None, None, 'tp', 'shard')
- grad_w_proj: float32 [2, 512, 512], P(None, 'tp', 'shard')
- grad_w_fc1: float32 [2, 512, 2048], P(None, 'shard', 'tp')
- grad_b_fc1: float32 [2, 32, 64], P(None, 'tp', 'shard')
- grad_w_fc2: float32 [2, 2048, 512], P(None, 'tp', 'shard')
- grad_gains: float32 [2, 2, 512], P(None, None, 'shard')
- grad_biases: float32 [2, 4, 512], P(None, None, 'shard')
The draws below stay inside these ranges and needn't reach their ends.
All inputs are finite; a program needn't handle non-finite values.
Results may differ from the reference program's by a relative error of at most 0.017.
Values may be sent and summed in bfloat16 or wider, within the bound.
No kernel may reach another device: no remote copies, remote signals or barrier semaphores. Data moves between devices by JAX's collectives and lax.ppermute only.
A program may use at most 128 MiB of HBM per device.

```python
import math
import jax
import jax.numpy as jnp
from jax import lax

D = 512
H = 8
HD = 64
FF = 2048
LAYERS = 2
SEQ_LEN = 1024
SEQS = 4


def with_spikes(entries, key, source, target, parts, factor):
    def block_of(position):
        return (jnp.arange(entries.shape[position]) // (entries.shape[position] // parts)).reshape((-1,) + (1,) * (entries.ndim - 1 - position))

    one_side = jax.random.permutation(key, parts)[block_of(target)]
    second = (block_of(target) + parts // 2) % parts
    return jnp.where((block_of(source) == one_side) | (block_of(source) == second), factor * entries, entries)


def block_scale(own_key, shape, split, low, largest):
    level = 1.0
    for axis_at, parts in split:
        steps = jax.random.uniform(jax.random.fold_in(jax.random.fold_in(own_key, 6), axis_at), (parts,), jnp.float32, low / len(split), largest / len(split))
        level = level * jnp.repeat(jnp.exp(steps), shape[axis_at] // parts).reshape((-1,) + (1,) * (len(shape) - 1 - axis_at))
    return level


def centred(rng, shape, scale, most, cuts=(), kind=jnp.bfloat16):
    entries = scale * jax.random.normal(rng, shape, jnp.float32)
    if cuts:
        entries = entries * block_scale(rng, shape, cuts, -0.22, 0.18)
    return jnp.clip(entries, -most, most).astype(kind)


def noise_with(stream_key, shape, deviation, reach, cuts, heavy, kind=jnp.bfloat16):
    entries = deviation * jax.random.normal(stream_key, shape, jnp.float32)
    if cuts:
        entries = entries * block_scale(stream_key, shape, cuts, -0.22, 0.18)
    return jnp.clip(with_spikes(entries, jax.random.fold_in(stream_key, 3), *heavy), -reach, reach).astype(kind)


def setup_inputs(seed: int = 0) -> dict:
    key_of = jax.random.split(jax.random.key(seed), 11)
    x_in = centred(key_of[0], (SEQ_LEN, SEQS, D), 1.0, 6.0, ((0, 8), (1, 4)))
    w_qkv = centred(key_of[1], (LAYERS, 3, D, D), D ** -0.5, 0.25, ((2, 4), (3, 2)))
    b_qv = centred(key_of[2], (LAYERS, 2, H, HD), 0.5, 3.0, ((2, 2), (3, 4)))
    w_proj = centred(key_of[3], (LAYERS, D, D), (D // 32) ** -0.5, 1.5, ((1, 2), (2, 4)))
    w_fc1 = centred(key_of[4], (LAYERS, D, FF), D ** -0.5, 0.25, ((1, 4), (2, 2)))
    b_fc1 = centred(key_of[5], (LAYERS, FF // 64, 64), 0.5, 3.0, ((1, 2), (2, 4)))
    w_fc2 = centred(key_of[6], (LAYERS, FF, D), FF ** -0.5, 0.125, ((1, 2), (2, 4)))
    gains = jnp.clip(1.0 + 0.18 * jax.random.normal(key_of[7], (LAYERS, 2, D), jnp.float32), 0.099609375, 1.8984375).astype(jnp.bfloat16)
    biases = centred(key_of[8], (LAYERS, 4, D), 0.5, 3.0, ((2, 4),))
    cotangent = noise_with(key_of[9], (SEQ_LEN, SEQS, D), 1.0, 6.0, ((0, 8), (1, 4)), (1, 2, 4, 2.0))
    return dict(x_in=x_in, w_qkv=w_qkv, b_qv=b_qv, w_proj=w_proj, w_fc1=w_fc1, b_fc1=b_fc1, w_fc2=w_fc2, gains=gains, biases=biases, cotangent=cotangent)


highest = lax.Precision.HIGHEST
epsilon = 1e-05
masked_value = -1e+30

@jax.custom_vjp
def low(v):
    return lax.optimization_barrier(v.astype(jnp.bfloat16)).astype(jnp.float32)

@jax.custom_vjp
def low_back(v):
    return v

def low_keep(v):
    return (low(v), None)

def low_pass(kept, grad):
    return (grad,)

def back_keep(v):
    return (v, None)

def back_low(kept, grad):
    return (low(grad),)
low.defvjp(low_keep, low_pass)
low_back.defvjp(back_keep, back_low)

def layer_norm(values, gain_row, bias_row):
    center = lax.optimization_barrier(jnp.mean(values, axis=-1, keepdims=True))
    shifted = values - center
    scale_inv = lax.rsqrt(lax.optimization_barrier(jnp.mean(shifted * shifted, axis=-1, keepdims=True)) + epsilon)
    return shifted * scale_inv * gain_row + bias_row

def gelu_tanh(values):
    return jax.nn.gelu(values, approximate=True)

def attention(queries, key_all, value_all):
    length = queries.shape[0]
    block_rows = min(512, length)
    count_blocks = length // block_rows
    scale_factor = queries.shape[-1] ** (-0.5)
    query_blocks = queries.reshape((count_blocks, block_rows) + queries.shape[1:])
    starts = jnp.arange(count_blocks, dtype=jnp.int32) * block_rows

    def one_block(inputs_pair):
        query_block, start_row = inputs_pair
        scores = jnp.einsum('qghe,kghe->ghqk', query_block, key_all, precision=highest) * scale_factor
        scores = low_back(scores)
        query_pos = start_row + jnp.arange(block_rows, dtype=jnp.int32)[:, None]
        key_pos = jnp.arange(length, dtype=jnp.int32)[None, :]
        scores = jnp.where(key_pos <= query_pos, scores, masked_value)
        row_top = lax.optimization_barrier(jnp.max(scores, axis=-1, keepdims=True))
        exponent = jnp.exp(scores - row_top)
        soft_probs = low(exponent / lax.optimization_barrier(jnp.sum(exponent, axis=-1, keepdims=True)))
        return jnp.einsum('ghqk,kghe->qghe', soft_probs, value_all, precision=highest)
    outputs = lax.map(jax.checkpoint(one_block), (query_blocks, starts))
    return outputs.reshape(queries.shape)

def layer_fn(state, w_qkv_l, b_qv_l, w_proj_l, w_fc1_l, b_fc1_l, w_fc2_l, gains_l, biases_l):
    length, group_size, width = state.shape
    heads_all, head_size = (b_qv_l.shape[1], b_qv_l.shape[2])
    normed_in = low(layer_norm(state, gains_l[0], biases_l[0]))
    qkv_bias = jnp.stack([b_qv_l[0].reshape(width), jnp.zeros((width,), state.dtype), b_qv_l[1].reshape(width)])
    qkv_all = jnp.einsum('lgd,cdf->lgcf', normed_in, w_qkv_l, precision=highest) + qkv_bias
    qkv_all = low_back(low(qkv_all))
    qkv_all = qkv_all.reshape(length, group_size, 3, heads_all, head_size)
    attn_out = attention(qkv_all[:, :, 0], qkv_all[:, :, 1], qkv_all[:, :, 2])
    attn_out = low_back(low(attn_out.reshape(length, group_size, width)))
    attn_proj = low_back(jnp.einsum('lgf,fd->lgd', attn_out, w_proj_l, precision=highest))
    middle = state + attn_proj + biases_l[1]
    normed_mid = low(layer_norm(middle, gains_l[1], biases_l[2]))
    pre_act = jnp.einsum('lgd,df->lgf', normed_mid, w_fc1_l, precision=highest) + b_fc1_l.reshape(-1)
    pre_act = low_back(pre_act)
    hidden = low(gelu_tanh(pre_act))
    mlp_out = low_back(jnp.einsum('lgf,fd->lgd', hidden, w_fc2_l, precision=highest))
    return middle + mlp_out + biases_l[3]

def forward(state, params):
    for index in range(LAYERS):
        state = layer_fn(state, *[member[index] for member in params])
    return state

def reference(x_in, w_qkv, b_qv, w_proj, w_fc1, b_fc1, w_fc2, gains, biases, cotangent):
    params = tuple((member.astype(jnp.float32) for member in (w_qkv, b_qv, w_proj, w_fc1, b_fc1, w_fc2, gains, biases)))
    group_size = math.gcd(SEQS, max(1, 4096 // SEQ_LEN))
    count_groups = SEQS // group_size
    inputs_all = x_in.astype(jnp.float32).reshape(SEQ_LEN, count_groups, group_size, D).transpose(1, 0, 2, 3)
    cot_all = cotangent.astype(jnp.float32).reshape(SEQ_LEN, count_groups, group_size, D).transpose(1, 0, 2, 3)

    def step(running, inputs_pair):
        state, cot_group = inputs_pair
        result, pull_back = jax.vjp(forward, state, params)
        grad_state, grad_params = pull_back(cot_group)
        running = tuple((total + extra for total, extra in zip(running, grad_params)))
        return (running, (result.astype(jnp.bfloat16), grad_state))
    zero_grads = tuple((jnp.zeros_like(member) for member in params))
    totals, (results, grad_states) = lax.scan(step, zero_grads, (inputs_all, cot_all))
    activations = results.transpose(1, 0, 2, 3).reshape(SEQ_LEN, SEQS, D)
    grad_x = grad_states.transpose(1, 0, 2, 3).reshape(SEQ_LEN, SEQS, D)
    return (activations, grad_x, totals[0], totals[1], totals[2], totals[3], totals[4], totals[5], totals[6], totals[7])
```

```python
import math

import jax
import jax.numpy as jnp
from jax import lax
from jax.sharding import PartitionSpec as P

epsilon = 1e-05
masked_value = -1e30
lanes = 128
f32 = jnp.float32
bf16 = jnp.bfloat16


def normalize(values):
    center = jnp.mean(values, axis=-1, keepdims=True)
    shifted = values - center
    scale_inv = lax.rsqrt(jnp.mean(shifted * shifted, axis=-1, keepdims=True) + epsilon)
    return (shifted * scale_inv, scale_inv)


def norm_back(grad_norm, normed, scale_inv):
    mean_grad = jnp.mean(grad_norm, axis=-1, keepdims=True)
    mean_prod = jnp.mean(grad_norm * normed, axis=-1, keepdims=True)
    return scale_inv * (grad_norm - mean_grad - normed * mean_prod)


def gelu_tanh(values):
    return jax.nn.gelu(values, approximate=True)


def dot(pattern, left, right):
    return jnp.einsum(pattern, left, right, preferred_element_type=f32)


def to_rows(array):
    rows, columns = array.shape[-2:]
    if columns % lanes or rows % 16:
        return array.reshape(-1, lanes)
    tiles = array.reshape(-1, rows, columns // lanes, lanes)
    return jnp.swapaxes(tiles, 1, 2).reshape(-1, lanes)


def from_rows(packed, shape):
    rows, columns = shape[-2:]
    lead = packed.shape[:-2]
    if columns % lanes or rows % 16:
        return packed.reshape(lead + tuple(shape))
    count = math.prod(shape[:-2])
    tiles = packed.reshape(lead + (count, columns // lanes, rows, lanes))
    return jnp.swapaxes(tiles, -3, -2).reshape(lead + tuple(shape))


def small_rows(arrays):
    flat = jnp.concatenate([array.reshape(-1) for array in arrays])
    size = -(-flat.shape[0] // (64 * lanes)) * 64 * lanes
    return jnp.pad(flat, (0, size - flat.shape[0])).reshape(-1, lanes)


def join(gathered, axis):
    moved = jnp.moveaxis(gathered, 0, axis)
    shape = moved.shape
    return moved.reshape(shape[:axis] + (shape[axis] * shape[axis + 1],) + shape[axis + 2 :])


def split(whole, axis, shards):
    shape = whole.shape
    parts = whole.reshape(shape[:axis] + (shards, shape[axis] // shards) + shape[axis + 1 :])
    return jnp.moveaxis(parts, axis, 0)


def swap_tp(values):
    return lax.ppermute(values, "tp", [(0, 1), (1, 0)])


def swap_core(values):
    return lax.ppermute(values, "ctx", [(0, 1), (1, 0), (2, 3), (3, 2)])


def swap_x(values):
    return lax.ppermute(values, "ctx", [(0, 2), (2, 0), (1, 3), (3, 1)])


def other_half(values):
    half = values.shape[0] // 2
    return jnp.concatenate([values[half:], values[:half]])


def gather_packed(packed, shards):
    quarter = packed.shape[0] // 4
    own = lax.dynamic_slice_in_dim(packed, lax.axis_index("ctx") * quarter, quarter, 0)
    return lax.all_gather(own, ("shard", "ctx"), axis=0, tiled=True).reshape(
        shards, packed.shape[0], lanes
    )


def halves(values, bit):
    half = values.shape[1] // 2
    keep = lax.dynamic_slice_in_dim(values, bit * half, half, 1)
    send = lax.dynamic_slice_in_dim(values, (1 - bit) * half, half, 1)
    return keep, send


def paired(own, other, bit):
    return jnp.where(
        bit == 0, jnp.concatenate([own, other]), jnp.concatenate([other, own])
    )


def reduce_packed(packed):
    place = lax.axis_index("ctx")
    core, chip = place % 2, place // 2
    keep, send = halves(packed, core)
    half = (keep.astype(f32) + swap_core(send).astype(f32)).astype(bf16)
    keep, send = halves(half, chip)
    quarter = (keep.astype(f32) + swap_x(send).astype(f32)).astype(bf16)
    parts = lax.all_to_all(quarter, "shard", split_axis=0, concat_axis=0, tiled=True)
    total = jnp.sum(parts.astype(f32), axis=0).astype(bf16)
    both = paired(total, swap_x(total), chip)
    return paired(both, swap_core(both), core)


def positions(offsets, tp_place, chunk, block):
    half = block // 2
    return chunk * block + (offsets + tp_place * half) % block


def attention_mask(block):
    place, tp_place = lax.axis_index("ctx"), lax.axis_index("tp")
    offsets = jnp.arange(block, dtype=jnp.int32)
    rows = positions(offsets, tp_place, place, block)
    keys = jnp.concatenate([positions(offsets, tp_place, place ^ j, block) for j in range(4)])
    return keys[None, :] <= rows[:, None]


def head_split(values, heads):
    return values.reshape(values.shape[0], heads, values.shape[1] // heads)


def attend(queries, key_all, value_all, mask, heads):
    scale_factor = (queries.shape[1] // heads) ** (-0.5)
    scores = dot("qhe,khe->hqk", head_split(queries, heads), head_split(key_all, heads))
    scores = jnp.where(mask, scores * scale_factor, masked_value)
    row_top = jnp.max(scores, axis=-1, keepdims=True)
    exponent = jnp.exp(scores - row_top)
    totals = jnp.sum(exponent, axis=-1, keepdims=True)
    probs = (exponent / totals).astype(bf16)
    out = dot("hqk,khe->qhe", probs, head_split(value_all, heads))
    return out.reshape(queries.shape).astype(bf16), row_top + jnp.log(totals)


def attend_back(queries, key_all, value_all, mask, heads, log_sums, grad_out):
    scale_factor = (queries.shape[1] // heads) ** (-0.5)
    query_heads, key_heads = head_split(queries, heads), head_split(key_all, heads)
    grad_heads = head_split(grad_out, heads)
    scores = dot("qhe,khe->hqk", query_heads, key_heads)
    scores = jnp.where(mask, scores * scale_factor, masked_value)
    probs = jnp.exp(scores - log_sums)
    grad_probs = dot("qhe,khe->hqk", grad_heads, head_split(value_all, heads))
    row_dot = jnp.sum(probs * grad_probs, axis=-1, keepdims=True)
    grad_scores = (probs * (grad_probs - row_dot)).astype(bf16)
    grad_q = dot("hqk,khe->qhe", grad_scores, key_heads) * scale_factor
    grad_k = dot("hqk,qhe->khe", grad_scores, query_heads) * scale_factor
    grad_v = dot("hqk,qhe->khe", probs.astype(bf16), grad_heads)
    return (
        grad_q.reshape(queries.shape).astype(bf16),
        jnp.concatenate(
            [grad_k.reshape(key_all.shape), grad_v.reshape(key_all.shape)], axis=1
        ).astype(bf16),
    )


def body(x_in, w_qkv, b_qv, w_proj, w_fc1, b_fc1, w_fc2, gains, biases, cotangent):
    depth = w_qkv.shape[0]
    shards = lax.axis_size("shard")
    own_rows, width = x_in.shape[0], x_in.shape[2]
    block = 2 * own_rows
    heads = b_qv.shape[2]
    half_width = w_qkv.shape[3]
    hidden = w_fc1.shape[2]

    small_shapes = [gains.shape, biases.shape, b_qv.shape, b_fc1.shape]
    small = small_rows([gains, biases, b_qv, b_fc1])
    group_a0 = jnp.concatenate([small, to_rows(w_qkv[0])])
    group_b0 = jnp.concatenate([to_rows(w_proj[0]), to_rows(w_fc1[0]), to_rows(w_fc2[0])])
    rest = []
    for index in range(1, depth):
        rest += [to_rows(w_qkv[index]), to_rows(w_proj[index]), to_rows(w_fc1[index]), to_rows(w_fc2[index])]
    group_rest = jnp.concatenate(rest)

    gathered_a0 = gather_packed(group_a0, shards)
    gathered_b0 = gather_packed(group_b0, shards)
    gathered_rest = gather_packed(group_rest, shards)

    def cutter(gathered, start):
        place = [start]

        def take(shape, axis):
            rows = math.prod(shape) // lanes
            piece = from_rows(gathered[:, place[0] : place[0] + rows], shape)
            place[0] += rows
            return join(piece, axis)

        return take

    shape_qkv, shape_proj = w_qkv.shape[1:], w_proj.shape[1:]
    shape_fc1, shape_fc2 = w_fc1.shape[1:], w_fc2.shape[1:]
    take_a, take_b, take_r = cutter(gathered_a0, small.shape[0]), cutter(gathered_b0, 0), cutter(gathered_rest, 0)
    weights = []
    for index in range(depth):
        take_q, take_o = (take_a, take_b) if index == 0 else (take_r, take_r)
        weights.append(
            (take_q(shape_qkv, 1), take_o(shape_proj, 1), take_o(shape_fc1, 0), take_o(shape_fc2, 1))
        )
    flat = gathered_a0[:, : small.shape[0]].reshape(shards, -1)
    vectors, start = [], 0
    for shape in small_shapes:
        size = math.prod(shape)
        piece = flat[:, start : start + size].reshape((shards,) + shape)
        vectors.append(join(piece, len(shape) - 1).astype(f32))
        start += size
    gain_all, bias_all, b_qv_all, b_fc1_all = vectors

    mask = attention_mask(block)
    x_own = x_in[:, 0]
    state = jnp.concatenate([x_own, swap_tp(x_own)]).astype(f32)
    g_own = cotangent[:, 0]
    grad_state = jnp.concatenate([g_own, swap_tp(g_own)]).astype(f32)

    stored = []
    for index in range(depth):
        w_query, w_out, w_first, w_second = weights[index]
        normed_in, scale_in = normalize(state)
        low_in = (normed_in * gain_all[index, 0] + bias_all[index, 0]).astype(bf16)
        bias_q = b_qv_all[index, 0].reshape(half_width)
        bias_v = b_qv_all[index, 1].reshape(half_width)
        queries = (dot("rd,df->rf", low_in, w_query[0]) + bias_q).astype(bf16)
        keys = dot("rd,df->rf", low_in, w_query[1]).astype(bf16)
        values = (dot("rd,df->rf", low_in, w_query[2]) + bias_v).astype(bf16)
        kv_own = jnp.concatenate([keys, values], axis=1)
        kv_chip = swap_x(kv_own)
        kv_all = jnp.concatenate([kv_own, swap_core(kv_own), kv_chip, swap_core(kv_chip)])
        key_all, value_all = kv_all[:, :half_width], kv_all[:, half_width:]
        attn, log_sums = attend(queries, key_all, value_all, mask, heads)
        attn_other = other_half(swap_tp(attn))
        w_out_other = swap_tp(w_out)
        middle = (
            state
            + dot("rf,fd->rd", attn, w_out)
            + dot("rf,fd->rd", attn_other, w_out_other)
            + bias_all[index, 1]
        )
        normed_mid, scale_mid = normalize(middle)
        low_mid = (normed_mid * gain_all[index, 1] + bias_all[index, 2]).astype(bf16)
        pre_act = dot("rd,df->rf", low_mid, w_first) + b_fc1_all[index].reshape(hidden)
        act = gelu_tanh(pre_act).astype(bf16)
        partial = dot("rf,fd->rd", act, w_second)
        if index == depth - 1:
            received = swap_tp(partial[own_rows:].astype(bf16)).astype(f32)
            output = middle[:own_rows] + partial[:own_rows] + received + bias_all[index, 3]
        else:
            received = other_half(swap_tp(partial.astype(bf16))).astype(f32)
            state = middle + partial + received + bias_all[index, 3]
        stored.append(
            (normed_in, scale_in, low_in, queries, key_all, value_all, log_sums, attn,
             normed_mid, scale_mid, low_mid, pre_act, act)
        )
    output = output.astype(bf16)[:, None]

    results = [None] * depth
    for index in reversed(range(depth)):
        w_query, w_out, w_first, w_second = weights[index]
        (normed_in, scale_in, low_in, queries, key_all, value_all, log_sums, attn,
         normed_mid, scale_mid, low_mid, pre_act, act) = stored[index]
        grad_bias_mlp = jnp.sum(grad_state, axis=0)
        grad_low = grad_state.astype(bf16)
        grad_hidden = dot("rd,fd->rf", grad_low, w_second)
        unused, gelu_pull = jax.vjp(gelu_tanh, pre_act)
        grad_pre = gelu_pull(grad_hidden)[0].astype(bf16)
        grad_w_second = dot("rf,rd->fd", act, grad_low)
        grad_w_first = dot("rd,rf->df", low_mid, grad_pre)
        grad_b_first = jnp.sum(grad_pre, axis=0, dtype=f32)
        partial = dot("rf,df->rd", grad_pre, w_first)
        mlp_rows = jnp.concatenate(
            [
                jax.vmap(to_rows)(split(grad_w_first.astype(bf16), 0, shards)),
                jax.vmap(to_rows)(split(grad_w_second.astype(bf16), 1, shards)),
            ],
            axis=1,
        )
        mlp_total = reduce_packed(mlp_rows)
        grad_mid = partial + other_half(swap_tp(partial.astype(bf16))).astype(f32)
        grad_gain_mid = jnp.sum(grad_mid * normed_mid, axis=0)
        grad_beta_mid = jnp.sum(grad_mid, axis=0)
        grad_middle = grad_state + norm_back(grad_mid * gain_all[index, 1], normed_mid, scale_mid)
        grad_bias_attn = jnp.sum(grad_middle, axis=0)
        grad_low = grad_middle.astype(bf16)
        grad_attn = dot("rd,fd->rf", grad_low, w_out).astype(bf16)
        grad_w_out = dot("rf,rd->fd", attn, grad_low)
        grad_q, grad_kv = attend_back(
            queries, key_all, value_all, mask, heads, log_sums, grad_attn
        )
        part = grad_kv.reshape(4, block, 2 * half_width)
        sent = swap_core(jnp.stack([part[1], part[3]])).astype(f32)
        mine = part[0].astype(f32) + sent[0]
        chip = (part[2].astype(f32) + sent[1]).astype(bf16)
        grad_kv = (mine + swap_x(chip).astype(f32)).astype(bf16)
        grad_qkv = jnp.stack([grad_q, grad_kv[:, :half_width], grad_kv[:, half_width:]])
        grad_w_query = dot("rd,crf->cdf", low_in, grad_qkv)
        grad_b_query = jnp.sum(grad_qkv[0::2], axis=1, dtype=f32)
        partial = dot("crf,cdf->rd", grad_qkv, w_query)
        grad_in = partial + other_half(swap_tp(partial.astype(bf16))).astype(f32)
        grad_gain_in = jnp.sum(grad_in * normed_in, axis=0)
        grad_beta_in = jnp.sum(grad_in, axis=0)
        grad_state = grad_middle + norm_back(grad_in * gain_all[index, 0], normed_in, scale_in)

        vectors = [
            jnp.stack([grad_gain_in, grad_gain_mid]),
            jnp.stack([grad_beta_in, grad_bias_attn, grad_beta_mid, grad_bias_mlp]),
            grad_b_query.reshape(2, heads, half_width // heads),
            grad_b_first.reshape(b_fc1_all.shape[1:]),
        ]
        parts = [split(vector, vector.ndim - 1, shards) for vector in vectors]
        part_shapes = [part.shape[1:] for part in parts]
        attn_rows = jnp.concatenate(
            [
                jax.vmap(to_rows)(split(grad_w_query.astype(bf16), 1, shards)),
                jax.vmap(to_rows)(split(grad_w_out.astype(bf16), 1, shards)),
                jax.vmap(lambda *own: small_rows(own))(*parts).astype(bf16),
            ],
            axis=1,
        )
        attn_total = reduce_packed(attn_rows)

        def pieces(total, shapes):
            place, out = 0, []
            for shape in shapes:
                rows = math.prod(shape) // lanes
                out.append(from_rows(total[place : place + rows], shape).astype(f32))
                place += rows
            return out, total[place:].reshape(-1)

        (out_fc1, out_fc2), unused = pieces(mlp_total, [shape_fc1, shape_fc2])
        (out_qkv, out_proj), tail = pieces(attn_total, [shape_qkv, shape_proj])
        small_out, start = [], 0
        for shape in part_shapes:
            size = math.prod(shape)
            small_out.append(tail[start : start + size].reshape(shape).astype(f32))
            start += size
        results[index] = (
            out_qkv, small_out[2], out_proj, out_fc1, small_out[3], out_fc2, small_out[0], small_out[1]
        )
    stacked = tuple(
        jnp.stack([results[index][member] for index in range(depth)]) for member in range(8)
    )
    return (output, grad_state[:own_rows, None]) + stacked


def solution(mesh):
    return jax.shard_map(
        body,
        mesh=mesh,
        in_specs=(
            P(("ctx", "tp"), "shard", None),
            P(None, None, "shard", "tp"),
            P(None, None, "tp", "shard"),
            P(None, "tp", "shard"),
            P(None, "shard", "tp"),
            P(None, "tp", "shard"),
            P(None, "tp", "shard"),
            P(None, None, "shard"),
            P(None, None, "shard"),
            P(("ctx", "tp"), "shard", None),
        ),
        out_specs=(
            P(("ctx", "tp"), "shard", None),
            P(("ctx", "tp"), "shard", None),
            P(None, None, "shard", "tp"),
            P(None, None, "tp", "shard"),
            P(None, "tp", "shard"),
            P(None, "shard", "tp"),
            P(None, "tp", "shard"),
            P(None, "tp", "shard"),
            P(None, None, "shard"),
            P(None, None, "shard"),
        ),
        check_vma=False,
    )
```

```python
import math

import jax
import jax.numpy as jnp
from jax import lax
from jax.experimental import pallas as pl
from jax.experimental.pallas import tpu as pltpu
from jax.sharding import PartitionSpec as P

epsilon = 1e-05
masked_value = -1e30
lanes = 128
f32 = jnp.float32
bf16 = jnp.bfloat16


def normalize(values):
    center = jnp.mean(values, axis=-1, keepdims=True)
    shifted = values - center
    scale_inv = lax.rsqrt(jnp.mean(shifted * shifted, axis=-1, keepdims=True) + epsilon)
    return (shifted * scale_inv, scale_inv)


def norm_back(grad_norm, normed, scale_inv):
    mean_grad = jnp.mean(grad_norm, axis=-1, keepdims=True)
    mean_prod = jnp.mean(grad_norm * normed, axis=-1, keepdims=True)
    return scale_inv * (grad_norm - mean_grad - normed * mean_prod)


def gelu_tanh(values):
    return jax.nn.gelu(values, approximate=True)


def dot(pattern, left, right):
    return jnp.einsum(pattern, left, right, preferred_element_type=f32)


def to_rows(array):
    rows, columns = array.shape[-2:]
    if columns % lanes or rows % 16:
        return array.reshape(-1, lanes)
    tiles = array.reshape(-1, rows, columns // lanes, lanes)
    return jnp.swapaxes(tiles, 1, 2).reshape(-1, lanes)


def from_rows(packed, shape):
    rows, columns = shape[-2:]
    lead = packed.shape[:-2]
    if columns % lanes or rows % 16:
        return packed.reshape(lead + tuple(shape))
    count = math.prod(shape[:-2])
    tiles = packed.reshape(lead + (count, columns // lanes, rows, lanes))
    return jnp.swapaxes(tiles, -3, -2).reshape(lead + tuple(shape))


def small_rows(arrays):
    flat = jnp.concatenate([array.reshape(-1) for array in arrays])
    size = -(-flat.shape[0] // (64 * lanes)) * 64 * lanes
    return jnp.pad(flat, (0, size - flat.shape[0])).reshape(-1, lanes)


def join(gathered, axis):
    moved = jnp.moveaxis(gathered, 0, axis)
    shape = moved.shape
    return moved.reshape(shape[:axis] + (shape[axis] * shape[axis + 1],) + shape[axis + 2 :])


def split(whole, axis, shards):
    shape = whole.shape
    parts = whole.reshape(shape[:axis] + (shards, shape[axis] // shards) + shape[axis + 1 :])
    return jnp.moveaxis(parts, axis, 0)


def swap_tp(values):
    return lax.ppermute(values, "tp", [(0, 1), (1, 0)])


def swap_core(values):
    return lax.ppermute(values, "ctx", [(0, 1), (1, 0), (2, 3), (3, 2)])


def swap_x(values):
    return lax.ppermute(values, "ctx", [(0, 2), (2, 0), (1, 3), (3, 1)])


def other_half(values):
    half = values.shape[0] // 2
    return jnp.concatenate([values[half:], values[:half]])


def gather_packed(packed, shards):
    quarter = packed.shape[0] // 4
    own = lax.dynamic_slice_in_dim(packed, lax.axis_index("ctx") * quarter, quarter, 0)
    return lax.all_gather(own, ("shard", "ctx"), axis=0, tiled=True).reshape(
        shards, packed.shape[0], lanes
    )


def halves(values, bit):
    half = values.shape[1] // 2
    keep = lax.dynamic_slice_in_dim(values, bit * half, half, 1)
    send = lax.dynamic_slice_in_dim(values, (1 - bit) * half, half, 1)
    return keep, send


def paired(own, other, bit):
    return jnp.where(
        bit == 0, jnp.concatenate([own, other]), jnp.concatenate([other, own])
    )


def reduce_packed(packed):
    place = lax.axis_index("ctx")
    core, chip = place % 2, place // 2
    keep, send = halves(packed, core)
    half = (keep.astype(f32) + swap_core(send).astype(f32)).astype(bf16)
    keep, send = halves(half, chip)
    quarter = (keep.astype(f32) + swap_x(send).astype(f32)).astype(bf16)
    parts = lax.all_to_all(quarter, "shard", split_axis=0, concat_axis=0, tiled=True)
    total = jnp.sum(parts.astype(f32), axis=0).astype(bf16)
    both = paired(total, swap_x(total), chip)
    return paired(both, swap_core(both), core)


def positions(offsets, tp_place, chunk, block):
    half = block // 2
    return chunk * block + (offsets + tp_place * half) % block


def attention_mask(block):
    place, tp_place = lax.axis_index("ctx"), lax.axis_index("tp")
    offsets = jnp.arange(block, dtype=jnp.int32)
    rows = positions(offsets, tp_place, place, block)
    keys = jnp.concatenate([positions(offsets, tp_place, place ^ j, block) for j in range(4)])
    return keys[None, :] <= rows[:, None]


def head_split(values, heads):
    return values.reshape(values.shape[0], heads, values.shape[1] // heads)


def attend(queries, key_all, value_all, mask, heads):
    scale_factor = (queries.shape[1] // heads) ** (-0.5)
    scores = dot("qhe,khe->hqk", head_split(queries, heads), head_split(key_all, heads))
    scores = jnp.where(mask, scores * scale_factor, masked_value)
    row_top = jnp.max(scores, axis=-1, keepdims=True)
    exponent = jnp.exp(scores - row_top)
    totals = jnp.sum(exponent, axis=-1, keepdims=True)
    probs = (exponent / totals).astype(bf16)
    out = dot("hqk,khe->qhe", probs, head_split(value_all, heads))
    return out.reshape(queries.shape).astype(bf16), row_top + jnp.log(totals)


def attend_back(queries, key_all, value_all, mask, heads, log_sums, grad_out):
    scale_factor = (queries.shape[1] // heads) ** (-0.5)
    query_heads, key_heads = head_split(queries, heads), head_split(key_all, heads)
    grad_heads = head_split(grad_out, heads)
    scores = dot("qhe,khe->hqk", query_heads, key_heads)
    scores = jnp.where(mask, scores * scale_factor, masked_value)
    probs = jnp.exp(scores - log_sums)
    grad_probs = dot("qhe,khe->hqk", grad_heads, head_split(value_all, heads))
    row_dot = jnp.sum(probs * grad_probs, axis=-1, keepdims=True)
    grad_scores = (probs * (grad_probs - row_dot)).astype(bf16)
    grad_q = dot("hqk,khe->qhe", grad_scores, key_heads) * scale_factor
    grad_k = dot("hqk,qhe->khe", grad_scores, query_heads) * scale_factor
    grad_v = dot("hqk,qhe->khe", probs.astype(bf16), grad_heads)
    return (
        grad_q.reshape(queries.shape).astype(bf16),
        jnp.concatenate(
            [grad_k.reshape(key_all.shape), grad_v.reshape(key_all.shape)], axis=1
        ).astype(bf16),
    )


def body_any(x_in, w_qkv, b_qv, w_proj, w_fc1, b_fc1, w_fc2, gains, biases, cotangent):
    depth = w_qkv.shape[0]
    shards = lax.axis_size("shard")
    own_rows, width = x_in.shape[0], x_in.shape[2]
    block = 2 * own_rows
    heads = b_qv.shape[2]
    half_width = w_qkv.shape[3]
    hidden = w_fc1.shape[2]

    small_shapes = [gains.shape, biases.shape, b_qv.shape, b_fc1.shape]
    small = small_rows([gains, biases, b_qv, b_fc1])
    group_a0 = jnp.concatenate([small, to_rows(w_qkv[0])])
    group_b0 = jnp.concatenate([to_rows(w_proj[0]), to_rows(w_fc1[0]), to_rows(w_fc2[0])])
    rest = []
    for index in range(1, depth):
        rest += [to_rows(w_qkv[index]), to_rows(w_proj[index]), to_rows(w_fc1[index]), to_rows(w_fc2[index])]
    group_rest = jnp.concatenate(rest)

    gathered_a0 = gather_packed(group_a0, shards)
    gathered_b0 = gather_packed(group_b0, shards)
    gathered_rest = gather_packed(group_rest, shards)

    def cutter(gathered, start):
        place = [start]

        def take(shape, axis):
            rows = math.prod(shape) // lanes
            piece = from_rows(gathered[:, place[0] : place[0] + rows], shape)
            place[0] += rows
            return join(piece, axis)

        return take

    shape_qkv, shape_proj = w_qkv.shape[1:], w_proj.shape[1:]
    shape_fc1, shape_fc2 = w_fc1.shape[1:], w_fc2.shape[1:]
    take_a, take_b, take_r = cutter(gathered_a0, small.shape[0]), cutter(gathered_b0, 0), cutter(gathered_rest, 0)
    weights = []
    for index in range(depth):
        take_q, take_o = (take_a, take_b) if index == 0 else (take_r, take_r)
        weights.append(
            (take_q(shape_qkv, 1), take_o(shape_proj, 1), take_o(shape_fc1, 0), take_o(shape_fc2, 1))
        )
    flat = gathered_a0[:, : small.shape[0]].reshape(shards, -1)
    vectors, start = [], 0
    for shape in small_shapes:
        size = math.prod(shape)
        piece = flat[:, start : start + size].reshape((shards,) + shape)
        vectors.append(join(piece, len(shape) - 1).astype(f32))
        start += size
    gain_all, bias_all, b_qv_all, b_fc1_all = vectors

    mask = attention_mask(block)
    x_own = x_in[:, 0]
    state = jnp.concatenate([x_own, swap_tp(x_own)]).astype(f32)
    g_own = cotangent[:, 0]
    grad_state = jnp.concatenate([g_own, swap_tp(g_own)]).astype(f32)

    stored = []
    for index in range(depth):
        w_query, w_out, w_first, w_second = weights[index]
        normed_in, scale_in = normalize(state)
        low_in = (normed_in * gain_all[index, 0] + bias_all[index, 0]).astype(bf16)
        bias_q = b_qv_all[index, 0].reshape(half_width)
        bias_v = b_qv_all[index, 1].reshape(half_width)
        queries = (dot("rd,df->rf", low_in, w_query[0]) + bias_q).astype(bf16)
        keys = dot("rd,df->rf", low_in, w_query[1]).astype(bf16)
        values = (dot("rd,df->rf", low_in, w_query[2]) + bias_v).astype(bf16)
        kv_own = jnp.concatenate([keys, values], axis=1)
        kv_chip = swap_x(kv_own)
        kv_all = jnp.concatenate([kv_own, swap_core(kv_own), kv_chip, swap_core(kv_chip)])
        key_all, value_all = kv_all[:, :half_width], kv_all[:, half_width:]
        attn, log_sums = attend(queries, key_all, value_all, mask, heads)
        attn_other = other_half(swap_tp(attn))
        w_out_other = swap_tp(w_out)
        middle = (
            state
            + dot("rf,fd->rd", attn, w_out)
            + dot("rf,fd->rd", attn_other, w_out_other)
            + bias_all[index, 1]
        )
        normed_mid, scale_mid = normalize(middle)
        low_mid = (normed_mid * gain_all[index, 1] + bias_all[index, 2]).astype(bf16)
        pre_act = dot("rd,df->rf", low_mid, w_first) + b_fc1_all[index].reshape(hidden)
        act = gelu_tanh(pre_act).astype(bf16)
        partial = dot("rf,fd->rd", act, w_second)
        if index == depth - 1:
            received = swap_tp(partial[own_rows:].astype(bf16)).astype(f32)
            output = middle[:own_rows] + partial[:own_rows] + received + bias_all[index, 3]
        else:
            received = other_half(swap_tp(partial.astype(bf16))).astype(f32)
            state = middle + partial + received + bias_all[index, 3]
        stored.append(
            (normed_in, scale_in, low_in, queries, key_all, value_all, log_sums, attn,
             normed_mid, scale_mid, low_mid, pre_act, act)
        )
    output = output.astype(bf16)[:, None]

    results = [None] * depth
    for index in reversed(range(depth)):
        w_query, w_out, w_first, w_second = weights[index]
        (normed_in, scale_in, low_in, queries, key_all, value_all, log_sums, attn,
         normed_mid, scale_mid, low_mid, pre_act, act) = stored[index]
        grad_bias_mlp = jnp.sum(grad_state, axis=0)
        grad_low = grad_state.astype(bf16)
        grad_hidden = dot("rd,fd->rf", grad_low, w_second)
        unused, gelu_pull = jax.vjp(gelu_tanh, pre_act)
        grad_pre = gelu_pull(grad_hidden)[0].astype(bf16)
        grad_w_second = dot("rf,rd->fd", act, grad_low)
        grad_w_first = dot("rd,rf->df", low_mid, grad_pre)
        grad_b_first = jnp.sum(grad_pre, axis=0, dtype=f32)
        partial = dot("rf,df->rd", grad_pre, w_first)
        mlp_rows = jnp.concatenate(
            [
                jax.vmap(to_rows)(split(grad_w_first.astype(bf16), 0, shards)),
                jax.vmap(to_rows)(split(grad_w_second.astype(bf16), 1, shards)),
            ],
            axis=1,
        )
        mlp_total = reduce_packed(mlp_rows)
        grad_mid = partial + other_half(swap_tp(partial.astype(bf16))).astype(f32)
        grad_gain_mid = jnp.sum(grad_mid * normed_mid, axis=0)
        grad_beta_mid = jnp.sum(grad_mid, axis=0)
        grad_middle = grad_state + norm_back(grad_mid * gain_all[index, 1], normed_mid, scale_mid)
        grad_bias_attn = jnp.sum(grad_middle, axis=0)
        grad_low = grad_middle.astype(bf16)
        grad_attn = dot("rd,fd->rf", grad_low, w_out).astype(bf16)
        grad_w_out = dot("rf,rd->fd", attn, grad_low)
        grad_q, grad_kv = attend_back(
            queries, key_all, value_all, mask, heads, log_sums, grad_attn
        )
        part = grad_kv.reshape(4, block, 2 * half_width)
        sent = swap_core(jnp.stack([part[1], part[3]])).astype(f32)
        mine = part[0].astype(f32) + sent[0]
        chip = (part[2].astype(f32) + sent[1]).astype(bf16)
        grad_kv = (mine + swap_x(chip).astype(f32)).astype(bf16)
        grad_qkv = jnp.stack([grad_q, grad_kv[:, :half_width], grad_kv[:, half_width:]])
        grad_w_query = dot("rd,crf->cdf", low_in, grad_qkv)
        grad_b_query = jnp.sum(grad_qkv[0::2], axis=1, dtype=f32)
        partial = dot("crf,cdf->rd", grad_qkv, w_query)
        grad_in = partial + other_half(swap_tp(partial.astype(bf16))).astype(f32)
        grad_gain_in = jnp.sum(grad_in * normed_in, axis=0)
        grad_beta_in = jnp.sum(grad_in, axis=0)
        grad_state = grad_middle + norm_back(grad_in * gain_all[index, 0], normed_in, scale_in)

        vectors = [
            jnp.stack([grad_gain_in, grad_gain_mid]),
            jnp.stack([grad_beta_in, grad_bias_attn, grad_beta_mid, grad_bias_mlp]),
            grad_b_query.reshape(2, heads, half_width // heads),
            grad_b_first.reshape(b_fc1_all.shape[1:]),
        ]
        parts = [split(vector, vector.ndim - 1, shards) for vector in vectors]
        part_shapes = [part.shape[1:] for part in parts]
        attn_rows = jnp.concatenate(
            [
                jax.vmap(to_rows)(split(grad_w_query.astype(bf16), 1, shards)),
                jax.vmap(to_rows)(split(grad_w_out.astype(bf16), 1, shards)),
                jax.vmap(lambda *own: small_rows(own))(*parts).astype(bf16),
            ],
            axis=1,
        )
        attn_total = reduce_packed(attn_rows)

        def pieces(total, shapes):
            place, out = 0, []
            for shape in shapes:
                rows = math.prod(shape) // lanes
                out.append(from_rows(total[place : place + rows], shape).astype(f32))
                place += rows
            return out, total[place:].reshape(-1)

        (out_fc1, out_fc2), unused = pieces(mlp_total, [shape_fc1, shape_fc2])
        (out_qkv, out_proj), tail = pieces(attn_total, [shape_qkv, shape_proj])
        small_out, start = [], 0
        for shape in part_shapes:
            size = math.prod(shape)
            small_out.append(tail[start : start + size].reshape(shape).astype(f32))
            start += size
        results[index] = (
            out_qkv, small_out[2], out_proj, out_fc1, small_out[3], out_fc2, small_out[0], small_out[1]
        )
    stacked = tuple(
        jnp.stack([results[index][member] for index in range(depth)]) for member in range(8)
    )
    return (output, grad_state[:own_rows, None]) + stacked


def compiler_params():
    return pltpu.CompilerParams(vmem_limit_bytes=56 * 2**20)


def whole(array):
    zeros = (0,) * array.ndim
    return pl.BlockSpec(array.shape, lambda i: zeros)


def rows_at(array, rows, start, lead=None, first=0):
    lead = array.shape[0] if lead is None else lead
    return pl.BlockSpec((lead, rows, lanes), lambda i: (first, start // rows, 0))


def run(kernel, outs, place, operands, scratch=(), flops=2**28):
    arrays, specs = [], []
    for operand in operands:
        array, spec = operand if isinstance(operand, tuple) else (operand, whole(operand))
        arrays.append(array)
        specs.append(spec)
    out_shape = [jax.ShapeDtypeStruct(shape, kind) for shape, kind in outs]
    moved = sum(array.size * array.dtype.itemsize for array in arrays)
    return pl.pallas_call(
        kernel,
        grid=(1,),
        out_shape=out_shape,
        in_specs=[pl.BlockSpec(memory_space=pltpu.SMEM)] + specs,
        out_specs=[whole(shape) for shape in out_shape],
        scratch_shapes=list(scratch),
        compiler_params=compiler_params(),
        cost_estimate=pl.CostEstimate(flops=flops, bytes_accessed=moved, transcendentals=0),
    )(place, *arrays)


def mm(left, right):
    return lax.dot_general(left, right, (((1,), (0,)), ((), ())), preferred_element_type=f32)


def mm_nt(left, right):
    return lax.dot_general(left, right, (((1,), (1,)), ((), ())), preferred_element_type=f32)


def mm_tn(left, right):
    return lax.dot_general(left, right, (((0,), (0,)), ((), ())), preferred_element_type=f32)


def lane_join(parts):
    return jnp.concatenate(parts, axis=1)


def row_join(parts):
    return jnp.concatenate(parts, axis=0)


class Pieces:
    def __init__(self, refs):
        self.local, self.far = refs[0], refs[1:]

    def tile(self, k, p, start, rows):
        if k == 0:
            return self.local[p, start : start + rows]
        return self.far[p][k - 1, start : start + rows]


def first_block(pieces, p):
    return row_join(
        [lane_join([pieces.tile(k, p, j * 128, 128) for j in range(2)]) for k in range(4)]
    )


def second_block(pieces, p):
    return lane_join([pieces.tile(k, p, 0, 256) for k in range(4)])


def small_row(small_local, small_far, row):
    parts = [small_local[0, row : row + 1]] + [small_far[k, row : row + 1] for k in range(3)]
    return lane_join(parts).astype(f32)


def spread(small_local, small_far, row, place_z, half, later=None):
    def rows_from(row):
        return row_join(
            [small_local[0, row : row + 1]] + [small_far[k, row : row + 1] for k in range(3)]
        ).astype(f32)

    source = rows_from(row)
    if later is not None:
        source = jnp.where(later == 0, source, rows_from(row + 1))
    source = source.astype(bf16)
    take = lax.broadcasted_iota(jnp.int32, (128, 256), 0)
    lane = lax.broadcasted_iota(jnp.int32, (128, 256), 1)
    wanted = half * 64 + (lane // 64) * 16 + lane % 16
    table = (take == wanted).astype(f32).astype(bf16)
    rows = mm(source, table)
    chunk = lax.broadcasted_iota(jnp.int32, (4, 256), 0)
    lane = lax.broadcasted_iota(jnp.int32, (4, 256), 1)
    keep = (lane % 64) // 16 == (place_z - chunk + 4) % 4
    return jnp.sum(jnp.where(keep, rows, 0.0), axis=0, keepdims=True)


def pack_kernel(kinds, has_small):
    def kernel(place, *refs):
        c = place[1]
        out, send = refs[-2:]
        start = 0
        for ref, kind in zip(refs, kinds):
            for q in range(4):
                to = q ^ c
                if kind == "first":
                    for j in range(2):
                        column = (2 * q + j) * 128
                        out[to, start + j * 128 : start + (j + 1) * 128] = ref[0, :, column : column + 128]
                elif kind == "second":
                    out[to, start : start + 256] = ref[0, q * 256 : (q + 1) * 256]
                elif kind == "proj":
                    out[to, start : start + 64] = ref[0, q * 64 : (q + 1) * 64]
                elif kind == "qkv":
                    for tile in range(6):
                        row = start + tile * 32
                        column = (tile % 2) * 128
                        out[to, row : row + 32] = ref[0, tile // 2, q * 32 : (q + 1) * 32, column : column + 128]
                else:
                    out[to, start : start + 32] = ref[...]
            start += kind_rows[kind]
        send[...] = out[0]

    return kernel


kind_rows = {"first": 256, "second": 256, "proj": 64, "qkv": 192, "small": 32}


def pack(place, kinds, arrays, index):
    rows = sum(kind_rows[kind] for kind in kinds)
    operands = []
    for kind, array in zip(kinds, arrays):
        if kind == "small":
            operands.append(array)
        else:
            block = (1,) + array.shape[1:]
            at = (index,) + (0,) * (array.ndim - 1)
            operands.append((array, pl.BlockSpec(block, lambda i, at=at: at)))
    return run(
        pack_kernel(kinds, False), [((4, rows, lanes), bf16), ((rows, lanes), bf16)], place, operands, flops=2**20
    )


def shift(values, step):
    return lax.ppermute(values, "shard", [(z, (z + step) % 4) for z in range(4)])


def spread_group(local, send):
    far = jnp.stack([shift(send, k) for k in (1, 2, 3)])
    far_chip = swap_x(far)
    return [local, far, swap_core(far), far_chip, swap_core(far_chip)]


def pieces_of(group, rows, start):
    return [(array, rows_at(array, rows, start)) for array in group]


def small_of(group):
    return [(group[0], rows_at(group[0], 32, 192, lead=1)), (group[1], rows_at(group[1], 32, 192))]


def query_kernel(index, first_layer):
    def kernel(place, *refs):
        c = place[1]
        if first_layer:
            own, peer, small_local, small_far = refs[:4]
            pieces = Pieces(refs[4:9])
            state_out, low_out, q_out, kv_out, w_out = refs[9:]
            state = row_join([own[...], peer[...]]).astype(f32)
        else:
            middle, mine, other, small_local, small_far = refs[:5]
            pieces = Pieces(refs[5:10])
            state_out, low_out, q_out, kv_out, w_out = refs[10:]
            received = row_join([other[128:], other[:128]])
            state = (
                middle[...]
                + mine[...].astype(f32)
                + received.astype(f32)
                + small_row(small_local, small_far, 4 + 4 * (index - 1) + 3)
            )
        for k in range(4):
            for p in range(4):
                for tile in range(6):
                    w_out[k, p ^ c, :, tile * 128 : (tile + 1) * 128] = pieces.tile(k, p, tile * 32, 32)
        state_out[...] = state
        normed, scale = normalize(state)
        low = (
            normed * small_row(small_local, small_far, 2 * index)
            + small_row(small_local, small_far, 4 + 4 * index)
        ).astype(bf16)
        low_out[...] = low
        w_all = w_out[...].reshape(512, 768)
        row = 12 + index
        bias_q = spread(small_local, small_far, row, place[0], 0)
        bias_v = spread(small_local, small_far, row, place[0], 1)
        kv_out[:, :256] = mm(low, w_all[:, 256:512]).astype(bf16)
        kv_out[:, 256:] = (mm(low, w_all[:, 512:]) + bias_v).astype(bf16)
        q_out[...] = (mm(low, w_all[:, :256]) + bias_q).astype(bf16)

    return kernel


def seen(place, j):
    c, t = place[1], place[2]
    if j:
        return None
    row = lax.broadcasted_iota(jnp.int32, (256, 256), 0) ^ (t * 128)
    key = lax.broadcasted_iota(jnp.int32, (256, 256), 1) ^ (t * 128)
    return key <= row


def masked_scores(query, chunks, own_mask, place):
    parts = []
    for j in range(4):
        scores = mm_nt(query, chunks[j]) * 0.125
        if j == 0:
            scores = jnp.where(own_mask, scores, masked_value)
        else:
            scores = jnp.where((place[1] ^ j) < place[1], scores, masked_value)
        parts.append(scores)
    return parts


def attend_kernel(place, *refs):
    c = place[1]
    q, chunks = refs[0], refs[1:5]
    pieces = Pieces(refs[5:10])
    attn_out, lse_out, partial_out, w_out = refs[10:]
    for k in range(4):
        for p in range(4):
            w_out[p ^ c, :, k * 128 : (k + 1) * 128] = pieces.tile(k, p, 0, 64)
    own_mask = seen(place, 0)
    results = []
    for head in range(4):
        low, high = head * 64, (head + 1) * 64
        parts = masked_scores(q[:, low:high], [chunk[:, low:high] for chunk in chunks], own_mask, place)
        scores = lane_join(parts)
        top = jnp.max(scores, axis=1, keepdims=True)
        exponent = jnp.exp(scores - top)
        total = jnp.sum(exponent, axis=1, keepdims=True)
        values = row_join([chunk[:, 256 + low : 256 + high] for chunk in chunks])
        results.append(mm(exponent.astype(bf16), values) / total)
        lse_out[:, head : head + 1] = top + jnp.log(total)
    attn = lane_join(results).astype(bf16)
    attn_out[...] = attn
    partial_out[...] = mm(attn, w_out[...].reshape(256, 512)).astype(bf16)


def mlp_kernel(index):
    def kernel(place, *refs):
        state, mine, other, small_local, small_far = refs[:5]
        first, second = Pieces(refs[5:10]), Pieces(refs[10:15])
        middle_out, low_out, pre_out, partial_out = refs[15:]
        received = row_join([other[128:], other[:128]])
        middle = (
            state[...]
            + mine[...].astype(f32)
            + received.astype(f32)
            + small_row(small_local, small_far, 4 + 4 * index + 1)
        )
        middle_out[...] = middle
        normed, scale = normalize(middle)
        low = (
            normed * small_row(small_local, small_far, 2 * index + 1)
            + small_row(small_local, small_far, 4 + 4 * index + 2)
        ).astype(bf16)
        low_out[...] = low
        total = None
        for p in range(4):
            q = p ^ place[1]
            bias = spread(small_local, small_far, 14 + 2 * index, place[0], q % 2, q // 2)
            pre = mm(low, first_block(first, p)) + bias
            pre_out[:, p * 256 : (p + 1) * 256] = pre
            act = gelu_tanh(pre).astype(bf16)
            part = mm(act, second_block(second, p))
            total = part if total is None else total + part
        partial_out[...] = total.astype(bf16)

    return kernel


root = math.sqrt(2 / math.pi)


def mlp_back(grad, pre_ref, low_ref, first, second, place, outs):
    partial_out, bias_out, b_first_out, keep, send = outs
    grad_low = grad.astype(bf16)
    bias_out[...] = jnp.sum(grad, axis=0, keepdims=True)
    total = None
    for p in range(4):
        pre = pre_ref[:, p * 256 : (p + 1) * 256]
        square = pre * pre
        wave = jnp.tanh(root * pre * (1 + 0.044715 * square))
        half = 0.5 * (1 + wave)
        act = (pre * half).astype(bf16)
        slope = half + 0.5 * pre * (1 - wave * wave) * root * (1 + 3 * 0.044715 * square)
        w_second = second_block(second, p)
        grad_pre = mm_nt(grad_low, w_second) * slope
        grad_pre_low = grad_pre.astype(bf16)
        b_first_out[p ^ place[1]] = jnp.sum(grad_pre_low.astype(f32), axis=0, keepdims=True)
        part = mm_nt(grad_pre_low, first_block(first, p))
        total = part if total is None else total + part
        to = keep if p % 2 == 0 else send
        grad_first = mm_tn(low_ref[...], grad_pre_low).astype(bf16)
        grad_second = mm_tn(act, grad_low).astype(bf16)
        for k in range(4):
            for j in range(2):
                to[p // 2, k, j * 128 : (j + 1) * 128] = grad_first[
                    k * 128 : (k + 1) * 128, j * 128 : (j + 1) * 128
                ]
            to[p // 2, k, 256:512] = grad_second[:, k * 128 : (k + 1) * 128]
    partial_out[...] = total.astype(bf16)


def norm_step(grad_out, gain, values):
    normed, scale = normalize(values)
    sums = row_join(
        [
            jnp.sum(grad_out * normed, axis=0, keepdims=True),
            jnp.sum(grad_out, axis=0, keepdims=True),
        ]
    )
    return norm_back(grad_out * gain, normed, scale), sums


def received_sum(mine, other):
    return mine[...].astype(f32) + row_join([other[128:], other[:128]]).astype(f32)


def top_kernel(place, *refs):
    own, peer, pre, low = refs[:4]
    first, second = Pieces(refs[4:9]), Pieces(refs[9:14])
    grad_out = refs[14]
    grad = row_join([own[...], peer[...]]).astype(f32)
    grad_out[...] = grad
    mlp_back(grad, pre, low, first, second, place, refs[15:])


def lower_kernel(index):
    def kernel(place, *refs):
        grad_mid, mine, other, state, small_local, small_far, pre, low = refs[:8]
        first, second = Pieces(refs[8:13]), Pieces(refs[13:18])
        grad_out, sums_out = refs[18:20]
        grad, sums = norm_step(
            received_sum(mine, other), small_row(small_local, small_far, 2 * (index + 1)), state[...]
        )
        sums_out[...] = sums
        grad = grad_mid[...] + grad
        grad_out[...] = grad
        mlp_back(grad, pre, low, first, second, place, refs[20:])

    return kernel


def attend_back_kernel(index):
    def kernel(place, *refs):
        mine, other, middle, grad_state, small_local, small_far = refs[:6]
        attn, w_out, q = refs[6:9]
        chunks, lse = refs[9:13], refs[13]
        grad_out, sums_out, gw_out, dq_out, keep, send = refs[14:]
        grad, sums = norm_step(
            received_sum(mine, other), small_row(small_local, small_far, 2 * index + 1), middle[...]
        )
        grad = grad_state[...] + grad
        grad_out[...] = grad
        sums_out[0:2] = sums
        sums_out[2:3] = jnp.sum(grad, axis=0, keepdims=True)
        grad_low = grad.astype(bf16)
        grad_attn = mm_nt(grad_low, w_out[...].reshape(256, 512)).astype(bf16)
        gw_out[...] = mm_tn(attn[...], grad_low).astype(bf16).reshape(4, 64, 512)
        own_mask = seen(place, 0)
        dq_all = []
        dk_all = [[] for j in range(4)]
        dv_all = [[] for j in range(4)]
        for head in range(4):
            low, high = head * 64, (head + 1) * 64
            query, grad_head = q[:, low:high], grad_attn[:, low:high]
            keys = [chunk[:, low:high] for chunk in chunks]
            row_dot = jnp.sum(
                grad_head.astype(f32) * attn[:, low:high].astype(f32), axis=1, keepdims=True
            )
            log_sum = lse[:, head : head + 1]
            parts = masked_scores(query, keys, own_mask, place)
            dq = None
            for j in range(4):
                probs = jnp.exp(parts[j] - log_sum)
                grad_probs = mm_nt(grad_head, chunks[j][:, 256 + low : 256 + high])
                grad_scores = (probs * (grad_probs - row_dot)).astype(bf16)
                part = mm(grad_scores, keys[j])
                dq = part if dq is None else dq + part
                dk_all[j].append(mm_tn(grad_scores, query) * 0.125)
                dv_all[j].append(mm_tn(probs.astype(bf16), grad_head))
            dq_all.append(dq * 0.125)
        dq_out[...] = lane_join(dq_all).astype(bf16)
        for j in range(4):
            to = keep if j % 2 == 0 else send
            to[j // 2, :, :256] = lane_join(dk_all[j]).astype(bf16)
            to[j // 2, :, 256:] = lane_join(dv_all[j]).astype(bf16)

    return kernel


def halve_kernel(place, *refs):
    count = (len(refs) - 2) // 2
    own_out, send_out = refs[-2:]
    for group in range(count):
        keep, got = refs[2 * group], refs[2 * group + 1]
        lead = len(keep.shape) == 4
        start = 0 if not lead else sum(refs[2 * g].shape[2] for g in range(group))
        for half, out in ((0, own_out), (1, send_out)):
            total = (keep[half].astype(f32) + got[half].astype(f32)).astype(bf16)
            if lead:
                out[:, start : start + keep.shape[2]] = total
            else:
                out[...] = total


def query_back_kernel(place, *refs):
    dq, dkv, got, low, w_ref, gw_ref = refs[:6]
    partial_out, b_out, keep, send, scratch = refs[6:]
    c = place[1]
    grad_kv = (dkv[...].astype(f32) + got[...].astype(f32)).astype(bf16)
    grad_qkv = lane_join([dq[...], grad_kv])
    partial_out[...] = mm_nt(grad_qkv, w_ref[...].reshape(512, 768)).astype(bf16)
    b_out[0:1] = jnp.sum(dq[...].astype(f32), axis=0, keepdims=True)
    b_out[1:2] = jnp.sum(grad_kv[:, 256:].astype(f32), axis=0, keepdims=True)
    scratch[...] = mm_tn(low[...], grad_qkv).astype(bf16).reshape(4, 4, 32, 768)
    for p in range(4):
        to = keep if p % 2 == 0 else send
        for k in range(4):
            for tile in range(6):
                to[p // 2, k, tile * 32 : (tile + 1) * 32] = scratch[
                    k, p ^ c, :, tile * 128 : (tile + 1) * 128
                ]
            to[p // 2, k, 192:256] = gw_ref[p ^ c, :, k * 128 : (k + 1) * 128]


def quarter_kernel(place, own, got, *outs):
    for k in range(4):
        outs[k][...] = (own[k].astype(f32) + got[k].astype(f32)).astype(bf16)


def total_kernel(place, own, one, two, three, out):
    total = own[...].astype(f32) + one[...].astype(f32)
    out[...] = (total + (two[...].astype(f32) + three[...].astype(f32))).astype(bf16)


def reduce_groups(place, groups):
    operands = []
    for keep, send in groups:
        operands += [keep, swap_core(send)]
    rows = sum(keep.shape[2] for keep, send in groups)
    own, send = run(halve_kernel, [((4, rows, lanes), bf16)] * 2, place, operands, flops=2**20)
    parts = run(quarter_kernel, [((rows, lanes), bf16)] * 4, place, [own, swap_x(send)], flops=2**20)
    got = [shift(parts[k], 4 - k) for k in (1, 2, 3)]
    (total,) = run(total_kernel, [((rows, lanes), bf16)], place, [parts[0]] + got, flops=2**20)
    chip = swap_x(total)
    return [total, swap_core(total), chip, swap_core(chip)]


def hidden_out_kernel(starts):
    def kernel(place, *refs):
        c = place[1]
        first_out, second_out, scratch = refs[-3:]
        for layer in range(2):
            for p in range(4):
                scratch[p] = refs[4 * layer + p][starts[layer] : starts[layer] + 512].astype(f32)
            for q in range(4):
                for j in range(2):
                    column = (2 * q + j) * 128
                    first_out[layer, :, column : column + 128] = scratch[q ^ c, j * 128 : (j + 1) * 128]
                second_out[layer, q * 256 : (q + 1) * 256] = scratch[q ^ c, 256:]

    return kernel


def heads_out_kernel(starts):
    def kernel(place, *refs):
        c = place[1]
        qkv_out, proj_out, scratch = refs[-3:]
        for layer in range(2):
            for p in range(4):
                scratch[p] = refs[4 * layer + p][starts[layer] : starts[layer] + 256].astype(f32)
            for q in range(4):
                for tile in range(6):
                    column = (tile % 2) * 128
                    qkv_out[layer, tile // 2, q * 32 : (q + 1) * 32, column : column + 128] = scratch[
                        q ^ c, tile * 32 : (tile + 1) * 32
                    ]
                proj_out[layer, q * 64 : (q + 1) * 64] = scratch[q ^ c, 192:]

    return kernel


def last_kernel(place, *refs):
    grad_mid, mine, other, state, small_local, small_far = refs[:6]
    sums_in = refs[6]
    sums_mid, bias_mlp, b_query, b_first = refs[7:9], refs[9:11], refs[11:13], refs[13:15]
    grad_out, out = refs[15:]
    grad, sums = norm_step(received_sum(mine, other), small_row(small_local, small_far, 0), state[...])
    grad_out[...] = grad_mid[:128] + grad[:128]
    for layer in range(2):
        inner = sums if layer == 0 else sums_in[...]
        mid = sums_mid[layer]
        rows = [
            (2 * layer, inner[0:1]),
            (2 * layer + 1, mid[0:1]),
            (4 + 4 * layer, inner[1:2]),
            (5 + 4 * layer, mid[2:3]),
            (6 + 4 * layer, mid[1:2]),
            (7 + 4 * layer, bias_mlp[layer][...]),
        ]
        for k in range(4):
            for row, value in rows:
                out[k, row : row + 1] = value[:, k * 128 : (k + 1) * 128]
            for channel in range(2):
                for j in range(2):
                    row = 12 + 4 * layer + 2 * channel + j
                    out[k, row : row + 1] = b_query[layer][channel : channel + 1, j * 128 : (j + 1) * 128]
            for q in range(4):
                for j in range(2):
                    row = 20 + 8 * layer + 2 * q + j
                    out[k, row : row + 1] = b_first[layer][q, :, j * 128 : (j + 1) * 128]
    out[:, 36:] = jnp.zeros((4, 4, lanes), f32)


def turn(values, place_z, back):
    rows = values.shape[0]
    chunks = values.reshape(rows, 4, lanes)
    order = (place_z - jnp.arange(4)) % 4
    return jnp.concatenate(
        [lax.dynamic_slice_in_dim(values, order[k] * lanes, lanes, 1) for k in range(4)], axis=1
    )


def body_four(x_in, w_qkv, b_qv, w_proj, w_fc1, b_fc1, w_fc2, gains, biases, cotangent):
    z, c, t = lax.axis_index("shard"), lax.axis_index("ctx"), lax.axis_index("tp")
    place = jnp.stack([z, c, t]).astype(jnp.int32)
    flat = jnp.concatenate([array.reshape(-1) for array in (gains, biases, b_qv, b_fc1)])
    small = jnp.pad(flat, (0, 32 * lanes - flat.shape[0])).reshape(32, lanes)

    group_a0 = spread_group(*pack(place, ("qkv", "small"), (w_qkv, small), 0))
    x_own = turn(x_in[:, 0], z, False)
    x_peer = swap_tp(x_own)
    kinds = ("first", "second", "proj", "qkv")
    group_b0 = spread_group(*pack(place, kinds[:3], (w_fc1, w_fc2, w_proj), 0))
    group_1 = spread_group(*pack(place, kinds, (w_fc1, w_fc2, w_proj, w_qkv), 1))
    g_own = turn(cotangent[:, 0], z, False)
    g_peer = swap_tp(g_own)

    small_parts = small_of(group_a0)
    parts = {
        "qkv": (pieces_of(group_a0, 192, 0), pieces_of(group_1, 192, 576)),
        "proj": (pieces_of(group_b0, 64, 512), pieces_of(group_1, 64, 512)),
        "first": (pieces_of(group_b0, 256, 0), pieces_of(group_1, 256, 0)),
        "second": (pieces_of(group_b0, 256, 256), pieces_of(group_1, 256, 256)),
    }
    square, wide = (256, 512), (256, 256)
    saved = []
    for layer in range(2):
        source = [x_own, x_peer] if layer == 0 else [middle, partial, swap_tp(partial)]
        state, low_in, q, kv, w_all = run(
            query_kernel(layer, layer == 0),
            [(square, f32), (square, bf16), (wide, bf16), (square, bf16), ((4, 4, 32, 768), bf16)],
            place,
            source + small_parts + parts["qkv"][layer],
        )
        kv_chip = swap_x(kv)
        chunks = [kv, swap_core(kv), kv_chip, swap_core(kv_chip)]
        attn, lse, partial, w_out = run(
            attend_kernel,
            [(wide, bf16), ((256, lanes), f32), (square, bf16), ((4, 64, 512), bf16)],
            place,
            [q] + chunks + parts["proj"][layer],
        )
        middle, low_mid, pre, partial = run(
            mlp_kernel(layer),
            [(square, f32), (square, bf16), ((256, 1024), f32), (square, bf16)],
            place,
            [state, partial, swap_tp(partial)] + small_parts + parts["first"][layer] + parts["second"][layer],
        )
        saved.append((state, low_in, q, chunks, w_all, attn, lse, w_out, middle, low_mid, pre))

    received = swap_tp(partial[128:]).astype(f32)
    output = None
    bias_last = jnp.concatenate([small_parts[0][0][0, 203:204], small_parts[1][0][:, 203]]).reshape(1, 512)
    output = middle[:128] + partial[:128].astype(f32) + received + bias_last.astype(f32)
    output = turn(output.astype(bf16), z, True)[:, None]

    hidden_outs = [
        (square, bf16),
        ((1, 512), f32),
        ((4, 1, 256), f32),
        ((2, 4, 512, lanes), bf16),
        ((2, 4, 512, lanes), bf16),
    ]
    totals, sums_mid, bias_mlp, b_query, b_first, waiting = {}, [0, 0], [0, 0], [0, 0], [0, 0], []
    for layer in (1, 0):
        state, low_in, q, chunks, w_all, attn, lse, w_out, middle, low_mid, pre = saved[layer]
        tail = [pre, low_mid] + parts["first"][layer] + parts["second"][layer]
        if layer == 1:
            grad_state, partial, bias_mlp[1], b_first[1], keep, send = run(
                top_kernel, [(square, f32)] + hidden_outs, place, [g_own, g_peer] + tail
            )
        else:
            grad_state, sums_in, partial, bias_mlp[0], b_first[0], keep, send = run(
                lower_kernel(0),
                [(square, f32), ((2, 512), f32)] + hidden_outs,
                place,
                [grad_mid, partial, swap_tp(partial), saved[1][0]] + small_parts + tail,
            )
        totals[layer] = reduce_groups(place, [(keep, send)] + waiting)
        grad_mid, sums_mid[layer], gw_out, dq, keep, send = run(
            attend_back_kernel(layer),
            [
                (square, f32),
                ((3, 512), f32),
                ((4, 64, 512), bf16),
                (wide, bf16),
                ((2, 256, 512), bf16),
                ((2, 256, 512), bf16),
            ],
            place,
            [partial, swap_tp(partial), middle, grad_state] + small_parts + [attn, w_out, q] + chunks + [lse],
        )
        dkv, chip = run(halve_kernel, [(square, bf16)] * 2, place, [keep, swap_core(send)], flops=2**20)
        partial, b_query[layer], keep, send = run(
            query_back_kernel,
            [
                (square, bf16),
                ((2, 256), f32),
                ((2, 4, 256, lanes), bf16),
                ((2, 4, 256, lanes), bf16),
            ],
            place,
            [dq, dkv, swap_x(chip), low_in, w_all, gw_out],
            scratch=[pltpu.VMEM((4, 4, 32, 768), bf16)],
        )
        waiting = [(keep, send)]
    last_total = reduce_groups(place, waiting)
    grad_x, sums = run(
        last_kernel,
        [((128, 512), f32), ((4, 40, lanes), f32)],
        place,
        [grad_mid, partial, swap_tp(partial), saved[0][0]]
        + small_parts
        + [sums_in]
        + sums_mid
        + bias_mlp
        + b_query
        + b_first,
    )
    grad_x = turn(grad_x, z, True)[:, None]
    sums = sums + swap_core(sums)
    sums = sums + swap_x(sums)
    got = [shift(sums[k], 4 - k) for k in (1, 2, 3)]
    total = sums[0] + got[0] + got[1] + got[2]
    grad_gains = total[:4].reshape(gains.shape)
    grad_biases = total[4:12].reshape(biases.shape)
    rest_q = total[12:20].reshape(2, 2, 4, 64)
    rest_f = total[20:36].reshape(2, 16, 64)
    grad_b_qv = lax.dynamic_slice_in_dim(rest_q, z * 16, 16, 3)
    grad_b_fc1 = lax.dynamic_slice_in_dim(rest_f, z * 16, 16, 2)

    grad_fc1, grad_fc2 = run(
        hidden_out_kernel((0, 0)),
        [(w_fc1.shape, f32), (w_fc2.shape, f32)],
        place,
        totals[0] + totals[1],
        scratch=[pltpu.VMEM((4, 512, lanes), f32)],
        flops=2**20,
    )
    grad_qkv, grad_proj = run(
        heads_out_kernel((0, 512)),
        [(w_qkv.shape, f32), (w_proj.shape, f32)],
        place,
        last_total + totals[0],
        scratch=[pltpu.VMEM((4, 256, lanes), f32)],
        flops=2**20,
    )
    return (
        output, grad_x, grad_qkv, grad_b_qv, grad_proj, grad_fc1, grad_b_fc1, grad_fc2, grad_gains, grad_biases
    )


def body(*args):
    x_in, w_qkv, b_qv, w_proj, w_fc1 = args[:5]
    expected = ((128, 1, 512), (2, 3, 128, 256), (2, 2, 4, 16), (2, 256, 128), (2, 128, 1024))
    sizes = (lax.axis_size("shard"), lax.axis_size("ctx"), lax.axis_size("tp"))
    shapes = tuple(array.shape for array in (x_in, w_qkv, b_qv, w_proj, w_fc1))
    if sizes == (4, 4, 2) and shapes == expected:
        return body_four(*args)
    return body_any(*args)


def solution(mesh):
    return jax.shard_map(
        body,
        mesh=mesh,
        in_specs=(
            P(("ctx", "tp"), "shard", None),
            P(None, None, "shard", "tp"),
            P(None, None, "tp", "shard"),
            P(None, "tp", "shard"),
            P(None, "shard", "tp"),
            P(None, "tp", "shard"),
            P(None, "tp", "shard"),
            P(None, None, "shard"),
            P(None, None, "shard"),
            P(("ctx", "tp"), "shard", None),
        ),
        out_specs=(
            P(("ctx", "tp"), "shard", None),
            P(("ctx", "tp"), "shard", None),
            P(None, None, "shard", "tp"),
            P(None, None, "tp", "shard"),
            P(None, "tp", "shard"),
            P(None, "shard", "tp"),
            P(None, "tp", "shard"),
            P(None, "tp", "shard"),
            P(None, None, "shard"),
            P(None, None, "shard"),
        ),
        check_vma=False,
    )
```

```python
import math

import jax
import jax.numpy as jnp
from jax import lax
from jax.experimental import pallas as pl
from jax.experimental.pallas import tpu as pltpu
from jax.sharding import PartitionSpec as P

epsilon = 1e-05
masked_value = -1e30
lanes = 128
f32 = jnp.float32
bf16 = jnp.bfloat16


def normalize(values):
    center = jnp.mean(values, axis=-1, keepdims=True)
    shifted = values - center
    scale_inv = lax.rsqrt(jnp.mean(shifted * shifted, axis=-1, keepdims=True) + epsilon)
    return (shifted * scale_inv, scale_inv)


def norm_back(grad_norm, normed, scale_inv):
    mean_grad = jnp.mean(grad_norm, axis=-1, keepdims=True)
    mean_prod = jnp.mean(grad_norm * normed, axis=-1, keepdims=True)
    return scale_inv * (grad_norm - mean_grad - normed * mean_prod)


def gelu_tanh(values):
    return jax.nn.gelu(values, approximate=True)


def dot(pattern, left, right):
    return jnp.einsum(pattern, left, right, preferred_element_type=f32)


def to_rows(array):
    rows, columns = array.shape[-2:]
    if columns % lanes or rows % 16:
        return array.reshape(-1, lanes)
    tiles = array.reshape(-1, rows, columns // lanes, lanes)
    return jnp.swapaxes(tiles, 1, 2).reshape(-1, lanes)


def from_rows(packed, shape):
    rows, columns = shape[-2:]
    lead = packed.shape[:-2]
    if columns % lanes or rows % 16:
        return packed.reshape(lead + tuple(shape))
    count = math.prod(shape[:-2])
    tiles = packed.reshape(lead + (count, columns // lanes, rows, lanes))
    return jnp.swapaxes(tiles, -3, -2).reshape(lead + tuple(shape))


def small_rows(arrays):
    flat = jnp.concatenate([array.reshape(-1) for array in arrays])
    size = -(-flat.shape[0] // (64 * lanes)) * 64 * lanes
    return jnp.pad(flat, (0, size - flat.shape[0])).reshape(-1, lanes)


def join(gathered, axis):
    moved = jnp.moveaxis(gathered, 0, axis)
    shape = moved.shape
    return moved.reshape(shape[:axis] + (shape[axis] * shape[axis + 1],) + shape[axis + 2 :])


def split(whole, axis, shards):
    shape = whole.shape
    parts = whole.reshape(shape[:axis] + (shards, shape[axis] // shards) + shape[axis + 1 :])
    return jnp.moveaxis(parts, axis, 0)


def swap_tp(values):
    return lax.ppermute(values, "tp", [(0, 1), (1, 0)])


def swap_core(values):
    return lax.ppermute(values, "ctx", [(0, 1), (1, 0), (2, 3), (3, 2)])


def swap_x(values):
    return lax.ppermute(values, "ctx", [(0, 2), (2, 0), (1, 3), (3, 1)])


def other_half(values):
    half = values.shape[0] // 2
    return jnp.concatenate([values[half:], values[:half]])


def gather_packed(packed, shards):
    quarter = packed.shape[0] // 4
    own = lax.dynamic_slice_in_dim(packed, lax.axis_index("ctx") * quarter, quarter, 0)
    return lax.all_gather(own, ("shard", "ctx"), axis=0, tiled=True).reshape(
        shards, packed.shape[0], lanes
    )


def halves(values, bit):
    half = values.shape[1] // 2
    keep = lax.dynamic_slice_in_dim(values, bit * half, half, 1)
    send = lax.dynamic_slice_in_dim(values, (1 - bit) * half, half, 1)
    return keep, send


def paired(own, other, bit):
    return jnp.where(
        bit == 0, jnp.concatenate([own, other]), jnp.concatenate([other, own])
    )


def reduce_packed(packed):
    place = lax.axis_index("ctx")
    core, chip = place % 2, place // 2
    keep, send = halves(packed, core)
    half = (keep.astype(f32) + swap_core(send).astype(f32)).astype(bf16)
    keep, send = halves(half, chip)
    quarter = (keep.astype(f32) + swap_x(send).astype(f32)).astype(bf16)
    parts = lax.all_to_all(quarter, "shard", split_axis=0, concat_axis=0, tiled=True)
    total = jnp.sum(parts.astype(f32), axis=0).astype(bf16)
    both = paired(total, swap_x(total), chip)
    return paired(both, swap_core(both), core)


def positions(offsets, tp_place, chunk, block):
    half = block // 2
    return chunk * block + (offsets + tp_place * half) % block


def attention_mask(block):
    place, tp_place = lax.axis_index("ctx"), lax.axis_index("tp")
    offsets = jnp.arange(block, dtype=jnp.int32)
    rows = positions(offsets, tp_place, place, block)
    keys = jnp.concatenate([positions(offsets, tp_place, place ^ j, block) for j in range(4)])
    return keys[None, :] <= rows[:, None]


def head_split(values, heads):
    return values.reshape(values.shape[0], heads, values.shape[1] // heads)


def attend(queries, key_all, value_all, mask, heads):
    scale_factor = (queries.shape[1] // heads) ** (-0.5)
    scores = dot("qhe,khe->hqk", head_split(queries, heads), head_split(key_all, heads))
    scores = jnp.where(mask, scores * scale_factor, masked_value)
    row_top = jnp.max(scores, axis=-1, keepdims=True)
    exponent = jnp.exp(scores - row_top)
    totals = jnp.sum(exponent, axis=-1, keepdims=True)
    probs = (exponent / totals).astype(bf16)
    out = dot("hqk,khe->qhe", probs, head_split(value_all, heads))
    return out.reshape(queries.shape).astype(bf16), row_top + jnp.log(totals)


def attend_back(queries, key_all, value_all, mask, heads, log_sums, grad_out):
    scale_factor = (queries.shape[1] // heads) ** (-0.5)
    query_heads, key_heads = head_split(queries, heads), head_split(key_all, heads)
    grad_heads = head_split(grad_out, heads)
    scores = dot("qhe,khe->hqk", query_heads, key_heads)
    scores = jnp.where(mask, scores * scale_factor, masked_value)
    probs = jnp.exp(scores - log_sums)
    grad_probs = dot("qhe,khe->hqk", grad_heads, head_split(value_all, heads))
    row_dot = jnp.sum(probs * grad_probs, axis=-1, keepdims=True)
    grad_scores = (probs * (grad_probs - row_dot)).astype(bf16)
    grad_q = dot("hqk,khe->qhe", grad_scores, key_heads) * scale_factor
    grad_k = dot("hqk,qhe->khe", grad_scores, query_heads) * scale_factor
    grad_v = dot("hqk,qhe->khe", probs.astype(bf16), grad_heads)
    return (
        grad_q.reshape(queries.shape).astype(bf16),
        jnp.concatenate(
            [grad_k.reshape(key_all.shape), grad_v.reshape(key_all.shape)], axis=1
        ).astype(bf16),
    )


def body_any(x_in, w_qkv, b_qv, w_proj, w_fc1, b_fc1, w_fc2, gains, biases, cotangent):
    depth = w_qkv.shape[0]
    shards = lax.axis_size("shard")
    own_rows, width = x_in.shape[0], x_in.shape[2]
    block = 2 * own_rows
    heads = b_qv.shape[2]
    half_width = w_qkv.shape[3]
    hidden = w_fc1.shape[2]

    small_shapes = [gains.shape, biases.shape, b_qv.shape, b_fc1.shape]
    small = small_rows([gains, biases, b_qv, b_fc1])
    group_a0 = jnp.concatenate([small, to_rows(w_qkv[0])])
    group_b0 = jnp.concatenate([to_rows(w_proj[0]), to_rows(w_fc1[0]), to_rows(w_fc2[0])])
    rest = []
    for index in range(1, depth):
        rest += [to_rows(w_qkv[index]), to_rows(w_proj[index]), to_rows(w_fc1[index]), to_rows(w_fc2[index])]
    group_rest = jnp.concatenate(rest)

    gathered_a0 = gather_packed(group_a0, shards)
    gathered_b0 = gather_packed(group_b0, shards)
    gathered_rest = gather_packed(group_rest, shards)

    def cutter(gathered, start):
        place = [start]

        def take(shape, axis):
            rows = math.prod(shape) // lanes
            piece = from_rows(gathered[:, place[0] : place[0] + rows], shape)
            place[0] += rows
            return join(piece, axis)

        return take

    shape_qkv, shape_proj = w_qkv.shape[1:], w_proj.shape[1:]
    shape_fc1, shape_fc2 = w_fc1.shape[1:], w_fc2.shape[1:]
    take_a, take_b, take_r = cutter(gathered_a0, small.shape[0]), cutter(gathered_b0, 0), cutter(gathered_rest, 0)
    weights = []
    for index in range(depth):
        take_q, take_o = (take_a, take_b) if index == 0 else (take_r, take_r)
        weights.append(
            (take_q(shape_qkv, 1), take_o(shape_proj, 1), take_o(shape_fc1, 0), take_o(shape_fc2, 1))
        )
    flat = gathered_a0[:, : small.shape[0]].reshape(shards, -1)
    vectors, start = [], 0
    for shape in small_shapes:
        size = math.prod(shape)
        piece = flat[:, start : start + size].reshape((shards,) + shape)
        vectors.append(join(piece, len(shape) - 1).astype(f32))
        start += size
    gain_all, bias_all, b_qv_all, b_fc1_all = vectors

    mask = attention_mask(block)
    x_own = x_in[:, 0]
    state = jnp.concatenate([x_own, swap_tp(x_own)]).astype(f32)
    g_own = cotangent[:, 0]
    grad_state = jnp.concatenate([g_own, swap_tp(g_own)]).astype(f32)

    stored = []
    for index in range(depth):
        w_query, w_out, w_first, w_second = weights[index]
        normed_in, scale_in = normalize(state)
        low_in = (normed_in * gain_all[index, 0] + bias_all[index, 0]).astype(bf16)
        bias_q = b_qv_all[index, 0].reshape(half_width)
        bias_v = b_qv_all[index, 1].reshape(half_width)
        queries = (dot("rd,df->rf", low_in, w_query[0]) + bias_q).astype(bf16)
        keys = dot("rd,df->rf", low_in, w_query[1]).astype(bf16)
        values = (dot("rd,df->rf", low_in, w_query[2]) + bias_v).astype(bf16)
        kv_own = jnp.concatenate([keys, values], axis=1)
        kv_chip = swap_x(kv_own)
        kv_all = jnp.concatenate([kv_own, swap_core(kv_own), kv_chip, swap_core(kv_chip)])
        key_all, value_all = kv_all[:, :half_width], kv_all[:, half_width:]
        attn, log_sums = attend(queries, key_all, value_all, mask, heads)
        attn_other = other_half(swap_tp(attn))
        w_out_other = swap_tp(w_out)
        middle = (
            state
            + dot("rf,fd->rd", attn, w_out)
            + dot("rf,fd->rd", attn_other, w_out_other)
            + bias_all[index, 1]
        )
        normed_mid, scale_mid = normalize(middle)
        low_mid = (normed_mid * gain_all[index, 1] + bias_all[index, 2]).astype(bf16)
        pre_act = dot("rd,df->rf", low_mid, w_first) + b_fc1_all[index].reshape(hidden)
        act = gelu_tanh(pre_act).astype(bf16)
        partial = dot("rf,fd->rd", act, w_second)
        if index == depth - 1:
            received = swap_tp(partial[own_rows:].astype(bf16)).astype(f32)
            output = middle[:own_rows] + partial[:own_rows] + received + bias_all[index, 3]
        else:
            received = other_half(swap_tp(partial.astype(bf16))).astype(f32)
            state = middle + partial + received + bias_all[index, 3]
        stored.append(
            (normed_in, scale_in, low_in, queries, key_all, value_all, log_sums, attn,
             normed_mid, scale_mid, low_mid, pre_act, act)
        )
    output = output.astype(bf16)[:, None]

    results = [None] * depth
    for index in reversed(range(depth)):
        w_query, w_out, w_first, w_second = weights[index]
        (normed_in, scale_in, low_in, queries, key_all, value_all, log_sums, attn,
         normed_mid, scale_mid, low_mid, pre_act, act) = stored[index]
        grad_bias_mlp = jnp.sum(grad_state, axis=0)
        grad_low = grad_state.astype(bf16)
        grad_hidden = dot("rd,fd->rf", grad_low, w_second)
        unused, gelu_pull = jax.vjp(gelu_tanh, pre_act)
        grad_pre = gelu_pull(grad_hidden)[0].astype(bf16)
        grad_w_second = dot("rf,rd->fd", act, grad_low)
        grad_w_first = dot("rd,rf->df", low_mid, grad_pre)
        grad_b_first = jnp.sum(grad_pre, axis=0, dtype=f32)
        partial = dot("rf,df->rd", grad_pre, w_first)
        mlp_rows = jnp.concatenate(
            [
                jax.vmap(to_rows)(split(grad_w_first.astype(bf16), 0, shards)),
                jax.vmap(to_rows)(split(grad_w_second.astype(bf16), 1, shards)),
            ],
            axis=1,
        )
        mlp_total = reduce_packed(mlp_rows)
        grad_mid = partial + other_half(swap_tp(partial.astype(bf16))).astype(f32)
        grad_gain_mid = jnp.sum(grad_mid * normed_mid, axis=0)
        grad_beta_mid = jnp.sum(grad_mid, axis=0)
        grad_middle = grad_state + norm_back(grad_mid * gain_all[index, 1], normed_mid, scale_mid)
        grad_bias_attn = jnp.sum(grad_middle, axis=0)
        grad_low = grad_middle.astype(bf16)
        grad_attn = dot("rd,fd->rf", grad_low, w_out).astype(bf16)
        grad_w_out = dot("rf,rd->fd", attn, grad_low)
        grad_q, grad_kv = attend_back(
            queries, key_all, value_all, mask, heads, log_sums, grad_attn
        )
        part = grad_kv.reshape(4, block, 2 * half_width)
        sent = swap_core(jnp.stack([part[1], part[3]])).astype(f32)
        mine = part[0].astype(f32) + sent[0]
        chip = (part[2].astype(f32) + sent[1]).astype(bf16)
        grad_kv = (mine + swap_x(chip).astype(f32)).astype(bf16)
        grad_qkv = jnp.stack([grad_q, grad_kv[:, :half_width], grad_kv[:, half_width:]])
        grad_w_query = dot("rd,crf->cdf", low_in, grad_qkv)
        grad_b_query = jnp.sum(grad_qkv[0::2], axis=1, dtype=f32)
        partial = dot("crf,cdf->rd", grad_qkv, w_query)
        grad_in = partial + other_half(swap_tp(partial.astype(bf16))).astype(f32)
        grad_gain_in = jnp.sum(grad_in * normed_in, axis=0)
        grad_beta_in = jnp.sum(grad_in, axis=0)
        grad_state = grad_middle + norm_back(grad_in * gain_all[index, 0], normed_in, scale_in)

        vectors = [
            jnp.stack([grad_gain_in, grad_gain_mid]),
            jnp.stack([grad_beta_in, grad_bias_attn, grad_beta_mid, grad_bias_mlp]),
            grad_b_query.reshape(2, heads, half_width // heads),
            grad_b_first.reshape(b_fc1_all.shape[1:]),
        ]
        parts = [split(vector, vector.ndim - 1, shards) for vector in vectors]
        part_shapes = [part.shape[1:] for part in parts]
        attn_rows = jnp.concatenate(
            [
                jax.vmap(to_rows)(split(grad_w_query.astype(bf16), 1, shards)),
                jax.vmap(to_rows)(split(grad_w_out.astype(bf16), 1, shards)),
                jax.vmap(lambda *own: small_rows(own))(*parts).astype(bf16),
            ],
            axis=1,
        )
        attn_total = reduce_packed(attn_rows)

        def pieces(total, shapes):
            place, out = 0, []
            for shape in shapes:
                rows = math.prod(shape) // lanes
                out.append(from_rows(total[place : place + rows], shape).astype(f32))
                place += rows
            return out, total[place:].reshape(-1)

        (out_fc1, out_fc2), unused = pieces(mlp_total, [shape_fc1, shape_fc2])
        (out_qkv, out_proj), tail = pieces(attn_total, [shape_qkv, shape_proj])
        small_out, start = [], 0
        for shape in part_shapes:
            size = math.prod(shape)
            small_out.append(tail[start : start + size].reshape(shape).astype(f32))
            start += size
        results[index] = (
            out_qkv, small_out[2], out_proj, out_fc1, small_out[3], out_fc2, small_out[0], small_out[1]
        )
    stacked = tuple(
        jnp.stack([results[index][member] for index in range(depth)]) for member in range(8)
    )
    return (output, grad_state[:own_rows, None]) + stacked


def compiler_params():
    return pltpu.CompilerParams(vmem_limit_bytes=56 * 2**20)


def whole(array):
    zeros = (0,) * array.ndim
    return pl.BlockSpec(array.shape, lambda i: zeros)


def rows_at(array, rows, start, lead=None, first=0):
    lead = array.shape[0] if lead is None else lead
    return pl.BlockSpec((lead, rows, lanes), lambda i: (first, start // rows, 0))


def run(kernel, outs, place, operands, scratch=(), flops=2**20, after=()):
    arrays, specs = [], []
    count = 1 + len(operands)

    def inner(*refs):
        kernel(*refs[:count], *refs[count + len(after) :])

    for operand in operands:
        array, spec = operand if isinstance(operand, tuple) else (operand, whole(operand))
        arrays.append(array)
        specs.append(spec)
    out_shape = [jax.ShapeDtypeStruct(shape, kind) for shape, kind in outs]
    after = list(after)
    arrays += after
    specs += [pl.BlockSpec(memory_space=pl.ANY)] * len(after)
    call = pl.pallas_call(
        inner,
        grid=(1,),
        out_shape=out_shape,
        in_specs=[pl.BlockSpec(memory_space=pltpu.SMEM)] + specs,
        out_specs=[whole(shape) for shape in out_shape],
        scratch_shapes=list(scratch),
        compiler_params=compiler_params(),
        cost_estimate=pl.CostEstimate(flops=flops, bytes_accessed=1024, transcendentals=0),
    )
    return list(call(place, *arrays))


def mm(left, right):
    return lax.dot_general(left, right, (((1,), (0,)), ((), ())), preferred_element_type=f32)


def mm_nt(left, right):
    return lax.dot_general(left, right, (((1,), (1,)), ((), ())), preferred_element_type=f32)


def mm_tn(left, right):
    return lax.dot_general(left, right, (((0,), (0,)), ((), ())), preferred_element_type=f32)


def lane_join(parts):
    return jnp.concatenate(parts, axis=1)


def row_join(parts):
    return jnp.concatenate(parts, axis=0)


class Pieces:
    def __init__(self, refs):
        self.local, self.far = refs[0], refs[1:]

    def tile(self, k, p, start, rows):
        if k == 0:
            return self.local[p, start : start + rows]
        return self.far[p][k - 1, start : start + rows]


def first_block(pieces, p):
    return row_join(
        [lane_join([pieces.tile(k, p, j * 128, 128) for j in range(2)]) for k in range(4)]
    )


def second_block(pieces, p):
    return lane_join([pieces.tile(k, p, 0, 256) for k in range(4)])


def small_row(small_local, small_far, row):
    parts = [small_local[0, row : row + 1]] + [small_far[k, row : row + 1] for k in range(3)]
    return lane_join(parts).astype(f32)


def spread(small_local, small_far, row, place_z, half, later=None):
    def rows_from(row):
        return row_join(
            [small_local[0, row : row + 1]] + [small_far[k, row : row + 1] for k in range(3)]
        ).astype(f32)

    source = rows_from(row)
    if later is not None:
        source = jnp.where(later == 0, source, rows_from(row + 1))
    source = source.astype(bf16)
    take = lax.broadcasted_iota(jnp.int32, (128, 256), 0)
    lane = lax.broadcasted_iota(jnp.int32, (128, 256), 1)
    wanted = half * 64 + (lane // 64) * 16 + lane % 16
    table = (take == wanted).astype(f32).astype(bf16)
    rows = mm(source, table)
    chunk = lax.broadcasted_iota(jnp.int32, (4, 256), 0)
    lane = lax.broadcasted_iota(jnp.int32, (4, 256), 1)
    keep = (lane % 64) // 16 == (place_z - chunk + 4) % 4
    return jnp.sum(jnp.where(keep, rows, 0.0), axis=0, keepdims=True)


def pack_kernel(kinds):
    def kernel(place, *refs):
        c = place[1]
        out, send = refs[-2:]
        start = 0
        for ref, kind in zip(refs, kinds):
            for q in range(4):
                to = q ^ c
                if kind == "first":
                    for j in range(2):
                        column = (2 * q + j) * 128
                        out[to, start + j * 128 : start + (j + 1) * 128] = ref[0, :, column : column + 128]
                elif kind == "second":
                    out[to, start : start + 256] = ref[0, q * 256 : (q + 1) * 256]
                elif kind == "proj":
                    out[to, start : start + 64] = ref[0, q * 64 : (q + 1) * 64]
                elif kind == "qkv":
                    for tile in range(6):
                        row = start + tile * 32
                        column = (tile % 2) * 128
                        out[to, row : row + 32] = ref[0, tile // 2, q * 32 : (q + 1) * 32, column : column + 128]
                else:
                    out[to, start : start + 32] = ref[...]
            start += kind_rows[kind]
        send[...] = out[0]

    return kernel


kind_rows = {"first": 256, "second": 256, "proj": 64, "qkv": 192, "small": 32}


def pack(place, kinds, arrays, index, after=()):
    rows = sum(kind_rows[kind] for kind in kinds)
    operands = []
    for kind, array in zip(kinds, arrays):
        if kind == "small":
            operands.append(array)
        else:
            block = (1,) + array.shape[1:]
            at = (index,) + (0,) * (array.ndim - 1)
            operands.append((array, pl.BlockSpec(block, lambda i, at=at: at)))
    return run(
        pack_kernel(kinds), [((4, rows, lanes), bf16), ((rows, lanes), bf16)], place, operands, flops=2**20, after=after
    )


def shift(values, step):
    return lax.ppermute(values, "shard", [(z, (z + step) % 4) for z in range(4)])


def far_chunks(send):
    return [shift(send, k) for k in (1, 2, 3)]


def stack_kernel(place, one, two, three, out):
    for k, ref in enumerate((one, two, three)):
        out[k] = ref[...]


def spread_group(place, local, got, after):
    (far,) = run(stack_kernel, [((3,) + got[0].shape, bf16)], place, got, flops=2**20, after=after)
    far_chip = swap_x(far)
    return [local, far, swap_core(far), far_chip, swap_core(far_chip)]


def pieces_of(group, rows, start):
    return [(array, rows_at(array, rows, start)) for array in group]


def small_of(group):
    return [(group[0], rows_at(group[0], 32, 256, lead=1)), (group[1], rows_at(group[1], 32, 256))]


def query_kernel(index, first_layer):
    def kernel(place, *refs):
        c = place[1]
        if first_layer:
            own, peer, small_local, small_far = refs[:4]
            pieces = Pieces(refs[4:9])
            later, later_out = refs[9], refs[15]
            later_out[...] = later[...]
            state_out, low_out, q_out, kv_out, w_out = refs[10:15]
            state = row_join([own[...], peer[...]]).astype(f32)
        else:
            middle, mine, other, small_local, small_far = refs[:5]
            pieces = Pieces(refs[5:10])
            state_out, low_out, q_out, kv_out, w_out = refs[10:]
            received = row_join([other[128:], other[:128]])
            state = (
                middle[...]
                + mine[...].astype(f32)
                + received.astype(f32)
                + small_row(small_local, small_far, 4 + 4 * (index - 1) + 3)
            )
        for k in range(4):
            for p in range(4):
                for tile in range(6):
                    w_out[k, p ^ c, :, tile * 128 : (tile + 1) * 128] = pieces.tile(k, p, tile * 32, 32)
        state_out[...] = state
        normed, scale = normalize(state)
        low = (
            normed * small_row(small_local, small_far, 2 * index)
            + small_row(small_local, small_far, 4 + 4 * index)
        ).astype(bf16)
        low_out[...] = low
        w_all = w_out[...].reshape(512, 768)
        row = 12 + index
        bias_q = spread(small_local, small_far, row, place[0], 0)
        bias_v = spread(small_local, small_far, row, place[0], 1)
        kv_out[:, :256] = mm(low, w_all[:, 256:512]).astype(bf16)
        kv_out[:, 256:] = (mm(low, w_all[:, 512:]) + bias_v).astype(bf16)
        q_out[...] = (mm(low, w_all[:, :256]) + bias_q).astype(bf16)

    return kernel


def seen(place, j):
    c, t = place[1], place[2]
    if j:
        return None
    row = lax.broadcasted_iota(jnp.int32, (256, 256), 0) ^ (t * 128)
    key = lax.broadcasted_iota(jnp.int32, (256, 256), 1) ^ (t * 128)
    return key <= row


def masked_scores(query, chunks, own_mask, place):
    parts = []
    for j in range(4):
        scores = mm_nt(query, chunks[j]) * 0.125
        if j == 0:
            scores = jnp.where(own_mask, scores, masked_value)
        else:
            scores = jnp.where((place[1] ^ j) < place[1], scores, masked_value)
        parts.append(scores)
    return parts


def attend_kernel(place, *refs):
    c = place[1]
    q, chunks = refs[0], refs[1:5]
    pieces = Pieces(refs[5:10])
    attn_out, lse_out, partial_out, w_out = refs[10:]
    for k in range(4):
        for p in range(4):
            w_out[p ^ c, :, k * 128 : (k + 1) * 128] = pieces.tile(k, p, 0, 64)
    own_mask = seen(place, 0)
    results = []
    for head in range(4):
        low, high = head * 64, (head + 1) * 64
        parts = masked_scores(q[:, low:high], [chunk[:, low:high] for chunk in chunks], own_mask, place)
        scores = lane_join(parts)
        top = jnp.max(scores, axis=1, keepdims=True)
        exponent = jnp.exp(scores - top)
        total = jnp.sum(exponent, axis=1, keepdims=True)
        values = row_join([chunk[:, 256 + low : 256 + high] for chunk in chunks])
        results.append(mm(exponent.astype(bf16), values) / total)
        lse_out[:, head : head + 1] = top + jnp.log(total)
    attn = lane_join(results).astype(bf16)
    attn_out[...] = attn
    partial_out[...] = mm(attn, w_out[...].reshape(256, 512)).astype(bf16)


def mlp_kernel(index):
    def kernel(place, *refs):
        state, mine, other, small_local, small_far = refs[:5]
        first, second = Pieces(refs[5:10]), Pieces(refs[10:15])
        middle_out, low_out, pre_out, partial_out = refs[15:]
        received = row_join([other[128:], other[:128]])
        middle = (
            state[...]
            + mine[...].astype(f32)
            + received.astype(f32)
            + small_row(small_local, small_far, 4 + 4 * index + 1)
        )
        middle_out[...] = middle
        normed, scale = normalize(middle)
        low = (
            normed * small_row(small_local, small_far, 2 * index + 1)
            + small_row(small_local, small_far, 4 + 4 * index + 2)
        ).astype(bf16)
        low_out[...] = low
        total = None
        for p in range(4):
            q = p ^ place[1]
            bias = spread(small_local, small_far, 14 + 2 * index, place[0], q % 2, q // 2)
            pre = mm(low, first_block(first, p)) + bias
            pre_out[:, p * 256 : (p + 1) * 256] = pre
            act = gelu_tanh(pre).astype(bf16)
            part = mm(act, second_block(second, p))
            total = part if total is None else total + part
        partial_out[...] = total.astype(bf16)

    return kernel


root = math.sqrt(2 / math.pi)


def mlp_back(grad, pre_ref, low_ref, first, second, place, outs):
    partial_out, bias_out, b_first_out, keep, send = outs
    grad_low = grad.astype(bf16)
    bias_out[...] = jnp.sum(grad, axis=0, keepdims=True)
    total = None
    for p in range(4):
        pre = pre_ref[:, p * 256 : (p + 1) * 256]
        square = pre * pre
        wave = jnp.tanh(root * pre * (1 + 0.044715 * square))
        half = 0.5 * (1 + wave)
        act = (pre * half).astype(bf16)
        slope = half + 0.5 * pre * (1 - wave * wave) * root * (1 + 3 * 0.044715 * square)
        w_second = second_block(second, p)
        grad_pre = mm_nt(grad_low, w_second) * slope
        grad_pre_low = grad_pre.astype(bf16)
        b_first_out[p ^ place[1]] = jnp.sum(grad_pre_low.astype(f32), axis=0, keepdims=True)
        part = mm_nt(grad_pre_low, first_block(first, p))
        total = part if total is None else total + part
        to = keep if p % 2 == 0 else send
        grad_first = mm_tn(low_ref[...], grad_pre_low).astype(bf16)
        grad_second = mm_tn(act, grad_low).astype(bf16)
        for k in range(4):
            for j in range(2):
                to[p // 2, k, j * 128 : (j + 1) * 128] = grad_first[
                    k * 128 : (k + 1) * 128, j * 128 : (j + 1) * 128
                ]
            to[p // 2, k, 256:512] = grad_second[:, k * 128 : (k + 1) * 128]
    partial_out[...] = total.astype(bf16)


def norm_step(grad_out, gain, values):
    normed, scale = normalize(values)
    sums = row_join(
        [
            jnp.sum(grad_out * normed, axis=0, keepdims=True),
            jnp.sum(grad_out, axis=0, keepdims=True),
        ]
    )
    return norm_back(grad_out * gain, normed, scale), sums


def received_sum(mine, other):
    return mine[...].astype(f32) + row_join([other[128:], other[:128]]).astype(f32)


def top_kernel(place, *refs):
    grad, pre, low = refs[:3]
    first, second = Pieces(refs[3:8]), Pieces(refs[8:13])
    mlp_back(grad[...], pre, low, first, second, place, refs[13:])


def lower_kernel(index):
    def kernel(place, *refs):
        grad_mid, mine, other, state, small_local, small_far, pre, low = refs[:8]
        first, second = Pieces(refs[8:13]), Pieces(refs[13:18])
        grad_out, sums_out = refs[18:20]
        grad, sums = norm_step(
            received_sum(mine, other), small_row(small_local, small_far, 2 * (index + 1)), state[...]
        )
        sums_out[...] = sums
        grad = grad_mid[...] + grad
        grad_out[...] = grad
        mlp_back(grad, pre, low, first, second, place, refs[20:])

    return kernel


def attend_back_kernel(index):
    def kernel(place, *refs):
        mine, other, middle, grad_state, small_local, small_far = refs[:6]
        attn, w_out, q = refs[6:9]
        chunks, lse = refs[9:13], refs[13]
        grad_out, sums_out, gw_out, dq_out, keep, send = refs[14:]
        grad, sums = norm_step(
            received_sum(mine, other), small_row(small_local, small_far, 2 * index + 1), middle[...]
        )
        grad = grad_state[...] + grad
        grad_out[...] = grad
        sums_out[0:2] = sums
        sums_out[2:3] = jnp.sum(grad, axis=0, keepdims=True)
        grad_low = grad.astype(bf16)
        grad_attn = mm_nt(grad_low, w_out[...].reshape(256, 512)).astype(bf16)
        gw_out[...] = mm_tn(attn[...], grad_low).astype(bf16).reshape(4, 64, 512)
        own_mask = seen(place, 0)
        dq_all = []
        dk_all = [[] for j in range(4)]
        dv_all = [[] for j in range(4)]
        for head in range(4):
            low, high = head * 64, (head + 1) * 64
            query, grad_head = q[:, low:high], grad_attn[:, low:high]
            keys = [chunk[:, low:high] for chunk in chunks]
            row_dot = jnp.sum(
                grad_head.astype(f32) * attn[:, low:high].astype(f32), axis=1, keepdims=True
            )
            log_sum = lse[:, head : head + 1]
            parts = masked_scores(query, keys, own_mask, place)
            dq = None
            for j in range(4):
                probs = jnp.exp(parts[j] - log_sum)
                grad_probs = mm_nt(grad_head, chunks[j][:, 256 + low : 256 + high])
                grad_scores = (probs * (grad_probs - row_dot)).astype(bf16)
                part = mm(grad_scores, keys[j])
                dq = part if dq is None else dq + part
                dk_all[j].append(mm_tn(grad_scores, query) * 0.125)
                dv_all[j].append(mm_tn(probs.astype(bf16), grad_head))
            dq_all.append(dq * 0.125)
        dq_out[...] = lane_join(dq_all).astype(bf16)
        for j in range(4):
            to = keep if j % 2 == 0 else send
            to[j // 2, :, :256] = lane_join(dk_all[j]).astype(bf16)
            to[j // 2, :, 256:] = lane_join(dv_all[j]).astype(bf16)

    return kernel


def halve_kernel(place, keep, got, own_out, send_out):
    own_out[...] = (keep[0].astype(f32) + got[0].astype(f32)).astype(bf16)
    send_out[...] = (keep[1].astype(f32) + got[1].astype(f32)).astype(bf16)


def query_back_kernel(place, *refs):
    dq, dkv, got, low, w_ref, gw_ref = refs[:6]
    partial_out, b_out, keep, send, scratch = refs[6:]
    c = place[1]
    grad_kv = (dkv[...].astype(f32) + got[...].astype(f32)).astype(bf16)
    grad_qkv = lane_join([dq[...], grad_kv])
    partial_out[...] = mm_nt(grad_qkv, w_ref[...].reshape(512, 768)).astype(bf16)
    b_out[0:1] = jnp.sum(dq[...].astype(f32), axis=0, keepdims=True)
    b_out[1:2] = jnp.sum(grad_kv[:, 256:].astype(f32), axis=0, keepdims=True)
    scratch[...] = mm_tn(low[...], grad_qkv).astype(bf16).reshape(4, 4, 32, 768)
    for p in range(4):
        to = keep if p % 2 == 0 else send
        for k in range(4):
            for tile in range(6):
                to[p // 2, k, tile * 32 : (tile + 1) * 32] = scratch[
                    k, p ^ c, :, tile * 128 : (tile + 1) * 128
                ]
            to[p // 2, k, 192:256] = gw_ref[p ^ c, :, k * 128 : (k + 1) * 128]


def quarter_kernel(place, own, got, *outs):
    for k in range(4):
        outs[k][...] = (own[k].astype(f32) + got[k].astype(f32)).astype(bf16)


def total_kernel(place, own, one, two, three, out):
    total = own[...].astype(f32) + one[...].astype(f32)
    out[...] = (total + (two[...].astype(f32) + three[...].astype(f32))).astype(bf16)


class Chain:
    def __init__(self, place, keep, send):
        self.place, self.rows = place, keep.shape[2]
        self.state = [keep, send]

    def halve(self, after=()):
        keep, send = self.state
        self.state = run(
            halve_kernel, [((4, self.rows, lanes), bf16)] * 2, self.place, [keep, swap_core(send)], flops=2**20, after=after
        )

    def quarter(self, after=()):
        own, send = self.state
        self.state = run(
            quarter_kernel, [((self.rows, lanes), bf16)] * 4, self.place, [own, swap_x(send)], flops=2**20, after=after
        )

    def total(self, after=()):
        got = [shift(self.state[k], 4 - k) for k in (1, 2, 3)]
        self.state = run(
            total_kernel, [((self.rows, lanes), bf16)], self.place, [self.state[0]] + got, flops=2**20, after=after
        )

    def collect(self):
        (total,) = self.state
        chip = swap_x(total)
        return [total, swap_core(total), chip, swap_core(chip)]


def hidden_out_kernel():
    def kernel(place, *refs):
        c = place[1]
        first_out, second_out, scratch = refs[-3:]
        for layer in range(2):
            for p in range(4):
                scratch[p] = refs[4 * layer + p][...].astype(f32)
            for q in range(4):
                for j in range(2):
                    column = (2 * q + j) * 128
                    first_out[layer, :, column : column + 128] = scratch[q ^ c, j * 128 : (j + 1) * 128]
                second_out[layer, q * 256 : (q + 1) * 256] = scratch[q ^ c, 256:]

    return kernel


def heads_out_kernel():
    def kernel(place, *refs):
        c = place[1]
        qkv_out, proj_out, scratch = refs[-3:]
        for layer in range(2):
            for p in range(4):
                scratch[p] = refs[4 * layer + p][...].astype(f32)
            for q in range(4):
                for tile in range(6):
                    column = (tile % 2) * 128
                    qkv_out[layer, tile // 2, q * 32 : (q + 1) * 32, column : column + 128] = scratch[
                        q ^ c, tile * 32 : (tile + 1) * 32
                    ]
                proj_out[layer, q * 64 : (q + 1) * 64] = scratch[q ^ c, 192:]

    return kernel


def last_kernel(place, *refs):
    grad_mid, mine, other, state, small_local, small_far = refs[:6]
    sums_in = refs[6]
    sums_mid, bias_mlp, b_query, b_first = refs[7:9], refs[9:11], refs[11:13], refs[13:15]
    grad_out, out = refs[15:]
    grad, sums = norm_step(received_sum(mine, other), small_row(small_local, small_far, 0), state[...])
    grad_out[...] = grad_mid[:128] + grad[:128]
    for layer in range(2):
        inner = sums if layer == 0 else sums_in[...]
        mid = sums_mid[layer]
        rows = [
            (2 * layer, inner[0:1]),
            (2 * layer + 1, mid[0:1]),
            (4 + 4 * layer, inner[1:2]),
            (5 + 4 * layer, mid[2:3]),
            (6 + 4 * layer, mid[1:2]),
            (7 + 4 * layer, bias_mlp[layer][...]),
        ]
        for k in range(4):
            for row, value in rows:
                out[k, row : row + 1] = value[:, k * 128 : (k + 1) * 128]
            for channel in range(2):
                for j in range(2):
                    row = 12 + 4 * layer + 2 * channel + j
                    out[k, row : row + 1] = b_query[layer][channel : channel + 1, j * 128 : (j + 1) * 128]
            for q in range(4):
                for j in range(2):
                    row = 20 + 8 * layer + 2 * q + j
                    out[k, row : row + 1] = b_first[layer][q, :, j * 128 : (j + 1) * 128]
    out[:, 36:] = jnp.zeros((4, 4, lanes), f32)


def turn(values, place_z, back):
    rows = values.shape[0]
    chunks = values.reshape(rows, 4, lanes)
    order = (place_z - jnp.arange(4)) % 4
    return jnp.concatenate(
        [lax.dynamic_slice_in_dim(values, order[k] * lanes, lanes, 1) for k in range(4)], axis=1
    )


def body_four(x_in, w_qkv, b_qv, w_proj, w_fc1, b_fc1, w_fc2, gains, biases, cotangent):
    z, c, t = lax.axis_index("shard"), lax.axis_index("ctx"), lax.axis_index("tp")
    place = jnp.stack([z, c, t]).astype(jnp.int32)
    flat = jnp.concatenate([array.reshape(-1) for array in (gains, biases, b_qv, b_fc1)])
    small = jnp.pad(flat, (0, 32 * lanes - flat.shape[0])).reshape(32, lanes)

    local_a, send_a = pack(place, ("qkv", "proj", "small"), (w_qkv, w_proj, small), 0)
    x_own = turn(x_in[:, 0], z, False)
    x_peer = swap_tp(x_own)
    got_a = far_chunks(send_a)
    group_a0 = spread_group(place, local_a, got_a, [])
    local_b, send_b = pack(place, ("first", "second"), (w_fc1, w_fc2), 0, after=got_a)
    got_b = far_chunks(send_b)
    kinds = ("first", "second", "proj", "qkv")
    local_1, send_1 = pack(place, kinds, (w_fc1, w_fc2, w_proj, w_qkv), 1, after=got_a + [send_b])
    g_own = turn(cotangent[:, 0], z, False)
    g_all = jnp.concatenate([g_own, swap_tp(g_own)]).astype(f32)

    small_parts = small_of(group_a0)
    parts = {
        "qkv": [pieces_of(group_a0, 192, 0)],
        "proj": [pieces_of(group_a0, 64, 192)],
        "first": [],
        "second": [],
    }
    square, wide = (256, 512), (256, 256)
    saved = []
    for layer in range(2):
        source = [x_own, x_peer] if layer == 0 else [middle, partial, swap_tp(partial)]
        extra = [send_1] if layer == 0 else []
        state, low_in, q, kv, w_all, *passed = run(
            query_kernel(layer, layer == 0),
            [(square, f32), (square, bf16), (wide, bf16), (square, bf16), ((4, 4, 32, 768), bf16)]
            + [(array.shape, bf16) for array in extra],
            place,
            source + small_parts + parts["qkv"][layer] + extra,
            after=got_b if layer == 0 else [],
        )
        if layer == 0:
            got_1 = far_chunks(passed[0])
        kv_chip = swap_x(kv)
        chunks = [kv, swap_core(kv), kv_chip, swap_core(kv_chip)]
        behind = []
        if layer == 0:
            group_b0 = spread_group(place, local_b, got_b, [kv])
            behind = [group_b0[1]]
        attn, lse, partial, w_out = run(
            attend_kernel,
            [(wide, bf16), ((256, lanes), f32), (square, bf16), ((4, 64, 512), bf16)],
            place,
            [q] + chunks + parts["proj"][layer],
            flops=2**33,
            after=behind,
        )
        received = swap_tp(partial)
        if layer == 0:
            first_received = received
            parts["first"].append(pieces_of(group_b0, 256, 0))
            parts["second"].append(pieces_of(group_b0, 256, 256))
        middle, low_mid, pre, partial = run(
            mlp_kernel(layer),
            [(square, f32), (square, bf16), ((256, 1024), f32), (square, bf16)],
            place,
            [state, partial, received] + small_parts + parts["first"][layer] + parts["second"][layer],
            flops=2**33,
        )
        if layer == 0:
            group_1 = spread_group(place, local_1, got_1, [first_received, group_b0[1]])
            parts["qkv"].append(pieces_of(group_1, 192, 576))
            parts["proj"].append(pieces_of(group_1, 64, 512))
            parts["first"].append(pieces_of(group_1, 256, 0))
            parts["second"].append(pieces_of(group_1, 256, 256))
        saved.append((state, low_in, q, chunks, w_all, attn, lse, w_out, middle, low_mid, pre))

    received = swap_tp(partial[128:]).astype(f32)
    output = None
    bias_last = jnp.concatenate([small_parts[0][0][0, 267:268], small_parts[1][0][:, 267]]).reshape(1, 512)
    output = middle[:128] + partial[:128].astype(f32) + received + bias_last.astype(f32)
    output = turn(output.astype(bf16), z, True)[:, None]

    hidden_outs = [
        (square, bf16),
        ((1, 512), f32),
        ((4, 1, 256), f32),
        ((2, 4, 512, lanes), bf16),
        ((2, 4, 512, lanes), bf16),
    ]
    sums_mid, bias_mlp, b_query, b_first = [0, 0], [0, 0], [0, 0], [0, 0]
    hidden, heads = [None, None], [None, None]
    for layer in (1, 0):
        state, low_in, q, chunks, w_all, attn, lse, w_out, middle, low_mid, pre = saved[layer]
        tail = [pre, low_mid] + parts["first"][layer] + parts["second"][layer]
        if layer == 1:
            grad_state = g_all
            partial, bias_mlp[1], b_first[1], keep, send = run(
                top_kernel, hidden_outs, place, [grad_state] + tail
            )
        else:
            heads[1].halve()
            grad_state, sums_in, partial, bias_mlp[0], b_first[0], keep, send = run(
                lower_kernel(0),
                [(square, f32), ((2, 512), f32)] + hidden_outs,
                place,
                [grad_mid, partial, swap_tp(partial), saved[1][0]] + small_parts + tail,
                after=heads[1].state,
            )
            hidden[1].total(after=[partial])
        hidden[layer] = Chain(place, keep, send)
        hidden[layer].halve()
        grad_mid, sums_mid[layer], gw_out, dq, keep, send = run(
            attend_back_kernel(layer),
            [
                (square, f32),
                ((3, 512), f32),
                ((4, 64, 512), bf16),
                (wide, bf16),
                ((2, 256, 512), bf16),
                ((2, 256, 512), bf16),
            ],
            place,
            [partial, swap_tp(partial), middle, grad_state] + small_parts + [attn, w_out, q] + chunks + [lse],
            after=hidden[layer].state + (hidden[1].state if layer == 0 else []),
        )
        dkv, chip = run(halve_kernel, [(square, bf16)] * 2, place, [keep, swap_core(send)], flops=2**20)
        hidden[layer].quarter(after=[chip])
        behind = list(hidden[layer].state)
        if layer == 0:
            heads[1].quarter(after=[chip])
            behind += heads[1].state
        partial, b_query[layer], keep, send = run(
            query_back_kernel,
            [
                (square, bf16),
                ((2, 256), f32),
                ((2, 4, 256, lanes), bf16),
                ((2, 4, 256, lanes), bf16),
            ],
            place,
            [dq, dkv, swap_x(chip), low_in, w_all, gw_out],
            scratch=[pltpu.VMEM((4, 4, 32, 768), bf16)],
            after=behind,
        )
        heads[layer] = Chain(place, keep, send)
    heads[0].halve()
    grad_x, sums = run(
        last_kernel,
        [((128, 512), f32), ((4, 40, lanes), f32)],
        place,
        [grad_mid, partial, swap_tp(partial), saved[0][0]]
        + small_parts
        + [sums_in]
        + sums_mid
        + bias_mlp
        + b_query
        + b_first,
        after=heads[0].state,
    )
    heads[1].total()
    hidden[0].total()
    heads[0].quarter()
    heads[0].total()
    grad_x = turn(grad_x, z, True)[:, None]
    sums = sums + swap_core(sums)
    sums = sums + swap_x(sums)
    got = [shift(sums[k], 4 - k) for k in (1, 2, 3)]
    total = sums[0] + got[0] + got[1] + got[2]
    grad_gains = total[:4].reshape(gains.shape)
    grad_biases = total[4:12].reshape(biases.shape)
    rest_q = total[12:20].reshape(2, 2, 4, 64)
    rest_f = total[20:36].reshape(2, 16, 64)
    grad_b_qv = lax.dynamic_slice_in_dim(rest_q, z * 16, 16, 3)
    grad_b_fc1 = lax.dynamic_slice_in_dim(rest_f, z * 16, 16, 2)

    grad_fc1, grad_fc2 = run(
        hidden_out_kernel(),
        [(w_fc1.shape, f32), (w_fc2.shape, f32)],
        place,
        hidden[0].collect() + hidden[1].collect(),
        scratch=[pltpu.VMEM((4, 512, lanes), f32)],
        flops=2**20,
    )
    grad_qkv, grad_proj = run(
        heads_out_kernel(),
        [(w_qkv.shape, f32), (w_proj.shape, f32)],
        place,
        heads[0].collect() + heads[1].collect(),
        scratch=[pltpu.VMEM((4, 256, lanes), f32)],
        flops=2**20,
    )
    return (
        output, grad_x, grad_qkv, grad_b_qv, grad_proj, grad_fc1, grad_b_fc1, grad_fc2, grad_gains, grad_biases
    )


def body(*args):
    x_in, w_qkv, b_qv, w_proj, w_fc1 = args[:5]
    expected = ((128, 1, 512), (2, 3, 128, 256), (2, 2, 4, 16), (2, 256, 128), (2, 128, 1024))
    sizes = (lax.axis_size("shard"), lax.axis_size("ctx"), lax.axis_size("tp"))
    shapes = tuple(array.shape for array in (x_in, w_qkv, b_qv, w_proj, w_fc1))
    if sizes == (4, 4, 2) and shapes == expected:
        return body_four(*args)
    return body_any(*args)


def solution(mesh):
    return jax.shard_map(
        body,
        mesh=mesh,
        in_specs=(
            P(("ctx", "tp"), "shard", None),
            P(None, None, "shard", "tp"),
            P(None, None, "tp", "shard"),
            P(None, "tp", "shard"),
            P(None, "shard", "tp"),
            P(None, "tp", "shard"),
            P(None, "tp", "shard"),
            P(None, None, "shard"),
            P(None, None, "shard"),
            P(("ctx", "tp"), "shard", None),
        ),
        out_specs=(
            P(("ctx", "tp"), "shard", None),
            P(("ctx", "tp"), "shard", None),
            P(None, None, "shard", "tp"),
            P(None, None, "tp", "shard"),
            P(None, "tp", "shard"),
            P(None, "shard", "tp"),
            P(None, "tp", "shard"),
            P(None, "tp", "shard"),
            P(None, None, "shard"),
            P(None, None, "shard"),
        ),
        check_vma=False,
    )
```

```python
import math

import jax
import jax.numpy as jnp
from jax import lax
from jax.experimental import pallas as pl
from jax.experimental.pallas import tpu as pltpu
from jax.sharding import PartitionSpec as P

epsilon = 1e-05
masked_value = -1e30
lanes = 128
f32 = jnp.float32
bf16 = jnp.bfloat16


def normalize(values):
    center = jnp.mean(values, axis=-1, keepdims=True)
    shifted = values - center
    scale_inv = lax.rsqrt(jnp.mean(shifted * shifted, axis=-1, keepdims=True) + epsilon)
    return (shifted * scale_inv, scale_inv)


def norm_back(grad_norm, normed, scale_inv):
    mean_grad = jnp.mean(grad_norm, axis=-1, keepdims=True)
    mean_prod = jnp.mean(grad_norm * normed, axis=-1, keepdims=True)
    return scale_inv * (grad_norm - mean_grad - normed * mean_prod)


def gelu_tanh(values):
    return jax.nn.gelu(values, approximate=True)


def dot(pattern, left, right):
    return jnp.einsum(pattern, left, right, preferred_element_type=f32)


def to_rows(array):
    rows, columns = array.shape[-2:]
    if columns % lanes or rows % 16:
        return array.reshape(-1, lanes)
    tiles = array.reshape(-1, rows, columns // lanes, lanes)
    return jnp.swapaxes(tiles, 1, 2).reshape(-1, lanes)


def from_rows(packed, shape):
    rows, columns = shape[-2:]
    lead = packed.shape[:-2]
    if columns % lanes or rows % 16:
        return packed.reshape(lead + tuple(shape))
    count = math.prod(shape[:-2])
    tiles = packed.reshape(lead + (count, columns // lanes, rows, lanes))
    return jnp.swapaxes(tiles, -3, -2).reshape(lead + tuple(shape))


def small_rows(arrays):
    flat = jnp.concatenate([array.reshape(-1) for array in arrays])
    size = -(-flat.shape[0] // (64 * lanes)) * 64 * lanes
    return jnp.pad(flat, (0, size - flat.shape[0])).reshape(-1, lanes)


def join(gathered, axis):
    moved = jnp.moveaxis(gathered, 0, axis)
    shape = moved.shape
    return moved.reshape(shape[:axis] + (shape[axis] * shape[axis + 1],) + shape[axis + 2 :])


def split(whole, axis, shards):
    shape = whole.shape
    parts = whole.reshape(shape[:axis] + (shards, shape[axis] // shards) + shape[axis + 1 :])
    return jnp.moveaxis(parts, axis, 0)


def swap_tp(values):
    return lax.ppermute(values, "tp", [(0, 1), (1, 0)])


def swap_core(values):
    return lax.ppermute(values, "ctx", [(0, 1), (1, 0), (2, 3), (3, 2)])


def swap_x(values):
    return lax.ppermute(values, "ctx", [(0, 2), (2, 0), (1, 3), (3, 1)])


def swap_both(values):
    return lax.ppermute(values, "ctx", [(0, 3), (3, 0), (1, 2), (2, 1)])


def other_half(values):
    half = values.shape[0] // 2
    return jnp.concatenate([values[half:], values[:half]])


def gather_packed(packed, shards):
    quarter = packed.shape[0] // 4
    own = lax.dynamic_slice_in_dim(packed, lax.axis_index("ctx") * quarter, quarter, 0)
    return lax.all_gather(own, ("shard", "ctx"), axis=0, tiled=True).reshape(
        shards, packed.shape[0], lanes
    )


def halves(values, bit):
    half = values.shape[1] // 2
    keep = lax.dynamic_slice_in_dim(values, bit * half, half, 1)
    send = lax.dynamic_slice_in_dim(values, (1 - bit) * half, half, 1)
    return keep, send


def paired(own, other, bit):
    return jnp.where(
        bit == 0, jnp.concatenate([own, other]), jnp.concatenate([other, own])
    )


def reduce_packed(packed):
    place = lax.axis_index("ctx")
    core, chip = place % 2, place // 2
    keep, send = halves(packed, core)
    half = (keep.astype(f32) + swap_core(send).astype(f32)).astype(bf16)
    keep, send = halves(half, chip)
    quarter = (keep.astype(f32) + swap_x(send).astype(f32)).astype(bf16)
    parts = lax.all_to_all(quarter, "shard", split_axis=0, concat_axis=0, tiled=True)
    total = jnp.sum(parts.astype(f32), axis=0).astype(bf16)
    both = paired(total, swap_x(total), chip)
    return paired(both, swap_core(both), core)


def positions(offsets, tp_place, chunk, block):
    half = block // 2
    return chunk * block + (offsets + tp_place * half) % block


def attention_mask(block):
    place, tp_place = lax.axis_index("ctx"), lax.axis_index("tp")
    offsets = jnp.arange(block, dtype=jnp.int32)
    rows = positions(offsets, tp_place, place, block)
    keys = jnp.concatenate([positions(offsets, tp_place, place ^ j, block) for j in range(4)])
    return keys[None, :] <= rows[:, None]


def head_split(values, heads):
    return values.reshape(values.shape[0], heads, values.shape[1] // heads)


def attend(queries, key_all, value_all, mask, heads):
    scale_factor = (queries.shape[1] // heads) ** (-0.5)
    scores = dot("qhe,khe->hqk", head_split(queries, heads), head_split(key_all, heads))
    scores = jnp.where(mask, scores * scale_factor, masked_value)
    row_top = jnp.max(scores, axis=-1, keepdims=True)
    exponent = jnp.exp(scores - row_top)
    totals = jnp.sum(exponent, axis=-1, keepdims=True)
    probs = (exponent / totals).astype(bf16)
    out = dot("hqk,khe->qhe", probs, head_split(value_all, heads))
    return out.reshape(queries.shape).astype(bf16), row_top + jnp.log(totals)


def attend_back(queries, key_all, value_all, mask, heads, log_sums, grad_out):
    scale_factor = (queries.shape[1] // heads) ** (-0.5)
    query_heads, key_heads = head_split(queries, heads), head_split(key_all, heads)
    grad_heads = head_split(grad_out, heads)
    scores = dot("qhe,khe->hqk", query_heads, key_heads)
    scores = jnp.where(mask, scores * scale_factor, masked_value)
    probs = jnp.exp(scores - log_sums)
    grad_probs = dot("qhe,khe->hqk", grad_heads, head_split(value_all, heads))
    row_dot = jnp.sum(probs * grad_probs, axis=-1, keepdims=True)
    grad_scores = (probs * (grad_probs - row_dot)).astype(bf16)
    grad_q = dot("hqk,khe->qhe", grad_scores, key_heads) * scale_factor
    grad_k = dot("hqk,qhe->khe", grad_scores, query_heads) * scale_factor
    grad_v = dot("hqk,qhe->khe", probs.astype(bf16), grad_heads)
    return (
        grad_q.reshape(queries.shape).astype(bf16),
        jnp.concatenate(
            [grad_k.reshape(key_all.shape), grad_v.reshape(key_all.shape)], axis=1
        ).astype(bf16),
    )


def body_any(x_in, w_qkv, b_qv, w_proj, w_fc1, b_fc1, w_fc2, gains, biases, cotangent):
    depth = w_qkv.shape[0]
    shards = lax.axis_size("shard")
    own_rows, width = x_in.shape[0], x_in.shape[2]
    block = 2 * own_rows
    heads = b_qv.shape[2]
    half_width = w_qkv.shape[3]
    hidden = w_fc1.shape[2]

    small_shapes = [gains.shape, biases.shape, b_qv.shape, b_fc1.shape]
    small = small_rows([gains, biases, b_qv, b_fc1])
    group_a0 = jnp.concatenate([small, to_rows(w_qkv[0])])
    group_b0 = jnp.concatenate([to_rows(w_proj[0]), to_rows(w_fc1[0]), to_rows(w_fc2[0])])
    rest = []
    for index in range(1, depth):
        rest += [to_rows(w_qkv[index]), to_rows(w_proj[index]), to_rows(w_fc1[index]), to_rows(w_fc2[index])]
    group_rest = jnp.concatenate(rest)

    gathered_a0 = gather_packed(group_a0, shards)
    gathered_b0 = gather_packed(group_b0, shards)
    gathered_rest = gather_packed(group_rest, shards)

    def cutter(gathered, start):
        place = [start]

        def take(shape, axis):
            rows = math.prod(shape) // lanes
            piece = from_rows(gathered[:, place[0] : place[0] + rows], shape)
            place[0] += rows
            return join(piece, axis)

        return take

    shape_qkv, shape_proj = w_qkv.shape[1:], w_proj.shape[1:]
    shape_fc1, shape_fc2 = w_fc1.shape[1:], w_fc2.shape[1:]
    take_a, take_b, take_r = cutter(gathered_a0, small.shape[0]), cutter(gathered_b0, 0), cutter(gathered_rest, 0)
    weights = []
    for index in range(depth):
        take_q, take_o = (take_a, take_b) if index == 0 else (take_r, take_r)
        weights.append(
            (take_q(shape_qkv, 1), take_o(shape_proj, 1), take_o(shape_fc1, 0), take_o(shape_fc2, 1))
        )
    flat = gathered_a0[:, : small.shape[0]].reshape(shards, -1)
    vectors, start = [], 0
    for shape in small_shapes:
        size = math.prod(shape)
        piece = flat[:, start : start + size].reshape((shards,) + shape)
        vectors.append(join(piece, len(shape) - 1).astype(f32))
        start += size
    gain_all, bias_all, b_qv_all, b_fc1_all = vectors

    mask = attention_mask(block)
    x_own = x_in[:, 0]
    state = jnp.concatenate([x_own, swap_tp(x_own)]).astype(f32)
    g_own = cotangent[:, 0]
    grad_state = jnp.concatenate([g_own, swap_tp(g_own)]).astype(f32)

    stored = []
    for index in range(depth):
        w_query, w_out, w_first, w_second = weights[index]
        normed_in, scale_in = normalize(state)
        low_in = (normed_in * gain_all[index, 0] + bias_all[index, 0]).astype(bf16)
        bias_q = b_qv_all[index, 0].reshape(half_width)
        bias_v = b_qv_all[index, 1].reshape(half_width)
        queries = (dot("rd,df->rf", low_in, w_query[0]) + bias_q).astype(bf16)
        keys = dot("rd,df->rf", low_in, w_query[1]).astype(bf16)
        values = (dot("rd,df->rf", low_in, w_query[2]) + bias_v).astype(bf16)
        kv_own = jnp.concatenate([keys, values], axis=1)
        kv_chip = swap_x(kv_own)
        kv_all = jnp.concatenate([kv_own, swap_core(kv_own), kv_chip, swap_core(kv_chip)])
        key_all, value_all = kv_all[:, :half_width], kv_all[:, half_width:]
        attn, log_sums = attend(queries, key_all, value_all, mask, heads)
        attn_other = other_half(swap_tp(attn))
        w_out_other = swap_tp(w_out)
        middle = (
            state
            + dot("rf,fd->rd", attn, w_out)
            + dot("rf,fd->rd", attn_other, w_out_other)
            + bias_all[index, 1]
        )
        normed_mid, scale_mid = normalize(middle)
        low_mid = (normed_mid * gain_all[index, 1] + bias_all[index, 2]).astype(bf16)
        pre_act = dot("rd,df->rf", low_mid, w_first) + b_fc1_all[index].reshape(hidden)
        act = gelu_tanh(pre_act).astype(bf16)
        partial = dot("rf,fd->rd", act, w_second)
        if index == depth - 1:
            received = swap_tp(partial[own_rows:].astype(bf16)).astype(f32)
            output = middle[:own_rows] + partial[:own_rows] + received + bias_all[index, 3]
        else:
            received = other_half(swap_tp(partial.astype(bf16))).astype(f32)
            state = middle + partial + received + bias_all[index, 3]
        stored.append(
            (normed_in, scale_in, low_in, queries, key_all, value_all, log_sums, attn,
             normed_mid, scale_mid, low_mid, pre_act, act)
        )
    output = output.astype(bf16)[:, None]

    results = [None] * depth
    for index in reversed(range(depth)):
        w_query, w_out, w_first, w_second = weights[index]
        (normed_in, scale_in, low_in, queries, key_all, value_all, log_sums, attn,
         normed_mid, scale_mid, low_mid, pre_act, act) = stored[index]
        grad_bias_mlp = jnp.sum(grad_state, axis=0)
        grad_low = grad_state.astype(bf16)
        grad_hidden = dot("rd,fd->rf", grad_low, w_second)
        unused, gelu_pull = jax.vjp(gelu_tanh, pre_act)
        grad_pre = gelu_pull(grad_hidden)[0].astype(bf16)
        grad_w_second = dot("rf,rd->fd", act, grad_low)
        grad_w_first = dot("rd,rf->df", low_mid, grad_pre)
        grad_b_first = jnp.sum(grad_pre, axis=0, dtype=f32)
        partial = dot("rf,df->rd", grad_pre, w_first)
        mlp_rows = jnp.concatenate(
            [
                jax.vmap(to_rows)(split(grad_w_first.astype(bf16), 0, shards)),
                jax.vmap(to_rows)(split(grad_w_second.astype(bf16), 1, shards)),
            ],
            axis=1,
        )
        mlp_total = reduce_packed(mlp_rows)
        grad_mid = partial + other_half(swap_tp(partial.astype(bf16))).astype(f32)
        grad_gain_mid = jnp.sum(grad_mid * normed_mid, axis=0)
        grad_beta_mid = jnp.sum(grad_mid, axis=0)
        grad_middle = grad_state + norm_back(grad_mid * gain_all[index, 1], normed_mid, scale_mid)
        grad_bias_attn = jnp.sum(grad_middle, axis=0)
        grad_low = grad_middle.astype(bf16)
        grad_attn = dot("rd,fd->rf", grad_low, w_out).astype(bf16)
        grad_w_out = dot("rf,rd->fd", attn, grad_low)
        grad_q, grad_kv = attend_back(
            queries, key_all, value_all, mask, heads, log_sums, grad_attn
        )
        part = grad_kv.reshape(4, block, 2 * half_width)
        sent = swap_core(jnp.stack([part[1], part[3]])).astype(f32)
        mine = part[0].astype(f32) + sent[0]
        chip = (part[2].astype(f32) + sent[1]).astype(bf16)
        grad_kv = (mine + swap_x(chip).astype(f32)).astype(bf16)
        grad_qkv = jnp.stack([grad_q, grad_kv[:, :half_width], grad_kv[:, half_width:]])
        grad_w_query = dot("rd,crf->cdf", low_in, grad_qkv)
        grad_b_query = jnp.sum(grad_qkv[0::2], axis=1, dtype=f32)
        partial = dot("crf,cdf->rd", grad_qkv, w_query)
        grad_in = partial + other_half(swap_tp(partial.astype(bf16))).astype(f32)
        grad_gain_in = jnp.sum(grad_in * normed_in, axis=0)
        grad_beta_in = jnp.sum(grad_in, axis=0)
        grad_state = grad_middle + norm_back(grad_in * gain_all[index, 0], normed_in, scale_in)

        vectors = [
            jnp.stack([grad_gain_in, grad_gain_mid]),
            jnp.stack([grad_beta_in, grad_bias_attn, grad_beta_mid, grad_bias_mlp]),
            grad_b_query.reshape(2, heads, half_width // heads),
            grad_b_first.reshape(b_fc1_all.shape[1:]),
        ]
        parts = [split(vector, vector.ndim - 1, shards) for vector in vectors]
        part_shapes = [part.shape[1:] for part in parts]
        attn_rows = jnp.concatenate(
            [
                jax.vmap(to_rows)(split(grad_w_query.astype(bf16), 1, shards)),
                jax.vmap(to_rows)(split(grad_w_out.astype(bf16), 1, shards)),
                jax.vmap(lambda *own: small_rows(own))(*parts).astype(bf16),
            ],
            axis=1,
        )
        attn_total = reduce_packed(attn_rows)

        def pieces(total, shapes):
            place, out = 0, []
            for shape in shapes:
                rows = math.prod(shape) // lanes
                out.append(from_rows(total[place : place + rows], shape).astype(f32))
                place += rows
            return out, total[place:].reshape(-1)

        (out_fc1, out_fc2), unused = pieces(mlp_total, [shape_fc1, shape_fc2])
        (out_qkv, out_proj), tail = pieces(attn_total, [shape_qkv, shape_proj])
        small_out, start = [], 0
        for shape in part_shapes:
            size = math.prod(shape)
            small_out.append(tail[start : start + size].reshape(shape).astype(f32))
            start += size
        results[index] = (
            out_qkv, small_out[2], out_proj, out_fc1, small_out[3], out_fc2, small_out[0], small_out[1]
        )
    stacked = tuple(
        jnp.stack([results[index][member] for index in range(depth)]) for member in range(8)
    )
    return (output, grad_state[:own_rows, None]) + stacked


def compiler_params():
    return pltpu.CompilerParams(vmem_limit_bytes=56 * 2**20)


def whole(array):
    zeros = (0,) * array.ndim
    return pl.BlockSpec(array.shape, lambda i: zeros)


def rows_at(array, rows, start, lead=None, first=0):
    lead = array.shape[0] if lead is None else lead
    return pl.BlockSpec((lead, rows, lanes), lambda i: (first, start // rows, 0))


def run(kernel, outs, place, operands, scratch=(), flops=2**20, after=()):
    arrays, specs = [], []
    count = 1 + len(operands)

    def inner(*refs):
        kernel(*refs[:count], *refs[count + len(after) :])

    for operand in operands:
        array, spec = operand if isinstance(operand, tuple) else (operand, whole(operand))
        arrays.append(array)
        specs.append(spec)
    out_shape = [jax.ShapeDtypeStruct(shape, kind) for shape, kind in outs]
    after = list(after)
    arrays += after
    specs += [pl.BlockSpec(memory_space=pl.ANY)] * len(after)
    call = pl.pallas_call(
        inner,
        grid=(1,),
        out_shape=out_shape,
        in_specs=[pl.BlockSpec(memory_space=pltpu.SMEM)] + specs,
        out_specs=[whole(shape) for shape in out_shape],
        scratch_shapes=list(scratch),
        compiler_params=compiler_params(),
        cost_estimate=pl.CostEstimate(flops=flops, bytes_accessed=1024, transcendentals=0),
    )
    return list(call(place, *arrays))


def mm(left, right):
    return lax.dot_general(left, right, (((1,), (0,)), ((), ())), preferred_element_type=f32)


def mm_nt(left, right):
    return lax.dot_general(left, right, (((1,), (1,)), ((), ())), preferred_element_type=f32)


def mm_tn(left, right):
    return lax.dot_general(left, right, (((0,), (0,)), ((), ())), preferred_element_type=f32)


def lane_join(parts):
    return jnp.concatenate(parts, axis=1)


def row_join(parts):
    return jnp.concatenate(parts, axis=0)


class Pieces:
    def __init__(self, refs):
        self.local, self.far = refs[0], refs[1:]

    def tile(self, k, p, start, rows):
        if k == 0:
            return self.local[p, start : start + rows]
        return self.far[p][k - 1, start : start + rows]


def first_block(pieces, p):
    return row_join(
        [lane_join([pieces.tile(k, p, j * 128, 128) for j in range(2)]) for k in range(4)]
    )


def second_block(pieces, p):
    return lane_join([pieces.tile(k, p, 0, 256) for k in range(4)])


def small_row(small_local, small_far, row):
    parts = [small_local[0, row : row + 1]] + [small_far[k, row : row + 1] for k in range(3)]
    return lane_join(parts).astype(f32)


def spread(small_local, small_far, row, place_z, half, later=None):
    def rows_from(row):
        return row_join(
            [small_local[0, row : row + 1]] + [small_far[k, row : row + 1] for k in range(3)]
        ).astype(f32)

    source = rows_from(row)
    if later is not None:
        source = jnp.where(later == 0, source, rows_from(row + 1))
    source = source.astype(bf16)
    take = lax.broadcasted_iota(jnp.int32, (128, 256), 0)
    lane = lax.broadcasted_iota(jnp.int32, (128, 256), 1)
    wanted = half * 64 + (lane // 64) * 16 + lane % 16
    table = (take == wanted).astype(f32).astype(bf16)
    rows = mm(source, table)
    chunk = lax.broadcasted_iota(jnp.int32, (4, 256), 0)
    lane = lax.broadcasted_iota(jnp.int32, (4, 256), 1)
    keep = (lane % 64) // 16 == (place_z - chunk + 4) % 4
    return jnp.sum(jnp.where(keep, rows, 0.0), axis=0, keepdims=True)


def pack_kernel(kinds):
    def kernel(place, *refs):
        c = place[1]
        out, send = refs[-2:]
        start = 0
        for ref, kind in zip(refs, kinds):
            for q in range(4):
                to = q ^ c
                if kind == "first":
                    for j in range(2):
                        column = (2 * q + j) * 128
                        out[to, start + j * 128 : start + (j + 1) * 128] = ref[0, :, column : column + 128]
                elif kind == "second":
                    out[to, start : start + 256] = ref[0, q * 256 : (q + 1) * 256]
                elif kind == "proj":
                    out[to, start : start + 64] = ref[0, q * 64 : (q + 1) * 64]
                elif kind == "qkv":
                    for tile in range(6):
                        row = start + tile * 32
                        column = (tile % 2) * 128
                        out[to, row : row + 32] = ref[0, tile // 2, q * 32 : (q + 1) * 32, column : column + 128]
                else:
                    out[to, start : start + 32] = ref[...]
            start += kind_rows[kind]
        send[...] = out[0]

    return kernel


kind_rows = {"first": 256, "second": 256, "proj": 64, "qkv": 192, "small": 32}


def pack(place, kinds, arrays, index, after=()):
    rows = sum(kind_rows[kind] for kind in kinds)
    operands = []
    for kind, array in zip(kinds, arrays):
        if kind == "small":
            operands.append(array)
        else:
            block = (1,) + array.shape[1:]
            at = (index,) + (0,) * (array.ndim - 1)
            operands.append((array, pl.BlockSpec(block, lambda i, at=at: at)))
    return run(
        pack_kernel(kinds), [((4, rows, lanes), bf16), ((rows, lanes), bf16)], place, operands, flops=2**20, after=after
    )


def shift(values, step):
    return lax.ppermute(values, "shard", [(z, (z + step) % 4) for z in range(4)])


def far_chunks(send):
    return [shift(send, k) for k in (1, 2, 3)]


def stack_kernel(place, one, two, three, out):
    for k, ref in enumerate((one, two, three)):
        out[k] = ref[...]


def stack(place, got, after=()):
    return run(stack_kernel, [((3,) + got[0].shape, bf16)], place, got, after=after)[0]


def copy_kernel(place, source, out):
    out[...] = source[...]


def hand_on(place, array, after):
    return run(copy_kernel, [(array.shape, bf16)], place, [array], after=after)[0]


def pieces_of(group, rows, start):
    return [(array, rows_at(array, rows, start)) for array in group]


def small_of(group):
    return [(group[0], rows_at(group[0], 32, 256, lead=1)), (group[1], rows_at(group[1], 32, 256))]


def query_kernel(index, first_layer):
    def kernel(place, *refs):
        c = place[1]
        if first_layer:
            own, peer, small_local, small_far = refs[:4]
            pieces = Pieces(refs[4:9])
            later, later_out, grad_out = refs[9], refs[15], refs[16]
            later_out[...] = later[...]
            grad_out[...] = row_join([own[128:], peer[128:]]).astype(f32)
            state_out, low_out, q_out, kv_out, w_out = refs[10:15]
            state = row_join([own[:128], peer[:128]]).astype(f32)
        else:
            middle, mine, other, small_local, small_far = refs[:5]
            pieces = Pieces(refs[5:10])
            state_out, low_out, q_out, kv_out, w_out = refs[10:]
            received = row_join([other[128:], other[:128]])
            state = (
                middle[...]
                + mine[...].astype(f32)
                + received.astype(f32)
                + small_row(small_local, small_far, 4 + 4 * (index - 1) + 3)
            )
        for k in range(4):
            for p in range(4):
                for tile in range(6):
                    w_out[k, p ^ c, :, tile * 128 : (tile + 1) * 128] = pieces.tile(k, p, tile * 32, 32)
        state_out[...] = state
        normed, scale = normalize(state)
        low = (
            normed * small_row(small_local, small_far, 2 * index)
            + small_row(small_local, small_far, 4 + 4 * index)
        ).astype(bf16)
        low_out[...] = low
        w_all = w_out[...].reshape(512, 768)
        row = 12 + index
        bias_q = spread(small_local, small_far, row, place[0], 0)
        bias_v = spread(small_local, small_far, row, place[0], 1)
        kv_out[:, :256] = mm(low, w_all[:, 256:512]).astype(bf16)
        kv_out[:, 256:] = (mm(low, w_all[:, 512:]) + bias_v).astype(bf16)
        q_out[...] = (mm(low, w_all[:, :256]) + bias_q).astype(bf16)

    return kernel


def seen(place, j):
    c, t = place[1], place[2]
    if j:
        return None
    row = lax.broadcasted_iota(jnp.int32, (256, 256), 0) ^ (t * 128)
    key = lax.broadcasted_iota(jnp.int32, (256, 256), 1) ^ (t * 128)
    return key <= row


def masked_scores(query, chunks, own_mask, place):
    parts = []
    for j in range(4):
        scores = mm_nt(query, chunks[j]) * 0.125
        if j == 0:
            scores = jnp.where(own_mask, scores, masked_value)
        else:
            scores = jnp.where((place[1] ^ j) < place[1], scores, masked_value)
        parts.append(scores)
    return parts


def attend_kernel(place, *refs):
    c = place[1]
    q, chunks = refs[0], refs[1:5]
    pieces = Pieces(refs[5:10])
    attn_out, lse_out, partial_out, w_out = refs[10:]
    for k in range(4):
        for p in range(4):
            w_out[p ^ c, :, k * 128 : (k + 1) * 128] = pieces.tile(k, p, 0, 64)
    own_mask = seen(place, 0)
    results = []
    for head in range(4):
        low, high = head * 64, (head + 1) * 64
        parts = masked_scores(q[:, low:high], [chunk[:, low:high] for chunk in chunks], own_mask, place)
        scores = lane_join(parts)
        top = jnp.max(scores, axis=1, keepdims=True)
        exponent = jnp.exp(scores - top)
        total = jnp.sum(exponent, axis=1, keepdims=True)
        values = row_join([chunk[:, 256 + low : 256 + high] for chunk in chunks])
        results.append(mm(exponent.astype(bf16), values) / total)
        lse_out[:, head : head + 1] = top + jnp.log(total)
    attn = lane_join(results).astype(bf16)
    attn_out[...] = attn
    partial_out[...] = mm(attn, w_out[...].reshape(256, 512)).astype(bf16)


def mlp_kernel(index):
    def kernel(place, *refs):
        state, mine, other, small_local, small_far = refs[:5]
        first, second = Pieces(refs[5:10]), Pieces(refs[10:15])
        middle_out, low_out, pre_out, partial_out = refs[15:]
        received = row_join([other[128:], other[:128]])
        middle = (
            state[...]
            + mine[...].astype(f32)
            + received.astype(f32)
            + small_row(small_local, small_far, 4 + 4 * index + 1)
        )
        middle_out[...] = middle
        normed, scale = normalize(middle)
        low = (
            normed * small_row(small_local, small_far, 2 * index + 1)
            + small_row(small_local, small_far, 4 + 4 * index + 2)
        ).astype(bf16)
        low_out[...] = low
        total = None
        for p in range(4):
            q = p ^ place[1]
            bias = spread(small_local, small_far, 14 + 2 * index, place[0], q % 2, q // 2)
            pre = mm(low, first_block(first, p)) + bias
            pre_out[:, p * 256 : (p + 1) * 256] = pre
            act = gelu_tanh(pre).astype(bf16)
            part = mm(act, second_block(second, p))
            total = part if total is None else total + part
        partial_out[...] = total.astype(bf16)

    return kernel


root = math.sqrt(2 / math.pi)


def mlp_back(grad, pre_ref, low_ref, first, second, place, outs):
    partial_out, bias_out, b_first_out, keep, send = outs
    grad_low = grad.astype(bf16)
    bias_out[...] = jnp.sum(grad, axis=0, keepdims=True)
    total = None
    for p in range(4):
        pre = pre_ref[:, p * 256 : (p + 1) * 256]
        square = pre * pre
        wave = jnp.tanh(root * pre * (1 + 0.044715 * square))
        half = 0.5 * (1 + wave)
        act = (pre * half).astype(bf16)
        slope = half + 0.5 * pre * (1 - wave * wave) * root * (1 + 3 * 0.044715 * square)
        w_second = second_block(second, p)
        grad_pre = mm_nt(grad_low, w_second) * slope
        grad_pre_low = grad_pre.astype(bf16)
        b_first_out[p ^ place[1]] = jnp.sum(grad_pre_low.astype(f32), axis=0, keepdims=True)
        part = mm_nt(grad_pre_low, first_block(first, p))
        total = part if total is None else total + part
        to = keep if p % 2 == 0 else send
        grad_first = mm_tn(low_ref[...], grad_pre_low).astype(bf16)
        grad_second = mm_tn(act, grad_low).astype(bf16)
        for k in range(4):
            for j in range(2):
                to[p // 2, k, j * 128 : (j + 1) * 128] = grad_first[
                    k * 128 : (k + 1) * 128, j * 128 : (j + 1) * 128
                ]
            to[p // 2, k, 256:512] = grad_second[:, k * 128 : (k + 1) * 128]
    partial_out[...] = total.astype(bf16)


def norm_step(grad_out, gain, values):
    normed, scale = normalize(values)
    sums = row_join(
        [
            jnp.sum(grad_out * normed, axis=0, keepdims=True),
            jnp.sum(grad_out, axis=0, keepdims=True),
        ]
    )
    return norm_back(grad_out * gain, normed, scale), sums


def received_sum(mine, other):
    return mine[...].astype(f32) + row_join([other[128:], other[:128]]).astype(f32)


def top_kernel(place, *refs):
    grad, pre, low = refs[:3]
    first, second = Pieces(refs[3:8]), Pieces(refs[8:13])
    mlp_back(grad[...], pre, low, first, second, place, refs[13:])


def lower_kernel(index):
    def kernel(place, *refs):
        grad_mid, mine, other, state, small_local, small_far, pre, low = refs[:8]
        first, second = Pieces(refs[8:13]), Pieces(refs[13:18])
        grad_out, sums_out = refs[18:20]
        grad, sums = norm_step(
            received_sum(mine, other), small_row(small_local, small_far, 2 * (index + 1)), state[...]
        )
        sums_out[...] = sums
        grad = grad_mid[...] + grad
        grad_out[...] = grad
        mlp_back(grad, pre, low, first, second, place, refs[20:])

    return kernel


def attend_back_kernel(index):
    def kernel(place, *refs):
        mine, other, middle, grad_state, small_local, small_far = refs[:6]
        attn, w_out, q = refs[6:9]
        chunks, lse = refs[9:13], refs[13]
        grad_out, sums_out, gw_out, dq_out, keep, send = refs[14:]
        grad, sums = norm_step(
            received_sum(mine, other), small_row(small_local, small_far, 2 * index + 1), middle[...]
        )
        grad = grad_state[...] + grad
        grad_out[...] = grad
        sums_out[0:2] = sums
        sums_out[2:3] = jnp.sum(grad, axis=0, keepdims=True)
        grad_low = grad.astype(bf16)
        grad_attn = mm_nt(grad_low, w_out[...].reshape(256, 512)).astype(bf16)
        gw_out[...] = mm_tn(attn[...], grad_low).astype(bf16).reshape(4, 64, 512)
        own_mask = seen(place, 0)
        dq_all = []
        dk_all = [[] for j in range(4)]
        dv_all = [[] for j in range(4)]
        for head in range(4):
            low, high = head * 64, (head + 1) * 64
            query, grad_head = q[:, low:high], grad_attn[:, low:high]
            keys = [chunk[:, low:high] for chunk in chunks]
            row_dot = jnp.sum(
                grad_head.astype(f32) * attn[:, low:high].astype(f32), axis=1, keepdims=True
            )
            log_sum = lse[:, head : head + 1]
            parts = masked_scores(query, keys, own_mask, place)
            dq = None
            for j in range(4):
                probs = jnp.exp(parts[j] - log_sum)
                grad_probs = mm_nt(grad_head, chunks[j][:, 256 + low : 256 + high])
                grad_scores = (probs * (grad_probs - row_dot)).astype(bf16)
                part = mm(grad_scores, keys[j])
                dq = part if dq is None else dq + part
                dk_all[j].append(mm_tn(grad_scores, query) * 0.125)
                dv_all[j].append(mm_tn(probs.astype(bf16), grad_head))
            dq_all.append(dq * 0.125)
        dq_out[...] = lane_join(dq_all).astype(bf16)
        for j in range(4):
            to = keep if j % 2 == 0 else send
            to[j // 2, :, :256] = lane_join(dk_all[j]).astype(bf16)
            to[j // 2, :, 256:] = lane_join(dv_all[j]).astype(bf16)

    return kernel


def halve_kernel(place, keep, got, own_out, send_out):
    own_out[...] = (keep[0].astype(f32) + got[0].astype(f32)).astype(bf16)
    send_out[...] = (keep[1].astype(f32) + got[1].astype(f32)).astype(bf16)


def query_back_kernel(place, *refs):
    dq, dkv, got, low, w_ref, gw_ref = refs[:6]
    partial_out, b_out, keep, send, scratch = refs[6:]
    c = place[1]
    grad_kv = (dkv[...].astype(f32) + got[...].astype(f32)).astype(bf16)
    grad_qkv = lane_join([dq[...], grad_kv])
    partial_out[...] = mm_nt(grad_qkv, w_ref[...].reshape(512, 768)).astype(bf16)
    b_out[0:1] = jnp.sum(dq[...].astype(f32), axis=0, keepdims=True)
    b_out[1:2] = jnp.sum(grad_kv[:, 256:].astype(f32), axis=0, keepdims=True)
    scratch[...] = mm_tn(low[...], grad_qkv).astype(bf16).reshape(4, 4, 32, 768)
    for p in range(4):
        to = keep if p % 2 == 0 else send
        for k in range(4):
            for tile in range(6):
                to[p // 2, k, tile * 32 : (tile + 1) * 32] = scratch[
                    k, p ^ c, :, tile * 128 : (tile + 1) * 128
                ]
            to[p // 2, k, 192:256] = gw_ref[p ^ c, :, k * 128 : (k + 1) * 128]


def four_kernel(place, one, two, three, four, out):
    out[...] = (one[...] + two[...]) + (three[...] + four[...])


def quarter_kernel(place, own, got, *outs):
    for k in range(4):
        outs[k][...] = (own[k].astype(f32) + got[k].astype(f32)).astype(bf16)


def total_kernel(place, own, one, two, three, out):
    total = own[...].astype(f32) + one[...].astype(f32)
    out[...] = (total + (two[...].astype(f32) + three[...].astype(f32))).astype(bf16)


class Chain:
    def __init__(self, place, keep, send):
        self.place, self.rows = place, keep.shape[2]
        self.state = [keep, send]

    def halve(self, after=()):
        keep, send = self.state
        self.state = run(
            halve_kernel, [((4, self.rows, lanes), bf16)] * 2, self.place, [keep, swap_core(send)], flops=2**20, after=after
        )

    def quarter(self, after=()):
        own, send = self.state
        self.state = run(
            quarter_kernel, [((self.rows, lanes), bf16)] * 4, self.place, [own, swap_x(send)], flops=2**20, after=after
        )

    def total(self, after=()):
        got = [shift(self.state[k], 4 - k) for k in (1, 2, 3)]
        self.state = run(
            total_kernel, [((self.rows, lanes), bf16)], self.place, [self.state[0]] + got, flops=2**20, after=after
        )

    def collect(self):
        (total,) = self.state
        chip = swap_x(total)
        return [total, swap_core(total), chip, swap_core(chip)]


def hidden_out_kernel(place, *refs):
    c = place[1]
    first_out, second_out, scratch = refs[-3:]
    for p in range(4):
        scratch[p] = refs[p][...].astype(f32)
    for q in range(4):
        for j in range(2):
            column = (2 * q + j) * 128
            first_out[0, :, column : column + 128] = scratch[q ^ c, j * 128 : (j + 1) * 128]
        second_out[0, q * 256 : (q + 1) * 256] = scratch[q ^ c, 256:]


def heads_out_kernel(place, *refs):
    c = place[1]
    qkv_out, proj_out, scratch = refs[-3:]
    for p in range(4):
        scratch[p] = refs[p][...].astype(f32)
    for q in range(4):
        for tile in range(6):
            column = (tile % 2) * 128
            qkv_out[0, tile // 2, q * 32 : (q + 1) * 32, column : column + 128] = scratch[
                q ^ c, tile * 32 : (tile + 1) * 32
            ]
        proj_out[0, q * 64 : (q + 1) * 64] = scratch[q ^ c, 192:]


def layer_out(kernel, place, totals, layer, shapes, before, after):
    rows = totals[0].shape[0]
    extra = list(before) + list(after)

    def inner(*refs):
        kernel(*refs[:5], *refs[5 + len(extra) :])

    def block(shape):
        at = (layer,) + (0,) * (len(shape) - 1)
        return pl.BlockSpec((1,) + tuple(shape[1:]), lambda i: at)

    return list(
        pl.pallas_call(
            inner,
            grid=(1,),
            out_shape=[jax.ShapeDtypeStruct(shape, f32) for shape in shapes],
            in_specs=[pl.BlockSpec(memory_space=pltpu.SMEM)]
            + [whole(total) for total in totals]
            + [pl.BlockSpec(memory_space=pl.ANY)] * len(extra),
            out_specs=[block(shape) for shape in shapes],
            scratch_shapes=[pltpu.VMEM((4, rows, lanes), f32)],
            input_output_aliases={5 + i: i for i in range(len(before))},
            compiler_params=compiler_params(),
            cost_estimate=pl.CostEstimate(flops=2**20, bytes_accessed=1024, transcendentals=0),
        )(place, *totals, *extra)
    )


def hidden_out(place, totals, layer, shape_one, shape_two, before, after=()):
    return layer_out(hidden_out_kernel, place, totals, layer, (shape_one, shape_two), before, after)


def heads_out(place, totals, layer, shape_one, shape_two, before, after=()):
    return layer_out(heads_out_kernel, place, totals, layer, (shape_one, shape_two), before, after)


def last_kernel(place, *refs):
    grad_mid, mine, other, state, small_local, small_far = refs[:6]
    sums_in = refs[6]
    sums_mid, bias_mlp, b_query, b_first = refs[7:9], refs[9:11], refs[11:13], refs[13:15]
    grad_out, out = refs[15:]
    grad, sums = norm_step(received_sum(mine, other), small_row(small_local, small_far, 0), state[...])
    grad_out[...] = grad_mid[:128] + grad[:128]
    for layer in range(2):
        inner = sums if layer == 0 else sums_in[...]
        mid = sums_mid[layer]
        rows = [
            (2 * layer, inner[0:1]),
            (2 * layer + 1, mid[0:1]),
            (4 + 4 * layer, inner[1:2]),
            (5 + 4 * layer, mid[2:3]),
            (6 + 4 * layer, mid[1:2]),
            (7 + 4 * layer, bias_mlp[layer][...]),
        ]
        for k in range(4):
            for row, value in rows:
                out[k, row : row + 1] = value[:, k * 128 : (k + 1) * 128]
            for channel in range(2):
                for j in range(2):
                    row = 12 + 4 * layer + 2 * channel + j
                    out[k, row : row + 1] = b_query[layer][channel : channel + 1, j * 128 : (j + 1) * 128]
            for q in range(4):
                for j in range(2):
                    row = 20 + 8 * layer + 2 * q + j
                    out[k, row : row + 1] = b_first[layer][q, :, j * 128 : (j + 1) * 128]
    out[:, 36:] = jnp.zeros((4, 4, lanes), f32)


def turn(values, place_z, back):
    rows = values.shape[0]
    chunks = values.reshape(rows, 4, lanes)
    order = (place_z - jnp.arange(4)) % 4
    return jnp.concatenate(
        [lax.dynamic_slice_in_dim(values, order[k] * lanes, lanes, 1) for k in range(4)], axis=1
    )


def body_four(x_in, w_qkv, b_qv, w_proj, w_fc1, b_fc1, w_fc2, gains, biases, cotangent):
    z, c, t = lax.axis_index("shard"), lax.axis_index("ctx"), lax.axis_index("tp")
    place = jnp.stack([z, c, t]).astype(jnp.int32)
    flat = jnp.concatenate([array.reshape(-1) for array in (gains, biases, b_qv, b_fc1)])
    small = jnp.pad(flat, (0, 32 * lanes - flat.shape[0])).reshape(32, lanes)

    local_a, send_a = pack(place, ("qkv", "proj", "small"), (w_qkv, w_proj, small), 0)
    pair_own = turn(jnp.concatenate([x_in[:, 0], cotangent[:, 0]]), z, False)
    pair_peer = swap_tp(pair_own)
    got_a = far_chunks(send_a)
    far_a = stack(place, got_a)
    chip_a = swap_x(far_a)
    group_a0 = [local_a, far_a, swap_core(far_a), chip_a, swap_core(chip_a)]
    local_b, send_b = pack(place, ("first", "second"), (w_fc1, w_fc2), 0, after=[far_a])
    got_b = far_chunks(send_b)
    kinds = ("first", "second", "proj", "qkv")
    local_1, send_1 = pack(place, kinds, (w_fc1, w_fc2, w_proj, w_qkv), 1, after=[far_a, send_b])

    small_parts = small_of(group_a0)
    parts = {
        "qkv": [pieces_of(group_a0, 192, 0)],
        "proj": [pieces_of(group_a0, 64, 192)],
        "first": [],
        "second": [],
    }
    square, wide = (256, 512), (256, 256)
    saved = []
    for layer in range(2):
        source = [pair_own, pair_peer] if layer == 0 else [middle, partial, received]
        extra = [send_1] if layer == 0 else []
        more = [(send_1.shape, bf16), (square, f32)] if layer == 0 else []
        state, low_in, q, kv, w_all, *passed = run(
            query_kernel(layer, layer == 0),
            [(square, f32), (square, bf16), (wide, bf16), (square, bf16), ((4, 4, 32, 768), bf16)] + more,
            place,
            source + small_parts + parts["qkv"][layer] + extra,
        )
        behind = []
        if layer == 0:
            got_1 = far_chunks(passed[0])
            g_all = passed[1]
            far_b = stack(place, got_b, [kv])
            behind = [far_b]
        kv_chip = swap_x(kv)
        chunks = [kv, swap_core(kv), kv_chip, swap_core(kv_chip)]
        attn, lse, partial, w_out = run(
            attend_kernel,
            [(wide, bf16), ((256, lanes), f32), (square, bf16), ((4, 64, 512), bf16)],
            place,
            [q] + chunks + parts["proj"][layer],
            after=behind,
        )
        received = swap_tp(partial)
        behind = []
        if layer == 0:
            chip_b = hand_on(place, swap_x(far_b), [received])
            group_b0 = [local_b, far_b, swap_core(far_b), chip_b, swap_core(chip_b)]
            parts["first"].append(pieces_of(group_b0, 256, 0))
            parts["second"].append(pieces_of(group_b0, 256, 256))
            far_1 = stack(place, got_1, [chip_b])
            behind = [far_1]
        middle, low_mid, pre, partial = run(
            mlp_kernel(layer),
            [(square, f32), (square, bf16), ((256, 1024), f32), (square, bf16)],
            place,
            [state, partial, received] + small_parts + parts["first"][layer] + parts["second"][layer],
            after=behind,
        )
        if layer == 0:
            received = swap_tp(partial)
            chip_1 = hand_on(place, swap_x(far_1), [received])
            group_1 = [local_1, far_1, swap_core(far_1), chip_1, swap_core(chip_1)]
            parts["qkv"].append(pieces_of(group_1, 192, 576))
            parts["proj"].append(pieces_of(group_1, 64, 512))
            parts["first"].append(pieces_of(group_1, 256, 0))
            parts["second"].append(pieces_of(group_1, 256, 256))
        saved.append((state, low_in, q, chunks, w_all, attn, lse, w_out, middle, low_mid, pre))

    received = swap_tp(partial[128:]).astype(f32)
    output = None
    bias_last = jnp.concatenate([small_parts[0][0][0, 267:268], small_parts[1][0][:, 267]]).reshape(1, 512)
    output = middle[:128] + partial[:128].astype(f32) + received + bias_last.astype(f32)
    output = turn(output.astype(bf16), z, True)[:, None]

    hidden_outs = [
        (square, bf16),
        ((1, 512), f32),
        ((4, 1, 256), f32),
        ((2, 4, 512, lanes), bf16),
        ((2, 4, 512, lanes), bf16),
    ]
    sums_mid, bias_mlp, b_query, b_first = [0, 0], [0, 0], [0, 0], [0, 0]
    hidden, heads = [None, None], [None, None]
    for layer in (1, 0):
        state, low_in, q, chunks, w_all, attn, lse, w_out, middle, low_mid, pre = saved[layer]
        tail = [pre, low_mid] + parts["first"][layer] + parts["second"][layer]
        if layer == 1:
            grad_state = g_all
            partial, bias_mlp[1], b_first[1], keep, send = run(
                top_kernel, hidden_outs, place, [grad_state] + tail
            )
            behind = []
        else:
            grad_state, sums_in, partial, bias_mlp[0], b_first[0], keep, send = run(
                lower_kernel(0),
                [(square, f32), ((2, 512), f32)] + hidden_outs,
                place,
                [grad_mid, partial, swap_tp(partial), saved[1][0]] + small_parts + tail,
                after=heads[1].state,
            )
            heads[1].quarter(after=[partial])
            behind = list(heads[1].state)
        hidden[layer] = Chain(place, keep, send)
        hidden[layer].halve()
        grad_mid, sums_mid[layer], gw_out, dq, keep, send = run(
            attend_back_kernel(layer),
            [
                (square, f32),
                ((3, 512), f32),
                ((4, 64, 512), bf16),
                (wide, bf16),
                ((2, 256, 512), bf16),
                ((2, 256, 512), bf16),
            ],
            place,
            [partial, swap_tp(partial), middle, grad_state] + small_parts + [attn, w_out, q] + chunks + [lse],
            after=hidden[layer].state + behind,
        )
        hidden[layer].quarter(after=[keep])
        behind = list(hidden[layer].state)
        if layer == 0:
            heads[1].total(after=[keep])
            behind += heads[1].state
        dkv, chip = run(halve_kernel, [(square, bf16)] * 2, place, [keep, swap_core(send)], after=behind)
        hidden[layer].total(after=[chip])
        if layer == 1:
            behind = [output]
        else:
            outs_hidden = hidden_out(place, hidden[1].collect(), 1, w_fc1.shape, w_fc2.shape, [], after=[chip])
            behind = list(outs_hidden)
        behind += hidden[layer].state
        partial, b_query[layer], keep, send = run(
            query_back_kernel,
            [
                (square, bf16),
                ((2, 256), f32),
                ((2, 4, 256, lanes), bf16),
                ((2, 4, 256, lanes), bf16),
            ],
            place,
            [dq, dkv, swap_x(chip), low_in, w_all, gw_out],
            scratch=[pltpu.VMEM((4, 4, 32, 768), bf16)],
            after=behind,
        )
        heads[layer] = Chain(place, keep, send)
        heads[layer].halve()
    grad_x, sums = run(
        last_kernel,
        [((128, 512), f32), ((4, 40, lanes), f32)],
        place,
        [grad_mid, partial, swap_tp(partial), saved[0][0]]
        + small_parts
        + [sums_in]
        + sums_mid
        + bias_mlp
        + b_query
        + b_first,
        after=heads[0].state,
    )
    heads[0].quarter(after=[grad_x])
    grad_x = turn(grad_x, z, True)[:, None]
    (sums,) = run(
        four_kernel,
        [((4, 40, lanes), f32)],
        place,
        [sums, swap_core(sums), swap_x(sums), swap_both(sums)],
        after=heads[0].state,
    )
    heads[0].total(after=[sums])
    outs_heads = heads_out(
        place, heads[1].collect(), 1, w_qkv.shape, w_proj.shape, [], after=heads[0].state
    )
    grad_fc1, grad_fc2 = hidden_out(
        place, hidden[0].collect(), 0, w_fc1.shape, w_fc2.shape, outs_hidden, after=heads[0].state
    )
    got = [shift(sums[k], 4 - k) for k in (1, 2, 3)]
    total = sums[0] + got[0] + got[1] + got[2]
    grad_gains = total[:4].reshape(gains.shape)
    grad_biases = total[4:12].reshape(biases.shape)
    rest_q = total[12:20].reshape(2, 2, 4, 64)
    rest_f = total[20:36].reshape(2, 16, 64)
    grad_b_qv = lax.dynamic_slice_in_dim(rest_q, z * 16, 16, 3)
    grad_b_fc1 = lax.dynamic_slice_in_dim(rest_f, z * 16, 16, 2)

    grad_qkv, grad_proj = heads_out(place, heads[0].collect(), 0, w_qkv.shape, w_proj.shape, outs_heads)
    return (
        output, grad_x, grad_qkv, grad_b_qv, grad_proj, grad_fc1, grad_b_fc1, grad_fc2, grad_gains, grad_biases
    )


def body(*args):
    x_in, w_qkv, b_qv, w_proj, w_fc1 = args[:5]
    expected = ((128, 1, 512), (2, 3, 128, 256), (2, 2, 4, 16), (2, 256, 128), (2, 128, 1024))
    sizes = (lax.axis_size("shard"), lax.axis_size("ctx"), lax.axis_size("tp"))
    shapes = tuple(array.shape for array in (x_in, w_qkv, b_qv, w_proj, w_fc1))
    if sizes == (4, 4, 2) and shapes == expected:
        return body_four(*args)
    return body_any(*args)


def solution(mesh):
    return jax.shard_map(
        body,
        mesh=mesh,
        in_specs=(
            P(("ctx", "tp"), "shard", None),
            P(None, None, "shard", "tp"),
            P(None, None, "tp", "shard"),
            P(None, "tp", "shard"),
            P(None, "shard", "tp"),
            P(None, "tp", "shard"),
            P(None, "tp", "shard"),
            P(None, None, "shard"),
            P(None, None, "shard"),
            P(("ctx", "tp"), "shard", None),
        ),
        out_specs=(
            P(("ctx", "tp"), "shard", None),
            P(("ctx", "tp"), "shard", None),
            P(None, None, "shard", "tp"),
            P(None, None, "tp", "shard"),
            P(None, "tp", "shard"),
            P(None, "shard", "tp"),
            P(None, "tp", "shard"),
            P(None, "tp", "shard"),
            P(None, None, "shard"),
            P(None, None, "shard"),
        ),
        check_vma=False,
    )
```

```python
import functools
import math

import jax
import jax.numpy as jnp
from jax import lax
from jax.experimental import pallas as pl
from jax.experimental.pallas import tpu as pltpu
from jax.sharding import PartitionSpec as P

epsilon = 1e-05
masked_value = -1e30
lanes = 128
f32 = jnp.float32
bf16 = jnp.bfloat16


def normalize(values):
    center = jnp.mean(values, axis=-1, keepdims=True)
    shifted = values - center
    scale_inv = lax.rsqrt(jnp.mean(shifted * shifted, axis=-1, keepdims=True) + epsilon)
    return (shifted * scale_inv, scale_inv)


def norm_back(grad_norm, normed, scale_inv):
    mean_grad = jnp.mean(grad_norm, axis=-1, keepdims=True)
    mean_prod = jnp.mean(grad_norm * normed, axis=-1, keepdims=True)
    return scale_inv * (grad_norm - mean_grad - normed * mean_prod)


def gelu_tanh(values):
    return jax.nn.gelu(values, approximate=True)


def dot(pattern, left, right):
    return jnp.einsum(pattern, left, right, preferred_element_type=f32)


def to_rows(array):
    rows, columns = array.shape[-2:]
    if columns % lanes or rows % 16:
        return array.reshape(-1, lanes)
    tiles = array.reshape(-1, rows, columns // lanes, lanes)
    return jnp.swapaxes(tiles, 1, 2).reshape(-1, lanes)


def from_rows(packed, shape):
    rows, columns = shape[-2:]
    lead = packed.shape[:-2]
    if columns % lanes or rows % 16:
        return packed.reshape(lead + tuple(shape))
    count = math.prod(shape[:-2])
    tiles = packed.reshape(lead + (count, columns // lanes, rows, lanes))
    return jnp.swapaxes(tiles, -3, -2).reshape(lead + tuple(shape))


def small_rows(arrays):
    flat = jnp.concatenate([array.reshape(-1) for array in arrays])
    size = -(-flat.shape[0] // (64 * lanes)) * 64 * lanes
    return jnp.pad(flat, (0, size - flat.shape[0])).reshape(-1, lanes)


def join(gathered, axis):
    moved = jnp.moveaxis(gathered, 0, axis)
    shape = moved.shape
    return moved.reshape(shape[:axis] + (shape[axis] * shape[axis + 1],) + shape[axis + 2 :])


def split(whole, axis, shards):
    shape = whole.shape
    parts = whole.reshape(shape[:axis] + (shards, shape[axis] // shards) + shape[axis + 1 :])
    return jnp.moveaxis(parts, axis, 0)


def swap_tp(values):
    return lax.ppermute(values, "tp", [(0, 1), (1, 0)])


def swap_core(values):
    return lax.ppermute(values, "ctx", [(0, 1), (1, 0), (2, 3), (3, 2)])


def swap_x(values):
    return lax.ppermute(values, "ctx", [(0, 2), (2, 0), (1, 3), (3, 1)])


def swap_both(values):
    return lax.ppermute(values, "ctx", [(0, 3), (3, 0), (1, 2), (2, 1)])


def other_half(values):
    half = values.shape[0] // 2
    return jnp.concatenate([values[half:], values[:half]])


def gather_packed(packed, shards):
    quarter = packed.shape[0] // 4
    own = lax.dynamic_slice_in_dim(packed, lax.axis_index("ctx") * quarter, quarter, 0)
    return lax.all_gather(own, ("shard", "ctx"), axis=0, tiled=True).reshape(
        shards, packed.shape[0], lanes
    )


def halves(values, bit):
    half = values.shape[1] // 2
    keep = lax.dynamic_slice_in_dim(values, bit * half, half, 1)
    send = lax.dynamic_slice_in_dim(values, (1 - bit) * half, half, 1)
    return keep, send


def paired(own, other, bit):
    return jnp.where(
        bit == 0, jnp.concatenate([own, other]), jnp.concatenate([other, own])
    )


def reduce_packed(packed):
    place = lax.axis_index("ctx")
    core, chip = place % 2, place // 2
    keep, send = halves(packed, core)
    half = (keep.astype(f32) + swap_core(send).astype(f32)).astype(bf16)
    keep, send = halves(half, chip)
    quarter = (keep.astype(f32) + swap_x(send).astype(f32)).astype(bf16)
    parts = lax.all_to_all(quarter, "shard", split_axis=0, concat_axis=0, tiled=True)
    total = jnp.sum(parts.astype(f32), axis=0).astype(bf16)
    both = paired(total, swap_x(total), chip)
    return paired(both, swap_core(both), core)


def positions(offsets, tp_place, chunk, block):
    half = block // 2
    return chunk * block + (offsets + tp_place * half) % block


def attention_mask(block):
    place, tp_place = lax.axis_index("ctx"), lax.axis_index("tp")
    offsets = jnp.arange(block, dtype=jnp.int32)
    rows = positions(offsets, tp_place, place, block)
    keys = jnp.concatenate([positions(offsets, tp_place, place ^ j, block) for j in range(4)])
    return keys[None, :] <= rows[:, None]


def head_split(values, heads):
    return values.reshape(values.shape[0], heads, values.shape[1] // heads)


def attend(queries, key_all, value_all, mask, heads):
    scale_factor = (queries.shape[1] // heads) ** (-0.5)
    scores = dot("qhe,khe->hqk", head_split(queries, heads), head_split(key_all, heads))
    scores = jnp.where(mask, scores * scale_factor, masked_value)
    row_top = jnp.max(scores, axis=-1, keepdims=True)
    exponent = jnp.exp(scores - row_top)
    totals = jnp.sum(exponent, axis=-1, keepdims=True)
    probs = (exponent / totals).astype(bf16)
    out = dot("hqk,khe->qhe", probs, head_split(value_all, heads))
    return out.reshape(queries.shape).astype(bf16), row_top + jnp.log(totals)


def attend_back(queries, key_all, value_all, mask, heads, log_sums, grad_out):
    scale_factor = (queries.shape[1] // heads) ** (-0.5)
    query_heads, key_heads = head_split(queries, heads), head_split(key_all, heads)
    grad_heads = head_split(grad_out, heads)
    scores = dot("qhe,khe->hqk", query_heads, key_heads)
    scores = jnp.where(mask, scores * scale_factor, masked_value)
    probs = jnp.exp(scores - log_sums)
    grad_probs = dot("qhe,khe->hqk", grad_heads, head_split(value_all, heads))
    row_dot = jnp.sum(probs * grad_probs, axis=-1, keepdims=True)
    grad_scores = (probs * (grad_probs - row_dot)).astype(bf16)
    grad_q = dot("hqk,khe->qhe", grad_scores, key_heads) * scale_factor
    grad_k = dot("hqk,qhe->khe", grad_scores, query_heads) * scale_factor
    grad_v = dot("hqk,qhe->khe", probs.astype(bf16), grad_heads)
    return (
        grad_q.reshape(queries.shape).astype(bf16),
        jnp.concatenate(
            [grad_k.reshape(key_all.shape), grad_v.reshape(key_all.shape)], axis=1
        ).astype(bf16),
    )


def body_any(x_in, w_qkv, b_qv, w_proj, w_fc1, b_fc1, w_fc2, gains, biases, cotangent):
    depth = w_qkv.shape[0]
    shards = lax.axis_size("shard")
    own_rows, width = x_in.shape[0], x_in.shape[2]
    block = 2 * own_rows
    heads = b_qv.shape[2]
    half_width = w_qkv.shape[3]
    hidden = w_fc1.shape[2]

    small_shapes = [gains.shape, biases.shape, b_qv.shape, b_fc1.shape]
    small = small_rows([gains, biases, b_qv, b_fc1])
    group_a0 = jnp.concatenate([small, to_rows(w_qkv[0])])
    group_b0 = jnp.concatenate([to_rows(w_proj[0]), to_rows(w_fc1[0]), to_rows(w_fc2[0])])
    rest = []
    for index in range(1, depth):
        rest += [to_rows(w_qkv[index]), to_rows(w_proj[index]), to_rows(w_fc1[index]), to_rows(w_fc2[index])]
    group_rest = jnp.concatenate(rest)

    gathered_a0 = gather_packed(group_a0, shards)
    gathered_b0 = gather_packed(group_b0, shards)
    gathered_rest = gather_packed(group_rest, shards)

    def cutter(gathered, start):
        place = [start]

        def take(shape, axis):
            rows = math.prod(shape) // lanes
            piece = from_rows(gathered[:, place[0] : place[0] + rows], shape)
            place[0] += rows
            return join(piece, axis)

        return take

    shape_qkv, shape_proj = w_qkv.shape[1:], w_proj.shape[1:]
    shape_fc1, shape_fc2 = w_fc1.shape[1:], w_fc2.shape[1:]
    take_a, take_b, take_r = cutter(gathered_a0, small.shape[0]), cutter(gathered_b0, 0), cutter(gathered_rest, 0)
    weights = []
    for index in range(depth):
        take_q, take_o = (take_a, take_b) if index == 0 else (take_r, take_r)
        weights.append(
            (take_q(shape_qkv, 1), take_o(shape_proj, 1), take_o(shape_fc1, 0), take_o(shape_fc2, 1))
        )
    flat = gathered_a0[:, : small.shape[0]].reshape(shards, -1)
    vectors, start = [], 0
    for shape in small_shapes:
        size = math.prod(shape)
        piece = flat[:, start : start + size].reshape((shards,) + shape)
        vectors.append(join(piece, len(shape) - 1).astype(f32))
        start += size
    gain_all, bias_all, b_qv_all, b_fc1_all = vectors

    mask = attention_mask(block)
    x_own = x_in[:, 0]
    state = jnp.concatenate([x_own, swap_tp(x_own)]).astype(f32)
    g_own = cotangent[:, 0]
    grad_state = jnp.concatenate([g_own, swap_tp(g_own)]).astype(f32)

    stored = []
    for index in range(depth):
        w_query, w_out, w_first, w_second = weights[index]
        normed_in, scale_in = normalize(state)
        low_in = (normed_in * gain_all[index, 0] + bias_all[index, 0]).astype(bf16)
        bias_q = b_qv_all[index, 0].reshape(half_width)
        bias_v = b_qv_all[index, 1].reshape(half_width)
        queries = (dot("rd,df->rf", low_in, w_query[0]) + bias_q).astype(bf16)
        keys = dot("rd,df->rf", low_in, w_query[1]).astype(bf16)
        values = (dot("rd,df->rf", low_in, w_query[2]) + bias_v).astype(bf16)
        kv_own = jnp.concatenate([keys, values], axis=1)
        kv_chip = swap_x(kv_own)
        kv_all = jnp.concatenate([kv_own, swap_core(kv_own), kv_chip, swap_core(kv_chip)])
        key_all, value_all = kv_all[:, :half_width], kv_all[:, half_width:]
        attn, log_sums = attend(queries, key_all, value_all, mask, heads)
        attn_other = other_half(swap_tp(attn))
        w_out_other = swap_tp(w_out)
        middle = (
            state
            + dot("rf,fd->rd", attn, w_out)
            + dot("rf,fd->rd", attn_other, w_out_other)
            + bias_all[index, 1]
        )
        normed_mid, scale_mid = normalize(middle)
        low_mid = (normed_mid * gain_all[index, 1] + bias_all[index, 2]).astype(bf16)
        pre_act = dot("rd,df->rf", low_mid, w_first) + b_fc1_all[index].reshape(hidden)
        act = gelu_tanh(pre_act).astype(bf16)
        partial = dot("rf,fd->rd", act, w_second)
        if index == depth - 1:
            received = swap_tp(partial[own_rows:].astype(bf16)).astype(f32)
            output = middle[:own_rows] + partial[:own_rows] + received + bias_all[index, 3]
        else:
            received = other_half(swap_tp(partial.astype(bf16))).astype(f32)
            state = middle + partial + received + bias_all[index, 3]
        stored.append(
            (normed_in, scale_in, low_in, queries, key_all, value_all, log_sums, attn,
             normed_mid, scale_mid, low_mid, pre_act, act)
        )
    output = output.astype(bf16)[:, None]

    results = [None] * depth
    for index in reversed(range(depth)):
        w_query, w_out, w_first, w_second = weights[index]
        (normed_in, scale_in, low_in, queries, key_all, value_all, log_sums, attn,
         normed_mid, scale_mid, low_mid, pre_act, act) = stored[index]
        grad_bias_mlp = jnp.sum(grad_state, axis=0)
        grad_low = grad_state.astype(bf16)
        grad_hidden = dot("rd,fd->rf", grad_low, w_second)
        unused, gelu_pull = jax.vjp(gelu_tanh, pre_act)
        grad_pre = gelu_pull(grad_hidden)[0].astype(bf16)
        grad_w_second = dot("rf,rd->fd", act, grad_low)
        grad_w_first = dot("rd,rf->df", low_mid, grad_pre)
        grad_b_first = jnp.sum(grad_pre, axis=0, dtype=f32)
        partial = dot("rf,df->rd", grad_pre, w_first)
        mlp_rows = jnp.concatenate(
            [
                jax.vmap(to_rows)(split(grad_w_first.astype(bf16), 0, shards)),
                jax.vmap(to_rows)(split(grad_w_second.astype(bf16), 1, shards)),
            ],
            axis=1,
        )
        mlp_total = reduce_packed(mlp_rows)
        grad_mid = partial + other_half(swap_tp(partial.astype(bf16))).astype(f32)
        grad_gain_mid = jnp.sum(grad_mid * normed_mid, axis=0)
        grad_beta_mid = jnp.sum(grad_mid, axis=0)
        grad_middle = grad_state + norm_back(grad_mid * gain_all[index, 1], normed_mid, scale_mid)
        grad_bias_attn = jnp.sum(grad_middle, axis=0)
        grad_low = grad_middle.astype(bf16)
        grad_attn = dot("rd,fd->rf", grad_low, w_out).astype(bf16)
        grad_w_out = dot("rf,rd->fd", attn, grad_low)
        grad_q, grad_kv = attend_back(
            queries, key_all, value_all, mask, heads, log_sums, grad_attn
        )
        part = grad_kv.reshape(4, block, 2 * half_width)
        sent = swap_core(jnp.stack([part[1], part[3]])).astype(f32)
        mine = part[0].astype(f32) + sent[0]
        chip = (part[2].astype(f32) + sent[1]).astype(bf16)
        grad_kv = (mine + swap_x(chip).astype(f32)).astype(bf16)
        grad_qkv = jnp.stack([grad_q, grad_kv[:, :half_width], grad_kv[:, half_width:]])
        grad_w_query = dot("rd,crf->cdf", low_in, grad_qkv)
        grad_b_query = jnp.sum(grad_qkv[0::2], axis=1, dtype=f32)
        partial = dot("crf,cdf->rd", grad_qkv, w_query)
        grad_in = partial + other_half(swap_tp(partial.astype(bf16))).astype(f32)
        grad_gain_in = jnp.sum(grad_in * normed_in, axis=0)
        grad_beta_in = jnp.sum(grad_in, axis=0)
        grad_state = grad_middle + norm_back(grad_in * gain_all[index, 0], normed_in, scale_in)

        vectors = [
            jnp.stack([grad_gain_in, grad_gain_mid]),
            jnp.stack([grad_beta_in, grad_bias_attn, grad_beta_mid, grad_bias_mlp]),
            grad_b_query.reshape(2, heads, half_width // heads),
            grad_b_first.reshape(b_fc1_all.shape[1:]),
        ]
        parts = [split(vector, vector.ndim - 1, shards) for vector in vectors]
        part_shapes = [part.shape[1:] for part in parts]
        attn_rows = jnp.concatenate(
            [
                jax.vmap(to_rows)(split(grad_w_query.astype(bf16), 1, shards)),
                jax.vmap(to_rows)(split(grad_w_out.astype(bf16), 1, shards)),
                jax.vmap(lambda *own: small_rows(own))(*parts).astype(bf16),
            ],
            axis=1,
        )
        attn_total = reduce_packed(attn_rows)

        def pieces(total, shapes):
            place, out = 0, []
            for shape in shapes:
                rows = math.prod(shape) // lanes
                out.append(from_rows(total[place : place + rows], shape).astype(f32))
                place += rows
            return out, total[place:].reshape(-1)

        (out_fc1, out_fc2), unused = pieces(mlp_total, [shape_fc1, shape_fc2])
        (out_qkv, out_proj), tail = pieces(attn_total, [shape_qkv, shape_proj])
        small_out, start = [], 0
        for shape in part_shapes:
            size = math.prod(shape)
            small_out.append(tail[start : start + size].reshape(shape).astype(f32))
            start += size
        results[index] = (
            out_qkv, small_out[2], out_proj, out_fc1, small_out[3], out_fc2, small_out[0], small_out[1]
        )
    stacked = tuple(
        jnp.stack([results[index][member] for index in range(depth)]) for member in range(8)
    )
    return (output, grad_state[:own_rows, None]) + stacked


def compiler_params():
    return pltpu.CompilerParams(vmem_limit_bytes=56 * 2**20)


def whole(array):
    zeros = (0,) * array.ndim
    return pl.BlockSpec(array.shape, lambda i: zeros)


def rows_at(array, rows, start, lead=None, first=0):
    lead = array.shape[0] if lead is None else lead
    return pl.BlockSpec((lead, rows, lanes), lambda i: (first, start // rows, 0))


def run(kernel, outs, place, operands, scratch=(), flops=2**20, after=()):
    arrays, specs = [], []
    count = 1 + len(operands)

    def inner(*refs):
        kernel(*refs[:count], *refs[count + len(after) :])

    for operand in operands:
        array, spec = operand if isinstance(operand, tuple) else (operand, whole(operand))
        arrays.append(array)
        specs.append(spec)
    out_shape = [jax.ShapeDtypeStruct(shape, kind) for shape, kind in outs]
    after = list(after)
    arrays += after
    specs += [pl.BlockSpec(memory_space=pl.ANY)] * len(after)
    call = pl.pallas_call(
        inner,
        grid=(1,),
        out_shape=out_shape,
        in_specs=[pl.BlockSpec(memory_space=pltpu.SMEM)] + specs,
        out_specs=[whole(shape) for shape in out_shape],
        scratch_shapes=list(scratch),
        compiler_params=compiler_params(),
        cost_estimate=pl.CostEstimate(flops=flops, bytes_accessed=1024, transcendentals=0),
    )
    return list(call(place, *arrays))


def mm(left, right):
    return lax.dot_general(left, right, (((1,), (0,)), ((), ())), preferred_element_type=f32)


def mm_nt(left, right):
    return lax.dot_general(left, right, (((1,), (1,)), ((), ())), preferred_element_type=f32)


def mm_tn(left, right):
    return lax.dot_general(left, right, (((0,), (0,)), ((), ())), preferred_element_type=f32)


def lane_join(parts):
    return jnp.concatenate(parts, axis=1)


def row_join(parts):
    return jnp.concatenate(parts, axis=0)


class Pieces:
    def __init__(self, refs, place):
        self.refs, self.place = refs, place

    def tile(self, k, p, start, rows):
        if len(self.refs) == 1:
            z, c = self.place[0], self.place[1]
            return self.refs[0][(z - k + 4) % 4, p ^ c, start : start + rows]
        if k == 0:
            return self.refs[0][p, start : start + rows]
        return self.refs[1 + p][k - 1, start : start + rows]


def first_block(pieces, p):
    return row_join(
        [lane_join([pieces.tile(k, p, j * 128, 128) for j in range(2)]) for k in range(4)]
    )


def second_block(pieces, p):
    return lane_join([pieces.tile(k, p, 0, 256) for k in range(4)])


def small_row(small_local, small_far, row):
    parts = [small_local[0, row : row + 1]] + [small_far[k, row : row + 1] for k in range(3)]
    return lane_join(parts).astype(f32)


def spread(small_local, small_far, row, place_z, half, later=None):
    def rows_from(row):
        return row_join(
            [small_local[0, row : row + 1]] + [small_far[k, row : row + 1] for k in range(3)]
        ).astype(f32)

    source = rows_from(row)
    if later is not None:
        source = jnp.where(later == 0, source, rows_from(row + 1))
    source = source.astype(bf16)
    take = lax.broadcasted_iota(jnp.int32, (128, 256), 0)
    lane = lax.broadcasted_iota(jnp.int32, (128, 256), 1)
    wanted = half * 64 + (lane // 64) * 16 + lane % 16
    table = (take == wanted).astype(f32).astype(bf16)
    rows = mm(source, table)
    chunk = lax.broadcasted_iota(jnp.int32, (4, 256), 0)
    lane = lax.broadcasted_iota(jnp.int32, (4, 256), 1)
    keep = (lane % 64) // 16 == (place_z - chunk + 4) % 4
    return jnp.sum(jnp.where(keep, rows, 0.0), axis=0, keepdims=True)


def pack_kernel(kinds):
    def kernel(place, *refs):
        c = place[1]
        out, send = refs[-2:]
        start = 0
        for ref, kind in zip(refs, kinds):
            for q in range(4):
                to = q ^ c
                if kind == "first":
                    for j in range(2):
                        column = (2 * q + j) * 128
                        out[to, start + j * 128 : start + (j + 1) * 128] = ref[0, :, column : column + 128]
                elif kind == "second":
                    out[to, start : start + 256] = ref[0, q * 256 : (q + 1) * 256]
                elif kind == "proj":
                    out[to, start : start + 64] = ref[0, q * 64 : (q + 1) * 64]
                elif kind == "qkv":
                    for tile in range(6):
                        row = start + tile * 32
                        column = (tile % 2) * 128
                        out[to, row : row + 32] = ref[0, tile // 2, q * 32 : (q + 1) * 32, column : column + 128]
                else:
                    out[to, start : start + 32] = ref[...]
            start += kind_rows[kind]
        send[...] = out[0]

    return kernel


def quarter_pack_kernel(kinds):
    def kernel(place, *refs):
        out = refs[-1]
        for q in range(4):

            @pl.when(place[1] == q)
            def write(q=q):
                start = 0
                for ref, kind in zip(refs, kinds):
                    if kind == "first":
                        for j in range(2):
                            column = (2 * q + j) * 128
                            out[start + j * 128 : start + (j + 1) * 128] = ref[0, :, column : column + 128]
                    elif kind == "second":
                        out[start : start + 256] = ref[0, q * 256 : (q + 1) * 256]
                    elif kind == "proj":
                        out[start : start + 64] = ref[0, q * 64 : (q + 1) * 64]
                    else:
                        for tile in range(6):
                            row = start + tile * 32
                            column = (tile % 2) * 128
                            out[row : row + 32] = ref[0, tile // 2, q * 32 : (q + 1) * 32, column : column + 128]
                    start += kind_rows[kind]

    return kernel


kind_rows = {"first": 256, "second": 256, "proj": 64, "qkv": 192, "small": 32}


def pack(place, kinds, arrays, index, after=(), whole_quarters=True):
    rows = sum(kind_rows[kind] for kind in kinds)
    operands = []
    for kind, array in zip(kinds, arrays):
        if kind == "small":
            operands.append(array)
        else:
            block = (1,) + array.shape[1:]
            at = (index,) + (0,) * (array.ndim - 1)
            operands.append((array, pl.BlockSpec(block, lambda i, at=at: at)))
    if not whole_quarters:
        return run(quarter_pack_kernel(kinds), [((rows, lanes), bf16)], place, operands, after=after)[0]
    return run(
        pack_kernel(kinds), [((4, rows, lanes), bf16), ((rows, lanes), bf16)], place, operands, after=after
    )


def gather(quarter):
    full = lax.all_gather(quarter, ("shard", "ctx"), axis=0)
    return full.reshape((4, 4) + quarter.shape)


def gathered_rows(array, rows, start):
    return [(array, pl.BlockSpec((4, 4, rows, lanes), lambda i: (0, 0, start // rows, 0)))]


def shift(values, step):
    return lax.ppermute(values, "shard", [(z, (z + step) % 4) for z in range(4)])


def far_chunks(send):
    return [shift(send, k) for k in (1, 2, 3)]


def stack_kernel(place, one, two, three, out):
    for k, ref in enumerate((one, two, three)):
        out[k] = ref[...]


def stack(place, got, after=()):
    return run(stack_kernel, [((3,) + got[0].shape, bf16)], place, got, after=after)[0]


def pieces_of(group, rows, start):
    return [(array, rows_at(array, rows, start)) for array in group]


def small_of(group):
    return [(group[0], rows_at(group[0], 32, 256, lead=1)), (group[1], rows_at(group[1], 32, 256))]


def query_kernel(index, first_layer):
    def kernel(place, *refs):
        c = place[1]
        if first_layer:
            own, peer, small_local, small_far = refs[:4]
            pieces = Pieces(refs[4:9], place)
            grad_out = refs[14]
            grad_out[...] = row_join([own[128:], peer[128:]]).astype(f32)
            state_out, low_out, q_out, kv_out, w_out = refs[9:14]
            state = row_join([own[:128], peer[:128]]).astype(f32)
        else:
            middle, mine, other, small_local, small_far = refs[:5]
            pieces = Pieces(refs[5:6], place)
            state_out, low_out, q_out, kv_out, w_out = refs[6:]
            received = row_join([other[128:], other[:128]])
            state = (
                middle[...]
                + mine[...].astype(f32)
                + received.astype(f32)
                + small_row(small_local, small_far, 4 + 4 * (index - 1) + 3)
            )
        for k in range(4):
            for p in range(4):
                for tile in range(6):
                    w_out[k, p ^ c, :, tile * 128 : (tile + 1) * 128] = pieces.tile(k, p, tile * 32, 32)
        state_out[...] = state
        normed, scale = normalize(state)
        low = (
            normed * small_row(small_local, small_far, 2 * index)
            + small_row(small_local, small_far, 4 + 4 * index)
        ).astype(bf16)
        low_out[...] = low
        w_all = w_out[...].reshape(512, 768)
        row = 12 + index
        bias_q = spread(small_local, small_far, row, place[0], 0)
        bias_v = spread(small_local, small_far, row, place[0], 1)
        kv_out[:, :256] = mm(low, w_all[:, 256:512]).astype(bf16)
        kv_out[:, 256:] = (mm(low, w_all[:, 512:]) + bias_v).astype(bf16)
        q_out[...] = (mm(low, w_all[:, :256]) + bias_q).astype(bf16)

    return kernel


def seen(place, j):
    c, t = place[1], place[2]
    if j:
        return None
    row = lax.broadcasted_iota(jnp.int32, (256, 256), 0) ^ (t * 128)
    key = lax.broadcasted_iota(jnp.int32, (256, 256), 1) ^ (t * 128)
    return key <= row


def masked_scores(query, chunks, own_mask, place):
    parts = []
    for j in range(4):
        scores = mm_nt(query, chunks[j]) * 0.125
        if j == 0:
            scores = jnp.where(own_mask, scores, masked_value)
        else:
            scores = jnp.where((place[1] ^ j) < place[1], scores, masked_value)
        parts.append(scores)
    return parts


def attend_kernel(count, place, *refs):
    c = place[1]
    q, chunks = refs[0], refs[1:5]
    pieces = Pieces(refs[5 : 5 + count], place)
    attn_out, lse_out, partial_out, w_out = refs[5 + count :]
    for k in range(4):
        for p in range(4):
            w_out[p ^ c, :, k * 128 : (k + 1) * 128] = pieces.tile(k, p, 0, 64)
    own_mask = seen(place, 0)
    results = []
    for head in range(4):
        low, high = head * 64, (head + 1) * 64
        parts = masked_scores(q[:, low:high], [chunk[:, low:high] for chunk in chunks], own_mask, place)
        scores = lane_join(parts)
        top = jnp.max(scores, axis=1, keepdims=True)
        exponent = jnp.exp(scores - top)
        total = jnp.sum(exponent, axis=1, keepdims=True)
        values = row_join([chunk[:, 256 + low : 256 + high] for chunk in chunks])
        results.append(mm(exponent.astype(bf16), values) / total)
        lse_out[:, head : head + 1] = top + jnp.log(total)
    attn = lane_join(results).astype(bf16)
    attn_out[...] = attn
    partial_out[...] = mm(attn, w_out[...].reshape(256, 512)).astype(bf16)


def mlp_kernel(index):
    def kernel(place, *refs):
        state, mine, other, small_local, small_far = refs[:5]
        first, second = Pieces(refs[5:6], place), Pieces(refs[6:7], place)
        middle_out, low_out, pre_out, partial_out = refs[7:]
        received = row_join([other[128:], other[:128]])
        middle = (
            state[...]
            + mine[...].astype(f32)
            + received.astype(f32)
            + small_row(small_local, small_far, 4 + 4 * index + 1)
        )
        middle_out[...] = middle
        normed, scale = normalize(middle)
        low = (
            normed * small_row(small_local, small_far, 2 * index + 1)
            + small_row(small_local, small_far, 4 + 4 * index + 2)
        ).astype(bf16)
        low_out[...] = low
        total = None
        for p in range(4):
            q = p ^ place[1]
            bias = spread(small_local, small_far, 14 + 2 * index, place[0], q % 2, q // 2)
            pre = mm(low, first_block(first, p)) + bias
            pre_out[:, p * 256 : (p + 1) * 256] = pre
            act = gelu_tanh(pre).astype(bf16)
            part = mm(act, second_block(second, p))
            total = part if total is None else total + part
        partial_out[...] = total.astype(bf16)

    return kernel


root = math.sqrt(2 / math.pi)


def mlp_back(grad, pre_ref, low_ref, first, second, place, outs):
    partial_out, bias_out, b_first_out, keep, send = outs
    grad_low = grad.astype(bf16)
    bias_out[...] = jnp.sum(grad, axis=0, keepdims=True)
    total = None
    for p in range(4):
        pre = pre_ref[:, p * 256 : (p + 1) * 256]
        square = pre * pre
        wave = jnp.tanh(root * pre * (1 + 0.044715 * square))
        half = 0.5 * (1 + wave)
        act = (pre * half).astype(bf16)
        slope = half + 0.5 * pre * (1 - wave * wave) * root * (1 + 3 * 0.044715 * square)
        w_second = second_block(second, p)
        grad_pre = mm_nt(grad_low, w_second) * slope
        grad_pre_low = grad_pre.astype(bf16)
        b_first_out[p ^ place[1]] = jnp.sum(grad_pre_low.astype(f32), axis=0, keepdims=True)
        part = mm_nt(grad_pre_low, first_block(first, p))
        total = part if total is None else total + part
        to = keep if p % 2 == 0 else send
        grad_first = mm_tn(low_ref[...], grad_pre_low).astype(bf16)
        grad_second = mm_tn(act, grad_low).astype(bf16)
        for k in range(4):
            for j in range(2):
                to[p // 2, k, j * 128 : (j + 1) * 128] = grad_first[
                    k * 128 : (k + 1) * 128, j * 128 : (j + 1) * 128
                ]
            to[p // 2, k, 256:512] = grad_second[:, k * 128 : (k + 1) * 128]
    partial_out[...] = total.astype(bf16)


def norm_step(grad_out, gain, values):
    normed, scale = normalize(values)
    sums = row_join(
        [
            jnp.sum(grad_out * normed, axis=0, keepdims=True),
            jnp.sum(grad_out, axis=0, keepdims=True),
        ]
    )
    return norm_back(grad_out * gain, normed, scale), sums


def received_sum(mine, other):
    return mine[...].astype(f32) + row_join([other[128:], other[:128]]).astype(f32)


def top_kernel(place, *refs):
    grad, pre, low = refs[:3]
    first, second = Pieces(refs[3:4], place), Pieces(refs[4:5], place)
    mlp_back(grad[...], pre, low, first, second, place, refs[5:])


def lower_kernel(index):
    def kernel(place, *refs):
        grad_mid, mine, other, state, small_local, small_far, pre, low = refs[:8]
        first, second = Pieces(refs[8:9], place), Pieces(refs[9:10], place)
        grad_out, sums_out = refs[10:12]
        grad, sums = norm_step(
            received_sum(mine, other), small_row(small_local, small_far, 2 * (index + 1)), state[...]
        )
        sums_out[...] = sums
        grad = grad_mid[...] + grad
        grad_out[...] = grad
        mlp_back(grad, pre, low, first, second, place, refs[12:])

    return kernel


def attend_back_kernel(index):
    def kernel(place, *refs):
        mine, other, middle, grad_state, small_local, small_far = refs[:6]
        attn, w_out, q = refs[6:9]
        chunks, lse = refs[9:13], refs[13]
        grad_out, sums_out, gw_out, dq_out, keep, send = refs[14:]
        grad, sums = norm_step(
            received_sum(mine, other), small_row(small_local, small_far, 2 * index + 1), middle[...]
        )
        grad = grad_state[...] + grad
        grad_out[...] = grad
        sums_out[0:2] = sums
        sums_out[2:3] = jnp.sum(grad, axis=0, keepdims=True)
        grad_low = grad.astype(bf16)
        grad_attn = mm_nt(grad_low, w_out[...].reshape(256, 512)).astype(bf16)
        gw_out[...] = mm_tn(attn[...], grad_low).astype(bf16).reshape(4, 64, 512)
        own_mask = seen(place, 0)
        dq_all = []
        dk_all = [[] for j in range(4)]
        dv_all = [[] for j in range(4)]
        for head in range(4):
            low, high = head * 64, (head + 1) * 64
            query, grad_head = q[:, low:high], grad_attn[:, low:high]
            keys = [chunk[:, low:high] for chunk in chunks]
            row_dot = jnp.sum(
                grad_head.astype(f32) * attn[:, low:high].astype(f32), axis=1, keepdims=True
            )
            log_sum = lse[:, head : head + 1]
            parts = masked_scores(query, keys, own_mask, place)
            dq = None
            for j in range(4):
                probs = jnp.exp(parts[j] - log_sum)
                grad_probs = mm_nt(grad_head, chunks[j][:, 256 + low : 256 + high])
                grad_scores = (probs * (grad_probs - row_dot)).astype(bf16)
                part = mm(grad_scores, keys[j])
                dq = part if dq is None else dq + part
                dk_all[j].append(mm_tn(grad_scores, query) * 0.125)
                dv_all[j].append(mm_tn(probs.astype(bf16), grad_head))
            dq_all.append(dq * 0.125)
        dq_out[...] = lane_join(dq_all).astype(bf16)
        for j in range(4):
            to = keep if j % 2 == 0 else send
            to[j // 2, :, :256] = lane_join(dk_all[j]).astype(bf16)
            to[j // 2, :, 256:] = lane_join(dv_all[j]).astype(bf16)

    return kernel


def halve_kernel(place, keep, got, own_out, send_out):
    own_out[...] = (keep[0].astype(f32) + got[0].astype(f32)).astype(bf16)
    send_out[...] = (keep[1].astype(f32) + got[1].astype(f32)).astype(bf16)


def halve_in_order(place, keep, got, out):
    z, chip = place[0], place[1] // 2
    for half in range(2):
        for k in range(4):
            total = keep[half, k].astype(f32) + got[half, k].astype(f32)
            out[half ^ chip, (z - k + 4) % 4] = total.astype(bf16)


def query_back_kernel(place, *refs):
    dq, dkv, got, low, w_ref, gw_ref = refs[:6]
    partial_out, b_out, keep, send, scratch = refs[6:]
    c = place[1]
    grad_kv = (dkv[...].astype(f32) + got[...].astype(f32)).astype(bf16)
    grad_qkv = lane_join([dq[...], grad_kv])
    partial_out[...] = mm_nt(grad_qkv, w_ref[...].reshape(512, 768)).astype(bf16)
    b_out[0:1] = jnp.sum(dq[...].astype(f32), axis=0, keepdims=True)
    b_out[1:2] = jnp.sum(grad_kv[:, 256:].astype(f32), axis=0, keepdims=True)
    scratch[...] = mm_tn(low[...], grad_qkv).astype(bf16).reshape(4, 4, 32, 768)
    for p in range(4):
        to = keep if p % 2 == 0 else send
        for k in range(4):
            for tile in range(6):
                to[p // 2, k, tile * 32 : (tile + 1) * 32] = scratch[
                    k, p ^ c, :, tile * 128 : (tile + 1) * 128
                ]
            to[p // 2, k, 192:256] = gw_ref[p ^ c, :, k * 128 : (k + 1) * 128]


def four_kernel(place, one, two, three, four, out):
    out[...] = (one[...] + two[...]) + (three[...] + four[...])


def quarter_kernel(place, own, got, *outs):
    for k in range(4):
        outs[k][...] = (own[k].astype(f32) + got[k].astype(f32)).astype(bf16)


def total_kernel(place, own, one, two, three, out):
    total = own[...].astype(f32) + one[...].astype(f32)
    out[...] = (total + (two[...].astype(f32) + three[...].astype(f32))).astype(bf16)


class Chain:
    def __init__(self, place, keep, send):
        self.place, self.rows = place, keep.shape[2]
        self.state = [keep, send]

    def halve(self, after=()):
        keep, send = self.state
        self.state = run(
            halve_kernel, [((4, self.rows, lanes), bf16)] * 2, self.place, [keep, swap_core(send)], flops=2**20, after=after
        )

    def quarter(self, after=()):
        own, send = self.state
        self.state = run(
            quarter_kernel, [((self.rows, lanes), bf16)] * 4, self.place, [own, swap_x(send)], flops=2**20, after=after
        )

    def total(self, after=()):
        got = [shift(self.state[k], 4 - k) for k in (1, 2, 3)]
        self.state = run(
            total_kernel, [((self.rows, lanes), bf16)], self.place, [self.state[0]] + got, flops=2**20, after=after
        )

    def collect(self):
        (total,) = self.state
        chip = swap_x(total)
        return [total, swap_core(total), chip, swap_core(chip)]


def spread_sum(place, keep, send, after=()):
    rows = keep.shape[2]
    (both,) = run(
        halve_in_order, [((2, 4, rows, lanes), bf16)], place, [keep, swap_core(send)], after=after
    )
    mine = lax.psum_scatter(both, "ctx", scatter_dimension=0, axis_index_groups=[[0, 2], [1, 3]])
    mine = lax.psum_scatter(mine, "shard", scatter_dimension=0)
    return both, lax.all_gather(mine, "ctx", axis=0)


def fill(place, refs, scratch):
    for p in range(4):
        if len(refs) == 1:
            scratch[p ^ place[1]] = refs[0][p].astype(f32)
        else:
            scratch[p] = refs[p][...].astype(f32)


def hidden_out_kernel(place, *refs):
    c = place[1]
    first_out, second_out, scratch = refs[-3:]
    fill(place, refs[:-3], scratch)
    for q in range(4):
        for j in range(2):
            column = (2 * q + j) * 128
            first_out[0, :, column : column + 128] = scratch[q ^ c, j * 128 : (j + 1) * 128]
        second_out[0, q * 256 : (q + 1) * 256] = scratch[q ^ c, 256:]


def heads_out_kernel(place, *refs):
    c = place[1]
    qkv_out, proj_out, scratch = refs[-3:]
    fill(place, refs[:-3], scratch)
    for q in range(4):
        for tile in range(6):
            column = (tile % 2) * 128
            qkv_out[0, tile // 2, q * 32 : (q + 1) * 32, column : column + 128] = scratch[
                q ^ c, tile * 32 : (tile + 1) * 32
            ]
        proj_out[0, q * 64 : (q + 1) * 64] = scratch[q ^ c, 192:]


def layer_out(kernel, place, totals, layer, shapes, before, after):
    rows = totals[0].shape[-2]
    extra = list(before) + list(after)
    count = 1 + len(totals)

    def inner(*refs):
        kernel(*refs[:count], *refs[count + len(extra) :])

    def block(shape):
        at = (layer,) + (0,) * (len(shape) - 1)
        return pl.BlockSpec((1,) + tuple(shape[1:]), lambda i: at)

    return list(
        pl.pallas_call(
            inner,
            grid=(1,),
            out_shape=[jax.ShapeDtypeStruct(shape, f32) for shape in shapes],
            in_specs=[pl.BlockSpec(memory_space=pltpu.SMEM)]
            + [whole(total) for total in totals]
            + [pl.BlockSpec(memory_space=pl.ANY)] * len(extra),
            out_specs=[block(shape) for shape in shapes],
            scratch_shapes=[pltpu.VMEM((4, rows, lanes), f32)],
            input_output_aliases={count + i: i for i in range(len(before))},
            compiler_params=compiler_params(),
            cost_estimate=pl.CostEstimate(flops=2**20, bytes_accessed=1024, transcendentals=0),
        )(place, *totals, *extra)
    )


def hidden_out(place, totals, layer, shape_one, shape_two, before, after=()):
    return layer_out(hidden_out_kernel, place, totals, layer, (shape_one, shape_two), before, after)


def heads_out(place, totals, layer, shape_one, shape_two, before, after=()):
    return layer_out(heads_out_kernel, place, totals, layer, (shape_one, shape_two), before, after)


def last_kernel(place, *refs):
    grad_mid, mine, other, state, small_local, small_far = refs[:6]
    sums_in = refs[6]
    sums_mid, bias_mlp, b_query, b_first = refs[7:9], refs[9:11], refs[11:13], refs[13:15]
    grad_out, out = refs[15:]
    grad, sums = norm_step(received_sum(mine, other), small_row(small_local, small_far, 0), state[...])
    grad_out[...] = grad_mid[:128] + grad[:128]
    for layer in range(2):
        inner = sums if layer == 0 else sums_in[...]
        mid = sums_mid[layer]
        rows = [
            (2 * layer, inner[0:1]),
            (2 * layer + 1, mid[0:1]),
            (4 + 4 * layer, inner[1:2]),
            (5 + 4 * layer, mid[2:3]),
            (6 + 4 * layer, mid[1:2]),
            (7 + 4 * layer, bias_mlp[layer][...]),
        ]
        for k in range(4):
            for row, value in rows:
                out[k, row : row + 1] = value[:, k * 128 : (k + 1) * 128]
            for channel in range(2):
                for j in range(2):
                    row = 12 + 4 * layer + 2 * channel + j
                    out[k, row : row + 1] = b_query[layer][channel : channel + 1, j * 128 : (j + 1) * 128]
            for q in range(4):
                for j in range(2):
                    row = 20 + 8 * layer + 2 * q + j
                    out[k, row : row + 1] = b_first[layer][q, :, j * 128 : (j + 1) * 128]
    out[:, 36:] = jnp.zeros((4, 4, lanes), f32)


def turn(values, place_z, back):
    rows = values.shape[0]
    chunks = values.reshape(rows, 4, lanes)
    order = (place_z - jnp.arange(4)) % 4
    return jnp.concatenate(
        [lax.dynamic_slice_in_dim(values, order[k] * lanes, lanes, 1) for k in range(4)], axis=1
    )


def body_four(x_in, w_qkv, b_qv, w_proj, w_fc1, b_fc1, w_fc2, gains, biases, cotangent):
    z, c, t = lax.axis_index("shard"), lax.axis_index("ctx"), lax.axis_index("tp")
    place = jnp.stack([z, c, t]).astype(jnp.int32)
    flat = jnp.concatenate([array.reshape(-1) for array in (gains, biases, b_qv, b_fc1)])
    small = jnp.pad(flat, (0, 32 * lanes - flat.shape[0])).reshape(32, lanes)

    local_a, send_a = pack(place, ("qkv", "proj", "small"), (w_qkv, w_proj, small), 0)
    pair_own = turn(jnp.concatenate([x_in[:, 0], cotangent[:, 0]]), z, False)
    pair_peer = swap_tp(pair_own)
    got_a = far_chunks(send_a)
    far_a = stack(place, got_a)
    chip_a = swap_x(far_a)
    group_a0 = [local_a, far_a, swap_core(far_a), chip_a, swap_core(chip_a)]
    send_b = pack(place, ("first", "second"), (w_fc1, w_fc2), 0, after=[far_a], whole_quarters=False)
    kinds = ("first", "second", "proj", "qkv")
    send_1 = pack(
        place, kinds, (w_fc1, w_fc2, w_proj, w_qkv), 1, after=[far_a, send_b], whole_quarters=False
    )
    full_b, full_1 = gather(send_b), gather(send_1)

    small_parts = small_of(group_a0)
    parts = {
        "qkv": [pieces_of(group_a0, 192, 0), gathered_rows(full_1, 192, 576)],
        "proj": [pieces_of(group_a0, 64, 192), gathered_rows(full_1, 64, 512)],
        "first": [gathered_rows(full_b, 256, 0), gathered_rows(full_1, 256, 0)],
        "second": [gathered_rows(full_b, 256, 256), gathered_rows(full_1, 256, 256)],
    }
    square, wide = (256, 512), (256, 256)
    saved = []
    for layer in range(2):
        source = [pair_own, pair_peer] if layer == 0 else [middle, partial, swap_tp(partial)]
        more = [(square, f32)] if layer == 0 else []
        state, low_in, q, kv, w_all, *passed = run(
            query_kernel(layer, layer == 0),
            [(square, f32), (square, bf16), (wide, bf16), (square, bf16), ((4, 4, 32, 768), bf16)] + more,
            place,
            source + small_parts + parts["qkv"][layer],
        )
        if layer == 0:
            g_all = passed[0]
        kv_chip = swap_x(kv)
        chunks = [kv, swap_core(kv), kv_chip, swap_core(kv_chip)]
        attn, lse, partial, w_out = run(
            functools.partial(attend_kernel, len(parts["proj"][layer])),
            [(wide, bf16), ((256, lanes), f32), (square, bf16), ((4, 64, 512), bf16)],
            place,
            [q] + chunks + parts["proj"][layer],
        )
        middle, low_mid, pre, partial = run(
            mlp_kernel(layer),
            [(square, f32), (square, bf16), ((256, 1024), f32), (square, bf16)],
            place,
            [state, partial, swap_tp(partial)] + small_parts + parts["first"][layer] + parts["second"][layer],
        )
        saved.append((state, low_in, q, chunks, w_all, attn, lse, w_out, middle, low_mid, pre))

    received = swap_tp(partial[128:]).astype(f32)
    output = None
    bias_last = jnp.concatenate([small_parts[0][0][0, 267:268], small_parts[1][0][:, 267]]).reshape(1, 512)
    output = middle[:128] + partial[:128].astype(f32) + received + bias_last.astype(f32)
    output = turn(output.astype(bf16), z, True)[:, None]

    hidden_outs = [
        (square, bf16),
        ((1, 512), f32),
        ((4, 1, 256), f32),
        ((2, 4, 512, lanes), bf16),
        ((2, 4, 512, lanes), bf16),
    ]
    sums_mid, bias_mlp, b_query, b_first = [0, 0], [0, 0], [0, 0], [0, 0]
    hidden = [None, None]
    for layer in (1, 0):
        state, low_in, q, chunks, w_all, attn, lse, w_out, middle, low_mid, pre = saved[layer]
        tail = [pre, low_mid] + parts["first"][layer] + parts["second"][layer]
        if layer == 1:
            grad_state = g_all
            partial, bias_mlp[1], b_first[1], keep, send = run(
                top_kernel, hidden_outs, place, [grad_state] + tail
            )
        else:
            half, heads_total = spread_sum(place, keep, send)
            grad_state, sums_in, partial, bias_mlp[0], b_first[0], keep, send = run(
                lower_kernel(0),
                [(square, f32), ((2, 512), f32)] + hidden_outs,
                place,
                [grad_mid, partial, swap_tp(partial), saved[1][0]] + small_parts + tail,
                after=[half],
            )
        half, hidden[layer] = spread_sum(place, keep, send)
        grad_mid, sums_mid[layer], gw_out, dq, keep, send = run(
            attend_back_kernel(layer),
            [
                (square, f32),
                ((3, 512), f32),
                ((4, 64, 512), bf16),
                (wide, bf16),
                ((2, 256, 512), bf16),
                ((2, 256, 512), bf16),
            ],
            place,
            [partial, swap_tp(partial), middle, grad_state] + small_parts + [attn, w_out, q] + chunks + [lse],
            after=[half],
        )
        dkv, chip = run(halve_kernel, [(square, bf16)] * 2, place, [keep, swap_core(send)])
        partial, b_query[layer], keep, send = run(
            query_back_kernel,
            [
                (square, bf16),
                ((2, 256), f32),
                ((2, 4, 256, lanes), bf16),
                ((2, 4, 256, lanes), bf16),
            ],
            place,
            [dq, dkv, swap_x(chip), low_in, w_all, gw_out],
            scratch=[pltpu.VMEM((4, 4, 32, 768), bf16)],
            after=[output] if layer == 1 else [],
        )
    last = Chain(place, keep, send)
    last.halve()
    grad_x, sums = run(
        last_kernel,
        [((128, 512), f32), ((4, 40, lanes), f32)],
        place,
        [grad_mid, partial, swap_tp(partial), saved[0][0]]
        + small_parts
        + [sums_in]
        + sums_mid
        + bias_mlp
        + b_query
        + b_first,
        after=last.state,
    )
    last.quarter(after=[grad_x])
    grad_x = turn(grad_x, z, True)[:, None]
    (sums,) = run(
        four_kernel,
        [((4, 40, lanes), f32)],
        place,
        [sums, swap_core(sums), swap_x(sums), swap_both(sums)],
        after=last.state,
    )
    last.total(after=[sums])
    outs_heads = heads_out(
        place, [heads_total], 1, w_qkv.shape, w_proj.shape, [], after=last.state
    )
    outs_hidden = hidden_out(place, [hidden[1]], 1, w_fc1.shape, w_fc2.shape, [], after=last.state)
    grad_fc1, grad_fc2 = hidden_out(place, [hidden[0]], 0, w_fc1.shape, w_fc2.shape, outs_hidden)
    got = [shift(sums[k], 4 - k) for k in (1, 2, 3)]
    total = sums[0] + got[0] + got[1] + got[2]
    grad_gains = total[:4].reshape(gains.shape)
    grad_biases = total[4:12].reshape(biases.shape)
    rest_q = total[12:20].reshape(2, 2, 4, 64)
    rest_f = total[20:36].reshape(2, 16, 64)
    grad_b_qv = lax.dynamic_slice_in_dim(rest_q, z * 16, 16, 3)
    grad_b_fc1 = lax.dynamic_slice_in_dim(rest_f, z * 16, 16, 2)

    grad_qkv, grad_proj = heads_out(place, last.collect(), 0, w_qkv.shape, w_proj.shape, outs_heads)
    return (
        output, grad_x, grad_qkv, grad_b_qv, grad_proj, grad_fc1, grad_b_fc1, grad_fc2, grad_gains, grad_biases
    )


def body(*args):
    x_in, w_qkv, b_qv, w_proj, w_fc1 = args[:5]
    expected = ((128, 1, 512), (2, 3, 128, 256), (2, 2, 4, 16), (2, 256, 128), (2, 128, 1024))
    sizes = (lax.axis_size("shard"), lax.axis_size("ctx"), lax.axis_size("tp"))
    shapes = tuple(array.shape for array in (x_in, w_qkv, b_qv, w_proj, w_fc1))
    if sizes == (4, 4, 2) and shapes == expected:
        return body_four(*args)
    return body_any(*args)


def solution(mesh):
    return jax.shard_map(
        body,
        mesh=mesh,
        in_specs=(
            P(("ctx", "tp"), "shard", None),
            P(None, None, "shard", "tp"),
            P(None, None, "tp", "shard"),
            P(None, "tp", "shard"),
            P(None, "shard", "tp"),
            P(None, "tp", "shard"),
            P(None, "tp", "shard"),
            P(None, None, "shard"),
            P(None, None, "shard"),
            P(("ctx", "tp"), "shard", None),
        ),
        out_specs=(
            P(("ctx", "tp"), "shard", None),
            P(("ctx", "tp"), "shard", None),
            P(None, None, "shard", "tp"),
            P(None, None, "tp", "shard"),
            P(None, "tp", "shard"),
            P(None, "shard", "tp"),
            P(None, "tp", "shard"),
            P(None, "tp", "shard"),
            P(None, None, "shard"),
            P(None, None, "shard"),
        ),
        check_vma=False,
    )
```

```python
import functools
import math

import jax
import jax.numpy as jnp
from jax import lax
from jax.experimental import pallas as pl
from jax.experimental.pallas import tpu as pltpu
from jax.sharding import PartitionSpec as P

epsilon = 1e-05
masked_value = -1e30
lanes = 128
f32 = jnp.float32
bf16 = jnp.bfloat16


def normalize(values):
    center = jnp.mean(values, axis=-1, keepdims=True)
    shifted = values - center
    scale_inv = lax.rsqrt(jnp.mean(shifted * shifted, axis=-1, keepdims=True) + epsilon)
    return (shifted * scale_inv, scale_inv)


def norm_back(grad_norm, normed, scale_inv):
    mean_grad = jnp.mean(grad_norm, axis=-1, keepdims=True)
    mean_prod = jnp.mean(grad_norm * normed, axis=-1, keepdims=True)
    return scale_inv * (grad_norm - mean_grad - normed * mean_prod)


def gelu_tanh(values):
    return jax.nn.gelu(values, approximate=True)


def dot(pattern, left, right):
    return jnp.einsum(pattern, left, right, preferred_element_type=f32)


def to_rows(array):
    rows, columns = array.shape[-2:]
    if columns % lanes or rows % 16:
        return array.reshape(-1, lanes)
    tiles = array.reshape(-1, rows, columns // lanes, lanes)
    return jnp.swapaxes(tiles, 1, 2).reshape(-1, lanes)


def from_rows(packed, shape):
    rows, columns = shape[-2:]
    lead = packed.shape[:-2]
    if columns % lanes or rows % 16:
        return packed.reshape(lead + tuple(shape))
    count = math.prod(shape[:-2])
    tiles = packed.reshape(lead + (count, columns // lanes, rows, lanes))
    return jnp.swapaxes(tiles, -3, -2).reshape(lead + tuple(shape))


def small_rows(arrays):
    flat = jnp.concatenate([array.reshape(-1) for array in arrays])
    size = -(-flat.shape[0] // (64 * lanes)) * 64 * lanes
    return jnp.pad(flat, (0, size - flat.shape[0])).reshape(-1, lanes)


def join(gathered, axis):
    moved = jnp.moveaxis(gathered, 0, axis)
    shape = moved.shape
    return moved.reshape(shape[:axis] + (shape[axis] * shape[axis + 1],) + shape[axis + 2 :])


def split(whole, axis, shards):
    shape = whole.shape
    parts = whole.reshape(shape[:axis] + (shards, shape[axis] // shards) + shape[axis + 1 :])
    return jnp.moveaxis(parts, axis, 0)


def swap_tp(values):
    return lax.ppermute(values, "tp", [(0, 1), (1, 0)])


def swap_core(values):
    return lax.ppermute(values, "ctx", [(0, 1), (1, 0), (2, 3), (3, 2)])


def swap_x(values):
    return lax.ppermute(values, "ctx", [(0, 2), (2, 0), (1, 3), (3, 1)])


def swap_both(values):
    return lax.ppermute(values, "ctx", [(0, 3), (3, 0), (1, 2), (2, 1)])


def other_half(values):
    half = values.shape[0] // 2
    return jnp.concatenate([values[half:], values[:half]])


def gather_packed(packed, shards):
    quarter = packed.shape[0] // 4
    own = lax.dynamic_slice_in_dim(packed, lax.axis_index("ctx") * quarter, quarter, 0)
    return lax.all_gather(own, ("shard", "ctx"), axis=0, tiled=True).reshape(
        shards, packed.shape[0], lanes
    )


def halves(values, bit):
    half = values.shape[1] // 2
    keep = lax.dynamic_slice_in_dim(values, bit * half, half, 1)
    send = lax.dynamic_slice_in_dim(values, (1 - bit) * half, half, 1)
    return keep, send


def paired(own, other, bit):
    return jnp.where(
        bit == 0, jnp.concatenate([own, other]), jnp.concatenate([other, own])
    )


def reduce_packed(packed):
    place = lax.axis_index("ctx")
    core, chip = place % 2, place // 2
    keep, send = halves(packed, core)
    half = (keep.astype(f32) + swap_core(send).astype(f32)).astype(bf16)
    keep, send = halves(half, chip)
    quarter = (keep.astype(f32) + swap_x(send).astype(f32)).astype(bf16)
    parts = lax.all_to_all(quarter, "shard", split_axis=0, concat_axis=0, tiled=True)
    total = jnp.sum(parts.astype(f32), axis=0).astype(bf16)
    both = paired(total, swap_x(total), chip)
    return paired(both, swap_core(both), core)


def positions(offsets, tp_place, chunk, block):
    half = block // 2
    return chunk * block + (offsets + tp_place * half) % block


def attention_mask(block):
    place, tp_place = lax.axis_index("ctx"), lax.axis_index("tp")
    offsets = jnp.arange(block, dtype=jnp.int32)
    rows = positions(offsets, tp_place, place, block)
    keys = jnp.concatenate([positions(offsets, tp_place, place ^ j, block) for j in range(4)])
    return keys[None, :] <= rows[:, None]


def head_split(values, heads):
    return values.reshape(values.shape[0], heads, values.shape[1] // heads)


def attend(queries, key_all, value_all, mask, heads):
    scale_factor = (queries.shape[1] // heads) ** (-0.5)
    scores = dot("qhe,khe->hqk", head_split(queries, heads), head_split(key_all, heads))
    scores = jnp.where(mask, scores * scale_factor, masked_value)
    row_top = jnp.max(scores, axis=-1, keepdims=True)
    exponent = jnp.exp(scores - row_top)
    totals = jnp.sum(exponent, axis=-1, keepdims=True)
    probs = (exponent / totals).astype(bf16)
    out = dot("hqk,khe->qhe", probs, head_split(value_all, heads))
    return out.reshape(queries.shape).astype(bf16), row_top + jnp.log(totals)


def attend_back(queries, key_all, value_all, mask, heads, log_sums, grad_out):
    scale_factor = (queries.shape[1] // heads) ** (-0.5)
    query_heads, key_heads = head_split(queries, heads), head_split(key_all, heads)
    grad_heads = head_split(grad_out, heads)
    scores = dot("qhe,khe->hqk", query_heads, key_heads)
    scores = jnp.where(mask, scores * scale_factor, masked_value)
    probs = jnp.exp(scores - log_sums)
    grad_probs = dot("qhe,khe->hqk", grad_heads, head_split(value_all, heads))
    row_dot = jnp.sum(probs * grad_probs, axis=-1, keepdims=True)
    grad_scores = (probs * (grad_probs - row_dot)).astype(bf16)
    grad_q = dot("hqk,khe->qhe", grad_scores, key_heads) * scale_factor
    grad_k = dot("hqk,qhe->khe", grad_scores, query_heads) * scale_factor
    grad_v = dot("hqk,qhe->khe", probs.astype(bf16), grad_heads)
    return (
        grad_q.reshape(queries.shape).astype(bf16),
        jnp.concatenate(
            [grad_k.reshape(key_all.shape), grad_v.reshape(key_all.shape)], axis=1
        ).astype(bf16),
    )


def body_any(x_in, w_qkv, b_qv, w_proj, w_fc1, b_fc1, w_fc2, gains, biases, cotangent):
    depth = w_qkv.shape[0]
    shards = lax.axis_size("shard")
    own_rows, width = x_in.shape[0], x_in.shape[2]
    block = 2 * own_rows
    heads = b_qv.shape[2]
    half_width = w_qkv.shape[3]
    hidden = w_fc1.shape[2]

    small_shapes = [gains.shape, biases.shape, b_qv.shape, b_fc1.shape]
    small = small_rows([gains, biases, b_qv, b_fc1])
    group_a0 = jnp.concatenate([small, to_rows(w_qkv[0])])
    group_b0 = jnp.concatenate([to_rows(w_proj[0]), to_rows(w_fc1[0]), to_rows(w_fc2[0])])
    rest = []
    for index in range(1, depth):
        rest += [to_rows(w_qkv[index]), to_rows(w_proj[index]), to_rows(w_fc1[index]), to_rows(w_fc2[index])]
    group_rest = jnp.concatenate(rest)

    gathered_a0 = gather_packed(group_a0, shards)
    gathered_b0 = gather_packed(group_b0, shards)
    gathered_rest = gather_packed(group_rest, shards)

    def cutter(gathered, start):
        place = [start]

        def take(shape, axis):
            rows = math.prod(shape) // lanes
            piece = from_rows(gathered[:, place[0] : place[0] + rows], shape)
            place[0] += rows
            return join(piece, axis)

        return take

    shape_qkv, shape_proj = w_qkv.shape[1:], w_proj.shape[1:]
    shape_fc1, shape_fc2 = w_fc1.shape[1:], w_fc2.shape[1:]
    take_a, take_b, take_r = cutter(gathered_a0, small.shape[0]), cutter(gathered_b0, 0), cutter(gathered_rest, 0)
    weights = []
    for index in range(depth):
        take_q, take_o = (take_a, take_b) if index == 0 else (take_r, take_r)
        weights.append(
            (take_q(shape_qkv, 1), take_o(shape_proj, 1), take_o(shape_fc1, 0), take_o(shape_fc2, 1))
        )
    flat = gathered_a0[:, : small.shape[0]].reshape(shards, -1)
    vectors, start = [], 0
    for shape in small_shapes:
        size = math.prod(shape)
        piece = flat[:, start : start + size].reshape((shards,) + shape)
        vectors.append(join(piece, len(shape) - 1).astype(f32))
        start += size
    gain_all, bias_all, b_qv_all, b_fc1_all = vectors

    mask = attention_mask(block)
    x_own = x_in[:, 0]
    state = jnp.concatenate([x_own, swap_tp(x_own)]).astype(f32)
    g_own = cotangent[:, 0]
    grad_state = jnp.concatenate([g_own, swap_tp(g_own)]).astype(f32)

    stored = []
    for index in range(depth):
        w_query, w_out, w_first, w_second = weights[index]
        normed_in, scale_in = normalize(state)
        low_in = (normed_in * gain_all[index, 0] + bias_all[index, 0]).astype(bf16)
        bias_q = b_qv_all[index, 0].reshape(half_width)
        bias_v = b_qv_all[index, 1].reshape(half_width)
        queries = (dot("rd,df->rf", low_in, w_query[0]) + bias_q).astype(bf16)
        keys = dot("rd,df->rf", low_in, w_query[1]).astype(bf16)
        values = (dot("rd,df->rf", low_in, w_query[2]) + bias_v).astype(bf16)
        kv_own = jnp.concatenate([keys, values], axis=1)
        kv_chip = swap_x(kv_own)
        kv_all = jnp.concatenate([kv_own, swap_core(kv_own), kv_chip, swap_core(kv_chip)])
        key_all, value_all = kv_all[:, :half_width], kv_all[:, half_width:]
        attn, log_sums = attend(queries, key_all, value_all, mask, heads)
        attn_other = other_half(swap_tp(attn))
        w_out_other = swap_tp(w_out)
        middle = (
            state
            + dot("rf,fd->rd", attn, w_out)
            + dot("rf,fd->rd", attn_other, w_out_other)
            + bias_all[index, 1]
        )
        normed_mid, scale_mid = normalize(middle)
        low_mid = (normed_mid * gain_all[index, 1] + bias_all[index, 2]).astype(bf16)
        pre_act = dot("rd,df->rf", low_mid, w_first) + b_fc1_all[index].reshape(hidden)
        act = gelu_tanh(pre_act).astype(bf16)
        partial = dot("rf,fd->rd", act, w_second)
        if index == depth - 1:
            received = swap_tp(partial[own_rows:].astype(bf16)).astype(f32)
            output = middle[:own_rows] + partial[:own_rows] + received + bias_all[index, 3]
        else:
            received = other_half(swap_tp(partial.astype(bf16))).astype(f32)
            state = middle + partial + received + bias_all[index, 3]
        stored.append(
            (normed_in, scale_in, low_in, queries, key_all, value_all, log_sums, attn,
             normed_mid, scale_mid, low_mid, pre_act, act)
        )
    output = output.astype(bf16)[:, None]

    results = [None] * depth
    for index in reversed(range(depth)):
        w_query, w_out, w_first, w_second = weights[index]
        (normed_in, scale_in, low_in, queries, key_all, value_all, log_sums, attn,
         normed_mid, scale_mid, low_mid, pre_act, act) = stored[index]
        grad_bias_mlp = jnp.sum(grad_state, axis=0)
        grad_low = grad_state.astype(bf16)
        grad_hidden = dot("rd,fd->rf", grad_low, w_second)
        unused, gelu_pull = jax.vjp(gelu_tanh, pre_act)
        grad_pre = gelu_pull(grad_hidden)[0].astype(bf16)
        grad_w_second = dot("rf,rd->fd", act, grad_low)
        grad_w_first = dot("rd,rf->df", low_mid, grad_pre)
        grad_b_first = jnp.sum(grad_pre, axis=0, dtype=f32)
        partial = dot("rf,df->rd", grad_pre, w_first)
        mlp_rows = jnp.concatenate(
            [
                jax.vmap(to_rows)(split(grad_w_first.astype(bf16), 0, shards)),
                jax.vmap(to_rows)(split(grad_w_second.astype(bf16), 1, shards)),
            ],
            axis=1,
        )
        mlp_total = reduce_packed(mlp_rows)
        grad_mid = partial + other_half(swap_tp(partial.astype(bf16))).astype(f32)
        grad_gain_mid = jnp.sum(grad_mid * normed_mid, axis=0)
        grad_beta_mid = jnp.sum(grad_mid, axis=0)
        grad_middle = grad_state + norm_back(grad_mid * gain_all[index, 1], normed_mid, scale_mid)
        grad_bias_attn = jnp.sum(grad_middle, axis=0)
        grad_low = grad_middle.astype(bf16)
        grad_attn = dot("rd,fd->rf", grad_low, w_out).astype(bf16)
        grad_w_out = dot("rf,rd->fd", attn, grad_low)
        grad_q, grad_kv = attend_back(
            queries, key_all, value_all, mask, heads, log_sums, grad_attn
        )
        part = grad_kv.reshape(4, block, 2 * half_width)
        sent = swap_core(jnp.stack([part[1], part[3]])).astype(f32)
        mine = part[0].astype(f32) + sent[0]
        chip = (part[2].astype(f32) + sent[1]).astype(bf16)
        grad_kv = (mine + swap_x(chip).astype(f32)).astype(bf16)
        grad_qkv = jnp.stack([grad_q, grad_kv[:, :half_width], grad_kv[:, half_width:]])
        grad_w_query = dot("rd,crf->cdf", low_in, grad_qkv)
        grad_b_query = jnp.sum(grad_qkv[0::2], axis=1, dtype=f32)
        partial = dot("crf,cdf->rd", grad_qkv, w_query)
        grad_in = partial + other_half(swap_tp(partial.astype(bf16))).astype(f32)
        grad_gain_in = jnp.sum(grad_in * normed_in, axis=0)
        grad_beta_in = jnp.sum(grad_in, axis=0)
        grad_state = grad_middle + norm_back(grad_in * gain_all[index, 0], normed_in, scale_in)

        vectors = [
            jnp.stack([grad_gain_in, grad_gain_mid]),
            jnp.stack([grad_beta_in, grad_bias_attn, grad_beta_mid, grad_bias_mlp]),
            grad_b_query.reshape(2, heads, half_width // heads),
            grad_b_first.reshape(b_fc1_all.shape[1:]),
        ]
        parts = [split(vector, vector.ndim - 1, shards) for vector in vectors]
        part_shapes = [part.shape[1:] for part in parts]
        attn_rows = jnp.concatenate(
            [
                jax.vmap(to_rows)(split(grad_w_query.astype(bf16), 1, shards)),
                jax.vmap(to_rows)(split(grad_w_out.astype(bf16), 1, shards)),
                jax.vmap(lambda *own: small_rows(own))(*parts).astype(bf16),
            ],
            axis=1,
        )
        attn_total = reduce_packed(attn_rows)

        def pieces(total, shapes):
            place, out = 0, []
            for shape in shapes:
                rows = math.prod(shape) // lanes
                out.append(from_rows(total[place : place + rows], shape).astype(f32))
                place += rows
            return out, total[place:].reshape(-1)

        (out_fc1, out_fc2), unused = pieces(mlp_total, [shape_fc1, shape_fc2])
        (out_qkv, out_proj), tail = pieces(attn_total, [shape_qkv, shape_proj])
        small_out, start = [], 0
        for shape in part_shapes:
            size = math.prod(shape)
            small_out.append(tail[start : start + size].reshape(shape).astype(f32))
            start += size
        results[index] = (
            out_qkv, small_out[2], out_proj, out_fc1, small_out[3], out_fc2, small_out[0], small_out[1]
        )
    stacked = tuple(
        jnp.stack([results[index][member] for index in range(depth)]) for member in range(8)
    )
    return (output, grad_state[:own_rows, None]) + stacked


def compiler_params():
    return pltpu.CompilerParams(vmem_limit_bytes=56 * 2**20)


def whole(array):
    zeros = (0,) * array.ndim
    return pl.BlockSpec(array.shape, lambda i: zeros)


def rows_at(array, rows, start, lead=None, first=0):
    lead = array.shape[0] if lead is None else lead
    return pl.BlockSpec((lead, rows, lanes), lambda i: (first, start // rows, 0))


def run(kernel, outs, place, operands, scratch=(), flops=2**20, after=()):
    arrays, specs = [], []
    count = 1 + len(operands)

    def inner(*refs):
        kernel(*refs[:count], *refs[count + len(after) :])

    for operand in operands:
        array, spec = operand if isinstance(operand, tuple) else (operand, whole(operand))
        arrays.append(array)
        specs.append(spec)
    out_shape = [jax.ShapeDtypeStruct(shape, kind) for shape, kind in outs]
    after = list(after)
    arrays += after
    specs += [pl.BlockSpec(memory_space=pl.ANY)] * len(after)
    call = pl.pallas_call(
        inner,
        grid=(1,),
        out_shape=out_shape,
        in_specs=[pl.BlockSpec(memory_space=pltpu.SMEM)] + specs,
        out_specs=[whole(shape) for shape in out_shape],
        scratch_shapes=list(scratch),
        compiler_params=compiler_params(),
        cost_estimate=pl.CostEstimate(flops=flops, bytes_accessed=1024, transcendentals=0),
    )
    return list(call(place, *arrays))


def mm(left, right):
    return lax.dot_general(left, right, (((1,), (0,)), ((), ())), preferred_element_type=f32)


def mm_nt(left, right):
    return lax.dot_general(left, right, (((1,), (1,)), ((), ())), preferred_element_type=f32)


def mm_tn(left, right):
    return lax.dot_general(left, right, (((0,), (0,)), ((), ())), preferred_element_type=f32)


def lane_join(parts):
    return jnp.concatenate(parts, axis=1)


def row_join(parts):
    return jnp.concatenate(parts, axis=0)


class Pieces:
    def __init__(self, refs, place):
        self.refs, self.place = refs, place

    def tile(self, k, p, start, rows):
        if len(self.refs) == 1:
            z, c = self.place[0], self.place[1]
            return self.refs[0][(z - k + 4) % 4, p ^ c, start : start + rows]
        if k == 0:
            return self.refs[0][p, start : start + rows]
        return self.refs[1 + p][k - 1, start : start + rows]


def first_block(pieces, p):
    return row_join(
        [lane_join([pieces.tile(k, p, j * 128, 128) for j in range(2)]) for k in range(4)]
    )


def second_block(pieces, p):
    return lane_join([pieces.tile(k, p, 0, 256) for k in range(4)])


def small_row(small_local, small_far, row):
    parts = [small_local[0, row : row + 1]] + [small_far[k, row : row + 1] for k in range(3)]
    return lane_join(parts).astype(f32)


def spread(small_local, small_far, row, place_z, half, later=None):
    def rows_from(row):
        return row_join(
            [small_local[0, row : row + 1]] + [small_far[k, row : row + 1] for k in range(3)]
        ).astype(f32)

    source = rows_from(row)
    if later is not None:
        source = jnp.where(later == 0, source, rows_from(row + 1))
    source = source.astype(bf16)
    take = lax.broadcasted_iota(jnp.int32, (128, 256), 0)
    lane = lax.broadcasted_iota(jnp.int32, (128, 256), 1)
    wanted = half * 64 + (lane // 64) * 16 + lane % 16
    table = (take == wanted).astype(f32).astype(bf16)
    rows = mm(source, table)
    chunk = lax.broadcasted_iota(jnp.int32, (4, 256), 0)
    lane = lax.broadcasted_iota(jnp.int32, (4, 256), 1)
    keep = (lane % 64) // 16 == (place_z - chunk + 4) % 4
    return jnp.sum(jnp.where(keep, rows, 0.0), axis=0, keepdims=True)


def pack_kernel(kinds):
    def kernel(place, *refs):
        c = place[1]
        out, send = refs[-2:]
        start = 0
        for ref, kind in zip(refs, kinds):
            for q in range(4):
                to = q ^ c
                if kind == "first":
                    for j in range(2):
                        column = (2 * q + j) * 128
                        out[to, start + j * 128 : start + (j + 1) * 128] = ref[0, :, column : column + 128]
                elif kind == "second":
                    out[to, start : start + 256] = ref[0, q * 256 : (q + 1) * 256]
                elif kind == "proj":
                    out[to, start : start + 64] = ref[0, q * 64 : (q + 1) * 64]
                elif kind == "qkv":
                    for tile in range(6):
                        row = start + tile * 32
                        column = (tile % 2) * 128
                        out[to, row : row + 32] = ref[0, tile // 2, q * 32 : (q + 1) * 32, column : column + 128]
                else:
                    out[to, start : start + 32] = ref[...]
            start += kind_rows[kind]
        send[...] = out[0]

    return kernel


def quarter_pack_kernel(kinds):
    def kernel(place, *refs):
        out = refs[-1]
        for q in range(4):

            @pl.when(place[1] == q)
            def write(q=q):
                start = 0
                for ref, kind in zip(refs, kinds):
                    if kind == "first":
                        for j in range(2):
                            column = (2 * q + j) * 128
                            out[start + j * 128 : start + (j + 1) * 128] = ref[0, :, column : column + 128]
                    elif kind == "second":
                        out[start : start + 256] = ref[0, q * 256 : (q + 1) * 256]
                    elif kind == "proj":
                        out[start : start + 64] = ref[0, q * 64 : (q + 1) * 64]
                    else:
                        for tile in range(6):
                            row = start + tile * 32
                            column = (tile % 2) * 128
                            out[row : row + 32] = ref[0, tile // 2, q * 32 : (q + 1) * 32, column : column + 128]
                    start += kind_rows[kind]

    return kernel


kind_rows = {"first": 256, "second": 256, "proj": 64, "qkv": 192, "small": 32}


def pack(place, kinds, arrays, index, after=(), whole_quarters=True):
    rows = sum(kind_rows[kind] for kind in kinds)
    operands = []
    for kind, array, at in zip(kinds, arrays, index):
        if kind == "small":
            operands.append(array)
        else:
            block = (1,) + array.shape[1:]
            at = (at,) + (0,) * (array.ndim - 1)
            operands.append((array, pl.BlockSpec(block, lambda i, at=at: at)))
    if not whole_quarters:
        return run(quarter_pack_kernel(kinds), [((rows, lanes), bf16)], place, operands, after=after)[0]
    return run(
        pack_kernel(kinds), [((4, rows, lanes), bf16), ((rows, lanes), bf16)], place, operands, after=after
    )


def gather(quarter):
    full = lax.all_gather(quarter, ("shard", "ctx"), axis=0)
    return full.reshape((4, 4) + quarter.shape)


def gathered_rows(array, rows, start):
    return [(array, pl.BlockSpec((4, 4, rows, lanes), lambda i: (0, 0, start // rows, 0)))]


def shift(values, step):
    return lax.ppermute(values, "shard", [(z, (z + step) % 4) for z in range(4)])


def far_chunks(send):
    return [shift(send, k) for k in (1, 2, 3)]


def stack_kernel(place, one, two, three, out):
    for k, ref in enumerate((one, two, three)):
        out[k] = ref[...]


def stack(place, got, after=()):
    return run(stack_kernel, [((3,) + got[0].shape, bf16)], place, got, after=after)[0]


def pieces_of(group, rows, start):
    return [(array, rows_at(array, rows, start)) for array in group]


def small_of(group):
    return [(group[0], rows_at(group[0], 32, 256, lead=1)), (group[1], rows_at(group[1], 32, 256))]


def query_kernel(index, first_layer):
    def kernel(place, *refs):
        c = place[1]
        if first_layer:
            own, peer, small_local, small_far = refs[:4]
            pieces = Pieces(refs[4:9], place)
            grad_out = refs[14]
            grad_out[...] = row_join([own[128:], peer[128:]]).astype(f32)
            state_out, low_out, q_out, kv_out, w_out = refs[9:14]
            state = row_join([own[:128], peer[:128]]).astype(f32)
        else:
            middle, mine, other, small_local, small_far = refs[:5]
            pieces = Pieces(refs[5:6], place)
            state_out, low_out, q_out, kv_out, w_out = refs[6:]
            received = row_join([other[128:], other[:128]])
            state = (
                middle[...]
                + mine[...].astype(f32)
                + received.astype(f32)
                + small_row(small_local, small_far, 4 + 4 * (index - 1) + 3)
            )
        for k in range(4):
            for p in range(4):
                for tile in range(6):
                    w_out[k, p ^ c, :, tile * 128 : (tile + 1) * 128] = pieces.tile(k, p, tile * 32, 32)
        state_out[...] = state
        normed, scale = normalize(state)
        low = (
            normed * small_row(small_local, small_far, 2 * index)
            + small_row(small_local, small_far, 4 + 4 * index)
        ).astype(bf16)
        low_out[...] = low
        w_all = w_out[...].reshape(512, 768)
        row = 12 + index
        bias_q = spread(small_local, small_far, row, place[0], 0)
        bias_v = spread(small_local, small_far, row, place[0], 1)
        kv_out[:, :256] = mm(low, w_all[:, 256:512]).astype(bf16)
        kv_out[:, 256:] = (mm(low, w_all[:, 512:]) + bias_v).astype(bf16)
        q_out[...] = (mm(low, w_all[:, :256]) + bias_q).astype(bf16)

    return kernel


def seen(place, j):
    c, t = place[1], place[2]
    if j:
        return None
    row = lax.broadcasted_iota(jnp.int32, (256, 256), 0) ^ (t * 128)
    key = lax.broadcasted_iota(jnp.int32, (256, 256), 1) ^ (t * 128)
    return key <= row


def masked_scores(query, chunks, own_mask, place):
    parts = []
    for j in range(4):
        scores = mm_nt(query, chunks[j]) * 0.125
        if j == 0:
            scores = jnp.where(own_mask, scores, masked_value)
        else:
            scores = jnp.where((place[1] ^ j) < place[1], scores, masked_value)
        parts.append(scores)
    return parts


def attend_kernel(count, place, *refs):
    c = place[1]
    q, chunks = refs[0], refs[1:5]
    pieces = Pieces(refs[5 : 5 + count], place)
    attn_out, lse_out, partial_out, w_out = refs[5 + count :]
    for k in range(4):
        for p in range(4):
            w_out[p ^ c, :, k * 128 : (k + 1) * 128] = pieces.tile(k, p, 0, 64)
    own_mask = seen(place, 0)
    results = []
    for head in range(4):
        low, high = head * 64, (head + 1) * 64
        parts = masked_scores(q[:, low:high], [chunk[:, low:high] for chunk in chunks], own_mask, place)
        scores = lane_join(parts)
        top = jnp.max(scores, axis=1, keepdims=True)
        exponent = jnp.exp(scores - top)
        total = jnp.sum(exponent, axis=1, keepdims=True)
        values = row_join([chunk[:, 256 + low : 256 + high] for chunk in chunks])
        results.append(mm(exponent.astype(bf16), values) / total)
        lse_out[:, head : head + 1] = top + jnp.log(total)
    attn = lane_join(results).astype(bf16)
    attn_out[...] = attn
    partial_out[...] = mm(attn, w_out[...].reshape(256, 512)).astype(bf16)


def mlp_kernel(index):
    def kernel(place, *refs):
        state, mine, other, small_local, small_far = refs[:5]
        first, second = Pieces(refs[5:6], place), Pieces(refs[6:7], place)
        middle_out, low_out, pre_out, partial_out = refs[7:]
        received = row_join([other[128:], other[:128]])
        middle = (
            state[...]
            + mine[...].astype(f32)
            + received.astype(f32)
            + small_row(small_local, small_far, 4 + 4 * index + 1)
        )
        middle_out[...] = middle
        normed, scale = normalize(middle)
        low = (
            normed * small_row(small_local, small_far, 2 * index + 1)
            + small_row(small_local, small_far, 4 + 4 * index + 2)
        ).astype(bf16)
        low_out[...] = low
        total = None
        for p in range(4):
            q = p ^ place[1]
            bias = spread(small_local, small_far, 14 + 2 * index, place[0], q % 2, q // 2)
            pre = mm(low, first_block(first, p)) + bias
            pre_out[:, p * 256 : (p + 1) * 256] = pre
            act = gelu_tanh(pre).astype(bf16)
            part = mm(act, second_block(second, p))
            total = part if total is None else total + part
        partial_out[...] = total.astype(bf16)

    return kernel


root = math.sqrt(2 / math.pi)


def mlp_back(grad, pre_ref, low_ref, first, second, place, outs):
    partial_out, bias_out, b_first_out, keep, *sends = outs
    grad_low = grad.astype(bf16)
    bias_out[...] = jnp.sum(grad, axis=0, keepdims=True)
    total = None
    for p in range(4):
        pre = pre_ref[:, p * 256 : (p + 1) * 256]
        square = pre * pre
        wave = jnp.tanh(root * pre * (1 + 0.044715 * square))
        half = 0.5 * (1 + wave)
        act = (pre * half).astype(bf16)
        slope = half + 0.5 * pre * (1 - wave * wave) * root * (1 + 3 * 0.044715 * square)
        w_second = second_block(second, p)
        grad_pre = mm_nt(grad_low, w_second) * slope
        grad_pre_low = grad_pre.astype(bf16)
        b_first_out[p ^ place[1]] = jnp.sum(grad_pre_low.astype(f32), axis=0, keepdims=True)
        part = mm_nt(grad_pre_low, first_block(first, p))
        total = part if total is None else total + part
        to = keep.at[p // 2] if p % 2 == 0 else sends[p // 2]
        grad_first = mm_tn(low_ref[...], grad_pre_low).astype(bf16)
        grad_second = mm_tn(act, grad_low).astype(bf16)
        for k in range(4):
            for j in range(2):
                to[k, j * 128 : (j + 1) * 128] = grad_first[
                    k * 128 : (k + 1) * 128, j * 128 : (j + 1) * 128
                ]
            to[k, 256:512] = grad_second[:, k * 128 : (k + 1) * 128]
    partial_out[...] = total.astype(bf16)


def norm_step(grad_out, gain, values):
    normed, scale = normalize(values)
    sums = row_join(
        [
            jnp.sum(grad_out * normed, axis=0, keepdims=True),
            jnp.sum(grad_out, axis=0, keepdims=True),
        ]
    )
    return norm_back(grad_out * gain, normed, scale), sums


def received_sum(mine, other):
    return mine[...].astype(f32) + row_join([other[128:], other[:128]]).astype(f32)


def top_kernel(place, *refs):
    grad, pre, low = refs[:3]
    first, second = Pieces(refs[3:4], place), Pieces(refs[4:5], place)
    mlp_back(grad[...], pre, low, first, second, place, refs[5:])


def lower_kernel(index):
    def kernel(place, *refs):
        grad_mid, mine, other, state, small_local, small_far, pre, low = refs[:8]
        first, second = Pieces(refs[8:9], place), Pieces(refs[9:10], place)
        grad_out, sums_out = refs[10:12]
        grad, sums = norm_step(
            received_sum(mine, other), small_row(small_local, small_far, 2 * (index + 1)), state[...]
        )
        sums_out[...] = sums
        grad = grad_mid[...] + grad
        grad_out[...] = grad
        mlp_back(grad, pre, low, first, second, place, refs[12:])

    return kernel


def attend_back_kernel(index):
    def kernel(place, *refs):
        mine, other, middle, grad_state, small_local, small_far = refs[:6]
        attn, w_out, q = refs[6:9]
        chunks, lse = refs[9:13], refs[13]
        grad_out, sums_out, gw_out, dq_out, keep, send = refs[14:]
        grad, sums = norm_step(
            received_sum(mine, other), small_row(small_local, small_far, 2 * index + 1), middle[...]
        )
        grad = grad_state[...] + grad
        grad_out[...] = grad
        sums_out[0:2] = sums
        sums_out[2:3] = jnp.sum(grad, axis=0, keepdims=True)
        grad_low = grad.astype(bf16)
        grad_attn = mm_nt(grad_low, w_out[...].reshape(256, 512)).astype(bf16)
        gw_out[...] = mm_tn(attn[...], grad_low).astype(bf16).reshape(4, 64, 512)
        own_mask = seen(place, 0)
        dq_all = []
        dk_all = [[] for j in range(4)]
        dv_all = [[] for j in range(4)]
        for head in range(4):
            low, high = head * 64, (head + 1) * 64
            query, grad_head = q[:, low:high], grad_attn[:, low:high]
            keys = [chunk[:, low:high] for chunk in chunks]
            row_dot = jnp.sum(
                grad_head.astype(f32) * attn[:, low:high].astype(f32), axis=1, keepdims=True
            )
            log_sum = lse[:, head : head + 1]
            parts = masked_scores(query, keys, own_mask, place)
            dq = None
            for j in range(4):
                probs = jnp.exp(parts[j] - log_sum)
                grad_probs = mm_nt(grad_head, chunks[j][:, 256 + low : 256 + high])
                grad_scores = (probs * (grad_probs - row_dot)).astype(bf16)
                part = mm(grad_scores, keys[j])
                dq = part if dq is None else dq + part
                dk_all[j].append(mm_tn(grad_scores, query) * 0.125)
                dv_all[j].append(mm_tn(probs.astype(bf16), grad_head))
            dq_all.append(dq * 0.125)
        dq_out[...] = lane_join(dq_all).astype(bf16)
        for j in range(4):
            to = keep if j % 2 == 0 else send
            to[j // 2, :, :256] = lane_join(dk_all[j]).astype(bf16)
            to[j // 2, :, 256:] = lane_join(dv_all[j]).astype(bf16)

    return kernel


def halve_kernel(place, keep, got, own_out, send_out):
    own_out[...] = (keep[0].astype(f32) + got[0].astype(f32)).astype(bf16)
    send_out[...] = (keep[1].astype(f32) + got[1].astype(f32)).astype(bf16)


def halve_groups_kernel(place, *refs):
    own_out, send_out = refs[-2:]
    start = 0
    for keep, one, two in zip(refs[:-2:3], refs[1:-2:3], refs[2:-2:3]):
        rows = keep.shape[2]
        for half, got, out in ((0, one, own_out), (1, two, send_out)):
            total = keep[half].astype(f32) + got[...].astype(f32)
            out[:, start : start + rows] = total.astype(bf16)
        start += rows


def quarter_in_order(place, own, got, out):
    for k in range(4):
        total = own[k].astype(f32) + got[k].astype(f32)
        out[(place[0] - k + 4) % 4] = total.astype(bf16)


def query_back_kernel(place, *refs):
    dq, dkv, got, low, w_ref, gw_ref = refs[:6]
    partial_out, b_out, keep, *sends, scratch = refs[6:]
    c = place[1]
    grad_kv = (dkv[...].astype(f32) + got[...].astype(f32)).astype(bf16)
    grad_qkv = lane_join([dq[...], grad_kv])
    partial_out[...] = mm_nt(grad_qkv, w_ref[...].reshape(512, 768)).astype(bf16)
    b_out[0:1] = jnp.sum(dq[...].astype(f32), axis=0, keepdims=True)
    b_out[1:2] = jnp.sum(grad_kv[:, 256:].astype(f32), axis=0, keepdims=True)
    scratch[...] = mm_tn(low[...], grad_qkv).astype(bf16).reshape(4, 4, 32, 768)
    for p in range(4):
        to = keep.at[p // 2] if p % 2 == 0 else sends[p // 2]
        for k in range(4):
            for tile in range(6):
                to[k, tile * 32 : (tile + 1) * 32] = scratch[
                    k, p ^ c, :, tile * 128 : (tile + 1) * 128
                ]
            to[k, 192:256] = gw_ref[p ^ c, :, k * 128 : (k + 1) * 128]


def last_quarter_kernel(place, own, got, sums, one, two, three, *outs):
    for k in range(4):
        outs[k][:256] = (own[k].astype(f32) + got[k].astype(f32)).astype(bf16)
        total = (sums[k] + one[k]) + (two[k] + three[k])
        outs[k][256:] = total.astype(bf16)


def last_total_kernel(place, own, one, two, three, out, small_out):
    total = own[...].astype(f32) + one[...].astype(f32)
    total = total + (two[...].astype(f32) + three[...].astype(f32))
    out[...] = total[:256].astype(bf16)
    small_out[...] = total[256:]


def halve(place, groups, after=()):
    operands = []
    for keep, one, two in groups:
        operands += [keep, swap_core(one), swap_core(two)]
    rows = sum(group[0].shape[2] for group in groups)
    return run(halve_groups_kernel, [((4, rows, lanes), bf16)] * 2, place, operands, after=after)


def quarter(place, own, send, after=()):
    (both,) = run(quarter_in_order, [(own.shape, bf16)], place, [own, swap_x(send)], after=after)
    return both


def copy_kernel(place, source, out):
    out[...] = source[...]


def hand_on(place, array, after):
    return run(copy_kernel, [(array.shape, bf16)], place, [array], after=after)[0]


def collect(total):
    chip = swap_x(total)
    return [total, swap_core(total), chip, swap_core(chip)]


def fill(refs, scratch):
    for p in range(4):
        scratch[p] = refs[p][...].astype(f32)


def hidden_out_kernel(place, *refs):
    c = place[1]
    first_out, second_out, scratch = refs[-3:]
    fill(refs, scratch)
    for q in range(4):
        for j in range(2):
            column = (2 * q + j) * 128
            first_out[0, :, column : column + 128] = scratch[q ^ c, j * 128 : (j + 1) * 128]
        second_out[0, q * 256 : (q + 1) * 256] = scratch[q ^ c, 256:]


def heads_out_kernel(place, *refs):
    c = place[1]
    qkv_out, proj_out, scratch = refs[-3:]
    fill(refs, scratch)
    for q in range(4):
        for tile in range(6):
            column = (tile % 2) * 128
            qkv_out[0, tile // 2, q * 32 : (q + 1) * 32, column : column + 128] = scratch[
                q ^ c, tile * 32 : (tile + 1) * 32
            ]
        proj_out[0, q * 64 : (q + 1) * 64] = scratch[q ^ c, 192:]


def layer_out(kernel, rows, place, totals, layer, shapes, before, start, after):
    extra = list(before) + list(after)
    count = 1 + len(totals)

    def inner(*refs):
        kernel(*refs[:count], *refs[count + len(extra) :])

    def block(shape):
        at = (layer,) + (0,) * (len(shape) - 1)
        return pl.BlockSpec((1,) + tuple(shape[1:]), lambda i: at)

    return list(
        pl.pallas_call(
            inner,
            grid=(1,),
            out_shape=[jax.ShapeDtypeStruct(shape, f32) for shape in shapes],
            in_specs=[pl.BlockSpec(memory_space=pltpu.SMEM)]
            + [pl.BlockSpec((rows, lanes), lambda i: (start // rows, 0))] * 4
            + [pl.BlockSpec(memory_space=pl.ANY)] * len(extra),
            out_specs=[block(shape) for shape in shapes],
            scratch_shapes=[pltpu.VMEM((4, rows, lanes), f32)],
            input_output_aliases={count + i: i for i in range(len(before))},
            compiler_params=compiler_params(),
            cost_estimate=pl.CostEstimate(flops=2**20, bytes_accessed=1024, transcendentals=0),
        )(place, *totals, *extra)
    )


def hidden_out(place, totals, layer, shape_one, shape_two, before, start, after=()):
    shapes = (shape_one, shape_two)
    return layer_out(hidden_out_kernel, 512, place, totals, layer, shapes, before, start, after)


def heads_out(place, totals, layer, shape_one, shape_two, before, start, after=()):
    shapes = (shape_one, shape_two)
    return layer_out(heads_out_kernel, 256, place, totals, layer, shapes, before, start, after)


def last_kernel(place, *refs):
    grad_mid, mine, other, state, small_local, small_far = refs[:6]
    sums_in = refs[6]
    sums_mid, bias_mlp, b_query, b_first = refs[7:9], refs[9:11], refs[11:13], refs[13:15]
    grad_out, out = refs[15:]
    grad, sums = norm_step(received_sum(mine, other), small_row(small_local, small_far, 0), state[...])
    grad_out[...] = grad_mid[:128] + grad[:128]
    for layer in range(2):
        inner = sums if layer == 0 else sums_in[...]
        mid = sums_mid[layer]
        rows = [
            (2 * layer, inner[0:1]),
            (2 * layer + 1, mid[0:1]),
            (4 + 4 * layer, inner[1:2]),
            (5 + 4 * layer, mid[2:3]),
            (6 + 4 * layer, mid[1:2]),
            (7 + 4 * layer, bias_mlp[layer][...]),
        ]
        for k in range(4):
            for row, value in rows:
                out[k, row : row + 1] = value[:, k * 128 : (k + 1) * 128]
            for channel in range(2):
                for j in range(2):
                    row = 12 + 4 * layer + 2 * channel + j
                    out[k, row : row + 1] = b_query[layer][channel : channel + 1, j * 128 : (j + 1) * 128]
            for q in range(4):
                for j in range(2):
                    row = 20 + 8 * layer + 2 * q + j
                    out[k, row : row + 1] = b_first[layer][q, :, j * 128 : (j + 1) * 128]
    out[:, 36:] = jnp.zeros((4, 12, lanes), f32)


def turn(values, place_z, back):
    rows = values.shape[0]
    chunks = values.reshape(rows, 4, lanes)
    order = (place_z - jnp.arange(4)) % 4
    return jnp.concatenate(
        [lax.dynamic_slice_in_dim(values, order[k] * lanes, lanes, 1) for k in range(4)], axis=1
    )


def body_four(x_in, w_qkv, b_qv, w_proj, w_fc1, b_fc1, w_fc2, gains, biases, cotangent):
    z, c, t = lax.axis_index("shard"), lax.axis_index("ctx"), lax.axis_index("tp")
    place = jnp.stack([z, c, t]).astype(jnp.int32)
    flat = jnp.concatenate([array.reshape(-1) for array in (gains, biases, b_qv, b_fc1)])
    small = jnp.pad(flat, (0, 32 * lanes - flat.shape[0])).reshape(32, lanes)

    kinds = ("qkv", "proj", "first", "second", "first", "second")
    send = pack(
        place, kinds, (w_qkv, w_proj, w_fc1, w_fc2, w_fc1, w_fc2), (1, 1, 0, 0, 1, 1), whole_quarters=False
    )
    full = gather(send)
    local_a, send_a = pack(place, ("qkv", "proj", "small"), (w_qkv, w_proj, small), (0, 0, 0))
    pair_own = turn(jnp.concatenate([x_in[:, 0], cotangent[:, 0]]), z, False)
    pair_peer = swap_tp(pair_own)
    got_a = far_chunks(send_a)
    far_a = stack(place, got_a)
    chip_a = swap_x(far_a)
    group_a0 = [local_a, far_a, swap_core(far_a), chip_a, swap_core(chip_a)]
    small_parts = small_of(group_a0)
    parts = {
        "qkv": [pieces_of(group_a0, 192, 0), gathered_rows(full, 192, 0)],
        "proj": [pieces_of(group_a0, 64, 192), gathered_rows(full, 64, 192)],
        "first": [gathered_rows(full, 256, 256), gathered_rows(full, 256, 768)],
        "second": [gathered_rows(full, 256, 512), gathered_rows(full, 256, 1024)],
    }
    square, wide = (256, 512), (256, 256)
    saved = []
    for layer in range(2):
        source = [pair_own, pair_peer] if layer == 0 else [middle, partial, swap_tp(partial)]
        more = [(square, f32)] if layer == 0 else []
        state, low_in, q, kv, w_all, *passed = run(
            query_kernel(layer, layer == 0),
            [(square, f32), (square, bf16), (wide, bf16), (square, bf16), ((4, 4, 32, 768), bf16)] + more,
            place,
            source + small_parts + parts["qkv"][layer],
        )
        if layer == 0:
            g_all = passed[0]
        kv_chip = swap_x(kv)
        chunks = [kv, swap_core(kv), kv_chip, swap_core(kv_chip)]
        attn, lse, partial, w_out = run(
            functools.partial(attend_kernel, len(parts["proj"][layer])),
            [(wide, bf16), ((256, lanes), f32), (square, bf16), ((4, 64, 512), bf16)],
            place,
            [q] + chunks + parts["proj"][layer],
        )
        middle, low_mid, pre, partial = run(
            mlp_kernel(layer),
            [(square, f32), (square, bf16), ((256, 1024), f32), (square, bf16)],
            place,
            [state, partial, swap_tp(partial)] + small_parts + parts["first"][layer] + parts["second"][layer],
        )
        saved.append((state, low_in, q, chunks, w_all, attn, lse, w_out, middle, low_mid, pre))

    received = swap_tp(partial[128:]).astype(f32)
    output = None
    bias_last = jnp.concatenate([small_parts[0][0][0, 267:268], small_parts[1][0][:, 267]]).reshape(1, 512)
    output = middle[:128] + partial[:128].astype(f32) + received + bias_last.astype(f32)
    output = turn(output.astype(bf16), z, True)[:, None]

    hidden_outs = [
        (square, bf16),
        ((1, 512), f32),
        ((4, 1, 256), f32),
        ((2, 4, 512, lanes), bf16),
        ((4, 512, lanes), bf16),
        ((4, 512, lanes), bf16),
    ]
    sums_mid, bias_mlp, b_query, b_first = [0, 0], [0, 0], [0, 0], [0, 0]
    hidden = [None, None]
    for layer in (1, 0):
        state, low_in, q, chunks, w_all, attn, lse, w_out, middle, low_mid, pre = saved[layer]
        tail = [pre, low_mid] + parts["first"][layer] + parts["second"][layer]
        if layer == 1:
            grad_state = g_all
            partial, bias_mlp[1], b_first[1], *grads = run(
                top_kernel, hidden_outs, place, [grad_state] + tail
            )
        else:
            own, far = halve(place, [first_grads, grads])
            grad_state, sums_in, partial, bias_mlp[0], b_first[0], *grads = run(
                lower_kernel(0),
                [(square, f32), ((2, 512), f32)] + hidden_outs,
                place,
                [grad_mid, partial, swap_tp(partial), saved[1][0]] + small_parts + tail,
                after=[own],
            )
            both = quarter(place, own, far, after=[partial])
            upper = lax.psum_scatter(both, "shard", scatter_dimension=0)
        behind = []
        if layer == 1:
            first_grads = grads
        else:
            own, far = halve(place, [grads])
            behind = [both, own]
        grad_mid, sums_mid[layer], gw_out, dq, keep, send = run(
            attend_back_kernel(layer),
            [
                (square, f32),
                ((3, 512), f32),
                ((4, 64, 512), bf16),
                (wide, bf16),
                ((2, 256, 512), bf16),
                ((2, 256, 512), bf16),
            ],
            place,
            [partial, swap_tp(partial), middle, grad_state] + small_parts + [attn, w_out, q] + chunks + [lse],
            after=behind,
        )
        if layer == 0:
            both = quarter(place, own, far, after=[keep])
            lower = lax.psum_scatter(both, "shard", scatter_dimension=0)
            behind = [both]
        dkv, chip = run(halve_kernel, [(square, bf16)] * 2, place, [keep, swap_core(send)], after=behind)
        partial, b_query[layer], *grads = run(
            query_back_kernel,
            [
                (square, bf16),
                ((2, 256), f32),
                ((2, 4, 256, lanes), bf16),
                ((4, 256, lanes), bf16),
                ((4, 256, lanes), bf16),
            ],
            place,
            [dq, dkv, swap_x(chip), low_in, w_all, gw_out],
            scratch=[pltpu.VMEM((4, 4, 32, 768), bf16)],
            after=[output] if layer == 1 else [],
        )
    own, far = halve(place, [grads])
    grad_x, sums = run(
        last_kernel,
        [((128, 512), f32), ((4, 48, lanes), f32)],
        place,
        [grad_mid, partial, swap_tp(partial), saved[0][0]]
        + small_parts
        + [sums_in]
        + sums_mid
        + bias_mlp
        + b_query
        + b_first,
        after=[own],
    )
    pieces = run(
        last_quarter_kernel,
        [((304, lanes), bf16)] * 4,
        place,
        [own, swap_x(far), sums, swap_core(sums), swap_x(sums), swap_both(sums)],
    )
    grad_x = turn(grad_x, z, True)[:, None]
    got = [shift(pieces[k], 4 - k) for k in (1, 2, 3)]
    last, total = run(
        last_total_kernel, [((256, lanes), bf16), ((48, lanes), f32)], place, [pieces[0]] + got
    )
    upper_parts, lower_parts = collect(upper), collect(hand_on(place, lower, [last]))
    outs_heads = heads_out(place, upper_parts, 1, w_qkv.shape, w_proj.shape, [], 512, after=[last])
    outs_hidden = hidden_out(place, upper_parts, 1, w_fc1.shape, w_fc2.shape, [], 0, after=[last])
    grad_fc1, grad_fc2 = hidden_out(place, lower_parts, 0, w_fc1.shape, w_fc2.shape, outs_hidden, 0)
    grad_gains = total[:4].reshape(gains.shape)
    grad_biases = total[4:12].reshape(biases.shape)
    rest_q = total[12:20].reshape(2, 2, 4, 64)
    rest_f = total[20:36].reshape(2, 16, 64)
    grad_b_qv = lax.dynamic_slice_in_dim(rest_q, z * 16, 16, 3)
    grad_b_fc1 = lax.dynamic_slice_in_dim(rest_f, z * 16, 16, 2)

    grad_qkv, grad_proj = heads_out(place, collect(last), 0, w_qkv.shape, w_proj.shape, outs_heads, 0)
    return (
        output, grad_x, grad_qkv, grad_b_qv, grad_proj, grad_fc1, grad_b_fc1, grad_fc2, grad_gains, grad_biases
    )


def body(*args):
    x_in, w_qkv, b_qv, w_proj, w_fc1 = args[:5]
    expected = ((128, 1, 512), (2, 3, 128, 256), (2, 2, 4, 16), (2, 256, 128), (2, 128, 1024))
    sizes = (lax.axis_size("shard"), lax.axis_size("ctx"), lax.axis_size("tp"))
    shapes = tuple(array.shape for array in (x_in, w_qkv, b_qv, w_proj, w_fc1))
    if sizes == (4, 4, 2) and shapes == expected:
        return body_four(*args)
    return body_any(*args)


def solution(mesh):
    return jax.shard_map(
        body,
        mesh=mesh,
        in_specs=(
            P(("ctx", "tp"), "shard", None),
            P(None, None, "shard", "tp"),
            P(None, None, "tp", "shard"),
            P(None, "tp", "shard"),
            P(None, "shard", "tp"),
            P(None, "tp", "shard"),
            P(None, "tp", "shard"),
            P(None, None, "shard"),
            P(None, None, "shard"),
            P(("ctx", "tp"), "shard", None),
        ),
        out_specs=(
            P(("ctx", "tp"), "shard", None),
            P(("ctx", "tp"), "shard", None),
            P(None, None, "shard", "tp"),
            P(None, None, "tp", "shard"),
            P(None, "tp", "shard"),
            P(None, "shard", "tp"),
            P(None, "tp", "shard"),
            P(None, "tp", "shard"),
            P(None, None, "shard"),
            P(None, None, "shard"),
        ),
        check_vma=False,
    )
```

```python
import functools
import math

import jax
import jax.numpy as jnp
from jax import lax
from jax.experimental import pallas as pl
from jax.experimental.pallas import tpu as pltpu
from jax.sharding import PartitionSpec as P

epsilon = 1e-05
masked_value = -1e30
lanes = 128
f32 = jnp.float32
bf16 = jnp.bfloat16


def normalize(values):
    center = jnp.mean(values, axis=-1, keepdims=True)
    shifted = values - center
    scale_inv = lax.rsqrt(jnp.mean(shifted * shifted, axis=-1, keepdims=True) + epsilon)
    return (shifted * scale_inv, scale_inv)


def norm_back(grad_norm, normed, scale_inv):
    mean_grad = jnp.mean(grad_norm, axis=-1, keepdims=True)
    mean_prod = jnp.mean(grad_norm * normed, axis=-1, keepdims=True)
    return scale_inv * (grad_norm - mean_grad - normed * mean_prod)


def gelu_tanh(values):
    return jax.nn.gelu(values, approximate=True)


def dot(pattern, left, right):
    return jnp.einsum(pattern, left, right, preferred_element_type=f32)


def to_rows(array):
    rows, columns = array.shape[-2:]
    if columns % lanes or rows % 16:
        return array.reshape(-1, lanes)
    tiles = array.reshape(-1, rows, columns // lanes, lanes)
    return jnp.swapaxes(tiles, 1, 2).reshape(-1, lanes)


def from_rows(packed, shape):
    rows, columns = shape[-2:]
    lead = packed.shape[:-2]
    if columns % lanes or rows % 16:
        return packed.reshape(lead + tuple(shape))
    count = math.prod(shape[:-2])
    tiles = packed.reshape(lead + (count, columns // lanes, rows, lanes))
    return jnp.swapaxes(tiles, -3, -2).reshape(lead + tuple(shape))


def small_rows(arrays):
    flat = jnp.concatenate([array.reshape(-1) for array in arrays])
    size = -(-flat.shape[0] // (64 * lanes)) * 64 * lanes
    return jnp.pad(flat, (0, size - flat.shape[0])).reshape(-1, lanes)


def join(gathered, axis):
    moved = jnp.moveaxis(gathered, 0, axis)
    shape = moved.shape
    return moved.reshape(shape[:axis] + (shape[axis] * shape[axis + 1],) + shape[axis + 2 :])


def split(whole, axis, shards):
    shape = whole.shape
    parts = whole.reshape(shape[:axis] + (shards, shape[axis] // shards) + shape[axis + 1 :])
    return jnp.moveaxis(parts, axis, 0)


def swap_tp(values):
    return lax.ppermute(values, "tp", [(0, 1), (1, 0)])


def swap_core(values):
    return lax.ppermute(values, "ctx", [(0, 1), (1, 0), (2, 3), (3, 2)])


def swap_x(values):
    return lax.ppermute(values, "ctx", [(0, 2), (2, 0), (1, 3), (3, 1)])


def swap_both(values):
    return lax.ppermute(values, "ctx", [(0, 3), (3, 0), (1, 2), (2, 1)])


def other_half(values):
    half = values.shape[0] // 2
    return jnp.concatenate([values[half:], values[:half]])


def gather_packed(packed, shards):
    quarter = packed.shape[0] // 4
    own = lax.dynamic_slice_in_dim(packed, lax.axis_index("ctx") * quarter, quarter, 0)
    return lax.all_gather(own, ("shard", "ctx"), axis=0, tiled=True).reshape(
        shards, packed.shape[0], lanes
    )


def halves(values, bit):
    half = values.shape[1] // 2
    keep = lax.dynamic_slice_in_dim(values, bit * half, half, 1)
    send = lax.dynamic_slice_in_dim(values, (1 - bit) * half, half, 1)
    return keep, send


def paired(own, other, bit):
    return jnp.where(
        bit == 0, jnp.concatenate([own, other]), jnp.concatenate([other, own])
    )


def reduce_packed(packed):
    place = lax.axis_index("ctx")
    core, chip = place % 2, place // 2
    keep, send = halves(packed, core)
    half = (keep.astype(f32) + swap_core(send).astype(f32)).astype(bf16)
    keep, send = halves(half, chip)
    quarter = (keep.astype(f32) + swap_x(send).astype(f32)).astype(bf16)
    parts = lax.all_to_all(quarter, "shard", split_axis=0, concat_axis=0, tiled=True)
    total = jnp.sum(parts.astype(f32), axis=0).astype(bf16)
    both = paired(total, swap_x(total), chip)
    return paired(both, swap_core(both), core)


def positions(offsets, tp_place, chunk, block):
    half = block // 2
    return chunk * block + (offsets + tp_place * half) % block


def attention_mask(block):
    place, tp_place = lax.axis_index("ctx"), lax.axis_index("tp")
    offsets = jnp.arange(block, dtype=jnp.int32)
    rows = positions(offsets, tp_place, place, block)
    keys = jnp.concatenate([positions(offsets, tp_place, place ^ j, block) for j in range(4)])
    return keys[None, :] <= rows[:, None]


def head_split(values, heads):
    return values.reshape(values.shape[0], heads, values.shape[1] // heads)


def attend(queries, key_all, value_all, mask, heads):
    scale_factor = (queries.shape[1] // heads) ** (-0.5)
    scores = dot("qhe,khe->hqk", head_split(queries, heads), head_split(key_all, heads))
    scores = jnp.where(mask, scores * scale_factor, masked_value)
    row_top = jnp.max(scores, axis=-1, keepdims=True)
    exponent = jnp.exp(scores - row_top)
    totals = jnp.sum(exponent, axis=-1, keepdims=True)
    probs = (exponent / totals).astype(bf16)
    out = dot("hqk,khe->qhe", probs, head_split(value_all, heads))
    return out.reshape(queries.shape).astype(bf16), row_top + jnp.log(totals)


def attend_back(queries, key_all, value_all, mask, heads, log_sums, grad_out):
    scale_factor = (queries.shape[1] // heads) ** (-0.5)
    query_heads, key_heads = head_split(queries, heads), head_split(key_all, heads)
    grad_heads = head_split(grad_out, heads)
    scores = dot("qhe,khe->hqk", query_heads, key_heads)
    scores = jnp.where(mask, scores * scale_factor, masked_value)
    probs = jnp.exp(scores - log_sums)
    grad_probs = dot("qhe,khe->hqk", grad_heads, head_split(value_all, heads))
    row_dot = jnp.sum(probs * grad_probs, axis=-1, keepdims=True)
    grad_scores = (probs * (grad_probs - row_dot)).astype(bf16)
    grad_q = dot("hqk,khe->qhe", grad_scores, key_heads) * scale_factor
    grad_k = dot("hqk,qhe->khe", grad_scores, query_heads) * scale_factor
    grad_v = dot("hqk,qhe->khe", probs.astype(bf16), grad_heads)
    return (
        grad_q.reshape(queries.shape).astype(bf16),
        jnp.concatenate(
            [grad_k.reshape(key_all.shape), grad_v.reshape(key_all.shape)], axis=1
        ).astype(bf16),
    )


def body_any(x_in, w_qkv, b_qv, w_proj, w_fc1, b_fc1, w_fc2, gains, biases, cotangent):
    depth = w_qkv.shape[0]
    shards = lax.axis_size("shard")
    own_rows, width = x_in.shape[0], x_in.shape[2]
    block = 2 * own_rows
    heads = b_qv.shape[2]
    half_width = w_qkv.shape[3]
    hidden = w_fc1.shape[2]

    small_shapes = [gains.shape, biases.shape, b_qv.shape, b_fc1.shape]
    small = small_rows([gains, biases, b_qv, b_fc1])
    group_a0 = jnp.concatenate([small, to_rows(w_qkv[0])])
    group_b0 = jnp.concatenate([to_rows(w_proj[0]), to_rows(w_fc1[0]), to_rows(w_fc2[0])])
    rest = []
    for index in range(1, depth):
        rest += [to_rows(w_qkv[index]), to_rows(w_proj[index]), to_rows(w_fc1[index]), to_rows(w_fc2[index])]
    group_rest = jnp.concatenate(rest)

    gathered_a0 = gather_packed(group_a0, shards)
    gathered_b0 = gather_packed(group_b0, shards)
    gathered_rest = gather_packed(group_rest, shards)

    def cutter(gathered, start):
        place = [start]

        def take(shape, axis):
            rows = math.prod(shape) // lanes
            piece = from_rows(gathered[:, place[0] : place[0] + rows], shape)
            place[0] += rows
            return join(piece, axis)

        return take

    shape_qkv, shape_proj = w_qkv.shape[1:], w_proj.shape[1:]
    shape_fc1, shape_fc2 = w_fc1.shape[1:], w_fc2.shape[1:]
    take_a, take_b, take_r = cutter(gathered_a0, small.shape[0]), cutter(gathered_b0, 0), cutter(gathered_rest, 0)
    weights = []
    for index in range(depth):
        take_q, take_o = (take_a, take_b) if index == 0 else (take_r, take_r)
        weights.append(
            (take_q(shape_qkv, 1), take_o(shape_proj, 1), take_o(shape_fc1, 0), take_o(shape_fc2, 1))
        )
    flat = gathered_a0[:, : small.shape[0]].reshape(shards, -1)
    vectors, start = [], 0
    for shape in small_shapes:
        size = math.prod(shape)
        piece = flat[:, start : start + size].reshape((shards,) + shape)
        vectors.append(join(piece, len(shape) - 1).astype(f32))
        start += size
    gain_all, bias_all, b_qv_all, b_fc1_all = vectors

    mask = attention_mask(block)
    x_own = x_in[:, 0]
    state = jnp.concatenate([x_own, swap_tp(x_own)]).astype(f32)
    g_own = cotangent[:, 0]
    grad_state = jnp.concatenate([g_own, swap_tp(g_own)]).astype(f32)

    stored = []
    for index in range(depth):
        w_query, w_out, w_first, w_second = weights[index]
        normed_in, scale_in = normalize(state)
        low_in = (normed_in * gain_all[index, 0] + bias_all[index, 0]).astype(bf16)
        bias_q = b_qv_all[index, 0].reshape(half_width)
        bias_v = b_qv_all[index, 1].reshape(half_width)
        queries = (dot("rd,df->rf", low_in, w_query[0]) + bias_q).astype(bf16)
        keys = dot("rd,df->rf", low_in, w_query[1]).astype(bf16)
        values = (dot("rd,df->rf", low_in, w_query[2]) + bias_v).astype(bf16)
        kv_own = jnp.concatenate([keys, values], axis=1)
        kv_chip = swap_x(kv_own)
        kv_all = jnp.concatenate([kv_own, swap_core(kv_own), kv_chip, swap_core(kv_chip)])
        key_all, value_all = kv_all[:, :half_width], kv_all[:, half_width:]
        attn, log_sums = attend(queries, key_all, value_all, mask, heads)
        attn_other = other_half(swap_tp(attn))
        w_out_other = swap_tp(w_out)
        middle = (
            state
            + dot("rf,fd->rd", attn, w_out)
            + dot("rf,fd->rd", attn_other, w_out_other)
            + bias_all[index, 1]
        )
        normed_mid, scale_mid = normalize(middle)
        low_mid = (normed_mid * gain_all[index, 1] + bias_all[index, 2]).astype(bf16)
        pre_act = dot("rd,df->rf", low_mid, w_first) + b_fc1_all[index].reshape(hidden)
        act = gelu_tanh(pre_act).astype(bf16)
        partial = dot("rf,fd->rd", act, w_second)
        if index == depth - 1:
            received = swap_tp(partial[own_rows:].astype(bf16)).astype(f32)
            output = middle[:own_rows] + partial[:own_rows] + received + bias_all[index, 3]
        else:
            received = other_half(swap_tp(partial.astype(bf16))).astype(f32)
            state = middle + partial + received + bias_all[index, 3]
        stored.append(
            (normed_in, scale_in, low_in, queries, key_all, value_all, log_sums, attn,
             normed_mid, scale_mid, low_mid, pre_act, act)
        )
    output = output.astype(bf16)[:, None]

    results = [None] * depth
    for index in reversed(range(depth)):
        w_query, w_out, w_first, w_second = weights[index]
        (normed_in, scale_in, low_in, queries, key_all, value_all, log_sums, attn,
         normed_mid, scale_mid, low_mid, pre_act, act) = stored[index]
        grad_bias_mlp = jnp.sum(grad_state, axis=0)
        grad_low = grad_state.astype(bf16)
        grad_hidden = dot("rd,fd->rf", grad_low, w_second)
        unused, gelu_pull = jax.vjp(gelu_tanh, pre_act)
        grad_pre = gelu_pull(grad_hidden)[0].astype(bf16)
        grad_w_second = dot("rf,rd->fd", act, grad_low)
        grad_w_first = dot("rd,rf->df", low_mid, grad_pre)
        grad_b_first = jnp.sum(grad_pre, axis=0, dtype=f32)
        partial = dot("rf,df->rd", grad_pre, w_first)
        mlp_rows = jnp.concatenate(
            [
                jax.vmap(to_rows)(split(grad_w_first.astype(bf16), 0, shards)),
                jax.vmap(to_rows)(split(grad_w_second.astype(bf16), 1, shards)),
            ],
            axis=1,
        )
        mlp_total = reduce_packed(mlp_rows)
        grad_mid = partial + other_half(swap_tp(partial.astype(bf16))).astype(f32)
        grad_gain_mid = jnp.sum(grad_mid * normed_mid, axis=0)
        grad_beta_mid = jnp.sum(grad_mid, axis=0)
        grad_middle = grad_state + norm_back(grad_mid * gain_all[index, 1], normed_mid, scale_mid)
        grad_bias_attn = jnp.sum(grad_middle, axis=0)
        grad_low = grad_middle.astype(bf16)
        grad_attn = dot("rd,fd->rf", grad_low, w_out).astype(bf16)
        grad_w_out = dot("rf,rd->fd", attn, grad_low)
        grad_q, grad_kv = attend_back(
            queries, key_all, value_all, mask, heads, log_sums, grad_attn
        )
        part = grad_kv.reshape(4, block, 2 * half_width)
        sent = swap_core(jnp.stack([part[1], part[3]])).astype(f32)
        mine = part[0].astype(f32) + sent[0]
        chip = (part[2].astype(f32) + sent[1]).astype(bf16)
        grad_kv = (mine + swap_x(chip).astype(f32)).astype(bf16)
        grad_qkv = jnp.stack([grad_q, grad_kv[:, :half_width], grad_kv[:, half_width:]])
        grad_w_query = dot("rd,crf->cdf", low_in, grad_qkv)
        grad_b_query = jnp.sum(grad_qkv[0::2], axis=1, dtype=f32)
        partial = dot("crf,cdf->rd", grad_qkv, w_query)
        grad_in = partial + other_half(swap_tp(partial.astype(bf16))).astype(f32)
        grad_gain_in = jnp.sum(grad_in * normed_in, axis=0)
        grad_beta_in = jnp.sum(grad_in, axis=0)
        grad_state = grad_middle + norm_back(grad_in * gain_all[index, 0], normed_in, scale_in)

        vectors = [
            jnp.stack([grad_gain_in, grad_gain_mid]),
            jnp.stack([grad_beta_in, grad_bias_attn, grad_beta_mid, grad_bias_mlp]),
            grad_b_query.reshape(2, heads, half_width // heads),
            grad_b_first.reshape(b_fc1_all.shape[1:]),
        ]
        parts = [split(vector, vector.ndim - 1, shards) for vector in vectors]
        part_shapes = [part.shape[1:] for part in parts]
        attn_rows = jnp.concatenate(
            [
                jax.vmap(to_rows)(split(grad_w_query.astype(bf16), 1, shards)),
                jax.vmap(to_rows)(split(grad_w_out.astype(bf16), 1, shards)),
                jax.vmap(lambda *own: small_rows(own))(*parts).astype(bf16),
            ],
            axis=1,
        )
        attn_total = reduce_packed(attn_rows)

        def pieces(total, shapes):
            place, out = 0, []
            for shape in shapes:
                rows = math.prod(shape) // lanes
                out.append(from_rows(total[place : place + rows], shape).astype(f32))
                place += rows
            return out, total[place:].reshape(-1)

        (out_fc1, out_fc2), unused = pieces(mlp_total, [shape_fc1, shape_fc2])
        (out_qkv, out_proj), tail = pieces(attn_total, [shape_qkv, shape_proj])
        small_out, start = [], 0
        for shape in part_shapes:
            size = math.prod(shape)
            small_out.append(tail[start : start + size].reshape(shape).astype(f32))
            start += size
        results[index] = (
            out_qkv, small_out[2], out_proj, out_fc1, small_out[3], out_fc2, small_out[0], small_out[1]
        )
    stacked = tuple(
        jnp.stack([results[index][member] for index in range(depth)]) for member in range(8)
    )
    return (output, grad_state[:own_rows, None]) + stacked


def compiler_params():
    return pltpu.CompilerParams(vmem_limit_bytes=56 * 2**20)


def whole(array):
    zeros = (0,) * array.ndim
    return pl.BlockSpec(array.shape, lambda i: zeros)


def rows_at(array, rows, start, lead=None, first=0):
    lead = array.shape[0] if lead is None else lead
    return pl.BlockSpec((lead, rows, lanes), lambda i: (first, start // rows, 0))


def run(kernel, outs, place, operands, scratch=(), flops=2**20, after=()):
    arrays, specs = [], []
    count = 1 + len(operands)

    def inner(*refs):
        kernel(*refs[:count], *refs[count + len(after) :])

    for operand in operands:
        array, spec = operand if isinstance(operand, tuple) else (operand, whole(operand))
        arrays.append(array)
        specs.append(spec)
    out_shape = [jax.ShapeDtypeStruct(shape, kind) for shape, kind in outs]
    after = list(after)
    arrays += after
    specs += [pl.BlockSpec(memory_space=pl.ANY)] * len(after)
    call = pl.pallas_call(
        inner,
        grid=(1,),
        out_shape=out_shape,
        in_specs=[pl.BlockSpec(memory_space=pltpu.SMEM)] + specs,
        out_specs=[whole(shape) for shape in out_shape],
        scratch_shapes=list(scratch),
        compiler_params=compiler_params(),
        cost_estimate=pl.CostEstimate(flops=flops, bytes_accessed=1024, transcendentals=0),
    )
    return list(call(place, *arrays))


def mm(left, right):
    return lax.dot_general(left, right, (((1,), (0,)), ((), ())), preferred_element_type=f32)


def mm_nt(left, right):
    return lax.dot_general(left, right, (((1,), (1,)), ((), ())), preferred_element_type=f32)


def mm_tn(left, right):
    return lax.dot_general(left, right, (((0,), (0,)), ((), ())), preferred_element_type=f32)


def lane_join(parts):
    return jnp.concatenate(parts, axis=1)


def row_join(parts):
    return jnp.concatenate(parts, axis=0)


class Pieces:
    def __init__(self, refs, place):
        self.refs, self.place = refs, place

    def tile(self, k, p, start, rows):
        if len(self.refs) == 1:
            z, c = self.place[0], self.place[1]
            return self.refs[0][(z - k + 4) % 4, p ^ c, start : start + rows]
        if k == 0:
            return self.refs[0][p, start : start + rows]
        return self.refs[1 + p][k - 1, start : start + rows]


def first_block(pieces, p):
    return row_join(
        [lane_join([pieces.tile(k, p, j * 128, 128) for j in range(2)]) for k in range(4)]
    )


def second_block(pieces, p):
    return lane_join([pieces.tile(k, p, 0, 256) for k in range(4)])


def small_row(small_local, small_far, row):
    parts = [small_local[0, row : row + 1]] + [small_far[k, row : row + 1] for k in range(3)]
    return lane_join(parts).astype(f32)


def spread(small_local, small_far, row, place_z, half, later=None):
    def rows_from(row):
        return row_join(
            [small_local[0, row : row + 1]] + [small_far[k, row : row + 1] for k in range(3)]
        ).astype(f32)

    source = rows_from(row)
    if later is not None:
        source = jnp.where(later == 0, source, rows_from(row + 1))
    source = source.astype(bf16)
    take = lax.broadcasted_iota(jnp.int32, (128, 256), 0)
    lane = lax.broadcasted_iota(jnp.int32, (128, 256), 1)
    wanted = half * 64 + (lane // 64) * 16 + lane % 16
    table = (take == wanted).astype(f32).astype(bf16)
    rows = mm(source, table)
    chunk = lax.broadcasted_iota(jnp.int32, (4, 256), 0)
    lane = lax.broadcasted_iota(jnp.int32, (4, 256), 1)
    keep = (lane % 64) // 16 == (place_z - chunk + 4) % 4
    return jnp.sum(jnp.where(keep, rows, 0.0), axis=0, keepdims=True)


def pack_kernel(kinds):
    def kernel(place, *refs):
        c = place[1]
        out, send = refs[-2:]
        start = 0
        for ref, kind in zip(refs, kinds):
            for q in range(4):
                to = q ^ c
                if kind == "first":
                    for j in range(2):
                        column = (2 * q + j) * 128
                        out[to, start + j * 128 : start + (j + 1) * 128] = ref[0, :, column : column + 128]
                elif kind == "second":
                    out[to, start : start + 256] = ref[0, q * 256 : (q + 1) * 256]
                elif kind == "proj":
                    out[to, start : start + 64] = ref[0, q * 64 : (q + 1) * 64]
                elif kind == "qkv":
                    for tile in range(6):
                        row = start + tile * 32
                        column = (tile % 2) * 128
                        out[to, row : row + 32] = ref[0, tile // 2, q * 32 : (q + 1) * 32, column : column + 128]
                else:
                    out[to, start : start + 32] = ref[...]
            start += kind_rows[kind]
        send[...] = out[0]

    return kernel


def quarter_pack_kernel(kinds):
    def kernel(place, *refs):
        out = refs[-1]
        for q in range(4):

            @pl.when(place[1] == q)
            def write(q=q):
                start = 0
                for ref, kind in zip(refs, kinds):
                    if kind == "first":
                        for j in range(2):
                            column = (2 * q + j) * 128
                            out[start + j * 128 : start + (j + 1) * 128] = ref[0, :, column : column + 128]
                    elif kind == "second":
                        out[start : start + 256] = ref[0, q * 256 : (q + 1) * 256]
                    elif kind == "proj":
                        out[start : start + 64] = ref[0, q * 64 : (q + 1) * 64]
                    else:
                        for tile in range(6):
                            row = start + tile * 32
                            column = (tile % 2) * 128
                            out[row : row + 32] = ref[0, tile // 2, q * 32 : (q + 1) * 32, column : column + 128]
                    start += kind_rows[kind]

    return kernel


kind_rows = {"first": 256, "second": 256, "proj": 64, "qkv": 192, "small": 32}


def pack(place, kinds, arrays, index, after=(), whole_quarters=True):
    rows = sum(kind_rows[kind] for kind in kinds)
    operands = []
    for kind, array, at in zip(kinds, arrays, index):
        if kind == "small":
            operands.append(array)
        else:
            block = (1,) + array.shape[1:]
            at = (at,) + (0,) * (array.ndim - 1)
            operands.append((array, pl.BlockSpec(block, lambda i, at=at: at)))
    if not whole_quarters:
        return run(quarter_pack_kernel(kinds), [((rows, lanes), bf16)], place, operands, after=after)[0]
    return run(
        pack_kernel(kinds), [((4, rows, lanes), bf16), ((rows, lanes), bf16)], place, operands, after=after
    )


def gather(quarter):
    full = lax.all_gather(quarter, ("shard", "ctx"), axis=0)
    return full.reshape((4, 4) + quarter.shape)


def gathered_rows(array, rows, start):
    return [(array, pl.BlockSpec((4, 4, rows, lanes), lambda i: (0, 0, start // rows, 0)))]


def shift(values, step):
    return lax.ppermute(values, "shard", [(z, (z + step) % 4) for z in range(4)])


def far_chunks(send):
    return [shift(send, k) for k in (1, 2, 3)]


def stack_kernel(place, one, two, three, out):
    for k, ref in enumerate((one, two, three)):
        out[k] = ref[...]


def stack(place, got, after=()):
    return run(stack_kernel, [((3,) + got[0].shape, bf16)], place, got, after=after)[0]


def pieces_of(group, rows, start):
    return [(array, rows_at(array, rows, start)) for array in group]


def small_of(group):
    return [(group[0], rows_at(group[0], 32, 256, lead=1)), (group[1], rows_at(group[1], 32, 256))]


def query_kernel(index, first_layer):
    def kernel(place, *refs):
        c = place[1]
        if first_layer:
            own, peer, small_local, small_far = refs[:4]
            pieces = Pieces(refs[4:9], place)
            grad_out = refs[14]
            grad_out[...] = row_join([own[128:], peer[128:]]).astype(f32)
            state_out, low_out, q_out, kv_out, w_out = refs[9:14]
            state = row_join([own[:128], peer[:128]]).astype(f32)
        else:
            middle, mine, other, small_local, small_far = refs[:5]
            pieces = Pieces(refs[5:6], place)
            state_out, low_out, q_out, kv_out, w_out = refs[6:]
            received = row_join([other[128:], other[:128]])
            state = (
                middle[...]
                + mine[...].astype(f32)
                + received.astype(f32)
                + small_row(small_local, small_far, 4 + 4 * (index - 1) + 3)
            )
        for k in range(4):
            for p in range(4):
                for tile in range(6):
                    w_out[k, p ^ c, :, tile * 128 : (tile + 1) * 128] = pieces.tile(k, p, tile * 32, 32)
        state_out[...] = state
        normed, scale = normalize(state)
        low = (
            normed * small_row(small_local, small_far, 2 * index)
            + small_row(small_local, small_far, 4 + 4 * index)
        ).astype(bf16)
        low_out[...] = low
        w_all = w_out[...].reshape(512, 768)
        row = 12 + index
        bias_q = spread(small_local, small_far, row, place[0], 0)
        bias_v = spread(small_local, small_far, row, place[0], 1)
        kv_out[:, :256] = mm(low, w_all[:, 256:512]).astype(bf16)
        kv_out[:, 256:] = (mm(low, w_all[:, 512:]) + bias_v).astype(bf16)
        q_out[...] = (mm(low, w_all[:, :256]) + bias_q).astype(bf16)

    return kernel


def seen(place, j):
    c, t = place[1], place[2]
    if j:
        return None
    row = lax.broadcasted_iota(jnp.int32, (256, 256), 0) ^ (t * 128)
    key = lax.broadcasted_iota(jnp.int32, (256, 256), 1) ^ (t * 128)
    return key <= row


def masked_scores(query, chunks, own_mask, place):
    parts = []
    for j in range(4):
        scores = mm_nt(query, chunks[j]) * 0.125
        if j == 0:
            scores = jnp.where(own_mask, scores, masked_value)
        else:
            scores = jnp.where((place[1] ^ j) < place[1], scores, masked_value)
        parts.append(scores)
    return parts


def attend_kernel(count, place, *refs):
    c = place[1]
    q, chunks = refs[0], refs[1:5]
    pieces = Pieces(refs[5 : 5 + count], place)
    attn_out, lse_out, partial_out, w_out = refs[5 + count :]
    for k in range(4):
        for p in range(4):
            w_out[p ^ c, :, k * 128 : (k + 1) * 128] = pieces.tile(k, p, 0, 64)
    own_mask = seen(place, 0)
    results = []
    for head in range(4):
        low, high = head * 64, (head + 1) * 64
        parts = masked_scores(q[:, low:high], [chunk[:, low:high] for chunk in chunks], own_mask, place)
        scores = lane_join(parts)
        top = jnp.max(scores, axis=1, keepdims=True)
        exponent = jnp.exp(scores - top)
        total = jnp.sum(exponent, axis=1, keepdims=True)
        values = row_join([chunk[:, 256 + low : 256 + high] for chunk in chunks])
        results.append(mm(exponent.astype(bf16), values) / total)
        lse_out[:, head : head + 1] = top + jnp.log(total)
    attn = lane_join(results).astype(bf16)
    attn_out[...] = attn
    partial_out[...] = mm(attn, w_out[...].reshape(256, 512)).astype(bf16)


def mlp_kernel(index):
    def kernel(place, *refs):
        state, mine, other, small_local, small_far = refs[:5]
        first, second = Pieces(refs[5:6], place), Pieces(refs[6:7], place)
        middle_out, low_out, pre_out, partial_out = refs[7:]
        received = row_join([other[128:], other[:128]])
        middle = (
            state[...]
            + mine[...].astype(f32)
            + received.astype(f32)
            + small_row(small_local, small_far, 4 + 4 * index + 1)
        )
        middle_out[...] = middle
        normed, scale = normalize(middle)
        low = (
            normed * small_row(small_local, small_far, 2 * index + 1)
            + small_row(small_local, small_far, 4 + 4 * index + 2)
        ).astype(bf16)
        low_out[...] = low
        total = None
        for p in range(4):
            q = p ^ place[1]
            bias = spread(small_local, small_far, 14 + 2 * index, place[0], q % 2, q // 2)
            pre = mm(low, first_block(first, p)) + bias
            pre_out[:, p * 256 : (p + 1) * 256] = pre
            act = gelu_tanh(pre).astype(bf16)
            part = mm(act, second_block(second, p))
            total = part if total is None else total + part
        partial_out[...] = total.astype(bf16)

    return kernel


root = math.sqrt(2 / math.pi)


def mlp_back(grad, pre_ref, low_ref, first, second, place, outs):
    partial_out, bias_out, b_first_out, keep, *sends = outs
    grad_low = grad.astype(bf16)
    bias_out[...] = jnp.sum(grad, axis=0, keepdims=True)
    total = None
    for p in range(4):
        pre = pre_ref[:, p * 256 : (p + 1) * 256]
        square = pre * pre
        wave = jnp.tanh(root * pre * (1 + 0.044715 * square))
        half = 0.5 * (1 + wave)
        act = (pre * half).astype(bf16)
        slope = half + 0.5 * pre * (1 - wave * wave) * root * (1 + 3 * 0.044715 * square)
        w_second = second_block(second, p)
        grad_pre = mm_nt(grad_low, w_second) * slope
        grad_pre_low = grad_pre.astype(bf16)
        b_first_out[p ^ place[1]] = jnp.sum(grad_pre_low.astype(f32), axis=0, keepdims=True)
        part = mm_nt(grad_pre_low, first_block(first, p))
        total = part if total is None else total + part
        to = keep.at[p // 2] if p % 2 == 0 else sends[p // 2]
        grad_first = mm_tn(low_ref[...], grad_pre_low).astype(bf16)
        grad_second = mm_tn(act, grad_low).astype(bf16)
        for k in range(4):
            for j in range(2):
                to[k, j * 128 : (j + 1) * 128] = grad_first[
                    k * 128 : (k + 1) * 128, j * 128 : (j + 1) * 128
                ]
            to[k, 256:512] = grad_second[:, k * 128 : (k + 1) * 128]
    partial_out[...] = total.astype(bf16)


def norm_step(grad_out, gain, values):
    normed, scale = normalize(values)
    sums = row_join(
        [
            jnp.sum(grad_out * normed, axis=0, keepdims=True),
            jnp.sum(grad_out, axis=0, keepdims=True),
        ]
    )
    return norm_back(grad_out * gain, normed, scale), sums


def received_sum(mine, other):
    return mine[...].astype(f32) + row_join([other[128:], other[:128]]).astype(f32)


def top_kernel(place, *refs):
    grad, pre, low = refs[:3]
    first, second = Pieces(refs[3:4], place), Pieces(refs[4:5], place)
    mlp_back(grad[...], pre, low, first, second, place, refs[5:])


def lower_kernel(index):
    def kernel(place, *refs):
        grad_mid, mine, other, state, small_local, small_far, pre, low = refs[:8]
        first, second = Pieces(refs[8:9], place), Pieces(refs[9:10], place)
        grad_out, sums_out = refs[10:12]
        grad, sums = norm_step(
            received_sum(mine, other), small_row(small_local, small_far, 2 * (index + 1)), state[...]
        )
        sums_out[...] = sums
        grad = grad_mid[...] + grad
        grad_out[...] = grad
        mlp_back(grad, pre, low, first, second, place, refs[12:])

    return kernel


def attend_back_kernel(index):
    def kernel(place, *refs):
        mine, other, middle, grad_state, small_local, small_far = refs[:6]
        attn, w_out, q = refs[6:9]
        chunks, lse = refs[9:13], refs[13]
        grad_out, sums_out, gw_out, dq_out, keep, send = refs[14:]
        grad, sums = norm_step(
            received_sum(mine, other), small_row(small_local, small_far, 2 * index + 1), middle[...]
        )
        grad = grad_state[...] + grad
        grad_out[...] = grad
        sums_out[0:2] = sums
        sums_out[2:3] = jnp.sum(grad, axis=0, keepdims=True)
        grad_low = grad.astype(bf16)
        grad_attn = mm_nt(grad_low, w_out[...].reshape(256, 512)).astype(bf16)
        gw_out[...] = mm_tn(attn[...], grad_low).astype(bf16).reshape(4, 64, 512)
        own_mask = seen(place, 0)
        dq_all = []
        dk_all = [[] for j in range(4)]
        dv_all = [[] for j in range(4)]
        for head in range(4):
            low, high = head * 64, (head + 1) * 64
            query, grad_head = q[:, low:high], grad_attn[:, low:high]
            keys = [chunk[:, low:high] for chunk in chunks]
            row_dot = jnp.sum(
                grad_head.astype(f32) * attn[:, low:high].astype(f32), axis=1, keepdims=True
            )
            log_sum = lse[:, head : head + 1]
            parts = masked_scores(query, keys, own_mask, place)
            dq = None
            for j in range(4):
                probs = jnp.exp(parts[j] - log_sum)
                grad_probs = mm_nt(grad_head, chunks[j][:, 256 + low : 256 + high])
                grad_scores = (probs * (grad_probs - row_dot)).astype(bf16)
                part = mm(grad_scores, keys[j])
                dq = part if dq is None else dq + part
                dk_all[j].append(mm_tn(grad_scores, query) * 0.125)
                dv_all[j].append(mm_tn(probs.astype(bf16), grad_head))
            dq_all.append(dq * 0.125)
        dq_out[...] = lane_join(dq_all).astype(bf16)
        for j in range(4):
            to = keep if j % 2 == 0 else send
            to[j // 2, :, :256] = lane_join(dk_all[j]).astype(bf16)
            to[j // 2, :, 256:] = lane_join(dv_all[j]).astype(bf16)

    return kernel


def halve_kernel(place, keep, got, own_out, send_out):
    own_out[...] = (keep[0].astype(f32) + got[0].astype(f32)).astype(bf16)
    send_out[...] = (keep[1].astype(f32) + got[1].astype(f32)).astype(bf16)


def halve_groups_kernel(place, *refs):
    own_out, send_out = refs[-2:]
    start = 0
    for keep, one, two in zip(refs[:-2:3], refs[1:-2:3], refs[2:-2:3]):
        rows = keep.shape[2]
        for half, got, out in ((0, one, own_out), (1, two, send_out)):
            total = keep[half].astype(f32) + got[...].astype(f32)
            out[:, start : start + rows] = total.astype(bf16)
        start += rows


def quarter_in_order(place, own, got, out):
    for k in range(4):
        total = own[k].astype(f32) + got[k].astype(f32)
        out[(place[0] - k + 4) % 4] = total.astype(bf16)


def query_back_kernel(place, *refs):
    dq, dkv, got, low, w_ref, gw_ref = refs[:6]
    partial_out, b_out, keep, *sends, scratch = refs[6:]
    c = place[1]
    grad_kv = (dkv[...].astype(f32) + got[...].astype(f32)).astype(bf16)
    grad_qkv = lane_join([dq[...], grad_kv])
    partial_out[...] = mm_nt(grad_qkv, w_ref[...].reshape(512, 768)).astype(bf16)
    b_out[0:1] = jnp.sum(dq[...].astype(f32), axis=0, keepdims=True)
    b_out[1:2] = jnp.sum(grad_kv[:, 256:].astype(f32), axis=0, keepdims=True)
    scratch[...] = mm_tn(low[...], grad_qkv).astype(bf16).reshape(4, 4, 32, 768)
    for p in range(4):
        to = keep.at[p // 2] if p % 2 == 0 else sends[p // 2]
        for k in range(4):
            for tile in range(6):
                to[k, tile * 32 : (tile + 1) * 32] = scratch[
                    k, p ^ c, :, tile * 128 : (tile + 1) * 128
                ]
            to[k, 192:256] = gw_ref[p ^ c, :, k * 128 : (k + 1) * 128]


def last_quarter_kernel(place, own, got, sums, *outs):
    for k in range(4):
        outs[k][:256] = (own[k].astype(f32) + got[k].astype(f32)).astype(bf16)
        outs[k][256:] = sums[k].astype(bf16)


def last_total_kernel(place, own, one, two, three, out):
    total = own[...].astype(f32) + one[...].astype(f32)
    out[...] = (total + (two[...].astype(f32) + three[...].astype(f32))).astype(bf16)


def halve(place, groups, after=()):
    operands = []
    for keep, one, two in groups:
        operands += [keep, swap_core(one), swap_core(two)]
    rows = sum(group[0].shape[2] for group in groups)
    return run(halve_groups_kernel, [((4, rows, lanes), bf16)] * 2, place, operands, after=after)


def quarter(place, own, send, after=()):
    (both,) = run(quarter_in_order, [(own.shape, bf16)], place, [own, swap_x(send)], after=after)
    return both


def copy_kernel(place, source, out):
    out[...] = source[...]


def hand_on(place, array, after):
    return run(copy_kernel, [(array.shape, bf16)], place, [array], after=after)[0]


def collect(total):
    chip = swap_x(total)
    return [total, swap_core(total), chip, swap_core(chip)]


def fill(refs, scratch):
    for p in range(4):
        scratch[p] = refs[p][...].astype(f32)


def hidden_out_kernel(place, *refs):
    c = place[1]
    first_out, second_out, scratch = refs[-3:]
    fill(refs, scratch)
    for q in range(4):
        for j in range(2):
            column = (2 * q + j) * 128
            first_out[0, :, column : column + 128] = scratch[q ^ c, j * 128 : (j + 1) * 128]
        second_out[0, q * 256 : (q + 1) * 256] = scratch[q ^ c, 256:]


def heads_out_kernel(place, *refs):
    c = place[1]
    qkv_out, proj_out, scratch = refs[-3:]
    fill(refs, scratch)
    for q in range(4):
        for tile in range(6):
            column = (tile % 2) * 128
            qkv_out[0, tile // 2, q * 32 : (q + 1) * 32, column : column + 128] = scratch[
                q ^ c, tile * 32 : (tile + 1) * 32
            ]
        proj_out[0, q * 64 : (q + 1) * 64] = scratch[q ^ c, 192:]


def layer_out(kernel, rows, place, totals, layer, shapes, before, start, after):
    extra = list(before) + list(after)
    count = 1 + len(totals)

    def inner(*refs):
        kernel(*refs[:count], *refs[count + len(extra) :])

    def block(shape):
        at = (layer,) + (0,) * (len(shape) - 1)
        return pl.BlockSpec((1,) + tuple(shape[1:]), lambda i: at)

    return list(
        pl.pallas_call(
            inner,
            grid=(1,),
            out_shape=[jax.ShapeDtypeStruct(shape, f32) for shape in shapes],
            in_specs=[pl.BlockSpec(memory_space=pltpu.SMEM)]
            + [pl.BlockSpec((rows, lanes), lambda i: (start // rows, 0))] * 4
            + [pl.BlockSpec(memory_space=pl.ANY)] * len(extra),
            out_specs=[block(shape) for shape in shapes],
            scratch_shapes=[pltpu.VMEM((4, rows, lanes), f32)],
            input_output_aliases={count + i: i for i in range(len(before))},
            compiler_params=compiler_params(),
            cost_estimate=pl.CostEstimate(flops=2**20, bytes_accessed=1024, transcendentals=0),
        )(place, *totals, *extra)
    )


def hidden_out(place, totals, layer, shape_one, shape_two, before, start, after=()):
    shapes = (shape_one, shape_two)
    return layer_out(hidden_out_kernel, 512, place, totals, layer, shapes, before, start, after)


def heads_out(place, totals, layer, shape_one, shape_two, before, start, after=()):
    shapes = (shape_one, shape_two)
    return layer_out(heads_out_kernel, 256, place, totals, layer, shapes, before, start, after)


def last_kernel(place, *refs):
    grad_mid, mine, other, state, small_local, small_far = refs[:6]
    sums_in = refs[6]
    sums_mid, bias_mlp, b_query, b_first = refs[7:9], refs[9:11], refs[11:13], refs[13:15]
    grad_out, out = refs[15:]
    grad, sums = norm_step(received_sum(mine, other), small_row(small_local, small_far, 0), state[...])
    grad_out[...] = grad_mid[:128] + grad[:128]
    for layer in range(2):
        inner = sums if layer == 0 else sums_in[...]
        mid = sums_mid[layer]
        rows = [
            (2 * layer, inner[0:1]),
            (2 * layer + 1, mid[0:1]),
            (4 + 4 * layer, inner[1:2]),
            (5 + 4 * layer, mid[2:3]),
            (6 + 4 * layer, mid[1:2]),
            (7 + 4 * layer, bias_mlp[layer][...]),
        ]
        for k in range(4):
            for row, value in rows:
                out[k, row : row + 1] = value[:, k * 128 : (k + 1) * 128]
            for channel in range(2):
                for j in range(2):
                    row = 12 + 4 * layer + 2 * channel + j
                    out[k, row : row + 1] = b_query[layer][channel : channel + 1, j * 128 : (j + 1) * 128]
            for q in range(4):
                for j in range(2):
                    row = 20 + 8 * layer + 2 * q + j
                    out[k, row : row + 1] = b_first[layer][q, :, j * 128 : (j + 1) * 128]
    out[:, 36:] = jnp.zeros((4, 12, lanes), f32)


def turn(values, place_z, back):
    rows = values.shape[0]
    chunks = values.reshape(rows, 4, lanes)
    order = (place_z - jnp.arange(4)) % 4
    return jnp.concatenate(
        [lax.dynamic_slice_in_dim(values, order[k] * lanes, lanes, 1) for k in range(4)], axis=1
    )


def body_four(x_in, w_qkv, b_qv, w_proj, w_fc1, b_fc1, w_fc2, gains, biases, cotangent):
    z, c, t = lax.axis_index("shard"), lax.axis_index("ctx"), lax.axis_index("tp")
    place = jnp.stack([z, c, t]).astype(jnp.int32)
    flat = jnp.concatenate([array.reshape(-1) for array in (gains, biases, b_qv, b_fc1)])
    small = jnp.pad(flat, (0, 32 * lanes - flat.shape[0])).reshape(32, lanes)

    kinds = ("qkv", "proj", "first", "second", "first", "second")
    send = pack(
        place, kinds, (w_qkv, w_proj, w_fc1, w_fc2, w_fc1, w_fc2), (1, 1, 0, 0, 1, 1), whole_quarters=False
    )
    full = gather(send)
    local_a, send_a = pack(place, ("qkv", "proj", "small"), (w_qkv, w_proj, small), (0, 0, 0))
    pair_own = turn(jnp.concatenate([x_in[:, 0], cotangent[:, 0]]), z, False)
    pair_peer = swap_tp(pair_own)
    got_a = far_chunks(send_a)
    far_a = stack(place, got_a)
    chip_a = swap_x(far_a)
    group_a0 = [local_a, far_a, swap_core(far_a), chip_a, swap_core(chip_a)]
    small_parts = small_of(group_a0)
    parts = {
        "qkv": [pieces_of(group_a0, 192, 0), gathered_rows(full, 192, 0)],
        "proj": [pieces_of(group_a0, 64, 192), gathered_rows(full, 64, 192)],
        "first": [gathered_rows(full, 256, 256), gathered_rows(full, 256, 768)],
        "second": [gathered_rows(full, 256, 512), gathered_rows(full, 256, 1024)],
    }
    square, wide = (256, 512), (256, 256)
    saved = []
    for layer in range(2):
        source = [pair_own, pair_peer] if layer == 0 else [middle, partial, swap_tp(partial)]
        more = [(square, f32)] if layer == 0 else []
        state, low_in, q, kv, w_all, *passed = run(
            query_kernel(layer, layer == 0),
            [(square, f32), (square, bf16), (wide, bf16), (square, bf16), ((4, 4, 32, 768), bf16)] + more,
            place,
            source + small_parts + parts["qkv"][layer],
        )
        if layer == 0:
            g_all = passed[0]
        kv_chip = swap_x(kv)
        chunks = [kv, swap_core(kv), kv_chip, swap_core(kv_chip)]
        attn, lse, partial, w_out = run(
            functools.partial(attend_kernel, len(parts["proj"][layer])),
            [(wide, bf16), ((256, lanes), f32), (square, bf16), ((4, 64, 512), bf16)],
            place,
            [q] + chunks + parts["proj"][layer],
        )
        middle, low_mid, pre, partial = run(
            mlp_kernel(layer),
            [(square, f32), (square, bf16), ((256, 1024), f32), (square, bf16)],
            place,
            [state, partial, swap_tp(partial)] + small_parts + parts["first"][layer] + parts["second"][layer],
        )
        saved.append((state, low_in, q, chunks, w_all, attn, lse, w_out, middle, low_mid, pre))

    received = swap_tp(partial[128:]).astype(f32)
    output = None
    bias_last = jnp.concatenate([small_parts[0][0][0, 267:268], small_parts[1][0][:, 267]]).reshape(1, 512)
    output = middle[:128] + partial[:128].astype(f32) + received + bias_last.astype(f32)
    output = turn(output.astype(bf16), z, True)[:, None]

    hidden_outs = [
        (square, bf16),
        ((1, 512), f32),
        ((4, 1, 256), f32),
        ((2, 4, 512, lanes), bf16),
        ((4, 512, lanes), bf16),
        ((4, 512, lanes), bf16),
    ]
    sums_mid, bias_mlp, b_query, b_first = [0, 0], [0, 0], [0, 0], [0, 0]
    hidden = [None, None]
    for layer in (1, 0):
        state, low_in, q, chunks, w_all, attn, lse, w_out, middle, low_mid, pre = saved[layer]
        tail = [pre, low_mid] + parts["first"][layer] + parts["second"][layer]
        if layer == 1:
            grad_state = g_all
            partial, bias_mlp[1], b_first[1], *grads = run(
                top_kernel, hidden_outs, place, [grad_state] + tail
            )
        else:
            own, far = halve(place, [grads])
            grad_state, sums_in, partial, bias_mlp[0], b_first[0], *grads = run(
                lower_kernel(0),
                [(square, f32), ((2, 512), f32)] + hidden_outs,
                place,
                [grad_mid, partial, swap_tp(partial), saved[1][0]] + small_parts + tail,
                after=[own],
            )
            both = quarter(place, own, far, after=[partial])
            heads_sum = lax.psum_scatter(both, "shard", scatter_dimension=0)
        own, far = halve(place, [grads])
        behind = [own] if layer == 1 else [both, own]
        grad_mid, sums_mid[layer], gw_out, dq, keep, send = run(
            attend_back_kernel(layer),
            [
                (square, f32),
                ((3, 512), f32),
                ((4, 64, 512), bf16),
                (wide, bf16),
                ((2, 256, 512), bf16),
                ((2, 256, 512), bf16),
            ],
            place,
            [partial, swap_tp(partial), middle, grad_state] + small_parts + [attn, w_out, q] + chunks + [lse],
            after=behind,
        )
        both = quarter(place, own, far, after=[keep])
        hidden[layer] = lax.psum_scatter(both, "shard", scatter_dimension=0)
        behind = [both]
        dkv, chip = run(halve_kernel, [(square, bf16)] * 2, place, [keep, swap_core(send)], after=behind)
        partial, b_query[layer], *grads = run(
            query_back_kernel,
            [
                (square, bf16),
                ((2, 256), f32),
                ((2, 4, 256, lanes), bf16),
                ((4, 256, lanes), bf16),
                ((4, 256, lanes), bf16),
            ],
            place,
            [dq, dkv, swap_x(chip), low_in, w_all, gw_out],
            scratch=[pltpu.VMEM((4, 4, 32, 768), bf16)],
            after=[output] if layer == 1 else [],
        )
    own, far = halve(place, [grads])
    grad_x, sums = run(
        last_kernel,
        [((128, 512), f32), ((4, 48, lanes), f32)],
        place,
        [grad_mid, partial, swap_tp(partial), saved[0][0]]
        + small_parts
        + [sums_in]
        + sums_mid
        + bias_mlp
        + b_query
        + b_first,
        after=[own],
    )
    pieces = run(last_quarter_kernel, [((304, lanes), bf16)] * 4, place, [own, swap_x(far), sums])
    grad_x = turn(grad_x, z, True)[:, None]
    outs_heads = heads_out(
        place, collect(heads_sum), 1, w_qkv.shape, w_proj.shape, [], 0, after=pieces[:1]
    )
    outs_hidden = hidden_out(
        place, collect(hidden[1]), 1, w_fc1.shape, w_fc2.shape, [], 0, after=pieces[:1]
    )
    lower = collect(hand_on(place, hidden[0], outs_heads + outs_hidden))
    got = [shift(pieces[k], 4 - k) for k in (1, 2, 3)]
    (last,) = run(
        last_total_kernel,
        [((304, lanes), bf16)],
        place,
        [pieces[0]] + got,
        after=outs_heads + outs_hidden,
    )
    last_parts = collect(last)
    grad_fc1, grad_fc2 = hidden_out(
        place, lower, 0, w_fc1.shape, w_fc2.shape, outs_hidden, 0, after=[last]
    )
    total = sum(part[256:].astype(f32) for part in last_parts)
    grad_gains = total[:4].reshape(gains.shape)
    grad_biases = total[4:12].reshape(biases.shape)
    rest_q = total[12:20].reshape(2, 2, 4, 64)
    rest_f = total[20:36].reshape(2, 16, 64)
    grad_b_qv = lax.dynamic_slice_in_dim(rest_q, z * 16, 16, 3)
    grad_b_fc1 = lax.dynamic_slice_in_dim(rest_f, z * 16, 16, 2)

    grad_qkv, grad_proj = heads_out(place, last_parts, 0, w_qkv.shape, w_proj.shape, outs_heads, 0)
    return (
        output, grad_x, grad_qkv, grad_b_qv, grad_proj, grad_fc1, grad_b_fc1, grad_fc2, grad_gains, grad_biases
    )


def body(*args):
    x_in, w_qkv, b_qv, w_proj, w_fc1 = args[:5]
    expected = ((128, 1, 512), (2, 3, 128, 256), (2, 2, 4, 16), (2, 256, 128), (2, 128, 1024))
    sizes = (lax.axis_size("shard"), lax.axis_size("ctx"), lax.axis_size("tp"))
    shapes = tuple(array.shape for array in (x_in, w_qkv, b_qv, w_proj, w_fc1))
    if sizes == (4, 4, 2) and shapes == expected:
        return body_four(*args)
    return body_any(*args)


def solution(mesh):
    return jax.shard_map(
        body,
        mesh=mesh,
        in_specs=(
            P(("ctx", "tp"), "shard", None),
            P(None, None, "shard", "tp"),
            P(None, None, "tp", "shard"),
            P(None, "tp", "shard"),
            P(None, "shard", "tp"),
            P(None, "tp", "shard"),
            P(None, "tp", "shard"),
            P(None, None, "shard"),
            P(None, None, "shard"),
            P(("ctx", "tp"), "shard", None),
        ),
        out_specs=(
            P(("ctx", "tp"), "shard", None),
            P(("ctx", "tp"), "shard", None),
            P(None, None, "shard", "tp"),
            P(None, None, "tp", "shard"),
            P(None, "tp", "shard"),
            P(None, "shard", "tp"),
            P(None, "tp", "shard"),
            P(None, "tp", "shard"),
            P(None, None, "shard"),
            P(None, None, "shard"),
        ),
        check_vma=False,
    )
```

```python
import functools
import math

import jax
import jax.numpy as jnp
from jax import lax
from jax.experimental import pallas as pl
from jax.experimental.pallas import tpu as pltpu
from jax.sharding import PartitionSpec as P

epsilon = 1e-05
masked_value = -1e30
lanes = 128
f32 = jnp.float32
bf16 = jnp.bfloat16


def normalize(values):
    center = jnp.mean(values, axis=-1, keepdims=True)
    shifted = values - center
    scale_inv = lax.rsqrt(jnp.mean(shifted * shifted, axis=-1, keepdims=True) + epsilon)
    return (shifted * scale_inv, scale_inv)


def norm_back(grad_norm, normed, scale_inv):
    mean_grad = jnp.mean(grad_norm, axis=-1, keepdims=True)
    mean_prod = jnp.mean(grad_norm * normed, axis=-1, keepdims=True)
    return scale_inv * (grad_norm - mean_grad - normed * mean_prod)


def gelu_tanh(values):
    return jax.nn.gelu(values, approximate=True)


def dot(pattern, left, right):
    return jnp.einsum(pattern, left, right, preferred_element_type=f32)


def to_rows(array):
    rows, columns = array.shape[-2:]
    if columns % lanes or rows % 16:
        return array.reshape(-1, lanes)
    tiles = array.reshape(-1, rows, columns // lanes, lanes)
    return jnp.swapaxes(tiles, 1, 2).reshape(-1, lanes)


def from_rows(packed, shape):
    rows, columns = shape[-2:]
    lead = packed.shape[:-2]
    if columns % lanes or rows % 16:
        return packed.reshape(lead + tuple(shape))
    count = math.prod(shape[:-2])
    tiles = packed.reshape(lead + (count, columns // lanes, rows, lanes))
    return jnp.swapaxes(tiles, -3, -2).reshape(lead + tuple(shape))


def small_rows(arrays):
    flat = jnp.concatenate([array.reshape(-1) for array in arrays])
    size = -(-flat.shape[0] // (64 * lanes)) * 64 * lanes
    return jnp.pad(flat, (0, size - flat.shape[0])).reshape(-1, lanes)


def join(gathered, axis):
    moved = jnp.moveaxis(gathered, 0, axis)
    shape = moved.shape
    return moved.reshape(shape[:axis] + (shape[axis] * shape[axis + 1],) + shape[axis + 2 :])


def split(whole, axis, shards):
    shape = whole.shape
    parts = whole.reshape(shape[:axis] + (shards, shape[axis] // shards) + shape[axis + 1 :])
    return jnp.moveaxis(parts, axis, 0)


def swap_tp(values):
    return lax.ppermute(values, "tp", [(0, 1), (1, 0)])


def swap_core(values):
    return lax.ppermute(values, "ctx", [(0, 1), (1, 0), (2, 3), (3, 2)])


def swap_x(values):
    return lax.ppermute(values, "ctx", [(0, 2), (2, 0), (1, 3), (3, 1)])


def swap_both(values):
    return lax.ppermute(values, "ctx", [(0, 3), (3, 0), (1, 2), (2, 1)])


def other_half(values):
    half = values.shape[0] // 2
    return jnp.concatenate([values[half:], values[:half]])


def gather_packed(packed, shards):
    quarter = packed.shape[0] // 4
    own = lax.dynamic_slice_in_dim(packed, lax.axis_index("ctx") * quarter, quarter, 0)
    return lax.all_gather(own, ("shard", "ctx"), axis=0, tiled=True).reshape(
        shards, packed.shape[0], lanes
    )


def halves(values, bit):
    half = values.shape[1] // 2
    keep = lax.dynamic_slice_in_dim(values, bit * half, half, 1)
    send = lax.dynamic_slice_in_dim(values, (1 - bit) * half, half, 1)
    return keep, send


def paired(own, other, bit):
    return jnp.where(
        bit == 0, jnp.concatenate([own, other]), jnp.concatenate([other, own])
    )


def reduce_packed(packed):
    place = lax.axis_index("ctx")
    core, chip = place % 2, place // 2
    keep, send = halves(packed, core)
    half = (keep.astype(f32) + swap_core(send).astype(f32)).astype(bf16)
    keep, send = halves(half, chip)
    quarter = (keep.astype(f32) + swap_x(send).astype(f32)).astype(bf16)
    parts = lax.all_to_all(quarter, "shard", split_axis=0, concat_axis=0, tiled=True)
    total = jnp.sum(parts.astype(f32), axis=0).astype(bf16)
    both = paired(total, swap_x(total), chip)
    return paired(both, swap_core(both), core)


def positions(offsets, tp_place, chunk, block):
    half = block // 2
    return chunk * block + (offsets + tp_place * half) % block


def attention_mask(block):
    place, tp_place = lax.axis_index("ctx"), lax.axis_index("tp")
    offsets = jnp.arange(block, dtype=jnp.int32)
    rows = positions(offsets, tp_place, place, block)
    keys = jnp.concatenate([positions(offsets, tp_place, place ^ j, block) for j in range(4)])
    return keys[None, :] <= rows[:, None]


def head_split(values, heads):
    return values.reshape(values.shape[0], heads, values.shape[1] // heads)


def attend(queries, key_all, value_all, mask, heads):
    scale_factor = (queries.shape[1] // heads) ** (-0.5)
    scores = dot("qhe,khe->hqk", head_split(queries, heads), head_split(key_all, heads))
    scores = jnp.where(mask, scores * scale_factor, masked_value)
    row_top = jnp.max(scores, axis=-1, keepdims=True)
    exponent = jnp.exp(scores - row_top)
    totals = jnp.sum(exponent, axis=-1, keepdims=True)
    probs = (exponent / totals).astype(bf16)
    out = dot("hqk,khe->qhe", probs, head_split(value_all, heads))
    return out.reshape(queries.shape).astype(bf16), row_top + jnp.log(totals)


def attend_back(queries, key_all, value_all, mask, heads, log_sums, grad_out):
    scale_factor = (queries.shape[1] // heads) ** (-0.5)
    query_heads, key_heads = head_split(queries, heads), head_split(key_all, heads)
    grad_heads = head_split(grad_out, heads)
    scores = dot("qhe,khe->hqk", query_heads, key_heads)
    scores = jnp.where(mask, scores * scale_factor, masked_value)
    probs = jnp.exp(scores - log_sums)
    grad_probs = dot("qhe,khe->hqk", grad_heads, head_split(value_all, heads))
    row_dot = jnp.sum(probs * grad_probs, axis=-1, keepdims=True)
    grad_scores = (probs * (grad_probs - row_dot)).astype(bf16)
    grad_q = dot("hqk,khe->qhe", grad_scores, key_heads) * scale_factor
    grad_k = dot("hqk,qhe->khe", grad_scores, query_heads) * scale_factor
    grad_v = dot("hqk,qhe->khe", probs.astype(bf16), grad_heads)
    return (
        grad_q.reshape(queries.shape).astype(bf16),
        jnp.concatenate(
            [grad_k.reshape(key_all.shape), grad_v.reshape(key_all.shape)], axis=1
        ).astype(bf16),
    )


def body_any(x_in, w_qkv, b_qv, w_proj, w_fc1, b_fc1, w_fc2, gains, biases, cotangent):
    depth = w_qkv.shape[0]
    shards = lax.axis_size("shard")
    own_rows, width = x_in.shape[0], x_in.shape[2]
    block = 2 * own_rows
    heads = b_qv.shape[2]
    half_width = w_qkv.shape[3]
    hidden = w_fc1.shape[2]

    small_shapes = [gains.shape, biases.shape, b_qv.shape, b_fc1.shape]
    small = small_rows([gains, biases, b_qv, b_fc1])
    group_a0 = jnp.concatenate([small, to_rows(w_qkv[0])])
    group_b0 = jnp.concatenate([to_rows(w_proj[0]), to_rows(w_fc1[0]), to_rows(w_fc2[0])])
    rest = []
    for index in range(1, depth):
        rest += [to_rows(w_qkv[index]), to_rows(w_proj[index]), to_rows(w_fc1[index]), to_rows(w_fc2[index])]
    group_rest = jnp.concatenate(rest)

    gathered_a0 = gather_packed(group_a0, shards)
    gathered_b0 = gather_packed(group_b0, shards)
    gathered_rest = gather_packed(group_rest, shards)

    def cutter(gathered, start):
        place = [start]

        def take(shape, axis):
            rows = math.prod(shape) // lanes
            piece = from_rows(gathered[:, place[0] : place[0] + rows], shape)
            place[0] += rows
            return join(piece, axis)

        return take

    shape_qkv, shape_proj = w_qkv.shape[1:], w_proj.shape[1:]
    shape_fc1, shape_fc2 = w_fc1.shape[1:], w_fc2.shape[1:]
    take_a, take_b, take_r = cutter(gathered_a0, small.shape[0]), cutter(gathered_b0, 0), cutter(gathered_rest, 0)
    weights = []
    for index in range(depth):
        take_q, take_o = (take_a, take_b) if index == 0 else (take_r, take_r)
        weights.append(
            (take_q(shape_qkv, 1), take_o(shape_proj, 1), take_o(shape_fc1, 0), take_o(shape_fc2, 1))
        )
    flat = gathered_a0[:, : small.shape[0]].reshape(shards, -1)
    vectors, start = [], 0
    for shape in small_shapes:
        size = math.prod(shape)
        piece = flat[:, start : start + size].reshape((shards,) + shape)
        vectors.append(join(piece, len(shape) - 1).astype(f32))
        start += size
    gain_all, bias_all, b_qv_all, b_fc1_all = vectors

    mask = attention_mask(block)
    x_own = x_in[:, 0]
    state = jnp.concatenate([x_own, swap_tp(x_own)]).astype(f32)
    g_own = cotangent[:, 0]
    grad_state = jnp.concatenate([g_own, swap_tp(g_own)]).astype(f32)

    stored = []
    for index in range(depth):
        w_query, w_out, w_first, w_second = weights[index]
        normed_in, scale_in = normalize(state)
        low_in = (normed_in * gain_all[index, 0] + bias_all[index, 0]).astype(bf16)
        bias_q = b_qv_all[index, 0].reshape(half_width)
        bias_v = b_qv_all[index, 1].reshape(half_width)
        queries = (dot("rd,df->rf", low_in, w_query[0]) + bias_q).astype(bf16)
        keys = dot("rd,df->rf", low_in, w_query[1]).astype(bf16)
        values = (dot("rd,df->rf", low_in, w_query[2]) + bias_v).astype(bf16)
        kv_own = jnp.concatenate([keys, values], axis=1)
        kv_chip = swap_x(kv_own)
        kv_all = jnp.concatenate([kv_own, swap_core(kv_own), kv_chip, swap_core(kv_chip)])
        key_all, value_all = kv_all[:, :half_width], kv_all[:, half_width:]
        attn, log_sums = attend(queries, key_all, value_all, mask, heads)
        attn_other = other_half(swap_tp(attn))
        w_out_other = swap_tp(w_out)
        middle = (
            state
            + dot("rf,fd->rd", attn, w_out)
            + dot("rf,fd->rd", attn_other, w_out_other)
            + bias_all[index, 1]
        )
        normed_mid, scale_mid = normalize(middle)
        low_mid = (normed_mid * gain_all[index, 1] + bias_all[index, 2]).astype(bf16)
        pre_act = dot("rd,df->rf", low_mid, w_first) + b_fc1_all[index].reshape(hidden)
        act = gelu_tanh(pre_act).astype(bf16)
        partial = dot("rf,fd->rd", act, w_second)
        if index == depth - 1:
            received = swap_tp(partial[own_rows:].astype(bf16)).astype(f32)
            output = middle[:own_rows] + partial[:own_rows] + received + bias_all[index, 3]
        else:
            received = other_half(swap_tp(partial.astype(bf16))).astype(f32)
            state = middle + partial + received + bias_all[index, 3]
        stored.append(
            (normed_in, scale_in, low_in, queries, key_all, value_all, log_sums, attn,
             normed_mid, scale_mid, low_mid, pre_act, act)
        )
    output = output.astype(bf16)[:, None]

    results = [None] * depth
    for index in reversed(range(depth)):
        w_query, w_out, w_first, w_second = weights[index]
        (normed_in, scale_in, low_in, queries, key_all, value_all, log_sums, attn,
         normed_mid, scale_mid, low_mid, pre_act, act) = stored[index]
        grad_bias_mlp = jnp.sum(grad_state, axis=0)
        grad_low = grad_state.astype(bf16)
        grad_hidden = dot("rd,fd->rf", grad_low, w_second)
        unused, gelu_pull = jax.vjp(gelu_tanh, pre_act)
        grad_pre = gelu_pull(grad_hidden)[0].astype(bf16)
        grad_w_second = dot("rf,rd->fd", act, grad_low)
        grad_w_first = dot("rd,rf->df", low_mid, grad_pre)
        grad_b_first = jnp.sum(grad_pre, axis=0, dtype=f32)
        partial = dot("rf,df->rd", grad_pre, w_first)
        mlp_rows = jnp.concatenate(
            [
                jax.vmap(to_rows)(split(grad_w_first.astype(bf16), 0, shards)),
                jax.vmap(to_rows)(split(grad_w_second.astype(bf16), 1, shards)),
            ],
            axis=1,
        )
        mlp_total = reduce_packed(mlp_rows)
        grad_mid = partial + other_half(swap_tp(partial.astype(bf16))).astype(f32)
        grad_gain_mid = jnp.sum(grad_mid * normed_mid, axis=0)
        grad_beta_mid = jnp.sum(grad_mid, axis=0)
        grad_middle = grad_state + norm_back(grad_mid * gain_all[index, 1], normed_mid, scale_mid)
        grad_bias_attn = jnp.sum(grad_middle, axis=0)
        grad_low = grad_middle.astype(bf16)
        grad_attn = dot("rd,fd->rf", grad_low, w_out).astype(bf16)
        grad_w_out = dot("rf,rd->fd", attn, grad_low)
        grad_q, grad_kv = attend_back(
            queries, key_all, value_all, mask, heads, log_sums, grad_attn
        )
        part = grad_kv.reshape(4, block, 2 * half_width)
        sent = swap_core(jnp.stack([part[1], part[3]])).astype(f32)
        mine = part[0].astype(f32) + sent[0]
        chip = (part[2].astype(f32) + sent[1]).astype(bf16)
        grad_kv = (mine + swap_x(chip).astype(f32)).astype(bf16)
        grad_qkv = jnp.stack([grad_q, grad_kv[:, :half_width], grad_kv[:, half_width:]])
        grad_w_query = dot("rd,crf->cdf", low_in, grad_qkv)
        grad_b_query = jnp.sum(grad_qkv[0::2], axis=1, dtype=f32)
        partial = dot("crf,cdf->rd", grad_qkv, w_query)
        grad_in = partial + other_half(swap_tp(partial.astype(bf16))).astype(f32)
        grad_gain_in = jnp.sum(grad_in * normed_in, axis=0)
        grad_beta_in = jnp.sum(grad_in, axis=0)
        grad_state = grad_middle + norm_back(grad_in * gain_all[index, 0], normed_in, scale_in)

        vectors = [
            jnp.stack([grad_gain_in, grad_gain_mid]),
            jnp.stack([grad_beta_in, grad_bias_attn, grad_beta_mid, grad_bias_mlp]),
            grad_b_query.reshape(2, heads, half_width // heads),
            grad_b_first.reshape(b_fc1_all.shape[1:]),
        ]
        parts = [split(vector, vector.ndim - 1, shards) for vector in vectors]
        part_shapes = [part.shape[1:] for part in parts]
        attn_rows = jnp.concatenate(
            [
                jax.vmap(to_rows)(split(grad_w_query.astype(bf16), 1, shards)),
                jax.vmap(to_rows)(split(grad_w_out.astype(bf16), 1, shards)),
                jax.vmap(lambda *own: small_rows(own))(*parts).astype(bf16),
            ],
            axis=1,
        )
        attn_total = reduce_packed(attn_rows)

        def pieces(total, shapes):
            place, out = 0, []
            for shape in shapes:
                rows = math.prod(shape) // lanes
                out.append(from_rows(total[place : place + rows], shape).astype(f32))
                place += rows
            return out, total[place:].reshape(-1)

        (out_fc1, out_fc2), unused = pieces(mlp_total, [shape_fc1, shape_fc2])
        (out_qkv, out_proj), tail = pieces(attn_total, [shape_qkv, shape_proj])
        small_out, start = [], 0
        for shape in part_shapes:
            size = math.prod(shape)
            small_out.append(tail[start : start + size].reshape(shape).astype(f32))
            start += size
        results[index] = (
            out_qkv, small_out[2], out_proj, out_fc1, small_out[3], out_fc2, small_out[0], small_out[1]
        )
    stacked = tuple(
        jnp.stack([results[index][member] for index in range(depth)]) for member in range(8)
    )
    return (output, grad_state[:own_rows, None]) + stacked


def compiler_params():
    return pltpu.CompilerParams(vmem_limit_bytes=56 * 2**20)


def whole(array):
    zeros = (0,) * array.ndim
    return pl.BlockSpec(array.shape, lambda i: zeros)


def rows_at(array, rows, start, lead=None, first=0):
    lead = array.shape[0] if lead is None else lead
    return pl.BlockSpec((lead, rows, lanes), lambda i: (first, start // rows, 0))


def run(kernel, outs, place, operands, scratch=(), flops=2**20, after=()):
    arrays, specs = [], []
    count = 1 + len(operands)

    def inner(*refs):
        kernel(*refs[:count], *refs[count + len(after) :])

    for operand in operands:
        array, spec = operand if isinstance(operand, tuple) else (operand, whole(operand))
        arrays.append(array)
        specs.append(spec)
    out_shape = [jax.ShapeDtypeStruct(shape, kind) for shape, kind in outs]
    after = list(after)
    arrays += after
    specs += [pl.BlockSpec(memory_space=pl.ANY)] * len(after)
    call = pl.pallas_call(
        inner,
        grid=(1,),
        out_shape=out_shape,
        in_specs=[pl.BlockSpec(memory_space=pltpu.SMEM)] + specs,
        out_specs=[whole(shape) for shape in out_shape],
        scratch_shapes=list(scratch),
        compiler_params=compiler_params(),
        cost_estimate=pl.CostEstimate(flops=flops, bytes_accessed=1024, transcendentals=0),
    )
    return list(call(place, *arrays))


def mm(left, right):
    return lax.dot_general(left, right, (((1,), (0,)), ((), ())), preferred_element_type=f32)


def mm_nt(left, right):
    return lax.dot_general(left, right, (((1,), (1,)), ((), ())), preferred_element_type=f32)


def mm_tn(left, right):
    return lax.dot_general(left, right, (((0,), (0,)), ((), ())), preferred_element_type=f32)


def lane_join(parts):
    return jnp.concatenate(parts, axis=1)


def row_join(parts):
    return jnp.concatenate(parts, axis=0)


class Pieces:
    def __init__(self, refs, place):
        self.refs, self.place = refs, place

    def tile(self, k, p, start, rows):
        if len(self.refs) == 1:
            z, c = self.place[0], self.place[1]
            return self.refs[0][(z - k + 4) % 4, p ^ c, start : start + rows]
        if k == 0:
            return self.refs[0][p, start : start + rows]
        return self.refs[1 + p][k - 1, start : start + rows]


def first_block(pieces, p):
    return row_join(
        [lane_join([pieces.tile(k, p, j * 128, 128) for j in range(2)]) for k in range(4)]
    )


def second_block(pieces, p):
    return lane_join([pieces.tile(k, p, 0, 256) for k in range(4)])


def small_row(small_local, small_far, row):
    parts = [small_local[0, row : row + 1]] + [small_far[k, row : row + 1] for k in range(3)]
    return lane_join(parts).astype(f32)


def spread(small_local, small_far, row, place_z, half, later=None):
    def rows_from(row):
        return row_join(
            [small_local[0, row : row + 1]] + [small_far[k, row : row + 1] for k in range(3)]
        ).astype(f32)

    source = rows_from(row)
    if later is not None:
        source = jnp.where(later == 0, source, rows_from(row + 1))
    source = source.astype(bf16)
    take = lax.broadcasted_iota(jnp.int32, (128, 256), 0)
    lane = lax.broadcasted_iota(jnp.int32, (128, 256), 1)
    wanted = half * 64 + (lane // 64) * 16 + lane % 16
    table = (take == wanted).astype(f32).astype(bf16)
    rows = mm(source, table)
    chunk = lax.broadcasted_iota(jnp.int32, (4, 256), 0)
    lane = lax.broadcasted_iota(jnp.int32, (4, 256), 1)
    keep = (lane % 64) // 16 == (place_z - chunk + 4) % 4
    return jnp.sum(jnp.where(keep, rows, 0.0), axis=0, keepdims=True)


def pack_kernel(kinds):
    def kernel(place, *refs):
        c = place[1]
        out, send = refs[-2:]
        start = 0
        for ref, kind in zip(refs, kinds):
            for q in range(4):
                to = q ^ c
                if kind == "first":
                    for j in range(2):
                        column = (2 * q + j) * 128
                        out[to, start + j * 128 : start + (j + 1) * 128] = ref[0, :, column : column + 128]
                elif kind == "second":
                    out[to, start : start + 256] = ref[0, q * 256 : (q + 1) * 256]
                elif kind == "proj":
                    out[to, start : start + 64] = ref[0, q * 64 : (q + 1) * 64]
                elif kind == "qkv":
                    for tile in range(6):
                        row = start + tile * 32
                        column = (tile % 2) * 128
                        out[to, row : row + 32] = ref[0, tile // 2, q * 32 : (q + 1) * 32, column : column + 128]
                else:
                    out[to, start : start + 32] = ref[...]
            start += kind_rows[kind]
        send[...] = out[0]

    return kernel


def quarter_pack_kernel(kinds):
    def kernel(place, *refs):
        out = refs[-1]
        for q in range(4):

            @pl.when(place[1] == q)
            def write(q=q):
                start = 0
                for ref, kind in zip(refs, kinds):
                    if kind == "first":
                        for j in range(2):
                            column = (2 * q + j) * 128
                            out[start + j * 128 : start + (j + 1) * 128] = ref[0, :, column : column + 128]
                    elif kind == "second":
                        out[start : start + 256] = ref[0, q * 256 : (q + 1) * 256]
                    elif kind == "proj":
                        out[start : start + 64] = ref[0, q * 64 : (q + 1) * 64]
                    else:
                        for tile in range(6):
                            row = start + tile * 32
                            column = (tile % 2) * 128
                            out[row : row + 32] = ref[0, tile // 2, q * 32 : (q + 1) * 32, column : column + 128]
                    start += kind_rows[kind]

    return kernel


kind_rows = {"first": 256, "second": 256, "proj": 64, "qkv": 192, "small": 32}


def pack(place, kinds, arrays, index, after=(), whole_quarters=True):
    rows = sum(kind_rows[kind] for kind in kinds)
    operands = []
    for kind, array, at in zip(kinds, arrays, index):
        if kind == "small":
            operands.append(array)
        else:
            block = (1,) + array.shape[1:]
            at = (at,) + (0,) * (array.ndim - 1)
            operands.append((array, pl.BlockSpec(block, lambda i, at=at: at)))
    if not whole_quarters:
        return run(quarter_pack_kernel(kinds), [((rows, lanes), bf16)], place, operands, after=after)[0]
    return run(
        pack_kernel(kinds), [((4, rows, lanes), bf16), ((rows, lanes), bf16)], place, operands, after=after
    )


def gather(quarter):
    full = lax.all_gather(quarter, ("shard", "ctx"), axis=0)
    return full.reshape((4, 4) + quarter.shape)


def gathered_rows(array, rows, start):
    return [(array, pl.BlockSpec((4, 4, rows, lanes), lambda i: (0, 0, start // rows, 0)))]


def shift(values, step):
    return lax.ppermute(values, "shard", [(z, (z + step) % 4) for z in range(4)])


def far_chunks(send):
    return [shift(send, k) for k in (1, 2, 3)]


def stack_kernel(place, one, two, three, out):
    for k, ref in enumerate((one, two, three)):
        out[k] = ref[...]


def stack(place, got, after=()):
    return run(stack_kernel, [((3,) + got[0].shape, bf16)], place, got, after=after)[0]


def pieces_of(group, rows, start):
    return [(array, rows_at(array, rows, start)) for array in group]


def small_of(group):
    return [(group[0], rows_at(group[0], 32, 256, lead=1)), (group[1], rows_at(group[1], 32, 256))]


def query_kernel(index, first_layer):
    def kernel(place, *refs):
        c = place[1]
        if first_layer:
            own, peer, small_local, small_far = refs[:4]
            pieces = Pieces(refs[4:9], place)
            grad_out = refs[14]
            grad_out[...] = row_join([own[128:], peer[128:]]).astype(f32)
            state_out, low_out, q_out, kv_out, w_out = refs[9:14]
            state = row_join([own[:128], peer[:128]]).astype(f32)
        else:
            middle, mine, other, small_local, small_far = refs[:5]
            pieces = Pieces(refs[5:6], place)
            state_out, low_out, q_out, kv_out, w_out = refs[6:]
            received = row_join([other[128:], other[:128]])
            state = (
                middle[...]
                + mine[...].astype(f32)
                + received.astype(f32)
                + small_row(small_local, small_far, 4 + 4 * (index - 1) + 3)
            )
        for k in range(4):
            for p in range(4):
                for tile in range(6):
                    w_out[k, p ^ c, :, tile * 128 : (tile + 1) * 128] = pieces.tile(k, p, tile * 32, 32)
        state_out[...] = state
        normed, scale = normalize(state)
        low = (
            normed * small_row(small_local, small_far, 2 * index)
            + small_row(small_local, small_far, 4 + 4 * index)
        ).astype(bf16)
        low_out[...] = low
        w_all = w_out[...].reshape(512, 768)
        row = 12 + index
        bias_q = spread(small_local, small_far, row, place[0], 0)
        bias_v = spread(small_local, small_far, row, place[0], 1)
        kv_out[:, :256] = mm(low, w_all[:, 256:512]).astype(bf16)
        kv_out[:, 256:] = (mm(low, w_all[:, 512:]) + bias_v).astype(bf16)
        q_out[...] = (mm(low, w_all[:, :256]) + bias_q).astype(bf16)

    return kernel


def seen(place, j):
    c, t = place[1], place[2]
    if j:
        return None
    row = lax.broadcasted_iota(jnp.int32, (256, 256), 0) ^ (t * 128)
    key = lax.broadcasted_iota(jnp.int32, (256, 256), 1) ^ (t * 128)
    return key <= row


def masked_scores(query, chunks, own_mask, place):
    parts = []
    for j in range(4):
        scores = mm_nt(query, chunks[j]) * 0.125
        if j == 0:
            scores = jnp.where(own_mask, scores, masked_value)
        else:
            scores = jnp.where((place[1] ^ j) < place[1], scores, masked_value)
        parts.append(scores)
    return parts


def attend_kernel(count, place, *refs):
    c = place[1]
    q, chunks = refs[0], refs[1:5]
    pieces = Pieces(refs[5 : 5 + count], place)
    attn_out, lse_out, partial_out, w_out = refs[5 + count :]
    for k in range(4):
        for p in range(4):
            w_out[p ^ c, :, k * 128 : (k + 1) * 128] = pieces.tile(k, p, 0, 64)
    own_mask = seen(place, 0)
    results = []
    for head in range(4):
        low, high = head * 64, (head + 1) * 64
        parts = masked_scores(q[:, low:high], [chunk[:, low:high] for chunk in chunks], own_mask, place)
        scores = lane_join(parts)
        top = jnp.max(scores, axis=1, keepdims=True)
        exponent = jnp.exp(scores - top)
        total = jnp.sum(exponent, axis=1, keepdims=True)
        values = row_join([chunk[:, 256 + low : 256 + high] for chunk in chunks])
        results.append(mm(exponent.astype(bf16), values) / total)
        lse_out[:, head : head + 1] = top + jnp.log(total)
    attn = lane_join(results).astype(bf16)
    attn_out[...] = attn
    partial_out[...] = mm(attn, w_out[...].reshape(256, 512)).astype(bf16)


def mlp_kernel(index):
    def kernel(place, *refs):
        state, mine, other, small_local, small_far = refs[:5]
        first, second = Pieces(refs[5:6], place), Pieces(refs[6:7], place)
        middle_out, low_out, pre_out, partial_out = refs[7:]
        received = row_join([other[128:], other[:128]])
        middle = (
            state[...]
            + mine[...].astype(f32)
            + received.astype(f32)
            + small_row(small_local, small_far, 4 + 4 * index + 1)
        )
        middle_out[...] = middle
        normed, scale = normalize(middle)
        low = (
            normed * small_row(small_local, small_far, 2 * index + 1)
            + small_row(small_local, small_far, 4 + 4 * index + 2)
        ).astype(bf16)
        low_out[...] = low
        total = None
        for p in range(4):
            q = p ^ place[1]
            bias = spread(small_local, small_far, 14 + 2 * index, place[0], q % 2, q // 2)
            pre = mm(low, first_block(first, p)) + bias
            pre_out[:, p * 256 : (p + 1) * 256] = pre
            act = gelu_tanh(pre).astype(bf16)
            part = mm(act, second_block(second, p))
            total = part if total is None else total + part
        partial_out[...] = total.astype(bf16)

    return kernel


root = math.sqrt(2 / math.pi)


def mlp_back(grad, pre_ref, low_ref, first, second, place, outs):
    partial_out, bias_out, b_first_out, keep, *sends = outs
    grad_low = grad.astype(bf16)
    bias_out[...] = jnp.sum(grad, axis=0, keepdims=True)
    total = None
    for p in range(4):
        pre = pre_ref[:, p * 256 : (p + 1) * 256]
        square = pre * pre
        wave = jnp.tanh(root * pre * (1 + 0.044715 * square))
        half = 0.5 * (1 + wave)
        act = (pre * half).astype(bf16)
        slope = half + 0.5 * pre * (1 - wave * wave) * root * (1 + 3 * 0.044715 * square)
        w_second = second_block(second, p)
        grad_pre = mm_nt(grad_low, w_second) * slope
        grad_pre_low = grad_pre.astype(bf16)
        b_first_out[p ^ place[1]] = jnp.sum(grad_pre_low.astype(f32), axis=0, keepdims=True)
        part = mm_nt(grad_pre_low, first_block(first, p))
        total = part if total is None else total + part
        to = keep.at[p // 2] if p % 2 == 0 else sends[p // 2]
        grad_first = mm_tn(low_ref[...], grad_pre_low).astype(bf16)
        grad_second = mm_tn(act, grad_low).astype(bf16)
        for k in range(4):
            for j in range(2):
                to[k, j * 128 : (j + 1) * 128] = grad_first[
                    k * 128 : (k + 1) * 128, j * 128 : (j + 1) * 128
                ]
            to[k, 256:512] = grad_second[:, k * 128 : (k + 1) * 128]
    partial_out[...] = total.astype(bf16)


def norm_step(grad_out, gain, values):
    normed, scale = normalize(values)
    sums = row_join(
        [
            jnp.sum(grad_out * normed, axis=0, keepdims=True),
            jnp.sum(grad_out, axis=0, keepdims=True),
        ]
    )
    return norm_back(grad_out * gain, normed, scale), sums


def received_sum(mine, other):
    return mine[...].astype(f32) + row_join([other[128:], other[:128]]).astype(f32)


def top_kernel(place, *refs):
    grad, pre, low = refs[:3]
    first, second = Pieces(refs[3:4], place), Pieces(refs[4:5], place)
    mlp_back(grad[...], pre, low, first, second, place, refs[5:])


def lower_kernel(index):
    def kernel(place, *refs):
        grad_mid, mine, other, state, small_local, small_far, pre, low = refs[:8]
        first, second = Pieces(refs[8:9], place), Pieces(refs[9:10], place)
        grad_out, sums_out = refs[10:12]
        grad, sums = norm_step(
            received_sum(mine, other), small_row(small_local, small_far, 2 * (index + 1)), state[...]
        )
        sums_out[...] = sums
        grad = grad_mid[...] + grad
        grad_out[...] = grad
        mlp_back(grad, pre, low, first, second, place, refs[12:])

    return kernel


def attend_back_kernel(index):
    def kernel(place, *refs):
        mine, other, middle, grad_state, small_local, small_far = refs[:6]
        attn, w_out, q = refs[6:9]
        chunks, lse = refs[9:13], refs[13]
        grad_out, sums_out, gw_out, dq_out, keep, send = refs[14:]
        grad, sums = norm_step(
            received_sum(mine, other), small_row(small_local, small_far, 2 * index + 1), middle[...]
        )
        grad = grad_state[...] + grad
        grad_out[...] = grad
        sums_out[0:2] = sums
        sums_out[2:3] = jnp.sum(grad, axis=0, keepdims=True)
        grad_low = grad.astype(bf16)
        grad_attn = mm_nt(grad_low, w_out[...].reshape(256, 512)).astype(bf16)
        gw_out[...] = mm_tn(attn[...], grad_low).astype(bf16).reshape(4, 64, 512)
        own_mask = seen(place, 0)
        dq_all = []
        dk_all = [[] for j in range(4)]
        dv_all = [[] for j in range(4)]
        for head in range(4):
            low, high = head * 64, (head + 1) * 64
            query, grad_head = q[:, low:high], grad_attn[:, low:high]
            keys = [chunk[:, low:high] for chunk in chunks]
            row_dot = jnp.sum(
                grad_head.astype(f32) * attn[:, low:high].astype(f32), axis=1, keepdims=True
            )
            log_sum = lse[:, head : head + 1]
            parts = masked_scores(query, keys, own_mask, place)
            dq = None
            for j in range(4):
                probs = jnp.exp(parts[j] - log_sum)
                grad_probs = mm_nt(grad_head, chunks[j][:, 256 + low : 256 + high])
                grad_scores = (probs * (grad_probs - row_dot)).astype(bf16)
                part = mm(grad_scores, keys[j])
                dq = part if dq is None else dq + part
                dk_all[j].append(mm_tn(grad_scores, query) * 0.125)
                dv_all[j].append(mm_tn(probs.astype(bf16), grad_head))
            dq_all.append(dq * 0.125)
        dq_out[...] = lane_join(dq_all).astype(bf16)
        for j in range(4):
            to = keep if j % 2 == 0 else send
            to[j // 2, :, :256] = lane_join(dk_all[j]).astype(bf16)
            to[j // 2, :, 256:] = lane_join(dv_all[j]).astype(bf16)

    return kernel


def halve_kernel(place, keep, got, own_out, send_out):
    own_out[...] = (keep[0].astype(f32) + got[0].astype(f32)).astype(bf16)
    send_out[...] = (keep[1].astype(f32) + got[1].astype(f32)).astype(bf16)


def halve_groups_kernel(place, *refs):
    own_out, send_out = refs[-2:]
    start = 0
    for keep, one, two in zip(refs[:-2:3], refs[1:-2:3], refs[2:-2:3]):
        rows = keep.shape[2]
        for half, got, out in ((0, one, own_out), (1, two, send_out)):
            total = keep[half].astype(f32) + got[...].astype(f32)
            out[:, start : start + rows] = total.astype(bf16)
        start += rows


def quarter_in_order(place, own, got, out):
    for k in range(4):
        total = own[k].astype(f32) + got[k].astype(f32)
        out[(place[0] - k + 4) % 4] = total.astype(bf16)


def query_back_kernel(place, *refs):
    dq, dkv, got, low, w_ref, gw_ref = refs[:6]
    partial_out, b_out, keep, *sends, scratch = refs[6:]
    c = place[1]
    grad_kv = (dkv[...].astype(f32) + got[...].astype(f32)).astype(bf16)
    grad_qkv = lane_join([dq[...], grad_kv])
    partial_out[...] = mm_nt(grad_qkv, w_ref[...].reshape(512, 768)).astype(bf16)
    b_out[0:1] = jnp.sum(dq[...].astype(f32), axis=0, keepdims=True)
    b_out[1:2] = jnp.sum(grad_kv[:, 256:].astype(f32), axis=0, keepdims=True)
    scratch[...] = mm_tn(low[...], grad_qkv).astype(bf16).reshape(4, 4, 32, 768)
    for p in range(4):
        to = keep.at[p // 2] if p % 2 == 0 else sends[p // 2]
        for k in range(4):
            for tile in range(6):
                to[k, tile * 32 : (tile + 1) * 32] = scratch[
                    k, p ^ c, :, tile * 128 : (tile + 1) * 128
                ]
            to[k, 192:256] = gw_ref[p ^ c, :, k * 128 : (k + 1) * 128]


def last_quarter_kernel(place, own, got, sums, *outs):
    for k in range(4):
        outs[k][:256] = (own[k].astype(f32) + got[k].astype(f32)).astype(bf16)
        outs[k][256:] = sums[k].astype(bf16)


def last_total_kernel(place, own, one, two, three, out):
    total = own[...].astype(f32) + one[...].astype(f32)
    out[...] = (total + (two[...].astype(f32) + three[...].astype(f32))).astype(bf16)


def halve(place, groups, after=()):
    operands = []
    for keep, one, two in groups:
        operands += [keep, swap_core(one), swap_core(two)]
    rows = sum(group[0].shape[2] for group in groups)
    return run(halve_groups_kernel, [((4, rows, lanes), bf16)] * 2, place, operands, after=after)


def quarter(place, own, send, after=()):
    (both,) = run(quarter_in_order, [(own.shape, bf16)], place, [own, swap_x(send)], after=after)
    return both


def join_kernel(place, one, two, three, out):
    out[:512], out[512:1024], out[1024:] = one[...], two[...], three[...]


def collect(total):
    chip = swap_x(total)
    return [total, swap_core(total), chip, swap_core(chip)]


def fill(refs, scratch):
    for p in range(4):
        scratch[p] = refs[p][...].astype(f32)


def hidden_out_kernel(place, *refs):
    c = place[1]
    first_out, second_out, scratch = refs[-3:]
    fill(refs, scratch)
    for q in range(4):
        for j in range(2):
            column = (2 * q + j) * 128
            first_out[0, :, column : column + 128] = scratch[q ^ c, j * 128 : (j + 1) * 128]
        second_out[0, q * 256 : (q + 1) * 256] = scratch[q ^ c, 256:]


def heads_out_kernel(place, *refs):
    c = place[1]
    qkv_out, proj_out, scratch = refs[-3:]
    fill(refs, scratch)
    for q in range(4):
        for tile in range(6):
            column = (tile % 2) * 128
            qkv_out[0, tile // 2, q * 32 : (q + 1) * 32, column : column + 128] = scratch[
                q ^ c, tile * 32 : (tile + 1) * 32
            ]
        proj_out[0, q * 64 : (q + 1) * 64] = scratch[q ^ c, 192:]


def layer_out(kernel, rows, place, totals, layer, shapes, before, start, after):
    extra = list(before) + list(after)
    count = 1 + len(totals)

    def inner(*refs):
        kernel(*refs[:count], *refs[count + len(extra) :])

    def block(shape):
        at = (layer,) + (0,) * (len(shape) - 1)
        return pl.BlockSpec((1,) + tuple(shape[1:]), lambda i: at)

    return list(
        pl.pallas_call(
            inner,
            grid=(1,),
            out_shape=[jax.ShapeDtypeStruct(shape, f32) for shape in shapes],
            in_specs=[pl.BlockSpec(memory_space=pltpu.SMEM)]
            + [pl.BlockSpec((rows, lanes), lambda i: (start // rows, 0))] * 4
            + [pl.BlockSpec(memory_space=pl.ANY)] * len(extra),
            out_specs=[block(shape) for shape in shapes],
            scratch_shapes=[pltpu.VMEM((4, rows, lanes), f32)],
            input_output_aliases={count + i: i for i in range(len(before))},
            compiler_params=compiler_params(),
            cost_estimate=pl.CostEstimate(flops=2**20, bytes_accessed=1024, transcendentals=0),
        )(place, *totals, *extra)
    )


def hidden_out(place, totals, layer, shape_one, shape_two, before, start, after=()):
    shapes = (shape_one, shape_two)
    return layer_out(hidden_out_kernel, 512, place, totals, layer, shapes, before, start, after)


def heads_out(place, totals, layer, shape_one, shape_two, before, start, after=()):
    shapes = (shape_one, shape_two)
    return layer_out(heads_out_kernel, 256, place, totals, layer, shapes, before, start, after)


def last_kernel(place, *refs):
    grad_mid, mine, other, state, small_local, small_far = refs[:6]
    sums_in = refs[6]
    sums_mid, bias_mlp, b_query, b_first = refs[7:9], refs[9:11], refs[11:13], refs[13:15]
    grad_out, out = refs[15:]
    grad, sums = norm_step(received_sum(mine, other), small_row(small_local, small_far, 0), state[...])
    grad_out[...] = grad_mid[:128] + grad[:128]
    for layer in range(2):
        inner = sums if layer == 0 else sums_in[...]
        mid = sums_mid[layer]
        rows = [
            (2 * layer, inner[0:1]),
            (2 * layer + 1, mid[0:1]),
            (4 + 4 * layer, inner[1:2]),
            (5 + 4 * layer, mid[2:3]),
            (6 + 4 * layer, mid[1:2]),
            (7 + 4 * layer, bias_mlp[layer][...]),
        ]
        for k in range(4):
            for row, value in rows:
                out[k, row : row + 1] = value[:, k * 128 : (k + 1) * 128]
            for channel in range(2):
                for j in range(2):
                    row = 12 + 4 * layer + 2 * channel + j
                    out[k, row : row + 1] = b_query[layer][channel : channel + 1, j * 128 : (j + 1) * 128]
            for q in range(4):
                for j in range(2):
                    row = 20 + 8 * layer + 2 * q + j
                    out[k, row : row + 1] = b_first[layer][q, :, j * 128 : (j + 1) * 128]
    out[:, 36:] = jnp.zeros((4, 12, lanes), f32)


def turn(values, place_z, back):
    rows = values.shape[0]
    chunks = values.reshape(rows, 4, lanes)
    order = (place_z - jnp.arange(4)) % 4
    return jnp.concatenate(
        [lax.dynamic_slice_in_dim(values, order[k] * lanes, lanes, 1) for k in range(4)], axis=1
    )


def body_four(x_in, w_qkv, b_qv, w_proj, w_fc1, b_fc1, w_fc2, gains, biases, cotangent):
    z, c, t = lax.axis_index("shard"), lax.axis_index("ctx"), lax.axis_index("tp")
    place = jnp.stack([z, c, t]).astype(jnp.int32)
    flat = jnp.concatenate([array.reshape(-1) for array in (gains, biases, b_qv, b_fc1)])
    small = jnp.pad(flat, (0, 32 * lanes - flat.shape[0])).reshape(32, lanes)

    kinds = ("qkv", "proj", "first", "second", "first", "second")
    send = pack(
        place, kinds, (w_qkv, w_proj, w_fc1, w_fc2, w_fc1, w_fc2), (1, 1, 0, 0, 1, 1), whole_quarters=False
    )
    full = gather(send)
    local_a, send_a = pack(place, ("qkv", "proj", "small"), (w_qkv, w_proj, small), (0, 0, 0))
    pair_own = turn(jnp.concatenate([x_in[:, 0], cotangent[:, 0]]), z, False)
    pair_peer = swap_tp(pair_own)
    got_a = far_chunks(send_a)
    far_a = stack(place, got_a)
    chip_a = swap_x(far_a)
    group_a0 = [local_a, far_a, swap_core(far_a), chip_a, swap_core(chip_a)]
    small_parts = small_of(group_a0)
    parts = {
        "qkv": [pieces_of(group_a0, 192, 0), gathered_rows(full, 192, 0)],
        "proj": [pieces_of(group_a0, 64, 192), gathered_rows(full, 64, 192)],
        "first": [gathered_rows(full, 256, 256), gathered_rows(full, 256, 768)],
        "second": [gathered_rows(full, 256, 512), gathered_rows(full, 256, 1024)],
    }
    square, wide = (256, 512), (256, 256)
    saved = []
    for layer in range(2):
        source = [pair_own, pair_peer] if layer == 0 else [middle, partial, swap_tp(partial)]
        more = [(square, f32)] if layer == 0 else []
        state, low_in, q, kv, w_all, *passed = run(
            query_kernel(layer, layer == 0),
            [(square, f32), (square, bf16), (wide, bf16), (square, bf16), ((4, 4, 32, 768), bf16)] + more,
            place,
            source + small_parts + parts["qkv"][layer],
        )
        if layer == 0:
            g_all = passed[0]
        kv_chip = swap_x(kv)
        chunks = [kv, swap_core(kv), kv_chip, swap_core(kv_chip)]
        attn, lse, partial, w_out = run(
            functools.partial(attend_kernel, len(parts["proj"][layer])),
            [(wide, bf16), ((256, lanes), f32), (square, bf16), ((4, 64, 512), bf16)],
            place,
            [q] + chunks + parts["proj"][layer],
        )
        middle, low_mid, pre, partial = run(
            mlp_kernel(layer),
            [(square, f32), (square, bf16), ((256, 1024), f32), (square, bf16)],
            place,
            [state, partial, swap_tp(partial)] + small_parts + parts["first"][layer] + parts["second"][layer],
        )
        saved.append((state, low_in, q, chunks, w_all, attn, lse, w_out, middle, low_mid, pre))

    received = swap_tp(partial[128:]).astype(f32)
    output = None
    bias_last = jnp.concatenate([small_parts[0][0][0, 267:268], small_parts[1][0][:, 267]]).reshape(1, 512)
    output = middle[:128] + partial[:128].astype(f32) + received + bias_last.astype(f32)
    output = turn(output.astype(bf16), z, True)[:, None]

    hidden_outs = [
        (square, bf16),
        ((1, 512), f32),
        ((4, 1, 256), f32),
        ((2, 4, 512, lanes), bf16),
        ((4, 512, lanes), bf16),
        ((4, 512, lanes), bf16),
    ]
    sums_mid, bias_mlp, b_query, b_first = [0, 0], [0, 0], [0, 0], [0, 0]
    hidden = [None, None]
    for layer in (1, 0):
        state, low_in, q, chunks, w_all, attn, lse, w_out, middle, low_mid, pre = saved[layer]
        tail = [pre, low_mid] + parts["first"][layer] + parts["second"][layer]
        if layer == 1:
            grad_state = g_all
            partial, bias_mlp[1], b_first[1], *grads = run(
                top_kernel, hidden_outs, place, [grad_state] + tail
            )
        else:
            own, far = halve(place, [grads])
            grad_state, sums_in, partial, bias_mlp[0], b_first[0], *grads = run(
                lower_kernel(0),
                [(square, f32), ((2, 512), f32)] + hidden_outs,
                place,
                [grad_mid, partial, swap_tp(partial), saved[1][0]] + small_parts + tail,
                after=[own],
            )
            both = quarter(place, own, far, after=[partial])
            heads_sum = lax.psum_scatter(both, "shard", scatter_dimension=0)
        own, far = halve(place, [grads])
        behind = [own] if layer == 1 else [both, own]
        grad_mid, sums_mid[layer], gw_out, dq, keep, send = run(
            attend_back_kernel(layer),
            [
                (square, f32),
                ((3, 512), f32),
                ((4, 64, 512), bf16),
                (wide, bf16),
                ((2, 256, 512), bf16),
                ((2, 256, 512), bf16),
            ],
            place,
            [partial, swap_tp(partial), middle, grad_state] + small_parts + [attn, w_out, q] + chunks + [lse],
            after=behind,
        )
        both = quarter(place, own, far, after=[keep])
        hidden[layer] = lax.psum_scatter(both, "shard", scatter_dimension=0)
        behind = [both]
        dkv, chip = run(halve_kernel, [(square, bf16)] * 2, place, [keep, swap_core(send)], after=behind)
        partial, b_query[layer], *grads = run(
            query_back_kernel,
            [
                (square, bf16),
                ((2, 256), f32),
                ((2, 4, 256, lanes), bf16),
                ((4, 256, lanes), bf16),
                ((4, 256, lanes), bf16),
            ],
            place,
            [dq, dkv, swap_x(chip), low_in, w_all, gw_out],
            scratch=[pltpu.VMEM((4, 4, 32, 768), bf16)],
            after=[output] if layer == 1 else [],
        )
    own, far = halve(place, [grads])
    grad_x, sums = run(
        last_kernel,
        [((128, 512), f32), ((4, 48, lanes), f32)],
        place,
        [grad_mid, partial, swap_tp(partial), saved[0][0]]
        + small_parts
        + [sums_in]
        + sums_mid
        + bias_mlp
        + b_query
        + b_first,
        after=[own],
    )
    pieces = run(last_quarter_kernel, [((304, lanes), bf16)] * 4, place, [own, swap_x(far), sums])
    grad_x = turn(grad_x, z, True)[:, None]
    (joined,) = run(
        join_kernel, [((1280, lanes), bf16)], place, [hidden[1], hidden[0], heads_sum], after=pieces[:1]
    )
    upper = collect(joined)
    got = [shift(pieces[k], 4 - k) for k in (1, 2, 3)]
    (last,) = run(
        last_total_kernel,
        [((304, lanes), bf16)],
        place,
        [pieces[0]] + got,
        after=upper[1:],
    )
    last_parts = collect(last)
    outs_heads = heads_out(place, upper, 1, w_qkv.shape, w_proj.shape, [], 1024, after=[last])
    outs_hidden = hidden_out(place, upper, 1, w_fc1.shape, w_fc2.shape, [], 0, after=[last])
    grad_fc1, grad_fc2 = hidden_out(
        place, upper, 0, w_fc1.shape, w_fc2.shape, outs_hidden, 512, after=[last]
    )
    total = sum(part[256:].astype(f32) for part in last_parts)
    grad_gains = total[:4].reshape(gains.shape)
    grad_biases = total[4:12].reshape(biases.shape)
    rest_q = total[12:20].reshape(2, 2, 4, 64)
    rest_f = total[20:36].reshape(2, 16, 64)
    grad_b_qv = lax.dynamic_slice_in_dim(rest_q, z * 16, 16, 3)
    grad_b_fc1 = lax.dynamic_slice_in_dim(rest_f, z * 16, 16, 2)

    grad_qkv, grad_proj = heads_out(place, last_parts, 0, w_qkv.shape, w_proj.shape, outs_heads, 0)
    return (
        output, grad_x, grad_qkv, grad_b_qv, grad_proj, grad_fc1, grad_b_fc1, grad_fc2, grad_gains, grad_biases
    )


def body(*args):
    x_in, w_qkv, b_qv, w_proj, w_fc1 = args[:5]
    expected = ((128, 1, 512), (2, 3, 128, 256), (2, 2, 4, 16), (2, 256, 128), (2, 128, 1024))
    sizes = (lax.axis_size("shard"), lax.axis_size("ctx"), lax.axis_size("tp"))
    shapes = tuple(array.shape for array in (x_in, w_qkv, b_qv, w_proj, w_fc1))
    if sizes == (4, 4, 2) and shapes == expected:
        return body_four(*args)
    return body_any(*args)


def solution(mesh):
    return jax.shard_map(
        body,
        mesh=mesh,
        in_specs=(
            P(("ctx", "tp"), "shard", None),
            P(None, None, "shard", "tp"),
            P(None, None, "tp", "shard"),
            P(None, "tp", "shard"),
            P(None, "shard", "tp"),
            P(None, "tp", "shard"),
            P(None, "tp", "shard"),
            P(None, None, "shard"),
            P(None, None, "shard"),
            P(("ctx", "tp"), "shard", None),
        ),
        out_specs=(
            P(("ctx", "tp"), "shard", None),
            P(("ctx", "tp"), "shard", None),
            P(None, None, "shard", "tp"),
            P(None, None, "tp", "shard"),
            P(None, "tp", "shard"),
            P(None, "shard", "tp"),
            P(None, "tp", "shard"),
            P(None, "tp", "shard"),
            P(None, None, "shard"),
            P(None, None, "shard"),
        ),
        check_vma=False,
    )
```

```python
import functools
import math

import jax
import jax.numpy as jnp
from jax import lax
from jax.experimental import pallas as pl
from jax.experimental.pallas import tpu as pltpu
from jax.sharding import PartitionSpec as P

epsilon = 1e-05
masked_value = -1e30
lanes = 128
f32 = jnp.float32
bf16 = jnp.bfloat16


def normalize(values):
    center = jnp.mean(values, axis=-1, keepdims=True)
    shifted = values - center
    scale_inv = lax.rsqrt(jnp.mean(shifted * shifted, axis=-1, keepdims=True) + epsilon)
    return (shifted * scale_inv, scale_inv)


def norm_back(grad_norm, normed, scale_inv):
    mean_grad = jnp.mean(grad_norm, axis=-1, keepdims=True)
    mean_prod = jnp.mean(grad_norm * normed, axis=-1, keepdims=True)
    return scale_inv * (grad_norm - mean_grad - normed * mean_prod)


def gelu_tanh(values):
    return jax.nn.gelu(values, approximate=True)


def dot(pattern, left, right):
    return jnp.einsum(pattern, left, right, preferred_element_type=f32)


def to_rows(array):
    rows, columns = array.shape[-2:]
    if columns % lanes or rows % 16:
        return array.reshape(-1, lanes)
    tiles = array.reshape(-1, rows, columns // lanes, lanes)
    return jnp.swapaxes(tiles, 1, 2).reshape(-1, lanes)


def from_rows(packed, shape):
    rows, columns = shape[-2:]
    lead = packed.shape[:-2]
    if columns % lanes or rows % 16:
        return packed.reshape(lead + tuple(shape))
    count = math.prod(shape[:-2])
    tiles = packed.reshape(lead + (count, columns // lanes, rows, lanes))
    return jnp.swapaxes(tiles, -3, -2).reshape(lead + tuple(shape))


def small_rows(arrays):
    flat = jnp.concatenate([array.reshape(-1) for array in arrays])
    size = -(-flat.shape[0] // (64 * lanes)) * 64 * lanes
    return jnp.pad(flat, (0, size - flat.shape[0])).reshape(-1, lanes)


def join(gathered, axis):
    moved = jnp.moveaxis(gathered, 0, axis)
    shape = moved.shape
    return moved.reshape(shape[:axis] + (shape[axis] * shape[axis + 1],) + shape[axis + 2 :])


def split(whole, axis, shards):
    shape = whole.shape
    parts = whole.reshape(shape[:axis] + (shards, shape[axis] // shards) + shape[axis + 1 :])
    return jnp.moveaxis(parts, axis, 0)


def swap_tp(values):
    return lax.ppermute(values, "tp", [(0, 1), (1, 0)])


def swap_core(values):
    return lax.ppermute(values, "ctx", [(0, 1), (1, 0), (2, 3), (3, 2)])


def swap_x(values):
    return lax.ppermute(values, "ctx", [(0, 2), (2, 0), (1, 3), (3, 1)])


def swap_both(values):
    return lax.ppermute(values, "ctx", [(0, 3), (3, 0), (1, 2), (2, 1)])


def other_half(values):
    half = values.shape[0] // 2
    return jnp.concatenate([values[half:], values[:half]])


def gather_packed(packed, shards):
    quarter = packed.shape[0] // 4
    own = lax.dynamic_slice_in_dim(packed, lax.axis_index("ctx") * quarter, quarter, 0)
    return lax.all_gather(own, ("shard", "ctx"), axis=0, tiled=True).reshape(
        shards, packed.shape[0], lanes
    )


def halves(values, bit):
    half = values.shape[1] // 2
    keep = lax.dynamic_slice_in_dim(values, bit * half, half, 1)
    send = lax.dynamic_slice_in_dim(values, (1 - bit) * half, half, 1)
    return keep, send


def paired(own, other, bit):
    return jnp.where(
        bit == 0, jnp.concatenate([own, other]), jnp.concatenate([other, own])
    )


def reduce_packed(packed):
    place = lax.axis_index("ctx")
    core, chip = place % 2, place // 2
    keep, send = halves(packed, core)
    half = (keep.astype(f32) + swap_core(send).astype(f32)).astype(bf16)
    keep, send = halves(half, chip)
    quarter = (keep.astype(f32) + swap_x(send).astype(f32)).astype(bf16)
    parts = lax.all_to_all(quarter, "shard", split_axis=0, concat_axis=0, tiled=True)
    total = jnp.sum(parts.astype(f32), axis=0).astype(bf16)
    both = paired(total, swap_x(total), chip)
    return paired(both, swap_core(both), core)


def positions(offsets, tp_place, chunk, block):
    half = block // 2
    return chunk * block + (offsets + tp_place * half) % block


def attention_mask(block):
    place, tp_place = lax.axis_index("ctx"), lax.axis_index("tp")
    offsets = jnp.arange(block, dtype=jnp.int32)
    rows = positions(offsets, tp_place, place, block)
    keys = jnp.concatenate([positions(offsets, tp_place, place ^ j, block) for j in range(4)])
    return keys[None, :] <= rows[:, None]


def head_split(values, heads):
    return values.reshape(values.shape[0], heads, values.shape[1] // heads)


def attend(queries, key_all, value_all, mask, heads):
    scale_factor = (queries.shape[1] // heads) ** (-0.5)
    scores = dot("qhe,khe->hqk", head_split(queries, heads), head_split(key_all, heads))
    scores = jnp.where(mask, scores * scale_factor, masked_value)
    row_top = jnp.max(scores, axis=-1, keepdims=True)
    exponent = jnp.exp(scores - row_top)
    totals = jnp.sum(exponent, axis=-1, keepdims=True)
    probs = (exponent / totals).astype(bf16)
    out = dot("hqk,khe->qhe", probs, head_split(value_all, heads))
    return out.reshape(queries.shape).astype(bf16), row_top + jnp.log(totals)


def attend_back(queries, key_all, value_all, mask, heads, log_sums, grad_out):
    scale_factor = (queries.shape[1] // heads) ** (-0.5)
    query_heads, key_heads = head_split(queries, heads), head_split(key_all, heads)
    grad_heads = head_split(grad_out, heads)
    scores = dot("qhe,khe->hqk", query_heads, key_heads)
    scores = jnp.where(mask, scores * scale_factor, masked_value)
    probs = jnp.exp(scores - log_sums)
    grad_probs = dot("qhe,khe->hqk", grad_heads, head_split(value_all, heads))
    row_dot = jnp.sum(probs * grad_probs, axis=-1, keepdims=True)
    grad_scores = (probs * (grad_probs - row_dot)).astype(bf16)
    grad_q = dot("hqk,khe->qhe", grad_scores, key_heads) * scale_factor
    grad_k = dot("hqk,qhe->khe", grad_scores, query_heads) * scale_factor
    grad_v = dot("hqk,qhe->khe", probs.astype(bf16), grad_heads)
    return (
        grad_q.reshape(queries.shape).astype(bf16),
        jnp.concatenate(
            [grad_k.reshape(key_all.shape), grad_v.reshape(key_all.shape)], axis=1
        ).astype(bf16),
    )


def body_any(x_in, w_qkv, b_qv, w_proj, w_fc1, b_fc1, w_fc2, gains, biases, cotangent):
    depth = w_qkv.shape[0]
    shards = lax.axis_size("shard")
    own_rows, width = x_in.shape[0], x_in.shape[2]
    block = 2 * own_rows
    heads = b_qv.shape[2]
    half_width = w_qkv.shape[3]
    hidden = w_fc1.shape[2]

    small_shapes = [gains.shape, biases.shape, b_qv.shape, b_fc1.shape]
    small = small_rows([gains, biases, b_qv, b_fc1])
    group_a0 = jnp.concatenate([small, to_rows(w_qkv[0])])
    group_b0 = jnp.concatenate([to_rows(w_proj[0]), to_rows(w_fc1[0]), to_rows(w_fc2[0])])
    rest = []
    for index in range(1, depth):
        rest += [to_rows(w_qkv[index]), to_rows(w_proj[index]), to_rows(w_fc1[index]), to_rows(w_fc2[index])]
    group_rest = jnp.concatenate(rest)

    gathered_a0 = gather_packed(group_a0, shards)
    gathered_b0 = gather_packed(group_b0, shards)
    gathered_rest = gather_packed(group_rest, shards)

    def cutter(gathered, start):
        place = [start]

        def take(shape, axis):
            rows = math.prod(shape) // lanes
            piece = from_rows(gathered[:, place[0] : place[0] + rows], shape)
            place[0] += rows
            return join(piece, axis)

        return take

    shape_qkv, shape_proj = w_qkv.shape[1:], w_proj.shape[1:]
    shape_fc1, shape_fc2 = w_fc1.shape[1:], w_fc2.shape[1:]
    take_a, take_b, take_r = cutter(gathered_a0, small.shape[0]), cutter(gathered_b0, 0), cutter(gathered_rest, 0)
    weights = []
    for index in range(depth):
        take_q, take_o = (take_a, take_b) if index == 0 else (take_r, take_r)
        weights.append(
            (take_q(shape_qkv, 1), take_o(shape_proj, 1), take_o(shape_fc1, 0), take_o(shape_fc2, 1))
        )
    flat = gathered_a0[:, : small.shape[0]].reshape(shards, -1)
    vectors, start = [], 0
    for shape in small_shapes:
        size = math.prod(shape)
        piece = flat[:, start : start + size].reshape((shards,) + shape)
        vectors.append(join(piece, len(shape) - 1).astype(f32))
        start += size
    gain_all, bias_all, b_qv_all, b_fc1_all = vectors

    mask = attention_mask(block)
    x_own = x_in[:, 0]
    state = jnp.concatenate([x_own, swap_tp(x_own)]).astype(f32)
    g_own = cotangent[:, 0]
    grad_state = jnp.concatenate([g_own, swap_tp(g_own)]).astype(f32)

    stored = []
    for index in range(depth):
        w_query, w_out, w_first, w_second = weights[index]
        normed_in, scale_in = normalize(state)
        low_in = (normed_in * gain_all[index, 0] + bias_all[index, 0]).astype(bf16)
        bias_q = b_qv_all[index, 0].reshape(half_width)
        bias_v = b_qv_all[index, 1].reshape(half_width)
        queries = (dot("rd,df->rf", low_in, w_query[0]) + bias_q).astype(bf16)
        keys = dot("rd,df->rf", low_in, w_query[1]).astype(bf16)
        values = (dot("rd,df->rf", low_in, w_query[2]) + bias_v).astype(bf16)
        kv_own = jnp.concatenate([keys, values], axis=1)
        kv_chip = swap_x(kv_own)
        kv_all = jnp.concatenate([kv_own, swap_core(kv_own), kv_chip, swap_core(kv_chip)])
        key_all, value_all = kv_all[:, :half_width], kv_all[:, half_width:]
        attn, log_sums = attend(queries, key_all, value_all, mask, heads)
        attn_other = other_half(swap_tp(attn))
        w_out_other = swap_tp(w_out)
        middle = (
            state
            + dot("rf,fd->rd", attn, w_out)
            + dot("rf,fd->rd", attn_other, w_out_other)
            + bias_all[index, 1]
        )
        normed_mid, scale_mid = normalize(middle)
        low_mid = (normed_mid * gain_all[index, 1] + bias_all[index, 2]).astype(bf16)
        pre_act = dot("rd,df->rf", low_mid, w_first) + b_fc1_all[index].reshape(hidden)
        act = gelu_tanh(pre_act).astype(bf16)
        partial = dot("rf,fd->rd", act, w_second)
        if index == depth - 1:
            received = swap_tp(partial[own_rows:].astype(bf16)).astype(f32)
            output = middle[:own_rows] + partial[:own_rows] + received + bias_all[index, 3]
        else:
            received = other_half(swap_tp(partial.astype(bf16))).astype(f32)
            state = middle + partial + received + bias_all[index, 3]
        stored.append(
            (normed_in, scale_in, low_in, queries, key_all, value_all, log_sums, attn,
             normed_mid, scale_mid, low_mid, pre_act, act)
        )
    output = output.astype(bf16)[:, None]

    results = [None] * depth
    for index in reversed(range(depth)):
        w_query, w_out, w_first, w_second = weights[index]
        (normed_in, scale_in, low_in, queries, key_all, value_all, log_sums, attn,
         normed_mid, scale_mid, low_mid, pre_act, act) = stored[index]
        grad_bias_mlp = jnp.sum(grad_state, axis=0)
        grad_low = grad_state.astype(bf16)
        grad_hidden = dot("rd,fd->rf", grad_low, w_second)
        unused, gelu_pull = jax.vjp(gelu_tanh, pre_act)
        grad_pre = gelu_pull(grad_hidden)[0].astype(bf16)
        grad_w_second = dot("rf,rd->fd", act, grad_low)
        grad_w_first = dot("rd,rf->df", low_mid, grad_pre)
        grad_b_first = jnp.sum(grad_pre, axis=0, dtype=f32)
        partial = dot("rf,df->rd", grad_pre, w_first)
        mlp_rows = jnp.concatenate(
            [
                jax.vmap(to_rows)(split(grad_w_first.astype(bf16), 0, shards)),
                jax.vmap(to_rows)(split(grad_w_second.astype(bf16), 1, shards)),
            ],
            axis=1,
        )
        mlp_total = reduce_packed(mlp_rows)
        grad_mid = partial + other_half(swap_tp(partial.astype(bf16))).astype(f32)
        grad_gain_mid = jnp.sum(grad_mid * normed_mid, axis=0)
        grad_beta_mid = jnp.sum(grad_mid, axis=0)
        grad_middle = grad_state + norm_back(grad_mid * gain_all[index, 1], normed_mid, scale_mid)
        grad_bias_attn = jnp.sum(grad_middle, axis=0)
        grad_low = grad_middle.astype(bf16)
        grad_attn = dot("rd,fd->rf", grad_low, w_out).astype(bf16)
        grad_w_out = dot("rf,rd->fd", attn, grad_low)
        grad_q, grad_kv = attend_back(
            queries, key_all, value_all, mask, heads, log_sums, grad_attn
        )
        part = grad_kv.reshape(4, block, 2 * half_width)
        sent = swap_core(jnp.stack([part[1], part[3]])).astype(f32)
        mine = part[0].astype(f32) + sent[0]
        chip = (part[2].astype(f32) + sent[1]).astype(bf16)
        grad_kv = (mine + swap_x(chip).astype(f32)).astype(bf16)
        grad_qkv = jnp.stack([grad_q, grad_kv[:, :half_width], grad_kv[:, half_width:]])
        grad_w_query = dot("rd,crf->cdf", low_in, grad_qkv)
        grad_b_query = jnp.sum(grad_qkv[0::2], axis=1, dtype=f32)
        partial = dot("crf,cdf->rd", grad_qkv, w_query)
        grad_in = partial + other_half(swap_tp(partial.astype(bf16))).astype(f32)
        grad_gain_in = jnp.sum(grad_in * normed_in, axis=0)
        grad_beta_in = jnp.sum(grad_in, axis=0)
        grad_state = grad_middle + norm_back(grad_in * gain_all[index, 0], normed_in, scale_in)

        vectors = [
            jnp.stack([grad_gain_in, grad_gain_mid]),
            jnp.stack([grad_beta_in, grad_bias_attn, grad_beta_mid, grad_bias_mlp]),
            grad_b_query.reshape(2, heads, half_width // heads),
            grad_b_first.reshape(b_fc1_all.shape[1:]),
        ]
        parts = [split(vector, vector.ndim - 1, shards) for vector in vectors]
        part_shapes = [part.shape[1:] for part in parts]
        attn_rows = jnp.concatenate(
            [
                jax.vmap(to_rows)(split(grad_w_query.astype(bf16), 1, shards)),
                jax.vmap(to_rows)(split(grad_w_out.astype(bf16), 1, shards)),
                jax.vmap(lambda *own: small_rows(own))(*parts).astype(bf16),
            ],
            axis=1,
        )
        attn_total = reduce_packed(attn_rows)

        def pieces(total, shapes):
            place, out = 0, []
            for shape in shapes:
                rows = math.prod(shape) // lanes
                out.append(from_rows(total[place : place + rows], shape).astype(f32))
                place += rows
            return out, total[place:].reshape(-1)

        (out_fc1, out_fc2), unused = pieces(mlp_total, [shape_fc1, shape_fc2])
        (out_qkv, out_proj), tail = pieces(attn_total, [shape_qkv, shape_proj])
        small_out, start = [], 0
        for shape in part_shapes:
            size = math.prod(shape)
            small_out.append(tail[start : start + size].reshape(shape).astype(f32))
            start += size
        results[index] = (
            out_qkv, small_out[2], out_proj, out_fc1, small_out[3], out_fc2, small_out[0], small_out[1]
        )
    stacked = tuple(
        jnp.stack([results[index][member] for index in range(depth)]) for member in range(8)
    )
    return (output, grad_state[:own_rows, None]) + stacked


def compiler_params():
    return pltpu.CompilerParams(vmem_limit_bytes=56 * 2**20)


def whole(array):
    zeros = (0,) * array.ndim
    return pl.BlockSpec(array.shape, lambda i: zeros)


def rows_at(array, rows, start, lead=None, first=0):
    lead = array.shape[0] if lead is None else lead
    return pl.BlockSpec((lead, rows, lanes), lambda i: (first, start // rows, 0))


def run(kernel, outs, place, operands, scratch=(), flops=2**20, after=()):
    arrays, specs = [], []
    count = 1 + len(operands)

    def inner(*refs):
        kernel(*refs[:count], *refs[count + len(after) :])

    for operand in operands:
        array, spec = operand if isinstance(operand, tuple) else (operand, whole(operand))
        arrays.append(array)
        specs.append(spec)
    out_shape = [jax.ShapeDtypeStruct(shape, kind) for shape, kind in outs]
    after = list(after)
    arrays += after
    specs += [pl.BlockSpec(memory_space=pl.ANY)] * len(after)
    call = pl.pallas_call(
        inner,
        grid=(1,),
        out_shape=out_shape,
        in_specs=[pl.BlockSpec(memory_space=pltpu.SMEM)] + specs,
        out_specs=[whole(shape) for shape in out_shape],
        scratch_shapes=list(scratch),
        compiler_params=compiler_params(),
        cost_estimate=pl.CostEstimate(flops=flops, bytes_accessed=1024, transcendentals=0),
    )
    return list(call(place, *arrays))


def mm(left, right):
    return lax.dot_general(left, right, (((1,), (0,)), ((), ())), preferred_element_type=f32)


def mm_nt(left, right):
    return lax.dot_general(left, right, (((1,), (1,)), ((), ())), preferred_element_type=f32)


def mm_tn(left, right):
    return lax.dot_general(left, right, (((0,), (0,)), ((), ())), preferred_element_type=f32)


def lane_join(parts):
    return jnp.concatenate(parts, axis=1)


def row_join(parts):
    return jnp.concatenate(parts, axis=0)


class Pieces:
    def __init__(self, refs, place):
        self.refs, self.place = refs, place

    def tile(self, k, p, start, rows):
        if len(self.refs) == 1:
            z, c = self.place[0], self.place[1]
            return self.refs[0][(z - k + 4) % 4, p ^ c, start : start + rows]
        if k == 0:
            return self.refs[0][p, start : start + rows]
        return self.refs[1 + p][k - 1, start : start + rows]


def first_block(pieces, p):
    return row_join(
        [lane_join([pieces.tile(k, p, j * 128, 128) for j in range(2)]) for k in range(4)]
    )


def second_block(pieces, p):
    return lane_join([pieces.tile(k, p, 0, 256) for k in range(4)])


def small_row(small_local, small_far, row):
    parts = [small_local[0, row : row + 1]] + [small_far[k, row : row + 1] for k in range(3)]
    return lane_join(parts).astype(f32)


def spread(small_local, small_far, row, place_z, half, later=None):
    def rows_from(row):
        return row_join(
            [small_local[0, row : row + 1]] + [small_far[k, row : row + 1] for k in range(3)]
        ).astype(f32)

    source = rows_from(row)
    if later is not None:
        source = jnp.where(later == 0, source, rows_from(row + 1))
    source = source.astype(bf16)
    take = lax.broadcasted_iota(jnp.int32, (128, 256), 0)
    lane = lax.broadcasted_iota(jnp.int32, (128, 256), 1)
    wanted = half * 64 + (lane // 64) * 16 + lane % 16
    table = (take == wanted).astype(f32).astype(bf16)
    rows = mm(source, table)
    chunk = lax.broadcasted_iota(jnp.int32, (4, 256), 0)
    lane = lax.broadcasted_iota(jnp.int32, (4, 256), 1)
    keep = (lane % 64) // 16 == (place_z - chunk + 4) % 4
    return jnp.sum(jnp.where(keep, rows, 0.0), axis=0, keepdims=True)


def pack_kernel(kinds):
    def kernel(place, *refs):
        c = place[1]
        out, send = refs[-2:]
        start = 0
        for ref, kind in zip(refs, kinds):
            for q in range(4):
                to = q ^ c
                if kind == "first":
                    for j in range(2):
                        column = (2 * q + j) * 128
                        out[to, start + j * 128 : start + (j + 1) * 128] = ref[0, :, column : column + 128]
                elif kind == "second":
                    out[to, start : start + 256] = ref[0, q * 256 : (q + 1) * 256]
                elif kind == "proj":
                    out[to, start : start + 64] = ref[0, q * 64 : (q + 1) * 64]
                elif kind == "qkv":
                    for tile in range(6):
                        row = start + tile * 32
                        column = (tile % 2) * 128
                        out[to, row : row + 32] = ref[0, tile // 2, q * 32 : (q + 1) * 32, column : column + 128]
                else:
                    out[to, start : start + 32] = ref[...]
            start += kind_rows[kind]
        send[...] = out[0]

    return kernel


def quarter_pack_kernel(kinds):
    def kernel(place, *refs):
        out = refs[-1]
        for q in range(4):

            @pl.when(place[1] == q)
            def write(q=q):
                start = 0
                for ref, kind in zip(refs, kinds):
                    if kind == "first":
                        for j in range(2):
                            column = (2 * q + j) * 128
                            out[start + j * 128 : start + (j + 1) * 128] = ref[0, :, column : column + 128]
                    elif kind == "second":
                        out[start : start + 256] = ref[0, q * 256 : (q + 1) * 256]
                    elif kind == "proj":
                        out[start : start + 64] = ref[0, q * 64 : (q + 1) * 64]
                    else:
                        for tile in range(6):
                            row = start + tile * 32
                            column = (tile % 2) * 128
                            out[row : row + 32] = ref[0, tile // 2, q * 32 : (q + 1) * 32, column : column + 128]
                    start += kind_rows[kind]

    return kernel


kind_rows = {"first": 256, "second": 256, "proj": 64, "qkv": 192, "small": 32}


def pack(place, kinds, arrays, index, after=(), whole_quarters=True):
    rows = sum(kind_rows[kind] for kind in kinds)
    operands = []
    for kind, array, at in zip(kinds, arrays, index):
        if kind == "small":
            operands.append(array)
        else:
            block = (1,) + array.shape[1:]
            at = (at,) + (0,) * (array.ndim - 1)
            operands.append((array, pl.BlockSpec(block, lambda i, at=at: at)))
    if not whole_quarters:
        return run(quarter_pack_kernel(kinds), [((rows, lanes), bf16)], place, operands, after=after)[0]
    return run(
        pack_kernel(kinds), [((4, rows, lanes), bf16), ((rows, lanes), bf16)], place, operands, after=after
    )


def gather(quarter):
    full = lax.all_gather(quarter, ("shard", "ctx"), axis=0)
    return full.reshape((4, 4) + quarter.shape)


def gathered_rows(array, rows, start):
    return [(array, pl.BlockSpec((4, 4, rows, lanes), lambda i: (0, 0, start // rows, 0)))]


def shift(values, step):
    return lax.ppermute(values, "shard", [(z, (z + step) % 4) for z in range(4)])


def far_chunks(send):
    return [shift(send, k) for k in (1, 2, 3)]


def stack_kernel(place, one, two, three, out):
    for k, ref in enumerate((one, two, three)):
        out[k] = ref[...]


def stack(place, got, after=()):
    return run(stack_kernel, [((3,) + got[0].shape, bf16)], place, got, after=after)[0]


def pieces_of(group, rows, start):
    return [(array, rows_at(array, rows, start)) for array in group]


def small_of(group):
    return [(group[0], rows_at(group[0], 32, 256, lead=1)), (group[1], rows_at(group[1], 32, 256))]


def query_kernel(index, first_layer):
    def kernel(place, *refs):
        c = place[1]
        if first_layer:
            own, peer, small_local, small_far = refs[:4]
            pieces = Pieces(refs[4:9], place)
            grad_out = refs[14]
            grad_out[...] = row_join([own[128:], peer[128:]]).astype(f32)
            state_out, low_out, q_out, kv_out, w_out = refs[9:14]
            state = row_join([own[:128], peer[:128]]).astype(f32)
        else:
            middle, mine, other, small_local, small_far = refs[:5]
            pieces = Pieces(refs[5:6], place)
            state_out, low_out, q_out, kv_out, w_out = refs[6:]
            received = row_join([other[128:], other[:128]])
            state = (
                middle[...]
                + mine[...].astype(f32)
                + received.astype(f32)
                + small_row(small_local, small_far, 4 + 4 * (index - 1) + 3)
            )
        for k in range(4):
            for p in range(4):
                for tile in range(6):
                    w_out[k, p ^ c, :, tile * 128 : (tile + 1) * 128] = pieces.tile(k, p, tile * 32, 32)
        state_out[...] = state
        normed, scale = normalize(state)
        low = (
            normed * small_row(small_local, small_far, 2 * index)
            + small_row(small_local, small_far, 4 + 4 * index)
        ).astype(bf16)
        low_out[...] = low
        w_all = w_out[...].reshape(512, 768)
        row = 12 + index
        bias_q = spread(small_local, small_far, row, place[0], 0)
        bias_v = spread(small_local, small_far, row, place[0], 1)
        kv_out[:, :256] = mm(low, w_all[:, 256:512]).astype(bf16)
        kv_out[:, 256:] = (mm(low, w_all[:, 512:]) + bias_v).astype(bf16)
        q_out[...] = (mm(low, w_all[:, :256]) + bias_q).astype(bf16)

    return kernel


def seen(place, j):
    c, t = place[1], place[2]
    if j:
        return None
    row = lax.broadcasted_iota(jnp.int32, (256, 256), 0) ^ (t * 128)
    key = lax.broadcasted_iota(jnp.int32, (256, 256), 1) ^ (t * 128)
    return key <= row


def masked_scores(query, chunks, own_mask, place):
    parts = []
    for j in range(4):
        scores = mm_nt(query, chunks[j]) * 0.125
        if j == 0:
            scores = jnp.where(own_mask, scores, masked_value)
        else:
            scores = jnp.where((place[1] ^ j) < place[1], scores, masked_value)
        parts.append(scores)
    return parts


def attend_kernel(count, place, *refs):
    c = place[1]
    q, chunks = refs[0], refs[1:5]
    pieces = Pieces(refs[5 : 5 + count], place)
    attn_out, lse_out, partial_out, w_out = refs[5 + count :]
    for k in range(4):
        for p in range(4):
            w_out[p ^ c, :, k * 128 : (k + 1) * 128] = pieces.tile(k, p, 0, 64)
    own_mask = seen(place, 0)
    results = []
    for head in range(4):
        low, high = head * 64, (head + 1) * 64
        parts = masked_scores(q[:, low:high], [chunk[:, low:high] for chunk in chunks], own_mask, place)
        scores = lane_join(parts)
        top = jnp.max(scores, axis=1, keepdims=True)
        exponent = jnp.exp(scores - top)
        total = jnp.sum(exponent, axis=1, keepdims=True)
        values = row_join([chunk[:, 256 + low : 256 + high] for chunk in chunks])
        results.append(mm(exponent.astype(bf16), values) / total)
        lse_out[:, head : head + 1] = top + jnp.log(total)
    attn = lane_join(results).astype(bf16)
    attn_out[...] = attn
    partial_out[...] = mm(attn, w_out[...].reshape(256, 512)).astype(bf16)


def mlp_kernel(index):
    def kernel(place, *refs):
        state, mine, other, small_local, small_far = refs[:5]
        first, second = Pieces(refs[5:6], place), Pieces(refs[6:7], place)
        middle_out, low_out, pre_out, partial_out = refs[7:]
        received = row_join([other[128:], other[:128]])
        middle = (
            state[...]
            + mine[...].astype(f32)
            + received.astype(f32)
            + small_row(small_local, small_far, 4 + 4 * index + 1)
        )
        middle_out[...] = middle
        normed, scale = normalize(middle)
        low = (
            normed * small_row(small_local, small_far, 2 * index + 1)
            + small_row(small_local, small_far, 4 + 4 * index + 2)
        ).astype(bf16)
        low_out[...] = low
        total = None
        for p in range(4):
            q = p ^ place[1]
            bias = spread(small_local, small_far, 14 + 2 * index, place[0], q % 2, q // 2)
            pre = mm(low, first_block(first, p)) + bias
            pre_out[:, p * 256 : (p + 1) * 256] = pre
            act = gelu_tanh(pre).astype(bf16)
            part = mm(act, second_block(second, p))
            total = part if total is None else total + part
        partial_out[...] = total.astype(bf16)

    return kernel


root = math.sqrt(2 / math.pi)


def mlp_back(grad, pre_ref, low_ref, first, second, place, outs):
    partial_out, bias_out, b_first_out, keep, *sends = outs
    grad_low = grad.astype(bf16)
    bias_out[...] = jnp.sum(grad, axis=0, keepdims=True)
    total = None
    for p in range(4):
        pre = pre_ref[:, p * 256 : (p + 1) * 256]
        square = pre * pre
        wave = jnp.tanh(root * pre * (1 + 0.044715 * square))
        half = 0.5 * (1 + wave)
        act = (pre * half).astype(bf16)
        slope = half + 0.5 * pre * (1 - wave * wave) * root * (1 + 3 * 0.044715 * square)
        w_second = second_block(second, p)
        grad_pre = mm_nt(grad_low, w_second) * slope
        grad_pre_low = grad_pre.astype(bf16)
        b_first_out[p ^ place[1]] = jnp.sum(grad_pre_low.astype(f32), axis=0, keepdims=True)
        part = mm_nt(grad_pre_low, first_block(first, p))
        total = part if total is None else total + part
        to = keep.at[p // 2] if p % 2 == 0 else sends[p // 2]
        grad_first = mm_tn(low_ref[...], grad_pre_low).astype(bf16)
        grad_second = mm_tn(act, grad_low).astype(bf16)
        for k in range(4):
            for j in range(2):
                to[k, j * 128 : (j + 1) * 128] = grad_first[
                    k * 128 : (k + 1) * 128, j * 128 : (j + 1) * 128
                ]
            to[k, 256:512] = grad_second[:, k * 128 : (k + 1) * 128]
    partial_out[...] = total.astype(bf16)


def norm_step(grad_out, gain, values):
    normed, scale = normalize(values)
    sums = row_join(
        [
            jnp.sum(grad_out * normed, axis=0, keepdims=True),
            jnp.sum(grad_out, axis=0, keepdims=True),
        ]
    )
    return norm_back(grad_out * gain, normed, scale), sums


def received_sum(mine, other):
    return mine[...].astype(f32) + row_join([other[128:], other[:128]]).astype(f32)


def top_kernel(place, *refs):
    grad, pre, low = refs[:3]
    first, second = Pieces(refs[3:4], place), Pieces(refs[4:5], place)
    mlp_back(grad[...], pre, low, first, second, place, refs[5:])


def lower_kernel(index):
    def kernel(place, *refs):
        grad_mid, mine, other, state, small_local, small_far, pre, low = refs[:8]
        first, second = Pieces(refs[8:9], place), Pieces(refs[9:10], place)
        grad_out, sums_out = refs[10:12]
        grad, sums = norm_step(
            received_sum(mine, other), small_row(small_local, small_far, 2 * (index + 1)), state[...]
        )
        sums_out[...] = sums
        grad = grad_mid[...] + grad
        grad_out[...] = grad
        mlp_back(grad, pre, low, first, second, place, refs[12:])

    return kernel


def attend_back_kernel(index):
    def kernel(place, *refs):
        mine, other, middle, grad_state, small_local, small_far = refs[:6]
        attn, w_out, q = refs[6:9]
        chunks, lse = refs[9:13], refs[13]
        grad_out, sums_out, gw_out, dq_out, keep, send = refs[14:]
        grad, sums = norm_step(
            received_sum(mine, other), small_row(small_local, small_far, 2 * index + 1), middle[...]
        )
        grad = grad_state[...] + grad
        grad_out[...] = grad
        sums_out[0:2] = sums
        sums_out[2:3] = jnp.sum(grad, axis=0, keepdims=True)
        grad_low = grad.astype(bf16)
        grad_attn = mm_nt(grad_low, w_out[...].reshape(256, 512)).astype(bf16)
        gw_out[...] = mm_tn(attn[...], grad_low).astype(bf16).reshape(4, 64, 512)
        own_mask = seen(place, 0)
        dq_all = []
        dk_all = [[] for j in range(4)]
        dv_all = [[] for j in range(4)]
        for head in range(4):
            low, high = head * 64, (head + 1) * 64
            query, grad_head = q[:, low:high], grad_attn[:, low:high]
            keys = [chunk[:, low:high] for chunk in chunks]
            row_dot = jnp.sum(
                grad_head.astype(f32) * attn[:, low:high].astype(f32), axis=1, keepdims=True
            )
            log_sum = lse[:, head : head + 1]
            parts = masked_scores(query, keys, own_mask, place)
            dq = None
            for j in range(4):
                probs = jnp.exp(parts[j] - log_sum)
                grad_probs = mm_nt(grad_head, chunks[j][:, 256 + low : 256 + high])
                grad_scores = (probs * (grad_probs - row_dot)).astype(bf16)
                part = mm(grad_scores, keys[j])
                dq = part if dq is None else dq + part
                dk_all[j].append(mm_tn(grad_scores, query) * 0.125)
                dv_all[j].append(mm_tn(probs.astype(bf16), grad_head))
            dq_all.append(dq * 0.125)
        dq_out[...] = lane_join(dq_all).astype(bf16)
        for j in range(4):
            to = keep if j % 2 == 0 else send
            to[j // 2, :, :256] = lane_join(dk_all[j]).astype(bf16)
            to[j // 2, :, 256:] = lane_join(dv_all[j]).astype(bf16)

    return kernel


def halve_kernel(place, keep, got, own_out, send_out):
    own_out[...] = (keep[0].astype(f32) + got[0].astype(f32)).astype(bf16)
    send_out[...] = (keep[1].astype(f32) + got[1].astype(f32)).astype(bf16)


def halve_groups_kernel(place, *refs):
    own_out, send_out = refs[-2:]
    start = 0
    for keep, one, two in zip(refs[:-2:3], refs[1:-2:3], refs[2:-2:3]):
        rows = keep.shape[2]
        for half, got, out in ((0, one, own_out), (1, two, send_out)):
            total = keep[half].astype(f32) + got[...].astype(f32)
            out[:, start : start + rows] = total.astype(bf16)
        start += rows


def quarter_in_order(place, own, got, out):
    for k in range(4):
        total = own[k].astype(f32) + got[k].astype(f32)
        out[(place[0] - k + 4) % 4] = total.astype(bf16)


def query_back_kernel(place, *refs):
    dq, dkv, got, low, w_ref, gw_ref = refs[:6]
    partial_out, b_out, keep, *sends, scratch = refs[6:]
    c = place[1]
    grad_kv = (dkv[...].astype(f32) + got[...].astype(f32)).astype(bf16)
    grad_qkv = lane_join([dq[...], grad_kv])
    partial_out[...] = mm_nt(grad_qkv, w_ref[...].reshape(512, 768)).astype(bf16)
    b_out[0:1] = jnp.sum(dq[...].astype(f32), axis=0, keepdims=True)
    b_out[1:2] = jnp.sum(grad_kv[:, 256:].astype(f32), axis=0, keepdims=True)
    scratch[...] = mm_tn(low[...], grad_qkv).astype(bf16).reshape(4, 4, 32, 768)
    for p in range(4):
        to = keep.at[p // 2] if p % 2 == 0 else sends[p // 2]
        for k in range(4):
            for tile in range(6):
                to[k, tile * 32 : (tile + 1) * 32] = scratch[
                    k, p ^ c, :, tile * 128 : (tile + 1) * 128
                ]
            to[k, 192:256] = gw_ref[p ^ c, :, k * 128 : (k + 1) * 128]


def last_quarter_kernel(place, own, got, sums, *outs):
    for k in range(4):
        outs[k][:256] = (own[k].astype(f32) + got[k].astype(f32)).astype(bf16)
        outs[k][256:] = sums[k].astype(bf16)


def last_total_kernel(place, own, one, two, three, out):
    total = own[...].astype(f32) + one[...].astype(f32)
    out[...] = (total + (two[...].astype(f32) + three[...].astype(f32))).astype(bf16)


def halve(place, groups, after=()):
    operands = []
    for keep, one, two in groups:
        operands += [keep, swap_core(one), swap_core(two)]
    rows = sum(group[0].shape[2] for group in groups)
    return run(halve_groups_kernel, [((4, rows, lanes), bf16)] * 2, place, operands, after=after)


def quarter(place, own, send, after=()):
    (both,) = run(quarter_in_order, [(own.shape, bf16)], place, [own, swap_x(send)], after=after)
    return both


def join_kernel(place, one, two, three, out):
    out[:512], out[512:1024], out[1024:] = one[...], two[...], three[...]


def collect(total):
    chip = swap_x(total)
    return [total, swap_core(total), chip, swap_core(chip)]


def fill(refs, scratch):
    for p in range(4):
        scratch[p] = refs[p][...].astype(f32)


def hidden_out_kernel(place, *refs):
    c = place[1]
    first_out, second_out, scratch = refs[-3:]
    fill(refs, scratch)
    for q in range(4):
        for j in range(2):
            column = (2 * q + j) * 128
            first_out[0, :, column : column + 128] = scratch[q ^ c, j * 128 : (j + 1) * 128]
        second_out[0, q * 256 : (q + 1) * 256] = scratch[q ^ c, 256:]


def heads_out_kernel(place, *refs):
    c = place[1]
    qkv_out, proj_out, scratch = refs[-3:]
    fill(refs, scratch)
    for q in range(4):
        for tile in range(6):
            column = (tile % 2) * 128
            qkv_out[0, tile // 2, q * 32 : (q + 1) * 32, column : column + 128] = scratch[
                q ^ c, tile * 32 : (tile + 1) * 32
            ]
        proj_out[0, q * 64 : (q + 1) * 64] = scratch[q ^ c, 192:]


def layer_out(kernel, rows, place, totals, layer, shapes, before, start, after):
    extra = list(before) + list(after)
    count = 1 + len(totals)

    def inner(*refs):
        kernel(*refs[:count], *refs[count + len(extra) :])

    def block(shape):
        at = (layer,) + (0,) * (len(shape) - 1)
        return pl.BlockSpec((1,) + tuple(shape[1:]), lambda i: at)

    return list(
        pl.pallas_call(
            inner,
            grid=(1,),
            out_shape=[jax.ShapeDtypeStruct(shape, f32) for shape in shapes],
            in_specs=[pl.BlockSpec(memory_space=pltpu.SMEM)]
            + [pl.BlockSpec((rows, lanes), lambda i: (start // rows, 0))] * 4
            + [pl.BlockSpec(memory_space=pl.ANY)] * len(extra),
            out_specs=[block(shape) for shape in shapes],
            scratch_shapes=[pltpu.VMEM((4, rows, lanes), f32)],
            input_output_aliases={count + i: i for i in range(len(before))},
            compiler_params=compiler_params(),
            cost_estimate=pl.CostEstimate(flops=2**20, bytes_accessed=1024, transcendentals=0),
        )(place, *totals, *extra)
    )


def hidden_out(place, totals, layer, shape_one, shape_two, before, start, after=()):
    shapes = (shape_one, shape_two)
    return layer_out(hidden_out_kernel, 512, place, totals, layer, shapes, before, start, after)


def heads_out(place, totals, layer, shape_one, shape_two, before, start, after=()):
    shapes = (shape_one, shape_two)
    return layer_out(heads_out_kernel, 256, place, totals, layer, shapes, before, start, after)


def last_kernel(place, *refs):
    grad_mid, mine, other, state, small_local, small_far = refs[:6]
    sums_in = refs[6]
    sums_mid, bias_mlp, b_query, b_first = refs[7:9], refs[9:11], refs[11:13], refs[13:15]
    grad_out, out = refs[15:]
    grad, sums = norm_step(received_sum(mine, other), small_row(small_local, small_far, 0), state[...])
    grad_out[...] = grad_mid[:128] + grad[:128]
    for layer in range(2):
        inner = sums if layer == 0 else sums_in[...]
        mid = sums_mid[layer]
        rows = [
            (2 * layer, inner[0:1]),
            (2 * layer + 1, mid[0:1]),
            (4 + 4 * layer, inner[1:2]),
            (5 + 4 * layer, mid[2:3]),
            (6 + 4 * layer, mid[1:2]),
            (7 + 4 * layer, bias_mlp[layer][...]),
        ]
        for k in range(4):
            for row, value in rows:
                out[k, row : row + 1] = value[:, k * 128 : (k + 1) * 128]
            for channel in range(2):
                for j in range(2):
                    row = 12 + 4 * layer + 2 * channel + j
                    out[k, row : row + 1] = b_query[layer][channel : channel + 1, j * 128 : (j + 1) * 128]
            for q in range(4):
                for j in range(2):
                    row = 20 + 8 * layer + 2 * q + j
                    out[k, row : row + 1] = b_first[layer][q, :, j * 128 : (j + 1) * 128]
    out[:, 36:] = jnp.zeros((4, 12, lanes), f32)


def turn(values, place_z, back):
    rows = values.shape[0]
    chunks = values.reshape(rows, 4, lanes)
    order = (place_z - jnp.arange(4)) % 4
    return jnp.concatenate(
        [lax.dynamic_slice_in_dim(values, order[k] * lanes, lanes, 1) for k in range(4)], axis=1
    )


def body_four(x_in, w_qkv, b_qv, w_proj, w_fc1, b_fc1, w_fc2, gains, biases, cotangent):
    z, c, t = lax.axis_index("shard"), lax.axis_index("ctx"), lax.axis_index("tp")
    place = jnp.stack([z, c, t]).astype(jnp.int32)
    flat = jnp.concatenate([array.reshape(-1) for array in (gains, biases, b_qv, b_fc1)])
    small = jnp.pad(flat, (0, 32 * lanes - flat.shape[0])).reshape(32, lanes)

    kinds = ("qkv", "proj", "first", "second", "first", "second")
    send = pack(
        place, kinds, (w_qkv, w_proj, w_fc1, w_fc2, w_fc1, w_fc2), (1, 1, 0, 0, 1, 1), whole_quarters=False
    )
    full = gather(send)
    local_a, send_a = pack(place, ("qkv", "proj", "small"), (w_qkv, w_proj, small), (0, 0, 0))
    pair_own = turn(jnp.concatenate([x_in[:, 0], cotangent[:, 0]]), z, False)
    pair_peer = swap_tp(pair_own)
    got_a = far_chunks(send_a)
    far_a = stack(place, got_a)
    chip_a = swap_x(far_a)
    group_a0 = [local_a, far_a, swap_core(far_a), chip_a, swap_core(chip_a)]
    small_parts = small_of(group_a0)
    parts = {
        "qkv": [pieces_of(group_a0, 192, 0), gathered_rows(full, 192, 0)],
        "proj": [pieces_of(group_a0, 64, 192), gathered_rows(full, 64, 192)],
        "first": [gathered_rows(full, 256, 256), gathered_rows(full, 256, 768)],
        "second": [gathered_rows(full, 256, 512), gathered_rows(full, 256, 1024)],
    }
    square, wide = (256, 512), (256, 256)
    saved = []
    for layer in range(2):
        source = [pair_own, pair_peer] if layer == 0 else [middle, partial, swap_tp(partial)]
        more = [(square, f32)] if layer == 0 else []
        state, low_in, q, kv, w_all, *passed = run(
            query_kernel(layer, layer == 0),
            [(square, f32), (square, bf16), (wide, bf16), (square, bf16), ((4, 4, 32, 768), bf16)] + more,
            place,
            source + small_parts + parts["qkv"][layer],
        )
        if layer == 0:
            g_all = passed[0]
        kv_chip = swap_x(kv)
        chunks = [kv, swap_core(kv), kv_chip, swap_core(kv_chip)]
        attn, lse, partial, w_out = run(
            functools.partial(attend_kernel, len(parts["proj"][layer])),
            [(wide, bf16), ((256, lanes), f32), (square, bf16), ((4, 64, 512), bf16)],
            place,
            [q] + chunks + parts["proj"][layer],
        )
        middle, low_mid, pre, partial = run(
            mlp_kernel(layer),
            [(square, f32), (square, bf16), ((256, 1024), f32), (square, bf16)],
            place,
            [state, partial, swap_tp(partial)] + small_parts + parts["first"][layer] + parts["second"][layer],
        )
        saved.append((state, low_in, q, chunks, w_all, attn, lse, w_out, middle, low_mid, pre))

    received = swap_tp(partial[128:]).astype(f32)
    output = None
    bias_last = jnp.concatenate([small_parts[0][0][0, 267:268], small_parts[1][0][:, 267]]).reshape(1, 512)
    output = middle[:128] + partial[:128].astype(f32) + received + bias_last.astype(f32)
    output = turn(output.astype(bf16), z, True)[:, None]

    hidden_outs = [
        (square, bf16),
        ((1, 512), f32),
        ((4, 1, 256), f32),
        ((2, 4, 512, lanes), bf16),
        ((4, 512, lanes), bf16),
        ((4, 512, lanes), bf16),
    ]
    sums_mid, bias_mlp, b_query, b_first = [0, 0], [0, 0], [0, 0], [0, 0]
    hidden = [None, None]
    for layer in (1, 0):
        state, low_in, q, chunks, w_all, attn, lse, w_out, middle, low_mid, pre = saved[layer]
        tail = [pre, low_mid] + parts["first"][layer] + parts["second"][layer]
        if layer == 1:
            grad_state = g_all
            partial, bias_mlp[1], b_first[1], *grads = run(
                top_kernel, hidden_outs, place, [grad_state] + tail
            )
        else:
            head_own, head_far = halve(place, [grads])
            grad_state, sums_in, partial, bias_mlp[0], b_first[0], *grads = run(
                lower_kernel(0),
                [(square, f32), ((2, 512), f32)] + hidden_outs,
                place,
                [grad_mid, partial, swap_tp(partial), saved[1][0]] + small_parts + tail,
                after=[head_own],
            )
        own, far = halve(place, [grads])
        behind = [own]
        if layer == 0:
            both = quarter(place, head_own, head_far, after=[own])
            heads_sum = lax.psum_scatter(both, "shard", scatter_dimension=0)
            behind = [both]
        grad_mid, sums_mid[layer], gw_out, dq, keep, send = run(
            attend_back_kernel(layer),
            [
                (square, f32),
                ((3, 512), f32),
                ((4, 64, 512), bf16),
                (wide, bf16),
                ((2, 256, 512), bf16),
                ((2, 256, 512), bf16),
            ],
            place,
            [partial, swap_tp(partial), middle, grad_state] + small_parts + [attn, w_out, q] + chunks + [lse],
            after=behind,
        )
        both = quarter(place, own, far, after=[keep])
        hidden[layer] = lax.psum_scatter(both, "shard", scatter_dimension=0)
        behind = [both]
        dkv, chip = run(halve_kernel, [(square, bf16)] * 2, place, [keep, swap_core(send)], after=behind)
        partial, b_query[layer], *grads = run(
            query_back_kernel,
            [
                (square, bf16),
                ((2, 256), f32),
                ((2, 4, 256, lanes), bf16),
                ((4, 256, lanes), bf16),
                ((4, 256, lanes), bf16),
            ],
            place,
            [dq, dkv, swap_x(chip), low_in, w_all, gw_out],
            scratch=[pltpu.VMEM((4, 4, 32, 768), bf16)],
            after=[output] if layer == 1 else [],
        )
    own, far = halve(place, [grads])
    grad_x, sums = run(
        last_kernel,
        [((128, 512), f32), ((4, 48, lanes), f32)],
        place,
        [grad_mid, partial, swap_tp(partial), saved[0][0]]
        + small_parts
        + [sums_in]
        + sums_mid
        + bias_mlp
        + b_query
        + b_first,
        after=[own],
    )
    pieces = run(last_quarter_kernel, [((304, lanes), bf16)] * 4, place, [own, swap_x(far), sums])
    grad_x = turn(grad_x, z, True)[:, None]
    (joined,) = run(
        join_kernel, [((1280, lanes), bf16)], place, [hidden[1], hidden[0], heads_sum], after=pieces[:1]
    )
    upper = collect(joined)
    got = [shift(pieces[k], 4 - k) for k in (1, 2, 3)]
    (last,) = run(
        last_total_kernel,
        [((304, lanes), bf16)],
        place,
        [pieces[0]] + got,
        after=upper[1:3],
    )
    last_parts = collect(last)
    outs_heads = heads_out(place, upper, 1, w_qkv.shape, w_proj.shape, [], 1024, after=[last])
    outs_hidden = hidden_out(place, upper, 1, w_fc1.shape, w_fc2.shape, [], 0, after=[last])
    grad_fc1, grad_fc2 = hidden_out(
        place, upper, 0, w_fc1.shape, w_fc2.shape, outs_hidden, 512, after=[last]
    )
    total = sum(part[256:].astype(f32) for part in last_parts)
    grad_gains = total[:4].reshape(gains.shape)
    grad_biases = total[4:12].reshape(biases.shape)
    rest_q = total[12:20].reshape(2, 2, 4, 64)
    rest_f = total[20:36].reshape(2, 16, 64)
    grad_b_qv = lax.dynamic_slice_in_dim(rest_q, z * 16, 16, 3)
    grad_b_fc1 = lax.dynamic_slice_in_dim(rest_f, z * 16, 16, 2)

    grad_qkv, grad_proj = heads_out(place, last_parts, 0, w_qkv.shape, w_proj.shape, outs_heads, 0)
    return (
        output, grad_x, grad_qkv, grad_b_qv, grad_proj, grad_fc1, grad_b_fc1, grad_fc2, grad_gains, grad_biases
    )


def body(*args):
    x_in, w_qkv, b_qv, w_proj, w_fc1 = args[:5]
    expected = ((128, 1, 512), (2, 3, 128, 256), (2, 2, 4, 16), (2, 256, 128), (2, 128, 1024))
    sizes = (lax.axis_size("shard"), lax.axis_size("ctx"), lax.axis_size("tp"))
    shapes = tuple(array.shape for array in (x_in, w_qkv, b_qv, w_proj, w_fc1))
    if sizes == (4, 4, 2) and shapes == expected:
        return body_four(*args)
    return body_any(*args)


def solution(mesh):
    return jax.shard_map(
        body,
        mesh=mesh,
        in_specs=(
            P(("ctx", "tp"), "shard", None),
            P(None, None, "shard", "tp"),
            P(None, None, "tp", "shard"),
            P(None, "tp", "shard"),
            P(None, "shard", "tp"),
            P(None, "tp", "shard"),
            P(None, "tp", "shard"),
            P(None, None, "shard"),
            P(None, None, "shard"),
            P(("ctx", "tp"), "shard", None),
        ),
        out_specs=(
            P(("ctx", "tp"), "shard", None),
            P(("ctx", "tp"), "shard", None),
            P(None, None, "shard", "tp"),
            P(None, None, "tp", "shard"),
            P(None, "tp", "shard"),
            P(None, "shard", "tp"),
            P(None, "tp", "shard"),
            P(None, "tp", "shard"),
            P(None, None, "shard"),
            P(None, None, "shard"),
        ),
        check_vma=False,
    )
```

```python
import functools
import math

import jax
import jax.numpy as jnp
from jax import lax
from jax.experimental import pallas as pl
from jax.experimental.pallas import tpu as pltpu
from jax.sharding import PartitionSpec as P

epsilon = 1e-05
masked_value = -1e30
lanes = 128
f32 = jnp.float32
bf16 = jnp.bfloat16


def normalize(values):
    center = jnp.mean(values, axis=-1, keepdims=True)
    shifted = values - center
    scale_inv = lax.rsqrt(jnp.mean(shifted * shifted, axis=-1, keepdims=True) + epsilon)
    return (shifted * scale_inv, scale_inv)


def norm_back(grad_norm, normed, scale_inv):
    mean_grad = jnp.mean(grad_norm, axis=-1, keepdims=True)
    mean_prod = jnp.mean(grad_norm * normed, axis=-1, keepdims=True)
    return scale_inv * (grad_norm - mean_grad - normed * mean_prod)


def gelu_tanh(values):
    return jax.nn.gelu(values, approximate=True)


def dot(pattern, left, right):
    return jnp.einsum(pattern, left, right, preferred_element_type=f32)


def to_rows(array):
    rows, columns = array.shape[-2:]
    if columns % lanes or rows % 16:
        return array.reshape(-1, lanes)
    tiles = array.reshape(-1, rows, columns // lanes, lanes)
    return jnp.swapaxes(tiles, 1, 2).reshape(-1, lanes)


def from_rows(packed, shape):
    rows, columns = shape[-2:]
    lead = packed.shape[:-2]
    if columns % lanes or rows % 16:
        return packed.reshape(lead + tuple(shape))
    count = math.prod(shape[:-2])
    tiles = packed.reshape(lead + (count, columns // lanes, rows, lanes))
    return jnp.swapaxes(tiles, -3, -2).reshape(lead + tuple(shape))


def small_rows(arrays):
    flat = jnp.concatenate([array.reshape(-1) for array in arrays])
    size = -(-flat.shape[0] // (64 * lanes)) * 64 * lanes
    return jnp.pad(flat, (0, size - flat.shape[0])).reshape(-1, lanes)


def join(gathered, axis):
    moved = jnp.moveaxis(gathered, 0, axis)
    shape = moved.shape
    return moved.reshape(shape[:axis] + (shape[axis] * shape[axis + 1],) + shape[axis + 2 :])


def split(whole, axis, shards):
    shape = whole.shape
    parts = whole.reshape(shape[:axis] + (shards, shape[axis] // shards) + shape[axis + 1 :])
    return jnp.moveaxis(parts, axis, 0)


def swap_tp(values):
    return lax.ppermute(values, "tp", [(0, 1), (1, 0)])


def swap_core(values):
    return lax.ppermute(values, "ctx", [(0, 1), (1, 0), (2, 3), (3, 2)])


def swap_x(values):
    return lax.ppermute(values, "ctx", [(0, 2), (2, 0), (1, 3), (3, 1)])


def swap_both(values):
    return lax.ppermute(values, "ctx", [(0, 3), (3, 0), (1, 2), (2, 1)])


def other_half(values):
    half = values.shape[0] // 2
    return jnp.concatenate([values[half:], values[:half]])


def gather_packed(packed, shards):
    quarter = packed.shape[0] // 4
    own = lax.dynamic_slice_in_dim(packed, lax.axis_index("ctx") * quarter, quarter, 0)
    return lax.all_gather(own, ("shard", "ctx"), axis=0, tiled=True).reshape(
        shards, packed.shape[0], lanes
    )


def halves(values, bit):
    half = values.shape[1] // 2
    keep = lax.dynamic_slice_in_dim(values, bit * half, half, 1)
    send = lax.dynamic_slice_in_dim(values, (1 - bit) * half, half, 1)
    return keep, send


def paired(own, other, bit):
    return jnp.where(
        bit == 0, jnp.concatenate([own, other]), jnp.concatenate([other, own])
    )


def reduce_packed(packed):
    place = lax.axis_index("ctx")
    core, chip = place % 2, place // 2
    keep, send = halves(packed, core)
    half = (keep.astype(f32) + swap_core(send).astype(f32)).astype(bf16)
    keep, send = halves(half, chip)
    quarter = (keep.astype(f32) + swap_x(send).astype(f32)).astype(bf16)
    parts = lax.all_to_all(quarter, "shard", split_axis=0, concat_axis=0, tiled=True)
    total = jnp.sum(parts.astype(f32), axis=0).astype(bf16)
    both = paired(total, swap_x(total), chip)
    return paired(both, swap_core(both), core)


def positions(offsets, tp_place, chunk, block):
    half = block // 2
    return chunk * block + (offsets + tp_place * half) % block


def attention_mask(block):
    place, tp_place = lax.axis_index("ctx"), lax.axis_index("tp")
    offsets = jnp.arange(block, dtype=jnp.int32)
    rows = positions(offsets, tp_place, place, block)
    keys = jnp.concatenate([positions(offsets, tp_place, place ^ j, block) for j in range(4)])
    return keys[None, :] <= rows[:, None]


def head_split(values, heads):
    return values.reshape(values.shape[0], heads, values.shape[1] // heads)


def attend(queries, key_all, value_all, mask, heads):
    scale_factor = (queries.shape[1] // heads) ** (-0.5)
    scores = dot("qhe,khe->hqk", head_split(queries, heads), head_split(key_all, heads))
    scores = jnp.where(mask, scores * scale_factor, masked_value)
    row_top = jnp.max(scores, axis=-1, keepdims=True)
    exponent = jnp.exp(scores - row_top)
    totals = jnp.sum(exponent, axis=-1, keepdims=True)
    probs = (exponent / totals).astype(bf16)
    out = dot("hqk,khe->qhe", probs, head_split(value_all, heads))
    return out.reshape(queries.shape).astype(bf16), row_top + jnp.log(totals)


def attend_back(queries, key_all, value_all, mask, heads, log_sums, grad_out):
    scale_factor = (queries.shape[1] // heads) ** (-0.5)
    query_heads, key_heads = head_split(queries, heads), head_split(key_all, heads)
    grad_heads = head_split(grad_out, heads)
    scores = dot("qhe,khe->hqk", query_heads, key_heads)
    scores = jnp.where(mask, scores * scale_factor, masked_value)
    probs = jnp.exp(scores - log_sums)
    grad_probs = dot("qhe,khe->hqk", grad_heads, head_split(value_all, heads))
    row_dot = jnp.sum(probs * grad_probs, axis=-1, keepdims=True)
    grad_scores = (probs * (grad_probs - row_dot)).astype(bf16)
    grad_q = dot("hqk,khe->qhe", grad_scores, key_heads) * scale_factor
    grad_k = dot("hqk,qhe->khe", grad_scores, query_heads) * scale_factor
    grad_v = dot("hqk,qhe->khe", probs.astype(bf16), grad_heads)
    return (
        grad_q.reshape(queries.shape).astype(bf16),
        jnp.concatenate(
            [grad_k.reshape(key_all.shape), grad_v.reshape(key_all.shape)], axis=1
        ).astype(bf16),
    )


def body_any(x_in, w_qkv, b_qv, w_proj, w_fc1, b_fc1, w_fc2, gains, biases, cotangent):
    depth = w_qkv.shape[0]
    shards = lax.axis_size("shard")
    own_rows, width = x_in.shape[0], x_in.shape[2]
    block = 2 * own_rows
    heads = b_qv.shape[2]
    half_width = w_qkv.shape[3]
    hidden = w_fc1.shape[2]

    small_shapes = [gains.shape, biases.shape, b_qv.shape, b_fc1.shape]
    small = small_rows([gains, biases, b_qv, b_fc1])
    group_a0 = jnp.concatenate([small, to_rows(w_qkv[0])])
    group_b0 = jnp.concatenate([to_rows(w_proj[0]), to_rows(w_fc1[0]), to_rows(w_fc2[0])])
    rest = []
    for index in range(1, depth):
        rest += [to_rows(w_qkv[index]), to_rows(w_proj[index]), to_rows(w_fc1[index]), to_rows(w_fc2[index])]
    group_rest = jnp.concatenate(rest)

    gathered_a0 = gather_packed(group_a0, shards)
    gathered_b0 = gather_packed(group_b0, shards)
    gathered_rest = gather_packed(group_rest, shards)

    def cutter(gathered, start):
        place = [start]

        def take(shape, axis):
            rows = math.prod(shape) // lanes
            piece = from_rows(gathered[:, place[0] : place[0] + rows], shape)
            place[0] += rows
            return join(piece, axis)

        return take

    shape_qkv, shape_proj = w_qkv.shape[1:], w_proj.shape[1:]
    shape_fc1, shape_fc2 = w_fc1.shape[1:], w_fc2.shape[1:]
    take_a, take_b, take_r = cutter(gathered_a0, small.shape[0]), cutter(gathered_b0, 0), cutter(gathered_rest, 0)
    weights = []
    for index in range(depth):
        take_q, take_o = (take_a, take_b) if index == 0 else (take_r, take_r)
        weights.append(
            (take_q(shape_qkv, 1), take_o(shape_proj, 1), take_o(shape_fc1, 0), take_o(shape_fc2, 1))
        )
    flat = gathered_a0[:, : small.shape[0]].reshape(shards, -1)
    vectors, start = [], 0
    for shape in small_shapes:
        size = math.prod(shape)
        piece = flat[:, start : start + size].reshape((shards,) + shape)
        vectors.append(join(piece, len(shape) - 1).astype(f32))
        start += size
    gain_all, bias_all, b_qv_all, b_fc1_all = vectors

    mask = attention_mask(block)
    x_own = x_in[:, 0]
    state = jnp.concatenate([x_own, swap_tp(x_own)]).astype(f32)
    g_own = cotangent[:, 0]
    grad_state = jnp.concatenate([g_own, swap_tp(g_own)]).astype(f32)

    stored = []
    for index in range(depth):
        w_query, w_out, w_first, w_second = weights[index]
        normed_in, scale_in = normalize(state)
        low_in = (normed_in * gain_all[index, 0] + bias_all[index, 0]).astype(bf16)
        bias_q = b_qv_all[index, 0].reshape(half_width)
        bias_v = b_qv_all[index, 1].reshape(half_width)
        queries = (dot("rd,df->rf", low_in, w_query[0]) + bias_q).astype(bf16)
        keys = dot("rd,df->rf", low_in, w_query[1]).astype(bf16)
        values = (dot("rd,df->rf", low_in, w_query[2]) + bias_v).astype(bf16)
        kv_own = jnp.concatenate([keys, values], axis=1)
        kv_chip = swap_x(kv_own)
        kv_all = jnp.concatenate([kv_own, swap_core(kv_own), kv_chip, swap_core(kv_chip)])
        key_all, value_all = kv_all[:, :half_width], kv_all[:, half_width:]
        attn, log_sums = attend(queries, key_all, value_all, mask, heads)
        attn_other = other_half(swap_tp(attn))
        w_out_other = swap_tp(w_out)
        middle = (
            state
            + dot("rf,fd->rd", attn, w_out)
            + dot("rf,fd->rd", attn_other, w_out_other)
            + bias_all[index, 1]
        )
        normed_mid, scale_mid = normalize(middle)
        low_mid = (normed_mid * gain_all[index, 1] + bias_all[index, 2]).astype(bf16)
        pre_act = dot("rd,df->rf", low_mid, w_first) + b_fc1_all[index].reshape(hidden)
        act = gelu_tanh(pre_act).astype(bf16)
        partial = dot("rf,fd->rd", act, w_second)
        if index == depth - 1:
            received = swap_tp(partial[own_rows:].astype(bf16)).astype(f32)
            output = middle[:own_rows] + partial[:own_rows] + received + bias_all[index, 3]
        else:
            received = other_half(swap_tp(partial.astype(bf16))).astype(f32)
            state = middle + partial + received + bias_all[index, 3]
        stored.append(
            (normed_in, scale_in, low_in, queries, key_all, value_all, log_sums, attn,
             normed_mid, scale_mid, low_mid, pre_act, act)
        )
    output = output.astype(bf16)[:, None]

    results = [None] * depth
    for index in reversed(range(depth)):
        w_query, w_out, w_first, w_second = weights[index]
        (normed_in, scale_in, low_in, queries, key_all, value_all, log_sums, attn,
         normed_mid, scale_mid, low_mid, pre_act, act) = stored[index]
        grad_bias_mlp = jnp.sum(grad_state, axis=0)
        grad_low = grad_state.astype(bf16)
        grad_hidden = dot("rd,fd->rf", grad_low, w_second)
        unused, gelu_pull = jax.vjp(gelu_tanh, pre_act)
        grad_pre = gelu_pull(grad_hidden)[0].astype(bf16)
        grad_w_second = dot("rf,rd->fd", act, grad_low)
        grad_w_first = dot("rd,rf->df", low_mid, grad_pre)
        grad_b_first = jnp.sum(grad_pre, axis=0, dtype=f32)
        partial = dot("rf,df->rd", grad_pre, w_first)
        mlp_rows = jnp.concatenate(
            [
                jax.vmap(to_rows)(split(grad_w_first.astype(bf16), 0, shards)),
                jax.vmap(to_rows)(split(grad_w_second.astype(bf16), 1, shards)),
            ],
            axis=1,
        )
        mlp_total = reduce_packed(mlp_rows)
        grad_mid = partial + other_half(swap_tp(partial.astype(bf16))).astype(f32)
        grad_gain_mid = jnp.sum(grad_mid * normed_mid, axis=0)
        grad_beta_mid = jnp.sum(grad_mid, axis=0)
        grad_middle = grad_state + norm_back(grad_mid * gain_all[index, 1], normed_mid, scale_mid)
        grad_bias_attn = jnp.sum(grad_middle, axis=0)
        grad_low = grad_middle.astype(bf16)
        grad_attn = dot("rd,fd->rf", grad_low, w_out).astype(bf16)
        grad_w_out = dot("rf,rd->fd", attn, grad_low)
        grad_q, grad_kv = attend_back(
            queries, key_all, value_all, mask, heads, log_sums, grad_attn
        )
        part = grad_kv.reshape(4, block, 2 * half_width)
        sent = swap_core(jnp.stack([part[1], part[3]])).astype(f32)
        mine = part[0].astype(f32) + sent[0]
        chip = (part[2].astype(f32) + sent[1]).astype(bf16)
        grad_kv = (mine + swap_x(chip).astype(f32)).astype(bf16)
        grad_qkv = jnp.stack([grad_q, grad_kv[:, :half_width], grad_kv[:, half_width:]])
        grad_w_query = dot("rd,crf->cdf", low_in, grad_qkv)
        grad_b_query = jnp.sum(grad_qkv[0::2], axis=1, dtype=f32)
        partial = dot("crf,cdf->rd", grad_qkv, w_query)
        grad_in = partial + other_half(swap_tp(partial.astype(bf16))).astype(f32)
        grad_gain_in = jnp.sum(grad_in * normed_in, axis=0)
        grad_beta_in = jnp.sum(grad_in, axis=0)
        grad_state = grad_middle + norm_back(grad_in * gain_all[index, 0], normed_in, scale_in)

        vectors = [
            jnp.stack([grad_gain_in, grad_gain_mid]),
            jnp.stack([grad_beta_in, grad_bias_attn, grad_beta_mid, grad_bias_mlp]),
            grad_b_query.reshape(2, heads, half_width // heads),
            grad_b_first.reshape(b_fc1_all.shape[1:]),
        ]
        parts = [split(vector, vector.ndim - 1, shards) for vector in vectors]
        part_shapes = [part.shape[1:] for part in parts]
        attn_rows = jnp.concatenate(
            [
                jax.vmap(to_rows)(split(grad_w_query.astype(bf16), 1, shards)),
                jax.vmap(to_rows)(split(grad_w_out.astype(bf16), 1, shards)),
                jax.vmap(lambda *own: small_rows(own))(*parts).astype(bf16),
            ],
            axis=1,
        )
        attn_total = reduce_packed(attn_rows)

        def pieces(total, shapes):
            place, out = 0, []
            for shape in shapes:
                rows = math.prod(shape) // lanes
                out.append(from_rows(total[place : place + rows], shape).astype(f32))
                place += rows
            return out, total[place:].reshape(-1)

        (out_fc1, out_fc2), unused = pieces(mlp_total, [shape_fc1, shape_fc2])
        (out_qkv, out_proj), tail = pieces(attn_total, [shape_qkv, shape_proj])
        small_out, start = [], 0
        for shape in part_shapes:
            size = math.prod(shape)
            small_out.append(tail[start : start + size].reshape(shape).astype(f32))
            start += size
        results[index] = (
            out_qkv, small_out[2], out_proj, out_fc1, small_out[3], out_fc2, small_out[0], small_out[1]
        )
    stacked = tuple(
        jnp.stack([results[index][member] for index in range(depth)]) for member in range(8)
    )
    return (output, grad_state[:own_rows, None]) + stacked


def compiler_params():
    return pltpu.CompilerParams(vmem_limit_bytes=56 * 2**20)


def whole(array):
    zeros = (0,) * array.ndim
    return pl.BlockSpec(array.shape, lambda i: zeros)


def rows_at(array, rows, start, lead=None, first=0):
    lead = array.shape[0] if lead is None else lead
    return pl.BlockSpec((lead, rows, lanes), lambda i: (first, start // rows, 0))


def run(kernel, outs, place, operands, scratch=(), flops=2**20, after=()):
    arrays, specs = [], []
    count = 1 + len(operands)

    def inner(*refs):
        kernel(*refs[:count], *refs[count + len(after) :])

    for operand in operands:
        array, spec = operand if isinstance(operand, tuple) else (operand, whole(operand))
        arrays.append(array)
        specs.append(spec)
    out_shape = [jax.ShapeDtypeStruct(shape, kind) for shape, kind in outs]
    after = list(after)
    arrays += after
    specs += [pl.BlockSpec(memory_space=pl.ANY)] * len(after)
    call = pl.pallas_call(
        inner,
        grid=(1,),
        out_shape=out_shape,
        in_specs=[pl.BlockSpec(memory_space=pltpu.SMEM)] + specs,
        out_specs=[whole(shape) for shape in out_shape],
        scratch_shapes=list(scratch),
        compiler_params=compiler_params(),
        cost_estimate=pl.CostEstimate(flops=flops, bytes_accessed=1024, transcendentals=0),
    )
    return list(call(place, *arrays))


def mm(left, right):
    return lax.dot_general(left, right, (((1,), (0,)), ((), ())), preferred_element_type=f32)


def mm_nt(left, right):
    return lax.dot_general(left, right, (((1,), (1,)), ((), ())), preferred_element_type=f32)


def mm_tn(left, right):
    return lax.dot_general(left, right, (((0,), (0,)), ((), ())), preferred_element_type=f32)


def lane_join(parts):
    return jnp.concatenate(parts, axis=1)


def row_join(parts):
    return jnp.concatenate(parts, axis=0)


class Pieces:
    def __init__(self, refs, place):
        self.refs, self.place = refs, place

    def tile(self, k, p, start, rows):
        if len(self.refs) == 1:
            z, c = self.place[0], self.place[1]
            return self.refs[0][(z - k + 4) % 4, p ^ c, start : start + rows]
        if k == 0:
            return self.refs[0][p, start : start + rows]
        return self.refs[1 + p][k - 1, start : start + rows]


def first_block(pieces, p):
    return row_join(
        [lane_join([pieces.tile(k, p, j * 128, 128) for j in range(2)]) for k in range(4)]
    )


def second_block(pieces, p):
    return lane_join([pieces.tile(k, p, 0, 256) for k in range(4)])


def small_row(small_local, small_far, row):
    parts = [small_local[0, row : row + 1]] + [small_far[k, row : row + 1] for k in range(3)]
    return lane_join(parts).astype(f32)


def spread(small_local, small_far, row, place_z, half, later=None):
    def rows_from(row):
        return row_join(
            [small_local[0, row : row + 1]] + [small_far[k, row : row + 1] for k in range(3)]
        ).astype(f32)

    source = rows_from(row)
    if later is not None:
        source = jnp.where(later == 0, source, rows_from(row + 1))
    source = source.astype(bf16)
    take = lax.broadcasted_iota(jnp.int32, (128, 256), 0)
    lane = lax.broadcasted_iota(jnp.int32, (128, 256), 1)
    wanted = half * 64 + (lane // 64) * 16 + lane % 16
    table = (take == wanted).astype(f32).astype(bf16)
    rows = mm(source, table)
    chunk = lax.broadcasted_iota(jnp.int32, (4, 256), 0)
    lane = lax.broadcasted_iota(jnp.int32, (4, 256), 1)
    keep = (lane % 64) // 16 == (place_z - chunk + 4) % 4
    return jnp.sum(jnp.where(keep, rows, 0.0), axis=0, keepdims=True)


def pack_kernel(kinds):
    def kernel(place, *refs):
        c = place[1]
        out, send = refs[-2:]
        start = 0
        for ref, kind in zip(refs, kinds):
            for q in range(4):
                to = q ^ c
                if kind == "first":
                    for j in range(2):
                        column = (2 * q + j) * 128
                        out[to, start + j * 128 : start + (j + 1) * 128] = ref[0, :, column : column + 128]
                elif kind == "second":
                    out[to, start : start + 256] = ref[0, q * 256 : (q + 1) * 256]
                elif kind == "proj":
                    out[to, start : start + 64] = ref[0, q * 64 : (q + 1) * 64]
                elif kind == "qkv":
                    for tile in range(6):
                        row = start + tile * 32
                        column = (tile % 2) * 128
                        out[to, row : row + 32] = ref[0, tile // 2, q * 32 : (q + 1) * 32, column : column + 128]
                else:
                    out[to, start : start + 32] = ref[...]
            start += kind_rows[kind]
        send[...] = out[0]

    return kernel


def quarter_pack_kernel(kinds):
    def kernel(place, *refs):
        out = refs[-1]
        for q in range(4):

            @pl.when(place[1] == q)
            def write(q=q):
                start = 0
                for ref, kind in zip(refs, kinds):
                    if kind == "first":
                        for j in range(2):
                            column = (2 * q + j) * 128
                            out[start + j * 128 : start + (j + 1) * 128] = ref[0, :, column : column + 128]
                    elif kind == "second":
                        out[start : start + 256] = ref[0, q * 256 : (q + 1) * 256]
                    elif kind == "proj":
                        out[start : start + 64] = ref[0, q * 64 : (q + 1) * 64]
                    else:
                        for tile in range(6):
                            row = start + tile * 32
                            column = (tile % 2) * 128
                            out[row : row + 32] = ref[0, tile // 2, q * 32 : (q + 1) * 32, column : column + 128]
                    start += kind_rows[kind]

    return kernel


kind_rows = {"first": 256, "second": 256, "proj": 64, "qkv": 192, "small": 32}


def pack(place, kinds, arrays, index, after=(), whole_quarters=True):
    rows = sum(kind_rows[kind] for kind in kinds)
    operands = []
    for kind, array, at in zip(kinds, arrays, index):
        if kind == "small":
            operands.append(array)
        else:
            block = (1,) + array.shape[1:]
            at = (at,) + (0,) * (array.ndim - 1)
            operands.append((array, pl.BlockSpec(block, lambda i, at=at: at)))
    if not whole_quarters:
        return run(quarter_pack_kernel(kinds), [((rows, lanes), bf16)], place, operands, after=after)[0]
    return run(
        pack_kernel(kinds), [((4, rows, lanes), bf16), ((rows, lanes), bf16)], place, operands, after=after
    )


def gather(quarter):
    full = lax.all_gather(quarter, ("shard", "ctx"), axis=0)
    return full.reshape((4, 4) + quarter.shape)


def gathered_rows(array, rows, start):
    return [(array, pl.BlockSpec((4, 4, rows, lanes), lambda i: (0, 0, start // rows, 0)))]


def shift(values, step):
    return lax.ppermute(values, "shard", [(z, (z + step) % 4) for z in range(4)])


def far_chunks(send):
    return [shift(send, k) for k in (1, 2, 3)]


def stack_kernel(place, one, two, three, out):
    for k, ref in enumerate((one, two, three)):
        out[k] = ref[...]


def stack(place, got, after=()):
    return run(stack_kernel, [((3,) + got[0].shape, bf16)], place, got, after=after)[0]


def pieces_of(group, rows, start):
    return [(array, rows_at(array, rows, start)) for array in group]


def small_of(group):
    return [(group[0], rows_at(group[0], 32, 256, lead=1)), (group[1], rows_at(group[1], 32, 256))]


def query_kernel(index, first_layer):
    def kernel(place, *refs):
        c = place[1]
        if first_layer:
            own, peer, small_local, small_far = refs[:4]
            pieces = Pieces(refs[4:9], place)
            grad_out = refs[14]
            grad_out[...] = row_join([own[128:], peer[128:]]).astype(f32)
            state_out, low_out, q_out, kv_out, w_out = refs[9:14]
            state = row_join([own[:128], peer[:128]]).astype(f32)
        else:
            middle, mine, other, small_local, small_far = refs[:5]
            pieces = Pieces(refs[5:6], place)
            state_out, low_out, q_out, kv_out, w_out = refs[6:]
            received = row_join([other[128:], other[:128]])
            state = (
                middle[...]
                + mine[...].astype(f32)
                + received.astype(f32)
                + small_row(small_local, small_far, 4 + 4 * (index - 1) + 3)
            )
        for k in range(4):
            for p in range(4):
                for tile in range(6):
                    w_out[k, p ^ c, :, tile * 128 : (tile + 1) * 128] = pieces.tile(k, p, tile * 32, 32)
        state_out[...] = state
        normed, scale = normalize(state)
        low = (
            normed * small_row(small_local, small_far, 2 * index)
            + small_row(small_local, small_far, 4 + 4 * index)
        ).astype(bf16)
        low_out[...] = low
        w_all = w_out[...].reshape(512, 768)
        row = 12 + index
        bias_q = spread(small_local, small_far, row, place[0], 0)
        bias_v = spread(small_local, small_far, row, place[0], 1)
        kv_out[:, :256] = mm(low, w_all[:, 256:512]).astype(bf16)
        kv_out[:, 256:] = (mm(low, w_all[:, 512:]) + bias_v).astype(bf16)
        q_out[...] = (mm(low, w_all[:, :256]) + bias_q).astype(bf16)

    return kernel


def seen(place, j):
    c, t = place[1], place[2]
    if j:
        return None
    row = lax.broadcasted_iota(jnp.int32, (256, 256), 0) ^ (t * 128)
    key = lax.broadcasted_iota(jnp.int32, (256, 256), 1) ^ (t * 128)
    return key <= row


def masked_scores(query, chunks, own_mask, place):
    parts = []
    for j in range(4):
        scores = mm_nt(query, chunks[j]) * 0.125
        if j == 0:
            scores = jnp.where(own_mask, scores, masked_value)
        else:
            scores = jnp.where((place[1] ^ j) < place[1], scores, masked_value)
        parts.append(scores)
    return parts


def attend_kernel(count, place, *refs):
    c = place[1]
    q, chunks = refs[0], refs[1:5]
    pieces = Pieces(refs[5 : 5 + count], place)
    attn_out, lse_out, partial_out, w_out = refs[5 + count :]
    for k in range(4):
        for p in range(4):
            w_out[p ^ c, :, k * 128 : (k + 1) * 128] = pieces.tile(k, p, 0, 64)
    own_mask = seen(place, 0)
    results = []
    for head in range(4):
        low, high = head * 64, (head + 1) * 64
        parts = masked_scores(q[:, low:high], [chunk[:, low:high] for chunk in chunks], own_mask, place)
        scores = lane_join(parts)
        top = jnp.max(scores, axis=1, keepdims=True)
        exponent = jnp.exp(scores - top)
        total = jnp.sum(exponent, axis=1, keepdims=True)
        values = row_join([chunk[:, 256 + low : 256 + high] for chunk in chunks])
        results.append(mm(exponent.astype(bf16), values) / total)
        lse_out[:, head : head + 1] = top + jnp.log(total)
    attn = lane_join(results).astype(bf16)
    attn_out[...] = attn
    partial_out[...] = mm(attn, w_out[...].reshape(256, 512)).astype(bf16)


def mlp_kernel(index):
    def kernel(place, *refs):
        state, mine, other, small_local, small_far = refs[:5]
        first, second = Pieces(refs[5:6], place), Pieces(refs[6:7], place)
        middle_out, low_out, pre_out, partial_out = refs[7:]
        received = row_join([other[128:], other[:128]])
        middle = (
            state[...]
            + mine[...].astype(f32)
            + received.astype(f32)
            + small_row(small_local, small_far, 4 + 4 * index + 1)
        )
        middle_out[...] = middle
        normed, scale = normalize(middle)
        low = (
            normed * small_row(small_local, small_far, 2 * index + 1)
            + small_row(small_local, small_far, 4 + 4 * index + 2)
        ).astype(bf16)
        low_out[...] = low
        total = None
        for p in range(4):
            q = p ^ place[1]
            bias = spread(small_local, small_far, 14 + 2 * index, place[0], q % 2, q // 2)
            pre = mm(low, first_block(first, p)) + bias
            pre_out[:, p * 256 : (p + 1) * 256] = pre
            act = gelu_tanh(pre).astype(bf16)
            part = mm(act, second_block(second, p))
            total = part if total is None else total + part
        partial_out[...] = total.astype(bf16)

    return kernel


root = math.sqrt(2 / math.pi)


def mlp_back(grad, pre_ref, low_ref, first, second, place, outs):
    partial_out, bias_out, b_first_out, keep, *sends = outs
    grad_low = grad.astype(bf16)
    bias_out[...] = jnp.sum(grad, axis=0, keepdims=True)
    total = None
    for p in range(4):
        pre = pre_ref[:, p * 256 : (p + 1) * 256]
        square = pre * pre
        wave = jnp.tanh(root * pre * (1 + 0.044715 * square))
        half = 0.5 * (1 + wave)
        act = (pre * half).astype(bf16)
        slope = half + 0.5 * pre * (1 - wave * wave) * root * (1 + 3 * 0.044715 * square)
        w_second = second_block(second, p)
        grad_pre = mm_nt(grad_low, w_second) * slope
        grad_pre_low = grad_pre.astype(bf16)
        b_first_out[p ^ place[1]] = jnp.sum(grad_pre_low.astype(f32), axis=0, keepdims=True)
        part = mm_nt(grad_pre_low, first_block(first, p))
        total = part if total is None else total + part
        to = keep.at[p // 2] if p % 2 == 0 else sends[p // 2]
        grad_first = mm_tn(low_ref[...], grad_pre_low).astype(bf16)
        grad_second = mm_tn(act, grad_low).astype(bf16)
        for k in range(4):
            for j in range(2):
                to[k, j * 128 : (j + 1) * 128] = grad_first[
                    k * 128 : (k + 1) * 128, j * 128 : (j + 1) * 128
                ]
            to[k, 256:512] = grad_second[:, k * 128 : (k + 1) * 128]
    partial_out[...] = total.astype(bf16)


def norm_step(grad_out, gain, values):
    normed, scale = normalize(values)
    sums = row_join(
        [
            jnp.sum(grad_out * normed, axis=0, keepdims=True),
            jnp.sum(grad_out, axis=0, keepdims=True),
        ]
    )
    return norm_back(grad_out * gain, normed, scale), sums


def received_sum(mine, other):
    return mine[...].astype(f32) + row_join([other[128:], other[:128]]).astype(f32)


def top_kernel(place, *refs):
    grad, pre, low = refs[:3]
    first, second = Pieces(refs[3:4], place), Pieces(refs[4:5], place)
    mlp_back(grad[...], pre, low, first, second, place, refs[5:])


def lower_kernel(index):
    def kernel(place, *refs):
        grad_mid, mine, other, state, small_local, small_far, pre, low = refs[:8]
        first, second = Pieces(refs[8:9], place), Pieces(refs[9:10], place)
        grad_out, sums_out = refs[10:12]
        grad, sums = norm_step(
            received_sum(mine, other), small_row(small_local, small_far, 2 * (index + 1)), state[...]
        )
        sums_out[...] = sums
        grad = grad_mid[...] + grad
        grad_out[...] = grad
        mlp_back(grad, pre, low, first, second, place, refs[12:])

    return kernel


def attend_back_kernel(index):
    def kernel(place, *refs):
        mine, other, middle, grad_state, small_local, small_far = refs[:6]
        attn, w_out, q = refs[6:9]
        chunks, lse = refs[9:13], refs[13]
        grad_out, sums_out, gw_out, dq_out, keep, send = refs[14:]
        grad, sums = norm_step(
            received_sum(mine, other), small_row(small_local, small_far, 2 * index + 1), middle[...]
        )
        grad = grad_state[...] + grad
        grad_out[...] = grad
        sums_out[0:2] = sums
        sums_out[2:3] = jnp.sum(grad, axis=0, keepdims=True)
        grad_low = grad.astype(bf16)
        grad_attn = mm_nt(grad_low, w_out[...].reshape(256, 512)).astype(bf16)
        gw_out[...] = mm_tn(attn[...], grad_low).astype(bf16).reshape(4, 64, 512)
        own_mask = seen(place, 0)
        dq_all = []
        dk_all = [[] for j in range(4)]
        dv_all = [[] for j in range(4)]
        for head in range(4):
            low, high = head * 64, (head + 1) * 64
            query, grad_head = q[:, low:high], grad_attn[:, low:high]
            keys = [chunk[:, low:high] for chunk in chunks]
            row_dot = jnp.sum(
                grad_head.astype(f32) * attn[:, low:high].astype(f32), axis=1, keepdims=True
            )
            log_sum = lse[:, head : head + 1]
            parts = masked_scores(query, keys, own_mask, place)
            dq = None
            for j in range(4):
                probs = jnp.exp(parts[j] - log_sum)
                grad_probs = mm_nt(grad_head, chunks[j][:, 256 + low : 256 + high])
                grad_scores = (probs * (grad_probs - row_dot)).astype(bf16)
                part = mm(grad_scores, keys[j])
                dq = part if dq is None else dq + part
                dk_all[j].append(mm_tn(grad_scores, query) * 0.125)
                dv_all[j].append(mm_tn(probs.astype(bf16), grad_head))
            dq_all.append(dq * 0.125)
        dq_out[...] = lane_join(dq_all).astype(bf16)
        for j in range(4):
            to = keep if j % 2 == 0 else send
            to[j // 2, :, :256] = lane_join(dk_all[j]).astype(bf16)
            to[j // 2, :, 256:] = lane_join(dv_all[j]).astype(bf16)

    return kernel


def halve_kernel(place, keep, got, own_out, send_out):
    own_out[...] = (keep[0].astype(f32) + got[0].astype(f32)).astype(bf16)
    send_out[...] = (keep[1].astype(f32) + got[1].astype(f32)).astype(bf16)


def halve_groups_kernel(place, *refs):
    own_out, send_out = refs[-2:]
    start = 0
    for keep, one, two in zip(refs[:-2:3], refs[1:-2:3], refs[2:-2:3]):
        rows = keep.shape[2]
        for half, got, out in ((0, one, own_out), (1, two, send_out)):
            total = keep[half].astype(f32) + got[...].astype(f32)
            out[:, start : start + rows] = total.astype(bf16)
        start += rows


def quarter_in_order(place, own, got, out):
    for k in range(4):
        total = own[k].astype(f32) + got[k].astype(f32)
        out[(place[0] - k + 4) % 4] = total.astype(bf16)


def query_back_kernel(place, *refs):
    dq, dkv, got, low, w_ref, gw_ref = refs[:6]
    partial_out, b_out, keep, *sends, scratch = refs[6:]
    c = place[1]
    grad_kv = (dkv[...].astype(f32) + got[...].astype(f32)).astype(bf16)
    grad_qkv = lane_join([dq[...], grad_kv])
    partial_out[...] = mm_nt(grad_qkv, w_ref[...].reshape(512, 768)).astype(bf16)
    b_out[0:1] = jnp.sum(dq[...].astype(f32), axis=0, keepdims=True)
    b_out[1:2] = jnp.sum(grad_kv[:, 256:].astype(f32), axis=0, keepdims=True)
    scratch[...] = mm_tn(low[...], grad_qkv).astype(bf16).reshape(4, 4, 32, 768)
    for p in range(4):
        to = keep.at[p // 2] if p % 2 == 0 else sends[p // 2]
        for k in range(4):
            for tile in range(6):
                to[k, tile * 32 : (tile + 1) * 32] = scratch[
                    k, p ^ c, :, tile * 128 : (tile + 1) * 128
                ]
            to[k, 192:256] = gw_ref[p ^ c, :, k * 128 : (k + 1) * 128]


def last_quarter_kernel(place, own, got, sums, *outs):
    for k in range(4):
        outs[k][:256] = (own[k].astype(f32) + got[k].astype(f32)).astype(bf16)
        outs[k][256:] = sums[k].astype(bf16)


def last_total_kernel(place, own, one, two, three, out):
    total = own[...].astype(f32) + one[...].astype(f32)
    out[...] = (total + (two[...].astype(f32) + three[...].astype(f32))).astype(bf16)


def small_kernel(place, one, two, three, four, out):
    total = one[256:].astype(f32) + two[256:].astype(f32)
    out[...] = total + (three[256:].astype(f32) + four[256:].astype(f32))


def halve(place, groups, after=()):
    operands = []
    for keep, one, two in groups:
        operands += [keep, swap_core(one), swap_core(two)]
    rows = sum(group[0].shape[2] for group in groups)
    return run(halve_groups_kernel, [((4, rows, lanes), bf16)] * 2, place, operands, after=after)


def quarter(place, own, send, after=()):
    (both,) = run(quarter_in_order, [(own.shape, bf16)], place, [own, swap_x(send)], after=after)
    return both


def join_kernel(place, one, two, three, out):
    out[:512], out[512:1024], out[1024:] = one[...], two[...], three[...]


def collect(total):
    chip = swap_x(total)
    return [total, swap_core(total), chip, swap_core(chip)]


def fill(refs, scratch):
    for p in range(4):
        scratch[p] = refs[p][...].astype(f32)


def hidden_out_kernel(place, *refs):
    c = place[1]
    first_out, second_out, scratch = refs[-3:]
    fill(refs, scratch)
    for q in range(4):
        for j in range(2):
            column = (2 * q + j) * 128
            first_out[0, :, column : column + 128] = scratch[q ^ c, j * 128 : (j + 1) * 128]
        second_out[0, q * 256 : (q + 1) * 256] = scratch[q ^ c, 256:]


def heads_out_kernel(place, *refs):
    c = place[1]
    qkv_out, proj_out, scratch = refs[-3:]
    fill(refs, scratch)
    for q in range(4):
        for tile in range(6):
            column = (tile % 2) * 128
            qkv_out[0, tile // 2, q * 32 : (q + 1) * 32, column : column + 128] = scratch[
                q ^ c, tile * 32 : (tile + 1) * 32
            ]
        proj_out[0, q * 64 : (q + 1) * 64] = scratch[q ^ c, 192:]


def layer_out(kernel, rows, place, totals, layer, shapes, before, start, after):
    extra = list(before) + list(after)
    count = 1 + len(totals)

    def inner(*refs):
        kernel(*refs[:count], *refs[count + len(extra) :])

    def block(shape):
        at = (layer,) + (0,) * (len(shape) - 1)
        return pl.BlockSpec((1,) + tuple(shape[1:]), lambda i: at)

    return list(
        pl.pallas_call(
            inner,
            grid=(1,),
            out_shape=[jax.ShapeDtypeStruct(shape, f32) for shape in shapes],
            in_specs=[pl.BlockSpec(memory_space=pltpu.SMEM)]
            + [pl.BlockSpec((rows, lanes), lambda i: (start // rows, 0))] * 4
            + [pl.BlockSpec(memory_space=pl.ANY)] * len(extra),
            out_specs=[block(shape) for shape in shapes],
            scratch_shapes=[pltpu.VMEM((4, rows, lanes), f32)],
            input_output_aliases={count + i: i for i in range(len(before))},
            compiler_params=compiler_params(),
            cost_estimate=pl.CostEstimate(flops=2**20, bytes_accessed=1024, transcendentals=0),
        )(place, *totals, *extra)
    )


def hidden_out(place, totals, layer, shape_one, shape_two, before, start, after=()):
    shapes = (shape_one, shape_two)
    return layer_out(hidden_out_kernel, 512, place, totals, layer, shapes, before, start, after)


def heads_out(place, totals, layer, shape_one, shape_two, before, start, after=()):
    shapes = (shape_one, shape_two)
    return layer_out(heads_out_kernel, 256, place, totals, layer, shapes, before, start, after)


def last_kernel(place, *refs):
    grad_mid, mine, other, state, small_local, small_far = refs[:6]
    sums_in = refs[6]
    sums_mid, bias_mlp, b_query, b_first = refs[7:9], refs[9:11], refs[11:13], refs[13:15]
    grad_out, out = refs[15:]
    grad, sums = norm_step(received_sum(mine, other), small_row(small_local, small_far, 0), state[...])
    grad_out[...] = grad_mid[:128] + grad[:128]
    for layer in range(2):
        inner = sums if layer == 0 else sums_in[...]
        mid = sums_mid[layer]
        rows = [
            (2 * layer, inner[0:1]),
            (2 * layer + 1, mid[0:1]),
            (4 + 4 * layer, inner[1:2]),
            (5 + 4 * layer, mid[2:3]),
            (6 + 4 * layer, mid[1:2]),
            (7 + 4 * layer, bias_mlp[layer][...]),
        ]
        for k in range(4):
            for row, value in rows:
                out[k, row : row + 1] = value[:, k * 128 : (k + 1) * 128]
            for channel in range(2):
                for j in range(2):
                    row = 12 + 4 * layer + 2 * channel + j
                    out[k, row : row + 1] = b_query[layer][channel : channel + 1, j * 128 : (j + 1) * 128]
            for q in range(4):
                for j in range(2):
                    row = 20 + 8 * layer + 2 * q + j
                    out[k, row : row + 1] = b_first[layer][q, :, j * 128 : (j + 1) * 128]
    out[:, 36:] = jnp.zeros((4, 12, lanes), f32)


def turn(values, place_z, back):
    rows = values.shape[0]
    chunks = values.reshape(rows, 4, lanes)
    order = (place_z - jnp.arange(4)) % 4
    return jnp.concatenate(
        [lax.dynamic_slice_in_dim(values, order[k] * lanes, lanes, 1) for k in range(4)], axis=1
    )


def body_four(x_in, w_qkv, b_qv, w_proj, w_fc1, b_fc1, w_fc2, gains, biases, cotangent):
    z, c, t = lax.axis_index("shard"), lax.axis_index("ctx"), lax.axis_index("tp")
    place = jnp.stack([z, c, t]).astype(jnp.int32)
    flat = jnp.concatenate([array.reshape(-1) for array in (gains, biases, b_qv, b_fc1)])
    small = jnp.pad(flat, (0, 32 * lanes - flat.shape[0])).reshape(32, lanes)

    kinds = ("qkv", "proj", "first", "second", "first", "second")
    send = pack(
        place, kinds, (w_qkv, w_proj, w_fc1, w_fc2, w_fc1, w_fc2), (1, 1, 0, 0, 1, 1), whole_quarters=False
    )
    full = gather(send)
    local_a, send_a = pack(place, ("qkv", "proj", "small"), (w_qkv, w_proj, small), (0, 0, 0))
    pair_own = turn(jnp.concatenate([x_in[:, 0], cotangent[:, 0]]), z, False)
    pair_peer = swap_tp(pair_own)
    got_a = far_chunks(send_a)
    far_a = stack(place, got_a)
    chip_a = swap_x(far_a)
    group_a0 = [local_a, far_a, swap_core(far_a), chip_a, swap_core(chip_a)]
    small_parts = small_of(group_a0)
    parts = {
        "qkv": [pieces_of(group_a0, 192, 0), gathered_rows(full, 192, 0)],
        "proj": [pieces_of(group_a0, 64, 192), gathered_rows(full, 64, 192)],
        "first": [gathered_rows(full, 256, 256), gathered_rows(full, 256, 768)],
        "second": [gathered_rows(full, 256, 512), gathered_rows(full, 256, 1024)],
    }
    square, wide = (256, 512), (256, 256)
    saved = []
    for layer in range(2):
        source = [pair_own, pair_peer] if layer == 0 else [middle, partial, swap_tp(partial)]
        more = [(square, f32)] if layer == 0 else []
        state, low_in, q, kv, w_all, *passed = run(
            query_kernel(layer, layer == 0),
            [(square, f32), (square, bf16), (wide, bf16), (square, bf16), ((4, 4, 32, 768), bf16)] + more,
            place,
            source + small_parts + parts["qkv"][layer],
        )
        if layer == 0:
            g_all = passed[0]
        kv_chip = swap_x(kv)
        chunks = [kv, swap_core(kv), kv_chip, swap_core(kv_chip)]
        attn, lse, partial, w_out = run(
            functools.partial(attend_kernel, len(parts["proj"][layer])),
            [(wide, bf16), ((256, lanes), f32), (square, bf16), ((4, 64, 512), bf16)],
            place,
            [q] + chunks + parts["proj"][layer],
        )
        middle, low_mid, pre, partial = run(
            mlp_kernel(layer),
            [(square, f32), (square, bf16), ((256, 1024), f32), (square, bf16)],
            place,
            [state, partial, swap_tp(partial)] + small_parts + parts["first"][layer] + parts["second"][layer],
        )
        saved.append((state, low_in, q, chunks, w_all, attn, lse, w_out, middle, low_mid, pre))

    received = swap_tp(partial[128:]).astype(f32)
    output = None
    bias_last = jnp.concatenate([small_parts[0][0][0, 267:268], small_parts[1][0][:, 267]]).reshape(1, 512)
    output = middle[:128] + partial[:128].astype(f32) + received + bias_last.astype(f32)
    output = turn(output.astype(bf16), z, True)[:, None]

    hidden_outs = [
        (square, bf16),
        ((1, 512), f32),
        ((4, 1, 256), f32),
        ((2, 4, 512, lanes), bf16),
        ((4, 512, lanes), bf16),
        ((4, 512, lanes), bf16),
    ]
    sums_mid, bias_mlp, b_query, b_first = [0, 0], [0, 0], [0, 0], [0, 0]
    hidden = [None, None]
    for layer in (1, 0):
        state, low_in, q, chunks, w_all, attn, lse, w_out, middle, low_mid, pre = saved[layer]
        tail = [pre, low_mid] + parts["first"][layer] + parts["second"][layer]
        if layer == 1:
            grad_state = g_all
            partial, bias_mlp[1], b_first[1], *grads = run(
                top_kernel, hidden_outs, place, [grad_state] + tail
            )
        else:
            head_own, head_far = halve(place, [grads])
            grad_state, sums_in, partial, bias_mlp[0], b_first[0], *grads = run(
                lower_kernel(0),
                [(square, f32), ((2, 512), f32)] + hidden_outs,
                place,
                [grad_mid, partial, swap_tp(partial), saved[1][0]] + small_parts + tail,
                after=[head_own],
            )
        own, far = halve(place, [grads])
        behind = [own]
        if layer == 0:
            both = quarter(place, head_own, head_far, after=[own])
            heads_sum = lax.psum_scatter(both, "shard", scatter_dimension=0)
            behind = [both]
        grad_mid, sums_mid[layer], gw_out, dq, keep, send = run(
            attend_back_kernel(layer),
            [
                (square, f32),
                ((3, 512), f32),
                ((4, 64, 512), bf16),
                (wide, bf16),
                ((2, 256, 512), bf16),
                ((2, 256, 512), bf16),
            ],
            place,
            [partial, swap_tp(partial), middle, grad_state] + small_parts + [attn, w_out, q] + chunks + [lse],
            after=behind,
        )
        both = quarter(place, own, far, after=[keep])
        hidden[layer] = lax.psum_scatter(both, "shard", scatter_dimension=0)
        behind = [both]
        dkv, chip = run(halve_kernel, [(square, bf16)] * 2, place, [keep, swap_core(send)], after=behind)
        partial, b_query[layer], *grads = run(
            query_back_kernel,
            [
                (square, bf16),
                ((2, 256), f32),
                ((2, 4, 256, lanes), bf16),
                ((4, 256, lanes), bf16),
                ((4, 256, lanes), bf16),
            ],
            place,
            [dq, dkv, swap_x(chip), low_in, w_all, gw_out],
            scratch=[pltpu.VMEM((4, 4, 32, 768), bf16)],
            after=[output] if layer == 1 else [],
        )
    own, far = halve(place, [grads])
    grad_x, sums = run(
        last_kernel,
        [((128, 512), f32), ((4, 48, lanes), f32)],
        place,
        [grad_mid, partial, swap_tp(partial), saved[0][0]]
        + small_parts
        + [sums_in]
        + sums_mid
        + bias_mlp
        + b_query
        + b_first,
        after=[own],
    )
    pieces = run(last_quarter_kernel, [((304, lanes), bf16)] * 4, place, [own, swap_x(far), sums])
    grad_x = turn(grad_x, z, True)[:, None]
    (joined,) = run(
        join_kernel, [((1280, lanes), bf16)], place, [hidden[1], hidden[0], heads_sum], after=pieces[:1]
    )
    upper = collect(joined)
    got = [shift(pieces[k], 4 - k) for k in (1, 2, 3)]
    (last,) = run(
        last_total_kernel,
        [((304, lanes), bf16)],
        place,
        [pieces[0]] + got,
        after=upper[1:3],
    )
    last_parts = collect(last)
    outs_heads = heads_out(place, upper, 1, w_qkv.shape, w_proj.shape, [], 1024, after=[last])
    outs_hidden = hidden_out(place, upper, 1, w_fc1.shape, w_fc2.shape, [], 0, after=[last])
    grad_fc1, grad_fc2 = hidden_out(
        place, upper, 0, w_fc1.shape, w_fc2.shape, outs_hidden, 512, after=[last]
    )
    (total,) = run(small_kernel, [((48, lanes), f32)], place, last_parts, after=[grad_fc1])
    grad_gains = total[:4].reshape(gains.shape)
    grad_biases = total[4:12].reshape(biases.shape)
    rest_q = total[12:20].reshape(2, 2, 4, 64)
    rest_f = total[20:36].reshape(2, 16, 64)
    grad_b_qv = lax.dynamic_slice_in_dim(rest_q, z * 16, 16, 3)
    grad_b_fc1 = lax.dynamic_slice_in_dim(rest_f, z * 16, 16, 2)

    grad_qkv, grad_proj = heads_out(place, last_parts, 0, w_qkv.shape, w_proj.shape, outs_heads, 0, after=[grad_fc1])
    return (
        output, grad_x, grad_qkv, grad_b_qv, grad_proj, grad_fc1, grad_b_fc1, grad_fc2, grad_gains, grad_biases
    )


def body(*args):
    x_in, w_qkv, b_qv, w_proj, w_fc1 = args[:5]
    expected = ((128, 1, 512), (2, 3, 128, 256), (2, 2, 4, 16), (2, 256, 128), (2, 128, 1024))
    sizes = (lax.axis_size("shard"), lax.axis_size("ctx"), lax.axis_size("tp"))
    shapes = tuple(array.shape for array in (x_in, w_qkv, b_qv, w_proj, w_fc1))
    if sizes == (4, 4, 2) and shapes == expected:
        return body_four(*args)
    return body_any(*args)


def solution(mesh):
    return jax.shard_map(
        body,
        mesh=mesh,
        in_specs=(
            P(("ctx", "tp"), "shard", None),
            P(None, None, "shard", "tp"),
            P(None, None, "tp", "shard"),
            P(None, "tp", "shard"),
            P(None, "shard", "tp"),
            P(None, "tp", "shard"),
            P(None, "tp", "shard"),
            P(None, None, "shard"),
            P(None, None, "shard"),
            P(("ctx", "tp"), "shard", None),
        ),
        out_specs=(
            P(("ctx", "tp"), "shard", None),
            P(("ctx", "tp"), "shard", None),
            P(None, None, "shard", "tp"),
            P(None, None, "tp", "shard"),
            P(None, "tp", "shard"),
            P(None, "shard", "tp"),
            P(None, "tp", "shard"),
            P(None, "tp", "shard"),
            P(None, None, "shard"),
            P(None, None, "shard"),
        ),
        check_vma=False,
    )
```
